32 devices in a mesh: mp: 2 (over x), dp: 4 (over z), outer: 4 (over y, core).
Axes of the slice: x: 2, y: 2, z: 4, core: 2. Of those that a mesh axis runs over, the one named last changes fastest.
Arguments:
- inputs: bfloat16 [16, 2560, 1024], P(('dp', 'outer'), 'mp'), may hold values from -6 to 6
- cotangent: bfloat16 [16, 2560, 1024], P(('dp', 'outer'), 'mp'), may hold values from -6 to 6
- lengths: int32 [16, 12], P(('dp', 'outer')), may hold values from 1 to 1280, 2560 in all within a row
- project_master: float32 [1024, 16, 192], P('dp', 'mp'), may hold values from -0.1875 to 0.1875
- project_first: float32 [1024, 16, 192], P('dp', 'mp'), may hold values from -0.0007324219 to 0.0007324219
- project_second: float32 [1024, 16, 192], P('dp', 'mp'), may hold values from 1.0490417e-08 to 4.196167e-08
- mixing_master: float32 [16, 64, 1024], P('mp', None, 'dp'), may hold values from -1 to 1
- mixing_first: float32 [16, 64, 1024], P('mp', None, 'dp'), may hold values from -0.00010681152 to 0.00010681152
- mixing_second: float32 [16, 64, 1024], P('mp', None, 'dp'), may hold values from 2.384186e-10 to 9.536744e-10
- expand_master: float32 [1024, 4096], P('dp', 'mp'), may hold values from -0.1875 to 0.1875
- expand_first: float32 [1024, 4096], P('dp', 'mp'), may hold values from -0.00021362305 to 0.00021362305
- expand_second: float32 [1024, 4096], P('dp', 'mp'), may hold values from 9.536744e-10 to 3.8146974e-09
- shrink_master: float32 [4096, 1024], P('mp', 'dp'), may hold values from -0.09375 to 0.09375
- shrink_first: float32 [4096, 1024], P('mp', 'dp'), may hold values from -0.0004272461 to 0.0004272461
- shrink_second: float32 [4096, 1024], P('mp', 'dp'), may hold values from 3.8146974e-09 to 1.525879e-08
- norm_master: float32 [2, 1024], P(None, 'dp'), may hold values from -0.5 to 1.5, as said below
- norm_first: float32 [2, 1024], P(None, 'dp'), may hold values from -0.0014648438 to 0.0014648438
- norm_second: float32 [2, 1024], P(None, 'dp'), may hold values from 4.053116e-08 to 1.6212464e-07
Outputs:
- block_out: bfloat16 [16, 2560, 1024], P(('dp', 'outer'), 'mp')
- input_grad: float32 [16, 2560, 1024], P(('dp', 'outer'), 'mp')
- project_next: float32 [1024, 16, 192], P('dp', 'mp')
- project_mean: float32 [1024, 16, 192], P('dp', 'mp')
- project_square: float32 [1024, 16, 192], P('dp', 'mp')
- project_copy: bfloat16 [1024, 16, 192], P('dp', 'mp')
- mixing_next: float32 [16, 64, 1024], P('mp', None, 'dp')
- mixing_mean: float32 [16, 64, 1024], P('mp', None, 'dp')
- mixing_square: float32 [16, 64, 1024], P('mp', None, 'dp')
- mixing_copy: bfloat16 [16, 64, 1024], P('mp', None, 'dp')
- expand_next: float32 [1024, 4096], P('dp', 'mp')
- expand_mean: float32 [1024, 4096], P('dp', 'mp')
- expand_square: float32 [1024, 4096], P('dp', 'mp')
- expand_copy: bfloat16 [1024, 4096], P('dp', 'mp')
- shrink_next: float32 [4096, 1024], P('mp', 'dp')
- shrink_mean: float32 [4096, 1024], P('mp', 'dp')
- shrink_square: float32 [4096, 1024], P('mp', 'dp')
- shrink_copy: bfloat16 [4096, 1024], P('mp', 'dp')
- norm_next: float32 [2, 1024], P(None, 'dp')
- norm_mean: float32 [2, 1024], P(None, 'dp')
- norm_square: float32 [2, 1024], P(None, 'dp')
- norm_copy: bfloat16 [2, 1024], P(None, 'dp')
- grad_norm: float32 [], replicated
The draws below stay inside these ranges and needn't reach their ends.
Inputs may be any that keep to these rules, and one draw needn't show every extreme that they name: Each row's lengths sum to 2560 and the longest is 1280. `norm_master`: row 0 holds gains, row 1 biases.
All inputs are finite; a program needn't handle non-finite values.
Results may differ from the reference program's by a relative error of at most 0.003.
The reference program's roundings to bfloat16 on the way count: a program that leaves them out, or rounds other values in their place, can miss the bound.
Values may be sent and summed in bfloat16 or wider, within the bound.
A program may use at most 448 MiB of HBM per device.

```python
import math
import jax
import jax.numpy as jnp
import numpy as np
from jax import lax

D = 1024
H = 16
HD = 64
ROT = 32
FF = 4096
LEN = 2560
NSEQ = 12
QB = 512
STEP = 10
MAXLEN = 1280
ROWS = 16


def draw_norm_master(key, part):
    gain_key = jax.random.fold_in(key, 11)
    bias_key = jax.random.fold_in(key, 12)
    gains = jax.random.uniform(gain_key, (1, D), jnp.float32, 0.5, 1.5)
    biases = jax.random.uniform(bias_key, (1, D), jnp.float32, -0.5, 0.5)
    return jnp.concatenate([gains, biases], axis=0)


def block_levels(stream_key, shape, pieces, least, largest):
    level, own = 1.0, jax.random.fold_in(stream_key, 6)
    for axis_at, blocks in pieces:
        heights = jnp.exp(jax.random.uniform(jax.random.fold_in(own, axis_at), (blocks,), jnp.float32, least / len(pieces), largest / len(pieces)))
        level = level * jnp.repeat(heights, shape[axis_at] // blocks).reshape([-1 if axis == axis_at else 1 for axis in range(len(shape))])
    return level


def length_profile(amount, total, reach, lean):
    weights = [(1 << 20) // math.isqrt(standing ** lean) + 1 for standing in range(2, amount + 1)]
    surplus, given = total - reach - (amount - 1), [1] * (amount - 1)
    while surplus > 0:
        candidates = [i for i in range(amount - 1) if given[i] < reach]
        whole, remaining = sum([weights[i] for i in candidates]), surplus
        for i in candidates:
            more = min(reach - given[i], max(1, remaining * weights[i] // whole), surplus)
            given[i] = given[i] + more
            surplus = surplus - more
    return np.array([reach] + given)


def ragged_sizes(rng, count, total, limit, lean):
    if count == 2:
        one = jax.random.randint(rng, (), max(1, total - limit), min(limit, total - 1) + 1)
        return jnp.stack([one, total - one])
    sizes = jnp.asarray(length_profile(count, total, limit, lean), jnp.int32)
    couples = (count - 1) // 2
    source_of, sink = sizes[1:1 + 2 * couples:2], sizes[2:2 + 2 * couples:2]
    room = jnp.minimum(source_of - 1, limit - sink)
    moved = jax.random.randint(jax.random.fold_in(rng, 1), (couples,), 0, 1 << 20) % (room + 1)
    sizes = sizes.at[1:1 + 2 * couples:2].set(source_of - moved).at[2:2 + 2 * couples:2].set(sink + moved)
    return sizes[jax.random.permutation(jax.random.fold_in(rng, 2), count)]


def gaussian(stream_key, shape, width, limit, pieces=(), kind=jnp.bfloat16):
    level = block_levels(stream_key, shape, pieces, -0.22, 0.18) if pieces else 1.0
    entries = jax.random.normal(stream_key, shape, jnp.float32) * width * level
    return jnp.minimum(jnp.maximum(entries, -limit), limit).astype(kind)


def setup_inputs(seed: int = 0) -> dict:
    key_of = jax.random.split(jax.random.key(seed), 19)
    inputs = gaussian(key_of[0], (ROWS, LEN, D), 1.0, 6.0, ((0, 16), (1, 2)))
    cotangent = gaussian(key_of[1], (ROWS, LEN, D), 1.0, 6.0, ((0, 16), (1, 2)))
    lengths = jax.vmap(lambda own: ragged_sizes(own, NSEQ, LEN, MAXLEN, 2))(jax.random.split(key_of[2], ROWS)).reshape((ROWS, NSEQ)).astype(jnp.int32)
    project_master = gaussian(key_of[3], (D, H, 3 * HD), D ** -0.5, 0.1875, ((0, 4), (1, 2)), jnp.float32)
    project_first = gaussian(key_of[4], (D, H, 3 * HD), (0.1 * (D * FF) ** -0.5), 0.0007324219, ((0, 4), (1, 2)), jnp.float32)
    project_second = jnp.clip(jnp.exp(math.log(4.1961669694501325e-08) - 1.3862944 * jax.random.uniform(key_of[5], (D, H, 3 * HD), jnp.float32) ** block_levels(key_of[5], (D, H, 3 * HD), ((0, 4), (1, 2)), -0.2, 0.2)), 1.0490417423625331e-08, 4.1961669694501325e-08)
    mixing_master = gaussian(key_of[6], (H, HD, D), (D // 32) ** -0.5, 1.0, ((0, 2), (2, 4)), jnp.float32)
    mixing_first = gaussian(key_of[7], (H, HD, D), (0.015 * (D * FF) ** -0.5), 0.00010681152, ((0, 2), (2, 4)), jnp.float32)
    mixing_second = jnp.clip(jnp.exp(math.log(9.536743617033494e-10) - 1.3862944 * jax.random.uniform(key_of[8], (H, HD, D), jnp.float32) ** block_levels(key_of[8], (H, HD, D), ((0, 2), (2, 4)), -0.2, 0.2)), 2.3841859042583735e-10, 9.536743617033494e-10)
    expand_master = gaussian(key_of[9], (D, FF), D ** -0.5, 0.1875, ((0, 4), (1, 2)), jnp.float32)
    expand_first = gaussian(key_of[10], (D, FF), (0.03 * (D * FF) ** -0.5), 0.00021362305, ((0, 4), (1, 2)), jnp.float32)
    expand_second = jnp.clip(jnp.exp(math.log(3.814697446813398e-09) - 1.3862944 * jax.random.uniform(key_of[11], (D, FF), jnp.float32) ** block_levels(key_of[11], (D, FF), ((0, 4), (1, 2)), -0.2, 0.2)), 9.536743617033494e-10, 3.814697446813398e-09)
    shrink_master = gaussian(key_of[12], (FF, D), FF ** -0.5, 0.09375, ((0, 2), (1, 4)), jnp.float32)
    shrink_first = gaussian(key_of[13], (FF, D), (0.06 * (D * FF) ** -0.5), 0.0004272461, ((0, 2), (1, 4)), jnp.float32)
    shrink_second = jnp.clip(jnp.exp(math.log(1.525878978725359e-08) - 1.3862944 * jax.random.uniform(key_of[14], (FF, D), jnp.float32) ** block_levels(key_of[14], (FF, D), ((0, 2), (1, 4)), -0.2, 0.2)), 3.814697446813398e-09, 1.525878978725359e-08)
    norm_master = draw_norm_master(jax.random.fold_in(key_of[18], 71), 0)
    norm_first = gaussian(key_of[16], (2, D), (0.2 * (D * FF) ** -0.5), 0.0014648438, ((1, 4),), jnp.float32)
    norm_second = jnp.clip(jnp.exp(math.log(1.6212463549436507e-07) - 1.3862944 * jax.random.uniform(key_of[17], (2, D), jnp.float32) ** block_levels(key_of[17], (2, D), ((1, 4),), -0.2, 0.2)), 4.0531158873591266e-08, 1.6212463549436507e-07)
    return {"inputs": inputs, "cotangent": cotangent, "lengths": lengths, "project_master": project_master, "project_first": project_first, "project_second": project_second, "mixing_master": mixing_master, "mixing_first": mixing_first, "mixing_second": mixing_second, "expand_master": expand_master, "expand_first": expand_first, "expand_second": expand_second, "shrink_master": shrink_master, "shrink_first": shrink_first, "shrink_second": shrink_second, "norm_master": norm_master, "norm_first": norm_first, "norm_second": norm_second}


norm_epsilon = 1e-05
beta_one = 0.9
beta_two = 0.95
adam_epsilon = 1e-08
decay_rate = 0.1
clip_level = 1.0
masked_value = -1e+30

@jax.custom_vjp
def low(v):
    return lax.optimization_barrier(v.astype(jnp.bfloat16)).astype(jnp.float32)

@jax.custom_vjp
def low_back(v):
    return v

def low_keep(v):
    return (low(v), None)

def low_pass(kept, grad):
    return (grad,)

def back_keep(v):
    return (v, None)

def back_low(kept, grad):
    return (low(grad),)
low.defvjp(low_keep, low_pass)
low_back.defvjp(back_keep, back_low)

def layout(sizes_row, count):
    ends = jnp.cumsum(sizes_row).astype(jnp.int32)
    places = jnp.arange(count, dtype=jnp.int32)
    passed = (ends[None, :] <= places[:, None]).astype(jnp.int32)
    segment = lax.optimization_barrier(jnp.sum(passed, axis=1)).astype(jnp.int32)
    begins = lax.optimization_barrier(jnp.sum(passed * sizes_row[None, :], axis=1)).astype(jnp.int32)
    return (segment, places - begins)

def rotary(vectors, places, direction):
    half_rot = ROT // 2
    counter = jnp.arange(half_rot, dtype=jnp.float32)
    frequency = jnp.exp(counter * (-2.0 * math.log(10000.0) / ROT))
    angles = places.astype(jnp.float32)[:, None] * frequency[None, :] * direction
    cosine = jnp.cos(angles)[:, None, :]
    sine = jnp.sin(angles)[:, None, :]
    first = vectors[..., :half_rot]
    second = vectors[..., half_rot:ROT]
    return jnp.concatenate([first * cosine - second * sine, second * cosine + first * sine, vectors[..., ROT:]], axis=-1)

def attend(query, keys, values, segment):
    count = query.shape[0]
    blocks = count // QB
    index = jnp.arange(count, dtype=jnp.int32)

    def score_block(items):
        block_query, block_segment, block_index = items
        raw = jnp.einsum('qhd,khd->hqk', block_query, keys, precision=lax.Precision.HIGHEST)
        scores = low_back(raw * HD ** (-0.5))
        allowed = (block_segment[:, None] == segment[None, :]) & (index[None, :] <= block_index[:, None])
        masked = jnp.where(allowed[None], scores, masked_value)
        top = lax.optimization_barrier(jnp.max(masked, axis=2, keepdims=True))
        shifted = jnp.exp(masked - top)
        shares = shifted / lax.optimization_barrier(jnp.sum(shifted, axis=2, keepdims=True))
        return jnp.einsum('hqk,khd->qhd', low(shares), values, precision=lax.Precision.HIGHEST)
    parts = lax.map(jax.checkpoint(score_block), (query.reshape(blocks, QB, H, HD), segment.reshape(blocks, QB), index.reshape(blocks, QB)))
    return parts.reshape(count, H, HD)

def row_forward(row_input, segment, places, project_weight, mixing_weight, expand_weight, shrink_weight, norm_weight):
    mean = lax.optimization_barrier(jnp.mean(row_input, axis=1, keepdims=True))
    centred = row_input - mean
    spread = lax.optimization_barrier(jnp.mean(centred * centred, axis=1, keepdims=True))
    normed = centred * lax.rsqrt(spread + norm_epsilon)
    hidden = low(normed * norm_weight[0] + norm_weight[1])
    projected = low_back(jnp.einsum('td,dhe->the', hidden, project_weight, precision=lax.Precision.HIGHEST))
    query = low(rotary(projected[..., :HD], places, 1.0))
    keys = low(rotary(projected[..., HD:2 * HD], places, 1.0))
    values = low(projected[..., 2 * HD:])
    mixed = low(low_back(attend(query, keys, values, segment)))
    attn_part = jnp.einsum('the,hed->td', mixed, mixing_weight, precision=lax.Precision.HIGHEST)
    lifted = low_back(jnp.dot(hidden, expand_weight, precision=lax.Precision.HIGHEST))
    activated = low(jax.nn.gelu(lifted, approximate=True))
    return row_input + attn_part + jnp.dot(activated, shrink_weight, precision=lax.Precision.HIGHEST)

def adam_update(master, first, second, gradient, rate, decay):
    first_new = beta_one * first + (1.0 - beta_one) * gradient
    second_new = beta_two * second + (1.0 - beta_two) * gradient * gradient
    first_hat = first_new / (1.0 - beta_one ** STEP)
    second_hat = second_new / (1.0 - beta_two ** STEP)
    master_new = master - rate * (first_hat / (jnp.sqrt(second_hat) + adam_epsilon) + decay * master)
    return (master_new, first_new, second_new, master_new.astype(jnp.bfloat16))

def reference(inputs, cotangent, lengths, project_master, project_first, project_second, mixing_master, mixing_first, mixing_second, expand_master, expand_first, expand_second, shrink_master, shrink_first, shrink_second, norm_master, norm_first, norm_second):
    masters = (project_master, mixing_master, expand_master, shrink_master, norm_master)

    def step_row(totals, items):
        row_input, row_back, sizes_row = items
        segment, places = layout(sizes_row, LEN)

        def forward(values_in, weight_p, weight_o, weight_u, weight_s, weight_n):
            return row_forward(values_in, segment, places, low(weight_p), low(weight_o), low(weight_u), low(weight_s), low(weight_n))
        result, pull = jax.vjp(forward, row_input.astype(jnp.float32), *masters)
        gradients = pull(row_back.astype(jnp.float32))
        summed = tuple((total + item for total, item in zip(totals, gradients[1:])))
        return (summed, (result.astype(jnp.bfloat16), gradients[0]))
    zeros = tuple((jnp.zeros(item.shape, jnp.float32) for item in masters))
    sums, (block_out, input_grad) = lax.scan(step_row, zeros, (inputs, cotangent, lengths))
    square = jnp.sum(sums[0] * sums[0]) + jnp.sum(sums[1] * sums[1]) + jnp.sum(sums[2] * sums[2]) + jnp.sum(sums[3] * sums[3]) + jnp.sum(sums[4] * sums[4])
    grad_norm = jnp.sqrt(square)
    factor = clip_level / jnp.maximum(grad_norm, clip_level)
    project_out = adam_update(project_master, project_first, project_second, factor * sums[0], D ** (-0.5), decay_rate)
    mixing_out = adam_update(mixing_master, mixing_first, mixing_second, factor * sums[1], (D // 32) ** (-0.5), decay_rate)
    expand_out = adam_update(expand_master, expand_first, expand_second, factor * sums[2], D ** (-0.5), decay_rate)
    shrink_out = adam_update(shrink_master, shrink_first, shrink_second, factor * sums[3], FF ** (-0.5), decay_rate)
    norm_out = adam_update(norm_master, norm_first, norm_second, factor * sums[4], 0.3, 0.0)
    return (block_out, input_grad, project_out[0], project_out[1], project_out[2], project_out[3], mixing_out[0], mixing_out[1], mixing_out[2], mixing_out[3], expand_out[0], expand_out[1], expand_out[2], expand_out[3], shrink_out[0], shrink_out[1], shrink_out[2], shrink_out[3], norm_out[0], norm_out[1], norm_out[2], norm_out[3], grad_norm)
```

```python
from functools import partial
import math

import jax
import jax.numpy as jnp
from jax import lax
from jax.experimental import pallas as pl
from jax.experimental.pallas import tpu as pltpu
from jax.sharding import PartitionSpec as P

D = 1024
HD = 64
ROT = 32
FF = 4096
STEP = 10


norm_epsilon = 1e-05
beta_one = 0.9
beta_two = 0.95
adam_epsilon = 1e-08
decay_rate = 0.1
clip_level = 1.0
masked_value = -1e30


def layout(sizes_row, count):
    number = jnp.arange(sizes_row.shape[0], dtype=jnp.int32)
    ends = jnp.sum(jnp.where(number[None, :] <= number[:, None], sizes_row[None, :], 0), axis=1)
    tokens = jnp.arange(count, dtype=jnp.int32)
    passed = (ends[:, None] <= tokens[None, :]).astype(jnp.int32)
    begins = jnp.sum(passed * sizes_row[:, None], axis=0)
    return (begins, tokens - begins)


def turns(places):
    half_rot = ROT // 2
    counter = jnp.arange(half_rot, dtype=jnp.float32)
    frequency = jnp.exp(counter * (-2.0 * math.log(10000.0) / ROT))
    angles = places.astype(jnp.float32)[None, :] * frequency[:, None]
    return jnp.cos(angles), jnp.sin(angles)


BQ = 256
BK = 256

def attend_kernel(together, first_block, proj_ref, back_ref, start_ref, cos_ref, sin_ref,
                  mixed_ref, grad_ref, q_ref, kt_ref, vt_ref, k_ref, v_ref, dk_ref, dv_ref,
                  shifted_ref, share_grad_ref, top_ref):
    count = proj_ref.shape[1]
    half = ROT // 2
    cosine, sine = cos_ref[...], sin_ref[...]
    scale = HD ** (-0.5)
    for h in range(together):
        base = h * 3 * HD
        def turned(at):
            a = proj_ref[at:at + half]
            b = proj_ref[at + half:at + ROT]
            return jnp.concatenate(
                [a * cosine - b * sine, b * cosine + a * sine, proj_ref[at + ROT:at + HD]], axis=0
            ).astype(jnp.bfloat16)
        q_ref[h] = (turned(base).astype(jnp.float32) * scale).astype(jnp.bfloat16)
        keys = turned(base + HD)
        values = proj_ref[base + 2 * HD:base + 3 * HD].astype(jnp.bfloat16)
        kt_ref[h] = keys
        vt_ref[h] = values
        k_ref[h] = keys.T
        v_ref[h] = values.T
    dk_ref[...] = jnp.zeros_like(dk_ref)
    dv_ref[...] = jnp.zeros_like(dv_ref)
    key_at = lax.broadcasted_iota(jnp.int32, (BK, BQ), 0)
    query_at = lax.broadcasted_iota(jnp.int32, (1, BQ), 1)
    nt = (((1,), (1,)), ((), ()))

    def query_block(i, _):
        columns = pl.ds(pl.multiple_of(i * BQ, BQ), BQ)
        start = start_ref[:, columns]
        own = query_at + i * BQ
        lowest = first_block[i]
        queries = [q_ref[h, :, columns] for h in range(together)]
        backs = [back_ref[h * HD:(h + 1) * HD, columns] for h in range(together)]

        def scores(j, carry):
            rows = pl.ds(pl.multiple_of(j * BK, BK), BK)
            allowed = (key_at >= start - j * BK) & (key_at <= own - j * BK)
            out = []
            for h in range(together):
                top, total, inner = carry[h]
                raw = jnp.dot(k_ref[h, rows, :], queries[h], preferred_element_type=jnp.float32)
                share_grad = jnp.dot(v_ref[h, rows, :], backs[h], preferred_element_type=jnp.float32)
                masked = jnp.where(allowed, raw, masked_value)
                here = jnp.max(masked, axis=0, keepdims=True)
                shifted = jnp.exp(masked - here)
                shifted_ref[h, j] = shifted
                share_grad_ref[h, j] = share_grad
                top_ref[h, j] = here
                new = jnp.maximum(top, here)
                old_by, here_by = jnp.exp(top - new), jnp.exp(here - new)
                total = total * old_by + jnp.sum(shifted, axis=0, keepdims=True) * here_by
                inner = inner * old_by + jnp.sum(shifted * share_grad, axis=0, keepdims=True) * here_by
                out.append((new, total, inner))
            return tuple(out)

        zero = jnp.zeros((1, BQ), jnp.float32)
        empty = (jnp.full((1, BQ), masked_value, jnp.float32), zero, zero)
        stats = lax.fori_loop(lowest, i + 1, scores, (empty,) * together)
        inverse = [1.0 / s[1] for s in stats]
        inners = [s[2] * r for s, r in zip(stats, inverse)]

        def sums(j, carry):
            rows = pl.ds(pl.multiple_of(j * BK, BK), BK)
            out = []
            for h in range(together):
                mixed, dq = carry[h]
                by = jnp.exp(top_ref[h, j] - stats[h][0]) * inverse[h]
                probs = shifted_ref[h, j] * by
                shares = probs.astype(jnp.bfloat16)
                score_grad = (probs * (share_grad_ref[h, j] - inners[h])).astype(jnp.bfloat16)
                mixed = mixed + jnp.dot(vt_ref[h, :, rows], shares, preferred_element_type=jnp.float32)
                dq = dq + jnp.dot(kt_ref[h, :, rows], score_grad, preferred_element_type=jnp.float32)
                dv_ref[h, :, rows] += lax.dot_general(backs[h], shares, nt, preferred_element_type=jnp.float32)
                dk_ref[h, :, rows] += lax.dot_general(queries[h], score_grad, nt, preferred_element_type=jnp.float32)
                out.append((mixed, dq))
            return tuple(out)

        nothing = jnp.zeros((HD, BQ), jnp.float32)
        results = lax.fori_loop(lowest, i + 1, sums, ((nothing, nothing),) * together)
        cos_here, sin_here = cos_ref[:, columns], sin_ref[:, columns]
        for h in range(together):
            mixed, dq = results[h]
            mixed_ref[h * HD:(h + 1) * HD, columns] = mixed.astype(jnp.bfloat16)
            dq = dq * scale
            a, b = dq[:half], dq[half:ROT]
            grad_ref[h * 3 * HD:h * 3 * HD + HD, columns] = jnp.concatenate(
                [a * cos_here + b * sin_here, b * cos_here - a * sin_here, dq[ROT:]], axis=0
            ).astype(jnp.bfloat16)
        return 0

    lax.fori_loop(0, count // BQ, query_block, 0)
    for h in range(together):
        base = h * 3 * HD + HD
        a, b = dk_ref[h, :half], dk_ref[h, half:ROT]
        grad_ref[base:base + HD] = jnp.concatenate(
            [a * cosine + b * sine, b * cosine - a * sine, dk_ref[h, ROT:]], axis=0
        ).astype(jnp.bfloat16)
        grad_ref[base + HD:base + 2 * HD] = dv_ref[h].astype(jnp.bfloat16)


def attend(projected, back, start, cosine, sine):
    heads = back.shape[0] // HD
    count = back.shape[1]
    together = 2 if heads % 2 == 0 else 1
    blocks = count // BK
    first_block = start[0, ::BQ] // BK
    half = ROT // 2
    whole = lambda rows: pl.BlockSpec((rows, count), lambda g, *_: (0, 0))
    mine = lambda rows: pl.BlockSpec((rows, count), lambda g, *_: (g, 0))
    pairs = heads * blocks * (blocks + 1) // 4
    return pl.pallas_call(
        partial(attend_kernel, together),
        grid_spec=pltpu.PrefetchScalarGridSpec(
            num_scalar_prefetch=1,
            grid=(heads // together,),
            in_specs=[mine(together * 3 * HD), mine(together * HD), whole(1), whole(half), whole(half)],
            out_specs=[mine(together * HD), mine(together * 3 * HD)],
            scratch_shapes=[
                pltpu.VMEM((together, HD, count), jnp.bfloat16),
                pltpu.VMEM((together, HD, count), jnp.bfloat16),
                pltpu.VMEM((together, HD, count), jnp.bfloat16),
                pltpu.VMEM((together, count, HD), jnp.bfloat16),
                pltpu.VMEM((together, count, HD), jnp.bfloat16),
                pltpu.VMEM((together, HD, count), jnp.float32),
                pltpu.VMEM((together, HD, count), jnp.float32),
                pltpu.VMEM((together, blocks, BK, BQ), jnp.float32),
                pltpu.VMEM((together, blocks, BK, BQ), jnp.float32),
                pltpu.VMEM((together, blocks, 1, BQ), jnp.float32),
            ],
        ),
        out_shape=[
            jax.ShapeDtypeStruct((heads * HD, count), jnp.bfloat16),
            jax.ShapeDtypeStruct((heads * 3 * HD, count), jnp.bfloat16),
        ],
        compiler_params=pltpu.CompilerParams(vmem_limit_bytes=48 * 2**20),
        cost_estimate=pl.CostEstimate(flops=pairs * 12 * BK * BQ * HD, bytes_accessed=heads * count * HD * 22, transcendentals=pairs * BK * BQ),
    )(first_block, projected, back, start, cosine, sine)


def layer_norm(rows_in, gain, bias):
    mean = jnp.mean(rows_in, axis=1, keepdims=True)
    centred = rows_in - mean
    spread = jnp.mean(centred * centred, axis=1, keepdims=True)
    normed = centred * lax.rsqrt(spread + norm_epsilon)
    return normed * gain + bias


def adam_update(master, first, second, gradient, rate, decay):
    first_new = beta_one * first + (1.0 - beta_one) * gradient
    second_new = beta_two * second + (1.0 - beta_two) * gradient * gradient
    first_hat = first_new / (1.0 - beta_one**STEP)
    second_hat = second_new / (1.0 - beta_two**STEP)
    master_new = master - rate * (
        first_hat / (jnp.sqrt(second_hat) + adam_epsilon) + decay * master
    )
    return (master_new, first_new, second_new, master_new.astype(jnp.bfloat16))


def local(
    inputs,
    cotangent,
    lengths,
    project_master,
    project_first,
    project_second,
    mixing_master,
    mixing_first,
    mixing_second,
    expand_master,
    expand_first,
    expand_second,
    shrink_master,
    shrink_first,
    shrink_second,
    norm_master,
    norm_first,
    norm_second,
):
    project_weight, mixing_weight, expand_weight, shrink_weight, norm_weight = (
        lax.all_gather(project_master.astype(jnp.bfloat16), "dp", axis=0, tiled=True),
        lax.all_gather(mixing_master.astype(jnp.bfloat16), "dp", axis=2, tiled=True),
        lax.all_gather(expand_master.astype(jnp.bfloat16), "dp", axis=0, tiled=True),
        lax.all_gather(shrink_master.astype(jnp.bfloat16), "dp", axis=1, tiled=True),
        lax.all_gather(norm_master.astype(jnp.bfloat16), "dp", axis=1, tiled=True),
    )
    gain = norm_weight[0].astype(jnp.float32)
    bias = norm_weight[1].astype(jnp.float32)
    rows_local = inputs[0].astype(jnp.float32)
    shaped, norm_pull = jax.vjp(layer_norm, rows_local, gain, bias)
    hidden_local = shaped.astype(jnp.bfloat16)
    hidden = lax.all_gather(hidden_local, "mp", axis=0, tiled=True)
    count = hidden.shape[0]
    begins, places = layout(lengths[0], count)
    cosine, sine = turns(places)
    heads_here = project_weight.shape[1]
    project_flat = project_weight.reshape(project_weight.shape[0], heads_here * 3 * HD)
    mixing_flat = mixing_weight.reshape(heads_here * HD, mixing_weight.shape[2])
    back_rows = lax.all_gather(cotangent[0], "mp", axis=0, tiled=True)
    projected = jnp.einsum("td,de->et", hidden, project_flat, preferred_element_type=jnp.float32)
    mixed_back = jnp.einsum(
        "td,fd->ft", back_rows, mixing_flat, preferred_element_type=jnp.float32
    ).astype(jnp.bfloat16)
    mixed, projected_grad = attend(projected, mixed_back, begins[None, :], cosine, sine)
    lifted = jnp.dot(hidden, expand_weight, preferred_element_type=jnp.float32)
    activated = jax.nn.gelu(lifted, approximate=True).astype(jnp.bfloat16)
    branch = lax.psum_scatter(
        jnp.einsum("ft,fd->td", mixed, mixing_flat, preferred_element_type=jnp.float32)
        + jnp.dot(activated, shrink_weight, preferred_element_type=jnp.float32),
        "mp",
        scatter_dimension=0,
        tiled=True,
    )
    block_out = (rows_local + branch).astype(jnp.bfloat16)[None]
    back_local = cotangent[0].astype(jnp.float32)
    shrink_gradient = jnp.einsum(
        "tf,td->fd", activated, back_rows, preferred_element_type=jnp.float32
    )
    active_grad = jnp.einsum(
        "td,fd->tf", back_rows, shrink_weight, preferred_element_type=jnp.float32
    )
    gelu_pull = jax.vjp(partial(jax.nn.gelu, approximate=True), lifted)[1]
    lifted_grad = gelu_pull(active_grad)[0].astype(jnp.bfloat16)
    expand_gradient = jnp.einsum(
        "td,tf->df", hidden, lifted_grad, preferred_element_type=jnp.float32
    )
    mixing_gradient = jnp.einsum(
        "ft,td->fd", mixed, back_rows, preferred_element_type=jnp.float32
    ).reshape(mixing_weight.shape)
    project_gradient = jnp.einsum(
        "td,et->de", hidden, projected_grad, preferred_element_type=jnp.float32
    ).reshape(project_weight.shape)
    hidden_grad = lax.psum_scatter(
        jnp.einsum("et,de->td", projected_grad, project_flat, preferred_element_type=jnp.float32)
        + jnp.einsum("tf,df->td", lifted_grad, expand_weight, preferred_element_type=jnp.float32),
        "mp",
        scatter_dimension=0,
        tiled=True,
    )
    rows_grad, gain_grad, bias_grad = norm_pull(hidden_grad)
    input_grad = (back_local + rows_grad)[None]
    norm_part = jnp.stack([gain_grad, bias_grad])
    project_gradient, mixing_gradient, expand_gradient, shrink_gradient, norm_piece = (
        lax.psum_scatter(project_gradient, "dp", scatter_dimension=0, tiled=True),
        lax.psum_scatter(mixing_gradient, "dp", scatter_dimension=2, tiled=True),
        lax.psum_scatter(expand_gradient, "dp", scatter_dimension=0, tiled=True),
        lax.psum_scatter(shrink_gradient, "dp", scatter_dimension=1, tiled=True),
        lax.psum_scatter(norm_part, "dp", scatter_dimension=1, tiled=True),
    )
    project_gradient, mixing_gradient, expand_gradient, shrink_gradient, norm_piece = lax.psum(
        (project_gradient, mixing_gradient, expand_gradient, shrink_gradient, norm_piece), "outer"
    )
    norm_gradient = lax.psum(norm_piece, "mp")
    head_first = (lax.axis_index("mp") == 0).astype(jnp.float32)
    own_square = (
        jnp.sum(project_gradient * project_gradient)
        + jnp.sum(mixing_gradient * mixing_gradient)
        + jnp.sum(expand_gradient * expand_gradient)
        + jnp.sum(shrink_gradient * shrink_gradient)
        + head_first * jnp.sum(norm_gradient * norm_gradient)
    )
    total_square = lax.psum(own_square, ("mp", "dp"))
    grad_norm = jnp.sqrt(total_square)
    factor = clip_level / jnp.maximum(grad_norm, clip_level)
    project_out = adam_update(
        project_master,
        project_first,
        project_second,
        factor * project_gradient,
        D ** (-0.5),
        decay_rate,
    )
    mixing_out = adam_update(
        mixing_master,
        mixing_first,
        mixing_second,
        factor * mixing_gradient,
        (D // 32) ** (-0.5),
        decay_rate,
    )
    expand_out = adam_update(
        expand_master,
        expand_first,
        expand_second,
        factor * expand_gradient,
        D ** (-0.5),
        decay_rate,
    )
    shrink_out = adam_update(
        shrink_master,
        shrink_first,
        shrink_second,
        factor * shrink_gradient,
        FF ** (-0.5),
        decay_rate,
    )
    norm_out = adam_update(norm_master, norm_first, norm_second, factor * norm_gradient, 0.3, 0.0)
    return (
        block_out,
        input_grad,
        project_out[0],
        project_out[1],
        project_out[2],
        project_out[3],
        mixing_out[0],
        mixing_out[1],
        mixing_out[2],
        mixing_out[3],
        expand_out[0],
        expand_out[1],
        expand_out[2],
        expand_out[3],
        shrink_out[0],
        shrink_out[1],
        shrink_out[2],
        shrink_out[3],
        norm_out[0],
        norm_out[1],
        norm_out[2],
        norm_out[3],
        grad_norm,
    )


def solution(mesh):
    in_specs = (
        P(("dp", "outer"), "mp", None),
        P(("dp", "outer"), "mp", None),
        P(("dp", "outer"), None),
        P("dp", "mp", None),
        P("dp", "mp", None),
        P("dp", "mp", None),
        P("mp", None, "dp"),
        P("mp", None, "dp"),
        P("mp", None, "dp"),
        P("dp", "mp"),
        P("dp", "mp"),
        P("dp", "mp"),
        P("mp", "dp"),
        P("mp", "dp"),
        P("mp", "dp"),
        P(None, "dp"),
        P(None, "dp"),
        P(None, "dp"),
    )
    out_specs = (
        P(("dp", "outer"), "mp", None),
        P(("dp", "outer"), "mp", None),
        P("dp", "mp", None),
        P("dp", "mp", None),
        P("dp", "mp", None),
        P("dp", "mp", None),
        P("mp", None, "dp"),
        P("mp", None, "dp"),
        P("mp", None, "dp"),
        P("mp", None, "dp"),
        P("dp", "mp"),
        P("dp", "mp"),
        P("dp", "mp"),
        P("dp", "mp"),
        P("mp", "dp"),
        P("mp", "dp"),
        P("mp", "dp"),
        P("mp", "dp"),
        P(None, "dp"),
        P(None, "dp"),
        P(None, "dp"),
        P(None, "dp"),
        P(),
    )
    return jax.shard_map(local, mesh=mesh, in_specs=in_specs, out_specs=out_specs, check_vma=False)
```

```python
from functools import partial
import math

import jax
import jax.numpy as jnp
from jax import lax
from jax.experimental import pallas as pl
from jax.experimental.pallas import tpu as pltpu
from jax.sharding import PartitionSpec as P

D = 1024
HD = 64
ROT = 32
FF = 4096
STEP = 10


norm_epsilon = 1e-05
beta_one = 0.9
beta_two = 0.95
adam_epsilon = 1e-08
decay_rate = 0.1
clip_level = 1.0
masked_value = -1e30


def layout(sizes_row, count):
    number = jnp.arange(sizes_row.shape[0], dtype=jnp.int32)
    ends = jnp.sum(jnp.where(number[None, :] <= number[:, None], sizes_row[None, :], 0), axis=1)
    tokens = jnp.arange(count, dtype=jnp.int32)
    passed = (ends[:, None] <= tokens[None, :]).astype(jnp.int32)
    begins = jnp.sum(passed * sizes_row[:, None], axis=0)
    return (begins, tokens - begins)


def turns(places):
    half_rot = ROT // 2
    counter = jnp.arange(half_rot, dtype=jnp.float32)
    frequency = jnp.exp(counter * (-2.0 * math.log(10000.0) / ROT))
    angles = places.astype(jnp.float32)[None, :] * frequency[:, None]
    return jnp.cos(angles), jnp.sin(angles)


BQ = 256
BK = 256


def attend_kernel(together, parts, *refs):
    facts = refs[0]
    projected_refs = refs[1 : 1 + parts]
    back_refs = refs[1 + parts : 1 + 2 * parts]
    start_ref, cos_ref, sin_ref = refs[1 + 2 * parts : 4 + 2 * parts]
    mixed_refs = refs[4 + 2 * parts : 4 + 3 * parts]
    grad_refs = refs[4 + 3 * parts : 4 + 4 * parts]
    (
        query_ref,
        key_columns_ref,
        value_columns_ref,
        key_ref,
        value_ref,
        back_ref,
        query_grad_ref,
        key_grad_ref,
        value_grad_ref,
        shifted_ref,
        share_grad_ref,
        top_ref,
    ) = refs[4 + 4 * parts :]
    width = projected_refs[0].shape[1]
    count = width * parts
    blocks = count // BQ
    turn = facts[blocks]
    half = ROT // 2
    scale = HD ** (-0.5)
    nt = (((1,), (1,)), ((), ()))

    def place_of(part):
        if parts == 1:
            return pl.ds(0, width)
        block = lax.rem(part * (blocks // parts) + blocks - turn, blocks)
        return pl.ds(pl.multiple_of(block * BQ, BQ), width)

    for part in range(parts):
        columns = slice(part * width, (part + 1) * width)
        cosine, sine = cos_ref[:, place_of(part)], sin_ref[:, place_of(part)]
        projected_ref = projected_refs[part]

        def turned(at):
            first = projected_ref[at : at + half]
            second = projected_ref[at + half : at + ROT]
            return jnp.concatenate(
                [
                    first * cosine - second * sine,
                    second * cosine + first * sine,
                    projected_ref[at + ROT : at + HD],
                ],
                axis=0,
            ).astype(jnp.bfloat16)

        for h in range(together):
            base = h * 3 * HD
            query_ref[h, :, columns] = (turned(base).astype(jnp.float32) * scale).astype(
                jnp.bfloat16
            )
            keys = turned(base + HD)
            values = projected_ref[base + 2 * HD : base + 3 * HD].astype(jnp.bfloat16)
            key_columns_ref[h, :, columns] = keys
            value_columns_ref[h, :, columns] = values
            key_ref[h, columns] = keys.T
            value_ref[h, columns] = values.T
            back_ref[h, :, columns] = back_refs[part][h * HD : (h + 1) * HD]
    key_grad_ref[...] = jnp.zeros_like(key_grad_ref)
    value_grad_ref[...] = jnp.zeros_like(value_grad_ref)
    key_at = lax.broadcasted_iota(jnp.int32, (BK, BQ), 0)
    query_at = lax.broadcasted_iota(jnp.int32, (1, BQ), 1)

    def stored(block):
        if parts == 1:
            return pl.ds(pl.multiple_of(block * BQ, BQ), BQ)
        return pl.ds(pl.multiple_of(lax.rem(block + turn, blocks) * BQ, BQ), BQ)

    def query_block(i, _):
        columns = stored(i)
        start = start_ref[:, pl.ds(pl.multiple_of(i * BQ, BQ), BQ)]
        own = query_at + i * BQ
        lowest = facts[i]
        queries = [query_ref[h, :, columns] for h in range(together)]
        backs = [back_ref[h, :, columns] for h in range(together)]

        def scores(j, carry):
            rows = stored(j)
            allowed = (key_at >= start - j * BK) & (key_at <= own - j * BK)
            out = []
            for h in range(together):
                top, total, inner = carry[h]
                raw = jnp.dot(key_ref[h, rows, :], queries[h], preferred_element_type=jnp.float32)
                share_grad = jnp.dot(
                    value_ref[h, rows, :], backs[h], preferred_element_type=jnp.float32
                )
                masked = jnp.where(allowed, raw, masked_value)
                here = jnp.max(masked, axis=0, keepdims=True)
                shifted = jnp.exp(masked - here)
                shifted_ref[h, j] = shifted
                share_grad_ref[h, j] = share_grad
                top_ref[h, j] = here
                new = jnp.maximum(top, here)
                old_by, here_by = jnp.exp(top - new), jnp.exp(here - new)
                total = total * old_by + jnp.sum(shifted, axis=0, keepdims=True) * here_by
                inner = (
                    inner * old_by
                    + jnp.sum(shifted * share_grad, axis=0, keepdims=True) * here_by
                )
                out.append((new, total, inner))
            return tuple(out)

        zero = jnp.zeros((1, BQ), jnp.float32)
        empty = (jnp.full((1, BQ), masked_value, jnp.float32), zero, zero)
        stats = lax.fori_loop(lowest, i + 1, scores, (empty,) * together)
        inverse = [1.0 / s[1] for s in stats]
        inners = [s[2] * r for s, r in zip(stats, inverse)]

        def sums(j, carry):
            rows = stored(j)
            out = []
            for h in range(together):
                mixed, query_grad = carry[h]
                by = jnp.exp(top_ref[h, j] - stats[h][0]) * inverse[h]
                probs = shifted_ref[h, j] * by
                shares = probs.astype(jnp.bfloat16)
                score_grad = (probs * (share_grad_ref[h, j] - inners[h])).astype(jnp.bfloat16)
                mixed = mixed + jnp.dot(
                    value_columns_ref[h, :, rows], shares, preferred_element_type=jnp.float32
                )
                query_grad = query_grad + jnp.dot(
                    key_columns_ref[h, :, rows], score_grad, preferred_element_type=jnp.float32
                )
                value_grad_ref[h, :, rows] += lax.dot_general(
                    backs[h], shares, nt, preferred_element_type=jnp.float32
                )
                key_grad_ref[h, :, rows] += lax.dot_general(
                    queries[h], score_grad, nt, preferred_element_type=jnp.float32
                )
                out.append((mixed, query_grad))
            return tuple(out)

        nothing = jnp.zeros((HD, BQ), jnp.float32)
        results = lax.fori_loop(lowest, i + 1, sums, ((nothing, nothing),) * together)
        for h in range(together):
            back_ref[h, :, columns] = results[h][0].astype(jnp.bfloat16)
            query_grad_ref[h, :, columns] = results[h][1] * scale
        return 0

    lax.fori_loop(0, blocks, query_block, 0)
    for part in range(parts):
        columns = slice(part * width, (part + 1) * width)
        cosine, sine = cos_ref[:, place_of(part)], sin_ref[:, place_of(part)]

        def turned_back(ref, h):
            first, second = ref[h, :half, columns], ref[h, half:ROT, columns]
            return jnp.concatenate(
                [
                    first * cosine + second * sine,
                    second * cosine - first * sine,
                    ref[h, ROT:, columns],
                ],
                axis=0,
            ).astype(jnp.bfloat16)

        for h in range(together):
            base = h * 3 * HD
            mixed_refs[part][h * HD : (h + 1) * HD] = back_ref[h, :, columns]
            grad_refs[part][base : base + HD] = turned_back(query_grad_ref, h)
            grad_refs[part][base + HD : base + 2 * HD] = turned_back(key_grad_ref, h)
            grad_refs[part][base + 2 * HD : base + 3 * HD] = value_grad_ref[h, :, columns].astype(
                jnp.bfloat16
            )


def attend(projected, back, begins, cosine, sine, offset):
    parts = len(projected)
    heads = back[0].shape[0] // HD
    width = back[0].shape[1]
    count = begins.shape[0]
    together = 2 if heads % 2 == 0 else 1
    blocks = count // BK
    half = ROT // 2
    turn = jnp.asarray(offset * ((blocks // parts) if parts > 1 else 0), jnp.int32)
    facts = jnp.concatenate([begins[::BQ] // BK, turn[None]])
    whole = lambda rows: pl.BlockSpec((rows, count), lambda g, *_: (0, 0))
    mine = lambda rows: pl.BlockSpec((rows, width), lambda g, *_: (g, 0))
    pairs = heads * blocks * 3
    results = pl.pallas_call(
        partial(attend_kernel, together, parts),
        grid_spec=pltpu.PrefetchScalarGridSpec(
            num_scalar_prefetch=1,
            grid=(heads // together,),
            in_specs=[mine(together * 3 * HD)] * parts
            + [mine(together * HD)] * parts
            + [whole(1), whole(half), whole(half)],
            out_specs=[mine(together * HD)] * parts + [mine(together * 3 * HD)] * parts,
            scratch_shapes=[
                pltpu.VMEM((together, HD, count), jnp.bfloat16),
                pltpu.VMEM((together, HD, count), jnp.bfloat16),
                pltpu.VMEM((together, HD, count), jnp.bfloat16),
                pltpu.VMEM((together, count, HD), jnp.bfloat16),
                pltpu.VMEM((together, count, HD), jnp.bfloat16),
                pltpu.VMEM((together, HD, count), jnp.bfloat16),
                pltpu.VMEM((together, HD, count), jnp.float32),
                pltpu.VMEM((together, HD, count), jnp.float32),
                pltpu.VMEM((together, HD, count), jnp.float32),
                pltpu.VMEM((together, blocks, BK, BQ), jnp.float32),
                pltpu.VMEM((together, blocks, BK, BQ), jnp.float32),
                pltpu.VMEM((together, blocks, 1, BQ), jnp.float32),
            ],
        ),
        out_shape=[jax.ShapeDtypeStruct((heads * HD, width), jnp.bfloat16)] * parts
        + [jax.ShapeDtypeStruct((heads * 3 * HD, width), jnp.bfloat16)] * parts,
        compiler_params=pltpu.CompilerParams(vmem_limit_bytes=48 * 2**20),
        cost_estimate=pl.CostEstimate(
            flops=pairs * 12 * BK * BQ * 256,
            bytes_accessed=heads * count * HD * 22,
            transcendentals=pairs * BK * BQ,
        ),
    )(facts, *projected, *back, begins[None, :], cosine, sine)
    return results[:parts], results[parts:]


def layer_norm(rows_in, gain, bias):
    mean = jnp.mean(rows_in, axis=1, keepdims=True)
    centred = rows_in - mean
    spread = jnp.mean(centred * centred, axis=1, keepdims=True)
    normed = centred * lax.rsqrt(spread + norm_epsilon)
    return normed * gain + bias


def adam_update(master, first, second, gradient, rate, decay):
    first_new = beta_one * first + (1.0 - beta_one) * gradient
    second_new = beta_two * second + (1.0 - beta_two) * gradient * gradient
    first_hat = first_new / (1.0 - beta_one**STEP)
    second_hat = second_new / (1.0 - beta_two**STEP)
    master_new = master - rate * (
        first_hat / (jnp.sqrt(second_hat) + adam_epsilon) + decay * master
    )
    return (master_new, first_new, second_new, master_new.astype(jnp.bfloat16))


def product(pattern, left, right):
    return jnp.einsum(pattern, left, right, preferred_element_type=jnp.float32)


def gelu_both(lifted, active_grad):
    activated, pull = jax.vjp(partial(jax.nn.gelu, approximate=True), lifted)
    return pull(active_grad)[0].astype(jnp.bfloat16)


def gelu(lifted):
    return jax.nn.gelu(lifted, approximate=True).astype(jnp.bfloat16)


def swap(array, axis, bit):
    size = lax.axis_size(axis)
    return lax.ppermute(array, axis, [(i, i ^ bit) for i in range(size)])


def ordered(index, mine, other, axis):
    return jnp.where(
        index == 0,
        jnp.concatenate([mine, other], axis=axis),
        jnp.concatenate([other, mine], axis=axis),
    )


class Paired:
    def __init__(self):
        outer = lax.axis_index("outer")
        self.far, self.near = outer // 2, outer % 2
        self.place = lax.axis_index("dp")
        self.deep = lax.axis_size("dp")

    def gather(self, master, cut, depth):
        half = master.shape[cut] // 2
        own = lax.dynamic_slice_in_dim(master, self.near * half, half, cut).astype(jnp.bfloat16)
        own = lax.all_gather(own, "dp", axis=depth, tiled=True)
        return jnp.concatenate([own, swap(own, "outer", 1)], axis=cut)

    def total(self, own, sibling, cut, depth):
        own = own + swap(sibling, "outer", 1)
        half = own.shape[cut] // 2
        keep = lax.dynamic_slice_in_dim(own, self.far * half, half, cut)
        send = lax.dynamic_slice_in_dim(own, (1 - self.far) * half, half, cut)
        keep = keep + swap(send.astype(jnp.bfloat16), "outer", 2).astype(jnp.float32)
        piece = keep.shape[depth] // self.deep

        def part(at):
            return lax.dynamic_slice_in_dim(keep, at * piece, piece, depth)

        result = part(self.place)
        for step in range(1, self.deep):
            target = lax.rem(self.place + step, self.deep)
            pairs = [(i, (i + step) % self.deep) for i in range(self.deep)]
            result = result + lax.ppermute(
                part(target).astype(jnp.bfloat16), "dp", pairs
            ).astype(jnp.float32)
        return result

    def spread(self, share, cut):
        pair = ordered(self.far, share, swap(share, "outer", 2), cut)
        return ordered(self.near, pair, swap(pair, "outer", 1), cut)


def local(
    inputs,
    cotangent,
    lengths,
    project_master,
    project_first,
    project_second,
    mixing_master,
    mixing_first,
    mixing_second,
    expand_master,
    expand_first,
    expand_second,
    shrink_master,
    shrink_first,
    shrink_second,
    norm_master,
    norm_first,
    norm_second,
):
    split, deep = lax.axis_size("mp"), lax.axis_size("dp")
    heads_here = project_master.shape[1]
    width = inputs.shape[1]
    paired = (
        split == 2
        and lax.axis_size("outer") == 4
        and heads_here % 4 == 0
        and width % BQ == 0
    )
    position = lax.axis_index("mp")
    count = width * split
    norm_weight = lax.all_gather(norm_master.astype(jnp.bfloat16), "dp", axis=1, tiled=True)
    gain = norm_weight[0].astype(jnp.float32)
    bias = norm_weight[1].astype(jnp.float32)
    project_flat = project_master.reshape(project_master.shape[0], heads_here * 3 * HD)
    mixing_flat = mixing_master.reshape(heads_here * HD, mixing_master.shape[2])
    masters = (project_flat, mixing_flat, expand_master, shrink_master)
    cuts, depths = (1, 0, 1, 0), (0, 1, 0, 1)
    rows_local = inputs[0].astype(jnp.float32)
    shaped, norm_pull = jax.vjp(layer_norm, rows_local, gain, bias)
    hidden_local = shaped.astype(jnp.bfloat16)
    begins, places = layout(lengths[0], count)
    cosine, sine = turns(places)
    if paired:
        plan = Paired()
        expand, shrink, mixing, project = (
            plan.gather(masters[k], cuts[k], depths[k]) for k in (2, 3, 1, 0)
        )
        backs = [cotangent[0], swap(cotangent[0], "mp", 1)]
        hiddens = [hidden_local, swap(hidden_local, "mp", 1)]
    else:
        project, mixing, expand, shrink = (
            lax.all_gather(master.astype(jnp.bfloat16), "dp", axis=depth, tiled=True)
            for master, depth in zip(masters, depths)
        )
        backs = [lax.all_gather(cotangent[0], "mp", axis=0, tiled=True)]
        hiddens = [lax.all_gather(hidden_local, "mp", axis=0, tiled=True)]

    def over_tokens(pattern, lefts, rights):
        return sum(product(pattern, left, right) for left, right in zip(lefts, rights))

    def weight_sum(pattern, lefts, rights, cut, depth):
        if not paired:
            term = over_tokens(pattern, lefts, rights)
            term = lax.psum_scatter(term, "dp", scatter_dimension=depth, tiled=True)
            return lax.psum(term, "outer")
        sources = rights if cut == 1 else lefts
        axis = 0 if pattern.split(",")[cut].index("t") == 1 else 1
        half = sources[0].shape[axis] // 2

        def term(near):
            chosen = [
                lax.slice_in_dim(v, near * half, (near + 1) * half, axis=axis) for v in sources
            ]
            return (
                over_tokens(pattern, lefts, chosen)
                if cut == 1
                else over_tokens(pattern, chosen, rights)
            )

        sibling = term(1)
        return plan.total(term(0), sibling, cut, depth)

    lifteds = [product("td,df->tf", hidden, expand) for hidden in hiddens]
    activated = [gelu(lifted) for lifted in lifteds]
    active_grads = [product("td,fd->tf", back, shrink) for back in backs]
    lifted_grads = [gelu_both(a, b) for a, b in zip(lifteds, active_grads)]
    shrink_sum = weight_sum("tf,td->fd", activated, backs, 0, 1)
    expand_sum = weight_sum("td,tf->df", hiddens, lifted_grads, 1, 0)
    projected = [product("td,de->et", hidden, project) for hidden in hiddens]
    mixed_backs = [product("td,fd->ft", back, mixing).astype(jnp.bfloat16) for back in backs]
    mixed, projected_grads = attend(projected, mixed_backs, begins, cosine, sine, position)
    mixing_sum = weight_sum("ft,td->fd", mixed, backs, 0, 1)
    project_sum = weight_sum("td,et->de", hiddens, projected_grads, 1, 0)
    hidden_grads = [
        product("et,de->td", a, project) + product("tf,df->td", b, expand)
        for a, b in zip(projected_grads, lifted_grads)
    ]
    branches = [
        product("ft,fd->td", a, mixing) + product("tf,fd->td", b, shrink)
        for a, b in zip(mixed, activated)
    ]

    def over_positions(terms):
        if paired:
            other = swap(terms[1].astype(jnp.bfloat16), "mp", 1)
            return terms[0] + other.astype(jnp.float32)
        return lax.psum_scatter(terms[0], "mp", scatter_dimension=0, tiled=True)

    rows_grad, gain_grad, bias_grad = norm_pull(over_positions(hidden_grads))
    input_grad = (cotangent[0].astype(jnp.float32) + rows_grad)[None]
    block_out = (rows_local + over_positions(branches)).astype(jnp.bfloat16)[None]
    sums = (project_sum, mixing_sum, expand_sum, shrink_sum)
    own_square = sum(jnp.sum(v * v) for v in sums)
    everywhere = ("mp", "dp", "outer")
    if not paired:
        own_square = own_square / lax.axis_size("outer")
    norm_all = lax.psum(
        jnp.concatenate([gain_grad, bias_grad, jnp.full((128,), own_square)]), everywhere
    )
    norm_full = norm_all[: 2 * D].reshape(2, D)
    grad_norm = jnp.sqrt(norm_all[2 * D] + jnp.sum(norm_full * norm_full))
    factor = clip_level / jnp.maximum(grad_norm, clip_level)
    norm_gradient = lax.dynamic_slice_in_dim(
        norm_full, lax.axis_index("dp") * (D // deep), D // deep, 1
    )
    gradients = [
        (plan.spread(v, cut) if paired else v).reshape(master.shape)
        for v, cut, master in zip(
            sums, cuts, (project_master, mixing_master, expand_master, shrink_master)
        )
    ]
    states = (
        (project_master, project_first, project_second, D ** (-0.5)),
        (mixing_master, mixing_first, mixing_second, (D // 32) ** (-0.5)),
        (expand_master, expand_first, expand_second, D ** (-0.5)),
        (shrink_master, shrink_first, shrink_second, FF ** (-0.5)),
    )
    results = [block_out, input_grad]
    for (master, first, second, rate), gradient in zip(states, gradients):
        results += adam_update(master, first, second, factor * gradient, rate, decay_rate)
    results += adam_update(norm_master, norm_first, norm_second, factor * norm_gradient, 0.3, 0.0)
    return (*results, grad_norm)


def solution(mesh):
    in_specs = (
        P(("dp", "outer"), "mp", None),
        P(("dp", "outer"), "mp", None),
        P(("dp", "outer"), None),
        P("dp", "mp", None),
        P("dp", "mp", None),
        P("dp", "mp", None),
        P("mp", None, "dp"),
        P("mp", None, "dp"),
        P("mp", None, "dp"),
        P("dp", "mp"),
        P("dp", "mp"),
        P("dp", "mp"),
        P("mp", "dp"),
        P("mp", "dp"),
        P("mp", "dp"),
        P(None, "dp"),
        P(None, "dp"),
        P(None, "dp"),
    )
    out_specs = (
        P(("dp", "outer"), "mp", None),
        P(("dp", "outer"), "mp", None),
        P("dp", "mp", None),
        P("dp", "mp", None),
        P("dp", "mp", None),
        P("dp", "mp", None),
        P("mp", None, "dp"),
        P("mp", None, "dp"),
        P("mp", None, "dp"),
        P("mp", None, "dp"),
        P("dp", "mp"),
        P("dp", "mp"),
        P("dp", "mp"),
        P("dp", "mp"),
        P("mp", "dp"),
        P("mp", "dp"),
        P("mp", "dp"),
        P("mp", "dp"),
        P(None, "dp"),
        P(None, "dp"),
        P(None, "dp"),
        P(None, "dp"),
        P(),
    )
    return jax.shard_map(local, mesh=mesh, in_specs=in_specs, out_specs=out_specs, check_vma=False)
```

```python
from functools import partial
import math

import jax
import jax.numpy as jnp
from jax import lax
from jax.experimental import pallas as pl
from jax.experimental.pallas import tpu as pltpu
from jax.sharding import PartitionSpec as P

D = 1024
HD = 64
ROT = 32
FF = 4096
STEP = 10


norm_epsilon = 1e-05
beta_one = 0.9
beta_two = 0.95
adam_epsilon = 1e-08
decay_rate = 0.1
clip_level = 1.0
masked_value = -1e30


def layout(sizes_row, count):
    number = jnp.arange(sizes_row.shape[0], dtype=jnp.int32)
    ends = jnp.sum(jnp.where(number[None, :] <= number[:, None], sizes_row[None, :], 0), axis=1)
    tokens = jnp.arange(count, dtype=jnp.int32)
    passed = (ends[:, None] <= tokens[None, :]).astype(jnp.int32)
    begins = jnp.sum(passed * sizes_row[:, None], axis=0)
    return (begins, tokens - begins)


def turns(places):
    half_rot = ROT // 2
    counter = jnp.arange(half_rot, dtype=jnp.float32)
    frequency = jnp.exp(counter * (-2.0 * math.log(10000.0) / ROT))
    angles = places.astype(jnp.float32)[None, :] * frequency[:, None]
    return jnp.cos(angles), jnp.sin(angles)


BQ = 256
BK = 256


def attend_kernel(together, parts, later, *refs):
    facts = refs[0]
    projected_refs = refs[1 : 1 + parts]
    back_refs = refs[1 + parts : 1 + 2 * parts]
    start_ref, cos_ref, sin_ref = refs[1 + 2 * parts : 4 + 2 * parts]
    refs = refs[: 4 + 2 * parts] + refs[4 + 2 * parts + later :]
    mixed_refs = refs[4 + 2 * parts : 4 + 3 * parts]
    grad_refs = refs[4 + 3 * parts : 4 + 4 * parts]
    (
        query_ref,
        key_columns_ref,
        value_columns_ref,
        key_ref,
        value_ref,
        back_ref,
        query_grad_ref,
        key_grad_ref,
        value_grad_ref,
        shifted_ref,
        share_grad_ref,
        top_ref,
    ) = refs[4 + 4 * parts :]
    width = projected_refs[0].shape[1]
    count = width * parts
    blocks = count // BQ
    turn = facts[blocks]
    half = ROT // 2
    scale = HD ** (-0.5)
    nt = (((1,), (1,)), ((), ()))

    def place_of(part):
        if parts == 1:
            return pl.ds(0, width)
        block = lax.rem(part * (blocks // parts) + blocks - turn, blocks)
        return pl.ds(pl.multiple_of(block * BQ, BQ), width)

    for part in range(parts):
        columns = slice(part * width, (part + 1) * width)
        cosine, sine = cos_ref[:, place_of(part)], sin_ref[:, place_of(part)]
        projected_ref = projected_refs[part]

        def turned(at):
            first = projected_ref[at : at + half]
            second = projected_ref[at + half : at + ROT]
            return jnp.concatenate(
                [
                    first * cosine - second * sine,
                    second * cosine + first * sine,
                    projected_ref[at + ROT : at + HD],
                ],
                axis=0,
            ).astype(jnp.bfloat16)

        for h in range(together):
            base = h * 3 * HD
            query_ref[h, :, columns] = (turned(base).astype(jnp.float32) * scale).astype(
                jnp.bfloat16
            )
            keys = turned(base + HD)
            values = projected_ref[base + 2 * HD : base + 3 * HD].astype(jnp.bfloat16)
            key_columns_ref[h, :, columns] = keys
            value_columns_ref[h, :, columns] = values
            key_ref[h, columns] = keys.T
            value_ref[h, columns] = values.T
            back_ref[h, :, columns] = back_refs[part][h * HD : (h + 1) * HD]
    key_grad_ref[...] = jnp.zeros_like(key_grad_ref)
    value_grad_ref[...] = jnp.zeros_like(value_grad_ref)
    key_at = lax.broadcasted_iota(jnp.int32, (BK, BQ), 0)
    query_at = lax.broadcasted_iota(jnp.int32, (1, BQ), 1)

    def stored(block):
        if parts == 1:
            return pl.ds(pl.multiple_of(block * BQ, BQ), BQ)
        return pl.ds(pl.multiple_of(lax.rem(block + turn, blocks) * BQ, BQ), BQ)

    def query_block(i, _):
        columns = stored(i)
        start = start_ref[:, pl.ds(pl.multiple_of(i * BQ, BQ), BQ)]
        own = query_at + i * BQ
        lowest = facts[i]
        queries = [query_ref[h, :, columns] for h in range(together)]
        backs = [back_ref[h, :, columns] for h in range(together)]

        def scores(j, carry):
            rows = stored(j)
            allowed = (key_at >= start - j * BK) & (key_at <= own - j * BK)
            out = []
            for h in range(together):
                top, total, inner = carry[h]
                raw = jnp.dot(key_ref[h, rows, :], queries[h], preferred_element_type=jnp.float32)
                share_grad = jnp.dot(
                    value_ref[h, rows, :], backs[h], preferred_element_type=jnp.float32
                )
                masked = jnp.where(allowed, raw, masked_value)
                here = jnp.max(masked, axis=0, keepdims=True)
                shifted = jnp.exp(masked - here)
                shifted_ref[h, j] = shifted
                share_grad_ref[h, j] = share_grad
                top_ref[h, j] = here
                new = jnp.maximum(top, here)
                old_by, here_by = jnp.exp(top - new), jnp.exp(here - new)
                total = total * old_by + jnp.sum(shifted, axis=0, keepdims=True) * here_by
                inner = (
                    inner * old_by
                    + jnp.sum(shifted * share_grad, axis=0, keepdims=True) * here_by
                )
                out.append((new, total, inner))
            return tuple(out)

        zero = jnp.zeros((1, BQ), jnp.float32)
        empty = (jnp.full((1, BQ), masked_value, jnp.float32), zero, zero)
        stats = lax.fori_loop(lowest, i + 1, scores, (empty,) * together)
        inverse = [1.0 / s[1] for s in stats]
        inners = [s[2] * r for s, r in zip(stats, inverse)]

        def sums(j, carry):
            rows = stored(j)
            out = []
            for h in range(together):
                mixed, query_grad = carry[h]
                by = jnp.exp(top_ref[h, j] - stats[h][0]) * inverse[h]
                probs = shifted_ref[h, j] * by
                shares = probs.astype(jnp.bfloat16)
                score_grad = (probs * (share_grad_ref[h, j] - inners[h])).astype(jnp.bfloat16)
                mixed = mixed + jnp.dot(
                    value_columns_ref[h, :, rows], shares, preferred_element_type=jnp.float32
                )
                query_grad = query_grad + jnp.dot(
                    key_columns_ref[h, :, rows], score_grad, preferred_element_type=jnp.float32
                )
                value_grad_ref[h, :, rows] += lax.dot_general(
                    backs[h], shares, nt, preferred_element_type=jnp.float32
                )
                key_grad_ref[h, :, rows] += lax.dot_general(
                    queries[h], score_grad, nt, preferred_element_type=jnp.float32
                )
                out.append((mixed, query_grad))
            return tuple(out)

        nothing = jnp.zeros((HD, BQ), jnp.float32)
        results = lax.fori_loop(lowest, i + 1, sums, ((nothing, nothing),) * together)
        for h in range(together):
            back_ref[h, :, columns] = results[h][0].astype(jnp.bfloat16)
            query_grad_ref[h, :, columns] = results[h][1] * scale
        return 0

    lax.fori_loop(0, blocks, query_block, 0)
    for part in range(parts):
        columns = slice(part * width, (part + 1) * width)
        cosine, sine = cos_ref[:, place_of(part)], sin_ref[:, place_of(part)]

        def turned_back(ref, h):
            first, second = ref[h, :half, columns], ref[h, half:ROT, columns]
            return jnp.concatenate(
                [
                    first * cosine + second * sine,
                    second * cosine - first * sine,
                    ref[h, ROT:, columns],
                ],
                axis=0,
            ).astype(jnp.bfloat16)

        for h in range(together):
            base = h * 3 * HD
            mixed_refs[part][h * HD : (h + 1) * HD] = back_ref[h, :, columns]
            grad_refs[part][base : base + HD] = turned_back(query_grad_ref, h)
            grad_refs[part][base + HD : base + 2 * HD] = turned_back(key_grad_ref, h)
            grad_refs[part][base + 2 * HD : base + 3 * HD] = value_grad_ref[h, :, columns].astype(
                jnp.bfloat16
            )


def attend(projected, back, begins, cosine, sine, offset, after=()):
    parts = len(projected)
    heads = back[0].shape[0] // HD
    width = back[0].shape[1]
    count = begins.shape[0]
    together = 2 if heads % 2 == 0 else 1
    blocks = count // BK
    half = ROT // 2
    turn = jnp.asarray(offset * ((blocks // parts) if parts > 1 else 0), jnp.int32)
    facts = jnp.concatenate([begins[::BQ] // BK, turn[None]])
    whole = lambda rows: pl.BlockSpec((rows, count), lambda g, *_: (0, 0))
    mine = lambda rows: pl.BlockSpec((rows, width), lambda g, *_: (g, 0))
    results = pl.pallas_call(
        partial(attend_kernel, together, parts, len(after)),
        grid_spec=pltpu.PrefetchScalarGridSpec(
            num_scalar_prefetch=1,
            grid=(heads // together,),
            in_specs=[mine(together * 3 * HD)] * parts
            + [mine(together * HD)] * parts
            + [whole(1), whole(half), whole(half)]
            + [pl.BlockSpec(memory_space=pl.ANY)] * len(after),
            out_specs=[mine(together * HD)] * parts + [mine(together * 3 * HD)] * parts,
            scratch_shapes=[
                pltpu.VMEM((together, HD, count), jnp.bfloat16),
                pltpu.VMEM((together, HD, count), jnp.bfloat16),
                pltpu.VMEM((together, HD, count), jnp.bfloat16),
                pltpu.VMEM((together, count, HD), jnp.bfloat16),
                pltpu.VMEM((together, count, HD), jnp.bfloat16),
                pltpu.VMEM((together, HD, count), jnp.bfloat16),
                pltpu.VMEM((together, HD, count), jnp.float32),
                pltpu.VMEM((together, HD, count), jnp.float32),
                pltpu.VMEM((together, HD, count), jnp.float32),
                pltpu.VMEM((together, blocks, BK, BQ), jnp.float32),
                pltpu.VMEM((together, blocks, BK, BQ), jnp.float32),
                pltpu.VMEM((together, blocks, 1, BQ), jnp.float32),
            ],
        ),
        out_shape=[jax.ShapeDtypeStruct((heads * HD, width), jnp.bfloat16)] * parts
        + [jax.ShapeDtypeStruct((heads * 3 * HD, width), jnp.bfloat16)] * parts,
        compiler_params=pltpu.CompilerParams(vmem_limit_bytes=48 * 2**20),
        cost_estimate=pl.CostEstimate(
            flops=2**20,
            bytes_accessed=2**20,
            transcendentals=0,
        ),
    )(facts, *projected, *back, begins[None, :], cosine, sine, *after)
    return results[:parts], results[parts:]


def layer_norm(rows_in, gain, bias):
    mean = jnp.mean(rows_in, axis=1, keepdims=True)
    centred = rows_in - mean
    spread = jnp.mean(centred * centred, axis=1, keepdims=True)
    normed = centred * lax.rsqrt(spread + norm_epsilon)
    return normed * gain + bias


def adam_update(master, first, second, gradient, rate, decay):
    first_new = beta_one * first + (1.0 - beta_one) * gradient
    second_new = beta_two * second + (1.0 - beta_two) * gradient * gradient
    first_hat = first_new / (1.0 - beta_one**STEP)
    second_hat = second_new / (1.0 - beta_two**STEP)
    master_new = master - rate * (
        first_hat / (jnp.sqrt(second_hat) + adam_epsilon) + decay * master
    )
    return (master_new, first_new, second_new, master_new.astype(jnp.bfloat16))


def product(pattern, left, right):
    return jnp.einsum(pattern, left, right, preferred_element_type=jnp.float32)


def gelu_both(lifted, active_grad):
    activated, pull = jax.vjp(partial(jax.nn.gelu, approximate=True), lifted)
    return pull(active_grad)[0].astype(jnp.bfloat16)


def gelu(lifted):
    return jax.nn.gelu(lifted, approximate=True).astype(jnp.bfloat16)


def swap(array, axis, bit):
    size = lax.axis_size(axis)
    return lax.ppermute(array, axis, [(i, i ^ bit) for i in range(size)])


def ordered(index, mine, other, axis):
    return jnp.where(
        index == 0,
        jnp.concatenate([mine, other], axis=axis),
        jnp.concatenate([other, mine], axis=axis),
    )


MESH = pl.DeviceIdType.MESH


def opening_kernel(
    expand_ref,
    shrink_ref,
    project_ref,
    mixing_ref,
    norm_ref,
    inputs_ref,
    back_ref,
    expand_out,
    shrink_out,
    project_out,
    mixing_out,
    norm_out,
    hidden_ref,
    other_back,
    expand_low,
    shrink_low,
    norm_low,
    norm_all,
    own_sem,
    norm_send,
    norm_recv,
    line_send,
    line_recv,
    far_send,
    far_recv,
    near_send,
    near_recv,
    row_sem,
):
    place, deep = lax.axis_index("dp"), 4
    outer = lax.axis_index("outer")
    far, near = outer // 2, outer % 2
    far_id = {"outer": (outer + 2) % 4}
    near_id = {"outer": outer + 1 - 2 * near}
    rows = expand_ref.shape[0]
    half = expand_ref.shape[1] // 2
    part = half // 2

    barrier = pltpu.get_barrier_semaphore()
    for step in range(1, deep):
        pl.semaphore_signal(
            barrier, inc=1, device_id={"dp": (place + step) % deep}, device_id_type=MESH
        )
    pl.semaphore_signal(barrier, inc=1, device_id=far_id, device_id_type=MESH)
    pl.semaphore_signal(barrier, inc=1, device_id=near_id, device_id_type=MESH)
    row_id = {"mp": 1 - lax.axis_index("mp")}
    pl.semaphore_signal(barrier, inc=1, device_id=row_id, device_id_type=MESH)

    expand_low[...] = expand_ref[...].astype(jnp.bfloat16)
    norm_low[...] = jnp.zeros_like(norm_low)
    norm_low[0:2] = norm_ref[...].astype(jnp.bfloat16).astype(jnp.float32)
    pl.semaphore_wait(barrier, deep + 2)

    def piece(w, which, at, side):
        across = pl.ds(pl.multiple_of(at * rows, rows), rows)
        along = pl.ds(pl.multiple_of(side * part, part), part)
        if w == 0:
            return expand_out.at[which, across, along]
        return shrink_out.at[which, along, across]

    def mine(w):
        along = pl.ds(pl.multiple_of(near * half + far * part, part), part)
        return expand_low.at[:, along] if w == 0 else shrink_low.at[along, :]

    def remote(source, target, send, recv, device):
        return pltpu.make_async_remote_copy(
            src_ref=source,
            dst_ref=target,
            send_sem=send,
            recv_sem=recv,
            device_id=device,
            device_id_type=MESH,
        )

    def line(w, way, step, source, at):
        to = place + 1 if way == 0 else place - 1
        return remote(
            source,
            piece(w, 0, at, far),
            line_send.at[w, way, step],
            line_recv.at[w, way, step],
            {"dp": to},
        )

    def can_send(way):
        return place < deep - 1 if way == 0 else place > 0

    def start_own(w):
        for way in range(2):

            @pl.when(can_send(way))
            def _(way=way):
                line(w, way, 0, mine(w), place).start()

    def own_copies(w):
        out = []
        for which in range(2):
            side = near + which - 2 * near * which
            along = pl.ds(pl.multiple_of(side * half, half), half)
            across = pl.ds(pl.multiple_of(place * rows, rows), rows)
            if w == 0:
                pair = (expand_low.at[:, along], expand_out.at[which, across, :])
            else:
                pair = (shrink_low.at[along, :], shrink_out.at[which, :, across])
            out.append(pltpu.make_async_copy(*pair, own_sem.at[w, which]))
        return out

    start_own(0)
    row_copy = remote(back_ref, other_back, row_sem.at[0], row_sem.at[1], row_id)
    row_copy.start()
    norm_copies = []
    for step in range(1, deep):
        copy = remote(
            norm_low,
            norm_all.at[step],
            norm_send.at[step],
            norm_recv.at[step],
            {"dp": (place + step) % deep},
        )
        copy.start()
        norm_copies.append(copy)
    shrink_low[...] = shrink_ref[...].astype(jnp.bfloat16)
    start_own(1)
    for w in range(2):
        for copy in own_copies(w):
            copy.start()
    heads = project_ref.shape[1] // 2
    units = mixing_ref.shape[0] // 2
    project_out[...] = project_ref[
        :, pl.ds(pl.multiple_of(near * heads, heads), heads)
    ].astype(jnp.bfloat16)
    mixing_out[...] = mixing_ref[
        pl.ds(pl.multiple_of(near * units, units), units), :
    ].astype(jnp.bfloat16)
    norm_all[0] = norm_low[...]
    for copy in norm_copies:
        copy.wait()
    for at in range(deep):
        norm_out[:, at * rows : (at + 1) * rows] = norm_all[(place - at + deep) % deep]
    gain, bias = norm_out[0:1], norm_out[1:2]
    tokens = inputs_ref.shape[0]
    height = 128

    def normalize(i, _):
        at = pl.ds(pl.multiple_of(i * height, height), height)
        x = inputs_ref[at, :].astype(jnp.float32)
        mean = jnp.mean(x, axis=1, keepdims=True)
        centred = x - mean
        spread = jnp.mean(centred * centred, axis=1, keepdims=True)
        normed = centred * lax.rsqrt(spread + norm_epsilon)
        hidden_ref[at, :] = (normed * gain + bias).astype(jnp.bfloat16)
        return 0

    lax.fori_loop(0, tokens // height, normalize, 0)

    def arrives(way, step):
        return place >= step if way == 0 else place + step < deep

    def at_of(way, step):
        return place - step if way == 0 else place + step

    def to_far(w, way, step):
        at = at_of(way, step)
        return remote(
            piece(w, 0, at, far),
            piece(w, 0, at, far),
            far_send.at[w, way, step - 1],
            far_recv.at[w, way, step - 1],
            far_id,
        )

    def from_far(w, way, step):
        at = at_of(way, step)
        return remote(
            piece(w, 0, at, 1 - far),
            piece(w, 0, at, 1 - far),
            far_send.at[w, way, step - 1],
            far_recv.at[w, way, step - 1],
            far_id,
        )

    def to_near(w, way, step, other):
        at = at_of(way, step)
        side = 1 - far if other else far
        return remote(
            piece(w, 0, at, side),
            piece(w, 1, at, side),
            near_send.at[w, way, step - 1, other],
            near_recv.at[w, way, step - 1, other],
            near_id,
        )

    order = [(w, step) for w in range(2) for step in range(1, deep)]

    def first_half(w, step):
        for way in range(2):

            @pl.when(arrives(way, step))
            def _(way=way):
                at = at_of(way, step)
                line(w, way, step - 1, mine(w), at).wait_recv()
                if step < deep - 1:

                    @pl.when(can_send(way))
                    def _():
                        line(w, way, step, piece(w, 0, at, far), at).start()

                to_far(w, way, step).start()
                to_near(w, way, step, 0).start()

    def second_half(w, step):
        for way in range(2):

            @pl.when(arrives(way, step))
            def _(way=way):
                from_far(w, way, step).wait_recv()
                to_near(w, way, step, 1).start()

    for n, (w, step) in enumerate(order):
        first_half(w, step)
        if n:
            second_half(*order[n - 1])
    second_half(*order[-1])
    row_copy.wait()
    for w in range(2):
        for copy in own_copies(w):
            copy.wait()
        for way in range(2):

            @pl.when(can_send(way))
            def _(way=way):
                line(w, way, 0, mine(w), place).wait_send()

            for step in range(1, deep):

                @pl.when(arrives(way, step))
                def _(way=way, step=step):
                    at = at_of(way, step)
                    if step < deep - 1:

                        @pl.when(can_send(way))
                        def _():
                            line(w, way, step, piece(w, 0, at, far), at).wait_send()

                    to_far(w, way, step).wait_send()
                    for other in range(2):
                        to_near(w, way, step, other).wait_send()
                        to_near(w, way, step, other).wait_recv()


def opening(expand, shrink, project, mixing, norm, inputs, back):
    deep = 4
    here = lambda: pl.BlockSpec(memory_space=pltpu.VMEM)
    rows, units = expand.shape
    low = jnp.bfloat16
    sem = pltpu.SemaphoreType.DMA
    return pl.pallas_call(
        opening_kernel,
        in_specs=[here() for _ in range(6)] + [pl.BlockSpec(memory_space=pl.ANY)],
        out_specs=[pl.BlockSpec(memory_space=pl.ANY)] * 2
        + [here() for _ in range(4)]
        + [pl.BlockSpec(memory_space=pl.ANY)],
        out_shape=[
            jax.ShapeDtypeStruct((2, rows * deep, units // 2), low),
            jax.ShapeDtypeStruct((2, units // 2, rows * deep), low),
            jax.ShapeDtypeStruct((project.shape[0], project.shape[1] // 2), low),
            jax.ShapeDtypeStruct((mixing.shape[0] // 2, mixing.shape[1]), low),
            jax.ShapeDtypeStruct((8, rows * deep), jnp.float32),
            jax.ShapeDtypeStruct(inputs.shape, low),
            jax.ShapeDtypeStruct(back.shape, low),
        ],
        scratch_shapes=[
            pltpu.VMEM(expand.shape, low),
            pltpu.VMEM(shrink.shape, low),
            pltpu.VMEM((8, norm.shape[1]), jnp.float32),
            pltpu.VMEM((deep, 8, norm.shape[1]), jnp.float32),
            sem((2, 2)),
            sem((deep,)),
            sem((deep,)),
            sem((2, 2, deep)),
            sem((2, 2, deep)),
            sem((2, 2, deep)),
            sem((2, 2, deep)),
            sem((2, 2, deep, 2)),
            sem((2, 2, deep, 2)),
            sem((2,)),
        ],
        compiler_params=pltpu.CompilerParams(
            collective_id=1, has_side_effects=True, vmem_limit_bytes=40 * 2**20
        ),
        cost_estimate=pl.CostEstimate(flops=0, bytes_accessed=2**20, transcendentals=0),
    )(expand, shrink, project, mixing, norm, inputs, back)


def total_kernel(term_ref, out_ref, first, second, first_send, first_recv, second_send, second_recv):
    split, outers, deep = first.shape[0] // 4, 4, second.shape[0]
    plane = split * outers
    place = lax.axis_index("dp")
    me = lax.axis_index("mp") * outers + lax.axis_index("outer")

    def plane_id(step):
        other = (me + step) % plane
        return {"mp": other // outers, "outer": other % outers}

    def line_id(step):
        return {"dp": (place + step) % deep}

    barrier = pltpu.get_barrier_semaphore()
    for step in range(1, plane):
        pl.semaphore_signal(barrier, inc=1, device_id=plane_id(step), device_id_type=MESH)
    for step in range(1, deep):
        pl.semaphore_signal(barrier, inc=1, device_id=line_id(step), device_id_type=MESH)
    pl.semaphore_wait(barrier, plane + deep - 2)

    def exchange(source, slots, send, recv, size, device):
        copies = []
        for step in range(1, size):
            copy = pltpu.make_async_remote_copy(
                src_ref=source,
                dst_ref=slots.at[step],
                send_sem=send.at[step],
                recv_sem=recv.at[step],
                device_id=device(step),
                device_id_type=MESH,
            )
            copy.start()
            copies.append(copy)
        slots[0] = source[...]
        for copy in copies:
            copy.wait()

    exchange(term_ref, first, first_send, first_recv, plane, plane_id)
    total = first[me]
    for at in range(1, plane):
        total = total + first[(me + plane - at) % plane]
    out_ref[...] = total
    exchange(out_ref, second, second_send, second_recv, deep, line_id)
    total = second[place]
    for at in range(1, deep):
        total = total + second[(place + deep - at) % deep]
    out_ref[...] = total


def total_over_all(term, split, deep):
    plane = split * 4
    sem = pltpu.SemaphoreType.DMA
    return pl.pallas_call(
        total_kernel,
        in_specs=[pl.BlockSpec(memory_space=pltpu.VMEM)],
        out_specs=pl.BlockSpec(memory_space=pltpu.VMEM),
        out_shape=jax.ShapeDtypeStruct(term.shape, term.dtype),
        scratch_shapes=[
            pltpu.VMEM((plane, *term.shape), term.dtype),
            pltpu.VMEM((deep, *term.shape), term.dtype),
            sem((plane,)),
            sem((plane,)),
            sem((deep,)),
            sem((deep,)),
        ],
        compiler_params=pltpu.CompilerParams(collective_id=2, has_side_effects=True),
    )(term)


class Paired:
    def __init__(self):
        outer = lax.axis_index("outer")
        self.far, self.near = outer // 2, outer % 2
        self.place = lax.axis_index("dp")
        self.deep = lax.axis_size("dp")

    def gather(self, own, cut, depth):
        own = lax.all_gather(own, "dp", axis=depth, tiled=True)
        return jnp.concatenate([own, swap(own, "outer", 1)], axis=cut)

    def gather_few(self, own, cut, depth):
        wide = list(own.shape)
        piece = wide[depth]
        wide[depth] *= self.deep
        out = jnp.zeros(wide, own.dtype)
        for step in range(self.deep):
            pairs = [(i, (i + step) % self.deep) for i in range(self.deep)]
            come = lax.ppermute(own, "dp", pairs) if step else own
            at = lax.rem(self.place - step + self.deep, self.deep)
            out = lax.dynamic_update_slice_in_dim(out, come, at * piece, depth)
        return jnp.concatenate([out, swap(out, "outer", 1)], axis=cut)

    def total(self, own, sibling, cut, depth):
        own = own + swap(sibling, "outer", 1)
        half = own.shape[cut] // 2
        keep = lax.dynamic_slice_in_dim(own, self.far * half, half, cut)
        send = lax.dynamic_slice_in_dim(own, (1 - self.far) * half, half, cut)
        keep = keep + swap(send.astype(jnp.bfloat16), "outer", 2).astype(jnp.float32)
        piece = keep.shape[depth] // self.deep

        def part(at):
            return lax.dynamic_slice_in_dim(keep, at * piece, piece, depth)

        result = part(self.place)
        for step in range(1, self.deep):
            target = lax.rem(self.place + step, self.deep)
            pairs = [(i, (i + step) % self.deep) for i in range(self.deep)]
            result = result + lax.ppermute(
                part(target).astype(jnp.bfloat16), "dp", pairs
            ).astype(jnp.float32)
        return result

    def spread(self, share, cut):
        pair = ordered(self.far, share, swap(share, "outer", 2), cut)
        return ordered(self.near, pair, swap(pair, "outer", 1), cut)


def local(
    inputs,
    cotangent,
    lengths,
    project_master,
    project_first,
    project_second,
    mixing_master,
    mixing_first,
    mixing_second,
    expand_master,
    expand_first,
    expand_second,
    shrink_master,
    shrink_first,
    shrink_second,
    norm_master,
    norm_first,
    norm_second,
):
    split, deep = lax.axis_size("mp"), lax.axis_size("dp")
    heads_here = project_master.shape[1]
    width = inputs.shape[1]
    paired = (
        split == 2
        and lax.axis_size("outer") == 4
        and heads_here % 4 == 0
        and width % BQ == 0
    )
    position = lax.axis_index("mp")
    count = width * split
    project_flat = project_master.reshape(project_master.shape[0], heads_here * 3 * HD)
    mixing_flat = mixing_master.reshape(heads_here * HD, mixing_master.shape[2])
    masters = (project_flat, mixing_flat, expand_master, shrink_master)
    cuts, depths = (1, 0, 1, 0), (0, 1, 0, 1)
    rows_local = inputs[0].astype(jnp.float32)
    begins, places = layout(lengths[0], count)
    cosine, sine = turns(places)
    if paired:
        plan = Paired()
        expand, shrink, project, mixing, norm_weight, hidden_local, other_back = opening(
            expand_master,
            shrink_master,
            project_flat,
            mixing_flat,
            norm_master,
            inputs[0],
            cotangent[0],
        )
        backs = [cotangent[0], other_back]
        expand = jnp.concatenate([expand[0], expand[1]], axis=1)
        shrink = shrink.reshape(-1, shrink.shape[2])
        project = plan.gather(project, 1, 0)
        mixing = plan.gather_few(mixing, 0, 1)
        gain, bias = norm_weight[0], norm_weight[1]
        norm_pull = jax.vjp(layer_norm, rows_local, gain, bias)[1]
        hiddens = [hidden_local, swap(hidden_local, "mp", 1)]
    else:
        norm_weight = lax.all_gather(norm_master.astype(jnp.bfloat16), "dp", axis=1, tiled=True)
        gain = norm_weight[0].astype(jnp.float32)
        bias = norm_weight[1].astype(jnp.float32)
        shaped, norm_pull = jax.vjp(layer_norm, rows_local, gain, bias)
        hidden_local = shaped.astype(jnp.bfloat16)
        project, mixing, expand, shrink = (
            lax.all_gather(master.astype(jnp.bfloat16), "dp", axis=depth, tiled=True)
            for master, depth in zip(masters, depths)
        )
        backs = [lax.all_gather(cotangent[0], "mp", axis=0, tiled=True)]
        hiddens = [lax.all_gather(hidden_local, "mp", axis=0, tiled=True)]

    def over_tokens(pattern, lefts, rights):
        return sum(product(pattern, left, right) for left, right in zip(lefts, rights))

    def weight_sum(pattern, lefts, rights, cut, depth):
        if not paired:
            term = over_tokens(pattern, lefts, rights)
            term = lax.psum_scatter(term, "dp", scatter_dimension=depth, tiled=True)
            return lax.psum(term, "outer"), ()
        sources = rights if cut == 1 else lefts
        axis = 0 if pattern.split(",")[cut].index("t") == 1 else 1
        half = sources[0].shape[axis] // 2

        def term(near):
            chosen = [
                lax.slice_in_dim(v, near * half, (near + 1) * half, axis=axis) for v in sources
            ]
            return (
                over_tokens(pattern, lefts, chosen)
                if cut == 1
                else over_tokens(pattern, chosen, rights)
            )

        sibling, own = term(1), term(0)
        return plan.total(own, sibling, cut, depth), (sibling, own)

    lifteds = [product("td,df->tf", hidden, expand) for hidden in hiddens]
    activated = [gelu(lifted) for lifted in lifteds]
    active_grads = [product("td,fd->tf", back, shrink) for back in backs]
    lifted_grads = [gelu_both(a, b) for a, b in zip(lifteds, active_grads)]
    shrink_sum, shrink_terms = weight_sum("tf,td->fd", activated, backs, 0, 1)
    expand_sum, expand_terms = weight_sum("td,tf->df", hiddens, lifted_grads, 1, 0)
    projected = [product("td,de->et", hidden, project) for hidden in hiddens]
    mixed_backs = [product("td,fd->ft", back, mixing).astype(jnp.bfloat16) for back in backs]
    mixed, projected_grads = attend(
        projected,
        mixed_backs,
        begins,
        cosine,
        sine,
        position,
        (*shrink_terms, *expand_terms),
    )
    mixing_sum, _ = weight_sum("ft,td->fd", mixed, backs, 0, 1)
    project_sum, _ = weight_sum("td,et->de", hiddens, projected_grads, 1, 0)
    hidden_grads = [
        product("et,de->td", a, project) + product("tf,df->td", b, expand)
        for a, b in zip(projected_grads, lifted_grads)
    ]
    branches = [
        product("ft,fd->td", a, mixing) + product("tf,fd->td", b, shrink)
        for a, b in zip(mixed, activated)
    ]

    def over_positions(terms):
        if paired:
            other = swap(terms[1].astype(jnp.bfloat16), "mp", 1)
            return terms[0] + other.astype(jnp.float32)
        return lax.psum_scatter(terms[0], "mp", scatter_dimension=0, tiled=True)

    rows_grad, gain_grad, bias_grad = norm_pull(over_positions(hidden_grads))
    input_grad = (cotangent[0].astype(jnp.float32) + rows_grad)[None]
    block_out = (rows_local + over_positions(branches)).astype(jnp.bfloat16)[None]
    sums = (project_sum, mixing_sum, expand_sum, shrink_sum)
    own_square = sum(jnp.sum(v * v) for v in sums)
    if not paired:
        own_square = own_square / lax.axis_size("outer")
    norm_terms = jnp.concatenate([gain_grad, bias_grad, jnp.full((D,), own_square)])
    norm_terms = norm_terms.reshape(-1, 128)
    if paired:
        norm_all = total_over_all(norm_terms, split, deep)
    else:
        norm_all = lax.psum(norm_terms, ("mp", "dp", "outer"))
    norm_all = norm_all.reshape(3, D)
    norm_full = norm_all[:2]
    grad_norm = jnp.sqrt(norm_all[2, 0] + jnp.sum(norm_full * norm_full))
    factor = clip_level / jnp.maximum(grad_norm, clip_level)
    norm_gradient = lax.dynamic_slice_in_dim(
        norm_full, lax.axis_index("dp") * (D // deep), D // deep, 1
    )
    gradients = [
        (plan.spread(v, cut) if paired else v).reshape(master.shape)
        for v, cut, master in zip(
            sums, cuts, (project_master, mixing_master, expand_master, shrink_master)
        )
    ]
    states = (
        (project_master, project_first, project_second, D ** (-0.5)),
        (mixing_master, mixing_first, mixing_second, (D // 32) ** (-0.5)),
        (expand_master, expand_first, expand_second, D ** (-0.5)),
        (shrink_master, shrink_first, shrink_second, FF ** (-0.5)),
    )
    results = [block_out, input_grad]
    for (master, first, second, rate), gradient in zip(states, gradients):
        results += adam_update(master, first, second, factor * gradient, rate, decay_rate)
    results += adam_update(norm_master, norm_first, norm_second, factor * norm_gradient, 0.3, 0.0)
    return (*results, grad_norm)


def solution(mesh):
    in_specs = (
        P(("dp", "outer"), "mp", None),
        P(("dp", "outer"), "mp", None),
        P(("dp", "outer"), None),
        P("dp", "mp", None),
        P("dp", "mp", None),
        P("dp", "mp", None),
        P("mp", None, "dp"),
        P("mp", None, "dp"),
        P("mp", None, "dp"),
        P("dp", "mp"),
        P("dp", "mp"),
        P("dp", "mp"),
        P("mp", "dp"),
        P("mp", "dp"),
        P("mp", "dp"),
        P(None, "dp"),
        P(None, "dp"),
        P(None, "dp"),
    )
    out_specs = (
        P(("dp", "outer"), "mp", None),
        P(("dp", "outer"), "mp", None),
        P("dp", "mp", None),
        P("dp", "mp", None),
        P("dp", "mp", None),
        P("dp", "mp", None),
        P("mp", None, "dp"),
        P("mp", None, "dp"),
        P("mp", None, "dp"),
        P("mp", None, "dp"),
        P("dp", "mp"),
        P("dp", "mp"),
        P("dp", "mp"),
        P("dp", "mp"),
        P("mp", "dp"),
        P("mp", "dp"),
        P("mp", "dp"),
        P("mp", "dp"),
        P(None, "dp"),
        P(None, "dp"),
        P(None, "dp"),
        P(None, "dp"),
        P(),
    )
    return jax.shard_map(local, mesh=mesh, in_specs=in_specs, out_specs=out_specs, check_vma=False)
```

```python
from functools import partial
import math

import jax
import jax.numpy as jnp
from jax import lax
from jax.experimental import pallas as pl
from jax.experimental.pallas import tpu as pltpu
from jax.sharding import PartitionSpec as P

D = 1024
HD = 64
ROT = 32
FF = 4096
STEP = 10


norm_epsilon = 1e-05
beta_one = 0.9
beta_two = 0.95
adam_epsilon = 1e-08
decay_rate = 0.1
clip_level = 1.0
masked_value = -1e30


def layout(sizes_row, count):
    number = jnp.arange(sizes_row.shape[0], dtype=jnp.int32)
    ends = jnp.sum(jnp.where(number[None, :] <= number[:, None], sizes_row[None, :], 0), axis=1)
    tokens = jnp.arange(count, dtype=jnp.int32)
    passed = (ends[:, None] <= tokens[None, :]).astype(jnp.int32)
    begins = jnp.sum(passed * sizes_row[:, None], axis=0)
    return (begins, tokens - begins)


def turns(places):
    half_rot = ROT // 2
    counter = jnp.arange(half_rot, dtype=jnp.float32)
    frequency = jnp.exp(counter * (-2.0 * math.log(10000.0) / ROT))
    angles = places.astype(jnp.float32)[None, :] * frequency[:, None]
    return jnp.cos(angles), jnp.sin(angles)


BQ = 256
BK = 256


def attend_kernel(together, parts, later, *refs):
    facts = refs[0]
    projected_refs = refs[1 : 1 + parts]
    back_refs = refs[1 + parts : 1 + 2 * parts]
    start_ref, cos_ref, sin_ref = refs[1 + 2 * parts : 4 + 2 * parts]
    refs = refs[: 4 + 2 * parts] + refs[4 + 2 * parts + later :]
    mixed_refs = refs[4 + 2 * parts : 4 + 3 * parts]
    grad_refs = refs[4 + 3 * parts : 4 + 4 * parts]
    (
        query_ref,
        key_columns_ref,
        value_columns_ref,
        key_ref,
        value_ref,
        back_ref,
        query_grad_ref,
        key_grad_ref,
        value_grad_ref,
        shifted_ref,
        share_grad_ref,
        top_ref,
    ) = refs[4 + 4 * parts :]
    width = projected_refs[0].shape[1]
    count = width * parts
    blocks = count // BQ
    turn = facts[blocks]
    half = ROT // 2
    scale = HD ** (-0.5)
    nt = (((1,), (1,)), ((), ()))

    def place_of(part):
        if parts == 1:
            return pl.ds(0, width)
        block = lax.rem(part * (blocks // parts) + blocks - turn, blocks)
        return pl.ds(pl.multiple_of(block * BQ, BQ), width)

    for part in range(parts):
        columns = slice(part * width, (part + 1) * width)
        cosine, sine = cos_ref[:, place_of(part)], sin_ref[:, place_of(part)]
        projected_ref = projected_refs[part]

        def turned(at):
            first = projected_ref[at : at + half]
            second = projected_ref[at + half : at + ROT]
            return jnp.concatenate(
                [
                    first * cosine - second * sine,
                    second * cosine + first * sine,
                    projected_ref[at + ROT : at + HD],
                ],
                axis=0,
            ).astype(jnp.bfloat16)

        for h in range(together):
            base = h * 3 * HD
            query_ref[h, :, columns] = (turned(base).astype(jnp.float32) * scale).astype(
                jnp.bfloat16
            )
            keys = turned(base + HD)
            values = projected_ref[base + 2 * HD : base + 3 * HD].astype(jnp.bfloat16)
            key_columns_ref[h, :, columns] = keys
            value_columns_ref[h, :, columns] = values
            key_ref[h, columns] = keys.T
            value_ref[h, columns] = values.T
            back_ref[h, :, columns] = back_refs[part][h * HD : (h + 1) * HD]
    key_grad_ref[...] = jnp.zeros_like(key_grad_ref)
    value_grad_ref[...] = jnp.zeros_like(value_grad_ref)
    key_at = lax.broadcasted_iota(jnp.int32, (BK, BQ), 0)
    query_at = lax.broadcasted_iota(jnp.int32, (1, BQ), 1)

    def stored(block):
        if parts == 1:
            return pl.ds(pl.multiple_of(block * BQ, BQ), BQ)
        return pl.ds(pl.multiple_of(lax.rem(block + turn, blocks) * BQ, BQ), BQ)

    def query_block(i, _):
        columns = stored(i)
        start = start_ref[:, pl.ds(pl.multiple_of(i * BQ, BQ), BQ)]
        own = query_at + i * BQ
        lowest = facts[i]
        queries = [query_ref[h, :, columns] for h in range(together)]
        backs = [back_ref[h, :, columns] for h in range(together)]

        def in_pairs(body, carry):
            twos = lax.div(i + 1 - lowest, 2)
            carry = lax.fori_loop(
                0, twos, lambda n, c: body((lowest + 2 * n, lowest + 2 * n + 1), c), carry
            )
            return lax.fori_loop(lowest + 2 * twos, i + 1, lambda n, c: body((n,), c), carry)

        def scores(group, carry):
            made = []
            for j in group:
                rows = stored(j)
                allowed = (key_at >= start - j * BK) & (key_at <= own - j * BK)
                for h in range(together):
                    raw = jnp.dot(
                        key_ref[h, rows, :], queries[h], preferred_element_type=jnp.float32
                    )
                    share_grad = jnp.dot(
                        value_ref[h, rows, :], backs[h], preferred_element_type=jnp.float32
                    )
                    masked = jnp.where(allowed, raw, masked_value)
                    here = jnp.max(masked, axis=0, keepdims=True)
                    shifted = jnp.exp(masked - here)
                    shifted_ref[h, j] = shifted
                    share_grad_ref[h, j] = share_grad
                    top_ref[h, j] = here
                    made.append(
                        (
                            here,
                            jnp.sum(shifted, axis=0, keepdims=True),
                            jnp.sum(shifted * share_grad, axis=0, keepdims=True),
                        )
                    )
            out = []
            for h in range(together):
                top, total, inner = carry[h]
                for here, here_total, here_inner in made[h::together]:
                    new = jnp.maximum(top, here)
                    old_by, here_by = jnp.exp(top - new), jnp.exp(here - new)
                    total = total * old_by + here_total * here_by
                    inner = inner * old_by + here_inner * here_by
                    top = new
                out.append((top, total, inner))
            return tuple(out)

        zero = jnp.zeros((1, BQ), jnp.float32)
        empty = (jnp.full((1, BQ), masked_value, jnp.float32), zero, zero)
        stats = in_pairs(scores, (empty,) * together)
        inverse = [1.0 / s[1] for s in stats]
        inners = [s[2] * r for s, r in zip(stats, inverse)]

        def sums(group, carry):
            out = list(carry)
            for j in group:
                rows = stored(j)
                for h in range(together):
                    mixed, query_grad = out[h]
                    by = jnp.exp(top_ref[h, j] - stats[h][0]) * inverse[h]
                    probs = shifted_ref[h, j] * by
                    shares = probs.astype(jnp.bfloat16)
                    score_grad = (probs * (share_grad_ref[h, j] - inners[h])).astype(jnp.bfloat16)
                    mixed = mixed + jnp.dot(
                        value_columns_ref[h, :, rows], shares, preferred_element_type=jnp.float32
                    )
                    query_grad = query_grad + jnp.dot(
                        key_columns_ref[h, :, rows], score_grad, preferred_element_type=jnp.float32
                    )
                    value_grad_ref[h, :, rows] += lax.dot_general(
                        backs[h], shares, nt, preferred_element_type=jnp.float32
                    )
                    key_grad_ref[h, :, rows] += lax.dot_general(
                        queries[h], score_grad, nt, preferred_element_type=jnp.float32
                    )
                    out[h] = (mixed, query_grad)
            return tuple(out)

        nothing = jnp.zeros((HD, BQ), jnp.float32)
        results = in_pairs(sums, ((nothing, nothing),) * together)
        for h in range(together):
            back_ref[h, :, columns] = results[h][0].astype(jnp.bfloat16)
            query_grad_ref[h, :, columns] = results[h][1] * scale
        return 0

    lax.fori_loop(0, blocks, query_block, 0)
    for part in range(parts):
        columns = slice(part * width, (part + 1) * width)
        cosine, sine = cos_ref[:, place_of(part)], sin_ref[:, place_of(part)]

        def turned_back(ref, h):
            first, second = ref[h, :half, columns], ref[h, half:ROT, columns]
            return jnp.concatenate(
                [
                    first * cosine + second * sine,
                    second * cosine - first * sine,
                    ref[h, ROT:, columns],
                ],
                axis=0,
            ).astype(jnp.bfloat16)

        for h in range(together):
            base = h * 3 * HD
            mixed_refs[part][h * HD : (h + 1) * HD] = back_ref[h, :, columns]
            grad_refs[part][base : base + HD] = turned_back(query_grad_ref, h)
            grad_refs[part][base + HD : base + 2 * HD] = turned_back(key_grad_ref, h)
            grad_refs[part][base + 2 * HD : base + 3 * HD] = value_grad_ref[h, :, columns].astype(
                jnp.bfloat16
            )


def attend(projected, back, begins, cosine, sine, offset, after=()):
    parts = len(projected)
    heads = back[0].shape[0] // HD
    width = back[0].shape[1]
    count = begins.shape[0]
    together = 2 if heads % 2 == 0 else 1
    blocks = count // BK
    half = ROT // 2
    turn = jnp.asarray(offset * ((blocks // parts) if parts > 1 else 0), jnp.int32)
    facts = jnp.concatenate([begins[::BQ] // BK, turn[None]])
    whole = lambda rows: pl.BlockSpec((rows, count), lambda g, *_: (0, 0))
    mine = lambda rows: pl.BlockSpec((rows, width), lambda g, *_: (g, 0))
    results = pl.pallas_call(
        partial(attend_kernel, together, parts, len(after)),
        grid_spec=pltpu.PrefetchScalarGridSpec(
            num_scalar_prefetch=1,
            grid=(heads // together,),
            in_specs=[mine(together * 3 * HD)] * parts
            + [mine(together * HD)] * parts
            + [whole(1), whole(half), whole(half)]
            + [pl.BlockSpec(memory_space=pl.ANY)] * len(after),
            out_specs=[mine(together * HD)] * parts + [mine(together * 3 * HD)] * parts,
            scratch_shapes=[
                pltpu.VMEM((together, HD, count), jnp.bfloat16),
                pltpu.VMEM((together, HD, count), jnp.bfloat16),
                pltpu.VMEM((together, HD, count), jnp.bfloat16),
                pltpu.VMEM((together, count, HD), jnp.bfloat16),
                pltpu.VMEM((together, count, HD), jnp.bfloat16),
                pltpu.VMEM((together, HD, count), jnp.bfloat16),
                pltpu.VMEM((together, HD, count), jnp.float32),
                pltpu.VMEM((together, HD, count), jnp.float32),
                pltpu.VMEM((together, HD, count), jnp.float32),
                pltpu.VMEM((together, blocks, BK, BQ), jnp.float32),
                pltpu.VMEM((together, blocks, BK, BQ), jnp.float32),
                pltpu.VMEM((together, blocks, 1, BQ), jnp.float32),
            ],
        ),
        out_shape=[jax.ShapeDtypeStruct((heads * HD, width), jnp.bfloat16)] * parts
        + [jax.ShapeDtypeStruct((heads * 3 * HD, width), jnp.bfloat16)] * parts,
        compiler_params=pltpu.CompilerParams(vmem_limit_bytes=48 * 2**20),
        cost_estimate=pl.CostEstimate(
            flops=2**20,
            bytes_accessed=2**20,
            transcendentals=0,
        ),
    )(facts, *projected, *back, begins[None, :], cosine, sine, *after)
    return results[:parts], results[parts:]


def layer_norm(rows_in, gain, bias):
    mean = jnp.mean(rows_in, axis=1, keepdims=True)
    centred = rows_in - mean
    spread = jnp.mean(centred * centred, axis=1, keepdims=True)
    normed = centred * lax.rsqrt(spread + norm_epsilon)
    return normed * gain + bias


def adam_update(master, first, second, gradient, rate, decay):
    first_new = beta_one * first + (1.0 - beta_one) * gradient
    second_new = beta_two * second + (1.0 - beta_two) * gradient * gradient
    first_hat = first_new / (1.0 - beta_one**STEP)
    second_hat = second_new / (1.0 - beta_two**STEP)
    master_new = master - rate * (
        first_hat / (jnp.sqrt(second_hat) + adam_epsilon) + decay * master
    )
    return (master_new, first_new, second_new, master_new.astype(jnp.bfloat16))


def product(pattern, left, right):
    return jnp.einsum(pattern, left, right, preferred_element_type=jnp.float32)


def gelu_both(lifted, active_grad):
    activated, pull = jax.vjp(partial(jax.nn.gelu, approximate=True), lifted)
    return pull(active_grad)[0].astype(jnp.bfloat16)


def gelu(lifted):
    return jax.nn.gelu(lifted, approximate=True).astype(jnp.bfloat16)


def swap(array, axis, bit):
    size = lax.axis_size(axis)
    return lax.ppermute(array, axis, [(i, i ^ bit) for i in range(size)])


def follow(array, *before):
    return lax.optimization_barrier((array, *before))[0]


def ordered(index, mine, other, axis):
    return jnp.where(
        index == 0,
        jnp.concatenate([mine, other], axis=axis),
        jnp.concatenate([other, mine], axis=axis),
    )


UNITS = 512
ROWS = 640


def feed_kernel(
    earlier,
    hidden_ref,
    back_ref,
    expand_ref,
    shrink_ref,
    *refs,
):
    if earlier:
        expand_before, shrink_before = refs[:2]
        refs = refs[2:]
    (
        expand_grad,
        shrink_grad,
        hidden_part,
        branch_part,
        activated_ref,
        lifted_grad_ref,
        turned_ref,
        hidden_sum,
        branch_sum,
    ) = refs
    step, steps = pl.program_id(0), pl.num_programs(0)
    tokens = hidden_ref.shape[0]
    f32 = jnp.float32
    nt = (((1,), (1,)), ((), ()))
    tn = (((0,), (0,)), ((), ()))
    slope = 0.7978845608028654

    @pl.when(step == 0)
    def _():
        turned_ref[...] = hidden_ref[...].T

    def block(at, first):
        hidden = hidden_ref[at, :]
        back = back_ref[at, :]
        lifted = jnp.dot(hidden, expand_ref[...], preferred_element_type=f32)
        active_grad = lax.dot_general(back, shrink_ref[...], nt, preferred_element_type=f32)
        square = lifted * lifted
        curve = jnp.tanh(slope * (lifted + 0.044715 * (square * lifted)))
        rise = 0.5 * (1.0 + curve)
        activated = (lifted * rise).astype(jnp.bfloat16)
        bend = 0.5 * lifted * (1.0 - curve * curve) * (slope + (3.0 * 0.044715 * slope) * square)
        lifted_grad = (active_grad * (rise + bend)).astype(jnp.bfloat16)
        activated_ref[at, :] = activated
        lifted_grad_ref[at, :] = lifted_grad
        branch = jnp.dot(activated, shrink_ref[...], preferred_element_type=f32)
        hidden_grad = lax.dot_general(lifted_grad, expand_ref[...], nt, preferred_element_type=f32)
        if first:
            branch_sum[at, :] = branch
            hidden_sum[at, :] = hidden_grad
        else:
            branch_sum[at, :] += branch
            hidden_sum[at, :] += hidden_grad

    def blocks(first):
        def one(i, _):
            block(pl.ds(pl.multiple_of(i * ROWS, ROWS), ROWS), first)
            return 0

        lax.fori_loop(0, tokens // ROWS, one, 0)

    @pl.when(step == 0)
    def _():
        blocks(True)

    @pl.when(step > 0)
    def _():
        blocks(False)

    made = lax.dot_general(activated_ref[...], back_ref[...], tn, preferred_element_type=f32)
    shrink_grad[...] = made + shrink_before[...] if earlier else made
    made = jnp.dot(turned_ref[...], lifted_grad_ref[...], preferred_element_type=f32)
    expand_grad[...] = made + expand_before[...] if earlier else made

    @pl.when(step == steps - 1)
    def _():
        hidden_part[...] = hidden_sum[...].astype(hidden_part.dtype)
        branch_part[...] = branch_sum[...].astype(branch_part.dtype)


def feed(hidden, back, expand, shrink, before, branch_type):
    tokens, width = hidden.shape
    units = 2 * expand.shape[2]
    tile = min(UNITS, expand.shape[2])
    steps = units // tile
    low, f32 = jnp.bfloat16, jnp.float32
    whole = pl.BlockSpec((tokens, width), lambda n: (0, 0), pipeline_mode=pl.Buffered(1))
    columns = pl.BlockSpec((width, tile), lambda n: (0, n))
    rows = pl.BlockSpec((tile, width), lambda n: (n, 0))
    return pl.pallas_call(
        partial(feed_kernel, bool(before)),
        grid=(steps,),
        in_specs=[
            whole,
            whole,
            pl.BlockSpec((None, width, tile), lambda n: (n * 2 // steps, 0, n % (steps // 2))),
            rows,
        ]
        + [columns, rows] * bool(before),
        out_specs=[columns, rows, whole, whole],
        out_shape=[
            jax.ShapeDtypeStruct((width, units), f32),
            jax.ShapeDtypeStruct((units, width), f32),
            jax.ShapeDtypeStruct((tokens, width), f32),
            jax.ShapeDtypeStruct((tokens, width), branch_type),
        ],
        scratch_shapes=[
            pltpu.VMEM((tokens, tile), low),
            pltpu.VMEM((tokens, tile), low),
            pltpu.VMEM((width, tokens), low),
            pltpu.VMEM((tokens, width), f32),
            pltpu.VMEM((tokens, width), f32),
        ],
        compiler_params=pltpu.CompilerParams(vmem_limit_bytes=56 * 2**20),
        cost_estimate=pl.CostEstimate(flops=2**20, bytes_accessed=2**20, transcendentals=0),
    )(hidden, back, expand, shrink, *before)


MESH = pl.DeviceIdType.MESH


def opening_kernel(
    expand_ref,
    shrink_ref,
    project_ref,
    mixing_ref,
    norm_ref,
    inputs_ref,
    back_ref,
    expand_out,
    shrink_out,
    project_out,
    mixing_out,
    norm_out,
    hidden_ref,
    other_back,
    expand_low,
    shrink_low,
    norm_low,
    norm_all,
    own_sem,
    norm_send,
    norm_recv,
    line_send,
    line_recv,
    far_send,
    far_recv,
    near_send,
    near_recv,
    row_sem,
):
    place, deep = lax.axis_index("dp"), 4
    outer = lax.axis_index("outer")
    far, near = outer // 2, outer % 2
    far_id = {"outer": (outer + 2) % 4}
    near_id = {"outer": outer + 1 - 2 * near}
    rows = expand_ref.shape[0]
    half = expand_ref.shape[1] // 2
    part = half // 2

    barrier = pltpu.get_barrier_semaphore()
    for step in range(1, deep):
        pl.semaphore_signal(
            barrier, inc=1, device_id={"dp": (place + step) % deep}, device_id_type=MESH
        )
    pl.semaphore_signal(barrier, inc=1, device_id=far_id, device_id_type=MESH)
    pl.semaphore_signal(barrier, inc=1, device_id=near_id, device_id_type=MESH)
    row_id = {"mp": 1 - lax.axis_index("mp")}
    pl.semaphore_signal(barrier, inc=1, device_id=row_id, device_id_type=MESH)

    expand_low[...] = expand_ref[...].astype(jnp.bfloat16)
    norm_low[...] = jnp.zeros_like(norm_low)
    norm_low[0:2] = norm_ref[...].astype(jnp.bfloat16).astype(jnp.float32)
    pl.semaphore_wait(barrier, deep + 2)

    def piece(w, which, at, side):
        across = pl.ds(pl.multiple_of(at * rows, rows), rows)
        along = pl.ds(pl.multiple_of(side * part, part), part)
        if w == 0:
            return expand_out.at[which, across, along]
        return shrink_out.at[which, along, across]

    def mine(w):
        along = pl.ds(pl.multiple_of(near * half + far * part, part), part)
        return expand_low.at[:, along] if w == 0 else shrink_low.at[along, :]

    def remote(source, target, send, recv, device):
        return pltpu.make_async_remote_copy(
            src_ref=source,
            dst_ref=target,
            send_sem=send,
            recv_sem=recv,
            device_id=device,
            device_id_type=MESH,
        )

    def line(w, way, step, source, at):
        to = place + 1 if way == 0 else place - 1
        return remote(
            source,
            piece(w, 0, at, far),
            line_send.at[w, way, step],
            line_recv.at[w, way, step],
            {"dp": to},
        )

    def can_send(way):
        return place < deep - 1 if way == 0 else place > 0

    def start_own(w):
        for way in range(2):

            @pl.when(can_send(way))
            def _(way=way):
                line(w, way, 0, mine(w), place).start()

    def own_copies(w):
        out = []
        for which in range(2):
            side = near + which - 2 * near * which
            along = pl.ds(pl.multiple_of(side * half, half), half)
            across = pl.ds(pl.multiple_of(place * rows, rows), rows)
            if w == 0:
                pair = (expand_low.at[:, along], expand_out.at[which, across, :])
            else:
                pair = (shrink_low.at[along, :], shrink_out.at[which, :, across])
            out.append(pltpu.make_async_copy(*pair, own_sem.at[w, which]))
        return out

    start_own(0)
    row_copy = remote(back_ref, other_back, row_sem.at[0], row_sem.at[1], row_id)
    row_copy.start()
    norm_copies = []
    for step in range(1, deep):
        copy = remote(
            norm_low,
            norm_all.at[step],
            norm_send.at[step],
            norm_recv.at[step],
            {"dp": (place + step) % deep},
        )
        copy.start()
        norm_copies.append(copy)
    shrink_low[...] = shrink_ref[...].astype(jnp.bfloat16)
    start_own(1)
    for w in range(2):
        for copy in own_copies(w):
            copy.start()
    heads = project_ref.shape[1] // 2
    units = mixing_ref.shape[0] // 2
    project_out[...] = project_ref[
        :, pl.ds(pl.multiple_of(near * heads, heads), heads)
    ].astype(jnp.bfloat16)
    mixing_out[...] = mixing_ref[
        pl.ds(pl.multiple_of(near * units, units), units), :
    ].astype(jnp.bfloat16)
    norm_all[0] = norm_low[...]
    for copy in norm_copies:
        copy.wait()
    for at in range(deep):
        norm_out[:, at * rows : (at + 1) * rows] = norm_all[(place - at + deep) % deep]
    gain, bias = norm_out[0:1], norm_out[1:2]
    tokens = inputs_ref.shape[0]
    height = 128

    def normalize(i, _):
        at = pl.ds(pl.multiple_of(i * height, height), height)
        x = inputs_ref[at, :].astype(jnp.float32)
        mean = jnp.mean(x, axis=1, keepdims=True)
        centred = x - mean
        spread = jnp.mean(centred * centred, axis=1, keepdims=True)
        normed = centred * lax.rsqrt(spread + norm_epsilon)
        hidden_ref[at, :] = (normed * gain + bias).astype(jnp.bfloat16)
        return 0

    lax.fori_loop(0, tokens // height, normalize, 0)

    def arrives(way, step):
        return place >= step if way == 0 else place + step < deep

    def at_of(way, step):
        return place - step if way == 0 else place + step

    def to_far(w, way, step):
        at = at_of(way, step)
        return remote(
            piece(w, 0, at, far),
            piece(w, 0, at, far),
            far_send.at[w, way, step - 1],
            far_recv.at[w, way, step - 1],
            far_id,
        )

    def from_far(w, way, step):
        at = at_of(way, step)
        return remote(
            piece(w, 0, at, 1 - far),
            piece(w, 0, at, 1 - far),
            far_send.at[w, way, step - 1],
            far_recv.at[w, way, step - 1],
            far_id,
        )

    def to_near(w, way, step, other):
        at = at_of(way, step)
        side = 1 - far if other else far
        return remote(
            piece(w, 0, at, side),
            piece(w, 1, at, side),
            near_send.at[w, way, step - 1, other],
            near_recv.at[w, way, step - 1, other],
            near_id,
        )

    order = [(w, step) for w in range(2) for step in range(1, deep)]

    def first_half(w, step):
        for way in range(2):

            @pl.when(arrives(way, step))
            def _(way=way):
                at = at_of(way, step)
                line(w, way, step - 1, mine(w), at).wait_recv()
                if step < deep - 1:

                    @pl.when(can_send(way))
                    def _():
                        line(w, way, step, piece(w, 0, at, far), at).start()

                to_far(w, way, step).start()
                to_near(w, way, step, 0).start()

    def second_half(w, step):
        for way in range(2):

            @pl.when(arrives(way, step))
            def _(way=way):
                from_far(w, way, step).wait_recv()
                to_near(w, way, step, 1).start()

    for n, (w, step) in enumerate(order):
        first_half(w, step)
        if n:
            second_half(*order[n - 1])
    second_half(*order[-1])
    row_copy.wait()
    for w in range(2):
        for copy in own_copies(w):
            copy.wait()
        for way in range(2):

            @pl.when(can_send(way))
            def _(way=way):
                line(w, way, 0, mine(w), place).wait_send()

            for step in range(1, deep):

                @pl.when(arrives(way, step))
                def _(way=way, step=step):
                    at = at_of(way, step)
                    if step < deep - 1:

                        @pl.when(can_send(way))
                        def _():
                            line(w, way, step, piece(w, 0, at, far), at).wait_send()

                    to_far(w, way, step).wait_send()
                    for other in range(2):
                        to_near(w, way, step, other).wait_send()
                        to_near(w, way, step, other).wait_recv()


def opening(expand, shrink, project, mixing, norm, inputs, back):
    deep = 4
    here = lambda: pl.BlockSpec(memory_space=pltpu.VMEM)
    rows, units = expand.shape
    low = jnp.bfloat16
    sem = pltpu.SemaphoreType.DMA
    return pl.pallas_call(
        opening_kernel,
        in_specs=[here() for _ in range(6)] + [pl.BlockSpec(memory_space=pl.ANY)],
        out_specs=[pl.BlockSpec(memory_space=pl.ANY)] * 2
        + [here() for _ in range(4)]
        + [pl.BlockSpec(memory_space=pl.ANY)],
        out_shape=[
            jax.ShapeDtypeStruct((2, rows * deep, units // 2), low),
            jax.ShapeDtypeStruct((2, units // 2, rows * deep), low),
            jax.ShapeDtypeStruct((project.shape[0], project.shape[1] // 2), low),
            jax.ShapeDtypeStruct((mixing.shape[0] // 2, mixing.shape[1]), low),
            jax.ShapeDtypeStruct((8, rows * deep), jnp.float32),
            jax.ShapeDtypeStruct(inputs.shape, low),
            jax.ShapeDtypeStruct(back.shape, low),
        ],
        scratch_shapes=[
            pltpu.VMEM(expand.shape, low),
            pltpu.VMEM(shrink.shape, low),
            pltpu.VMEM((8, norm.shape[1]), jnp.float32),
            pltpu.VMEM((deep, 8, norm.shape[1]), jnp.float32),
            sem((2, 2)),
            sem((deep,)),
            sem((deep,)),
            sem((2, 2, deep)),
            sem((2, 2, deep)),
            sem((2, 2, deep)),
            sem((2, 2, deep)),
            sem((2, 2, deep, 2)),
            sem((2, 2, deep, 2)),
            sem((2,)),
        ],
        compiler_params=pltpu.CompilerParams(
            collective_id=1, has_side_effects=True, vmem_limit_bytes=40 * 2**20
        ),
        cost_estimate=pl.CostEstimate(flops=0, bytes_accessed=2**20, transcendentals=0),
    )(expand, shrink, project, mixing, norm, inputs, back)


def total_kernel(term_ref, out_ref, first, second, first_send, first_recv, second_send, second_recv):
    split, outers, deep = first.shape[0] // 4, 4, second.shape[0]
    plane = split * outers
    place = lax.axis_index("dp")
    me = lax.axis_index("mp") * outers + lax.axis_index("outer")

    def plane_id(step):
        other = (me + step) % plane
        return {"mp": other // outers, "outer": other % outers}

    def line_id(step):
        return {"dp": (place + step) % deep}

    barrier = pltpu.get_barrier_semaphore()
    for step in range(1, plane):
        pl.semaphore_signal(barrier, inc=1, device_id=plane_id(step), device_id_type=MESH)
    for step in range(1, deep):
        pl.semaphore_signal(barrier, inc=1, device_id=line_id(step), device_id_type=MESH)
    pl.semaphore_wait(barrier, plane + deep - 2)

    def exchange(source, slots, send, recv, size, device):
        copies = []
        for step in range(1, size):
            copy = pltpu.make_async_remote_copy(
                src_ref=source,
                dst_ref=slots.at[step],
                send_sem=send.at[step],
                recv_sem=recv.at[step],
                device_id=device(step),
                device_id_type=MESH,
            )
            copy.start()
            copies.append(copy)
        slots[0] = source[...]
        for copy in copies:
            copy.wait()

    exchange(term_ref, first, first_send, first_recv, plane, plane_id)
    total = first[me]
    for at in range(1, plane):
        total = total + first[(me + plane - at) % plane]
    out_ref[...] = total
    exchange(out_ref, second, second_send, second_recv, deep, line_id)
    total = second[place]
    for at in range(1, deep):
        total = total + second[(place + deep - at) % deep]
    out_ref[...] = total


def total_over_all(term, split, deep):
    plane = split * 4
    sem = pltpu.SemaphoreType.DMA
    return pl.pallas_call(
        total_kernel,
        in_specs=[pl.BlockSpec(memory_space=pltpu.VMEM)],
        out_specs=pl.BlockSpec(memory_space=pltpu.VMEM),
        out_shape=jax.ShapeDtypeStruct(term.shape, term.dtype),
        scratch_shapes=[
            pltpu.VMEM((plane, *term.shape), term.dtype),
            pltpu.VMEM((deep, *term.shape), term.dtype),
            sem((plane,)),
            sem((plane,)),
            sem((deep,)),
            sem((deep,)),
        ],
        compiler_params=pltpu.CompilerParams(collective_id=2, has_side_effects=True),
    )(term)


class Paired:
    def __init__(self):
        outer = lax.axis_index("outer")
        self.far, self.near = outer // 2, outer % 2
        self.place = lax.axis_index("dp")
        self.deep = lax.axis_size("dp")

    def gather(self, own, cut, depth):
        own = lax.all_gather(own, "dp", axis=depth, tiled=True)
        return jnp.concatenate([own, swap(own, "outer", 1)], axis=cut)

    def gather_few(self, own, cut, depth):
        wide = list(own.shape)
        piece = wide[depth]
        wide[depth] *= self.deep
        out = jnp.zeros(wide, own.dtype)
        for step in range(self.deep):
            pairs = [(i, (i + step) % self.deep) for i in range(self.deep)]
            come = lax.ppermute(own, "dp", pairs) if step else own
            at = lax.rem(self.place - step + self.deep, self.deep)
            out = lax.dynamic_update_slice_in_dim(out, come, at * piece, depth)
        return jnp.concatenate([out, swap(out, "outer", 1)], axis=cut)

    def pair_sum(self, own, sibling, cut):
        own = own + swap(sibling, "outer", 1)
        half = own.shape[cut] // 2
        keep = lax.dynamic_slice_in_dim(own, self.far * half, half, cut)
        send = lax.dynamic_slice_in_dim(own, (1 - self.far) * half, half, cut)
        return keep, swap(send.astype(jnp.bfloat16), "outer", 2)

    def line_sum(self, keep, come, depth):
        keep = keep + come.astype(jnp.float32)
        piece = keep.shape[depth] // self.deep

        def part(at):
            return lax.dynamic_slice_in_dim(keep, at * piece, piece, depth)

        result = part(self.place)
        for step in range(1, self.deep):
            target = lax.rem(self.place + step, self.deep)
            pairs = [(i, (i + step) % self.deep) for i in range(self.deep)]
            result = result + lax.ppermute(
                part(target).astype(jnp.bfloat16), "dp", pairs
            ).astype(jnp.float32)
        return result

    def spread(self, share, cut):
        pair = ordered(self.far, share, swap(share, "outer", 2), cut)
        return ordered(self.near, pair, swap(pair, "outer", 1), cut)


def local(
    inputs,
    cotangent,
    lengths,
    project_master,
    project_first,
    project_second,
    mixing_master,
    mixing_first,
    mixing_second,
    expand_master,
    expand_first,
    expand_second,
    shrink_master,
    shrink_first,
    shrink_second,
    norm_master,
    norm_first,
    norm_second,
):
    split, deep = lax.axis_size("mp"), lax.axis_size("dp")
    heads_here = project_master.shape[1]
    width = inputs.shape[1]
    paired = (
        split == 2
        and lax.axis_size("outer") == 4
        and heads_here % 4 == 0
        and width % BQ == 0
    )
    position = lax.axis_index("mp")
    count = width * split
    project_flat = project_master.reshape(project_master.shape[0], heads_here * 3 * HD)
    mixing_flat = mixing_master.reshape(heads_here * HD, mixing_master.shape[2])
    masters = (project_flat, mixing_flat, expand_master, shrink_master)
    cuts, depths = (1, 0, 1, 0), (0, 1, 0, 1)
    rows_local = inputs[0].astype(jnp.float32)
    begins, places = layout(lengths[0], count)
    cosine, sine = turns(places)
    if paired:
        plan = Paired()
        expand, shrink, project, mixing, norm_weight, hidden_local, other_back = opening(
            expand_master,
            shrink_master,
            project_flat,
            mixing_flat,
            norm_master,
            inputs[0],
            cotangent[0],
        )
        backs = [cotangent[0], other_back]
        shrink = shrink.reshape(-1, shrink.shape[2])
        project = plan.gather(project, 1, 0)
        mixing = plan.gather_few(mixing, 0, 1)
        gain, bias = norm_weight[0], norm_weight[1]
        norm_pull = jax.vjp(layer_norm, rows_local, gain, bias)[1]
        hiddens = [hidden_local, swap(hidden_local, "mp", 1)]
    else:
        norm_weight = lax.all_gather(norm_master.astype(jnp.bfloat16), "dp", axis=1, tiled=True)
        gain = norm_weight[0].astype(jnp.float32)
        bias = norm_weight[1].astype(jnp.float32)
        shaped, norm_pull = jax.vjp(layer_norm, rows_local, gain, bias)
        hidden_local = shaped.astype(jnp.bfloat16)
        project, mixing, expand, shrink = (
            lax.all_gather(master.astype(jnp.bfloat16), "dp", axis=depth, tiled=True)
            for master, depth in zip(masters, depths)
        )
        backs = [lax.all_gather(cotangent[0], "mp", axis=0, tiled=True)]
        hiddens = [lax.all_gather(hidden_local, "mp", axis=0, tiled=True)]

    def over_tokens(pattern, lefts, rights):
        return sum(product(pattern, left, right) for left, right in zip(lefts, rights))

    def halves(pattern, lefts, rights, cut):
        sources = rights if cut == 1 else lefts
        axis = 0 if pattern.split(",")[cut].index("t") == 1 else 1
        half = sources[0].shape[axis] // 2
        out = []
        for near in (1, 0):
            chosen = [
                lax.slice_in_dim(v, near * half, (near + 1) * half, axis=axis) for v in sources
            ]
            pair = (lefts, chosen) if cut == 1 else (chosen, rights)
            out.append(over_tokens(pattern, *pair))
        return out

    back_local = cotangent[0].astype(jnp.float32)
    if paired:
        *grads, hidden_own, branch_own = feed(
            hiddens[0], backs[0], expand, shrink, (), jnp.float32
        )
        expand_grad, shrink_grad, hidden_other, branch_other = feed(
            hiddens[1], backs[1], expand, shrink, grads, jnp.bfloat16
        )
        hidden_parts = [hidden_own, hidden_other]
        half = expand_grad.shape[1] // 2
        shrink_keep, shrink_come = plan.pair_sum(shrink_grad[:half], shrink_grad[half:], 0)
        expand_keep, expand_come = plan.pair_sum(expand_grad[:, :half], expand_grad[:, half:], 1)
        branch_come = swap(branch_other, "mp", 1)
        mixing_other = swap(mixing, "mp", 1)
        projected = [product("td,de->et", hidden, project) for hidden in hiddens]
        mixed_backs = [product("td,fd->ft", back, mixing).astype(jnp.bfloat16) for back in backs]
        mixed, projected_grads = attend(
            projected,
            mixed_backs,
            begins,
            cosine,
            sine,
            position,
            (shrink_keep, expand_keep),
        )
        first_grad = follow(projected_grads[1], shrink_come, expand_come, branch_come)
        sent = (hidden_parts[1] + product("et,de->td", first_grad, project)).astype(jnp.bfloat16)
        hidden_come = swap(sent, "mp", 1)
        projected_grads = [follow(v, sent) for v in projected_grads]
        mixed = [follow(v, sent) for v in mixed]
        mixed_come = swap(mixed[1], "mp", 1)
        project_terms = halves("td,et->de", hiddens, projected_grads, 1)
        project_sum = plan.line_sum(*plan.pair_sum(project_terms[1], project_terms[0], 1), 0)
        mixing_terms = halves("ft,td->fd", mixed, backs, 0)
        mixing_sum = plan.line_sum(*plan.pair_sum(mixing_terms[1], mixing_terms[0], 0), 1)
        shrink_sum = plan.line_sum(shrink_keep, shrink_come, 1)
        expand_sum = plan.line_sum(expand_keep, expand_come, 0)
        hidden_grad = (
            hidden_parts[0]
            + product("et,de->td", projected_grads[0], project)
            + hidden_come.astype(jnp.float32)
        )
        branch = (
            branch_own
            + branch_come.astype(jnp.float32)
            + product("ft,fd->td", mixed[0], mixing)
            + product("ft,fd->td", mixed_come, mixing_other)
        )
    else:
        lifteds = [product("td,df->tf", hidden, expand) for hidden in hiddens]
        activated = [gelu(lifted) for lifted in lifteds]
        active_grads = [product("td,fd->tf", back, shrink) for back in backs]
        lifted_grads = [gelu_both(a, b) for a, b in zip(lifteds, active_grads)]
        hidden_parts = [product("tf,df->td", v, expand) for v in lifted_grads]
        branch_parts = [product("tf,fd->td", v, shrink) for v in activated]
        projected = [product("td,de->et", hidden, project) for hidden in hiddens]
        mixed_backs = [product("td,fd->ft", back, mixing).astype(jnp.bfloat16) for back in backs]
        mixed, projected_grads = attend(projected, mixed_backs, begins, cosine, sine, position)
        project_sum, mixing_sum, expand_sum, shrink_sum = (
            lax.psum(
                lax.psum_scatter(
                    over_tokens(pattern, lefts, rights),
                    "dp",
                    scatter_dimension=depth,
                    tiled=True,
                ),
                "outer",
            )
            for pattern, lefts, rights, depth in (
                ("td,et->de", hiddens, projected_grads, 0),
                ("ft,td->fd", mixed, backs, 1),
                ("td,tf->df", hiddens, lifted_grads, 0),
                ("tf,td->fd", activated, backs, 1),
            )
        )
        hidden_grad, branch = (
            lax.psum_scatter(v, "mp", scatter_dimension=0, tiled=True)
            for v in (
                hidden_parts[0] + product("et,de->td", projected_grads[0], project),
                branch_parts[0] + product("ft,fd->td", mixed[0], mixing),
            )
        )
    rows_grad, gain_grad, bias_grad = norm_pull(hidden_grad)
    input_grad = (back_local + rows_grad)[None]
    block_out = (rows_local + branch).astype(jnp.bfloat16)[None]
    sums = (project_sum, mixing_sum, expand_sum, shrink_sum)
    own_square = sum(jnp.sum(v * v) for v in sums)
    if not paired:
        own_square = own_square / lax.axis_size("outer")
    norm_terms = jnp.concatenate([gain_grad, bias_grad, jnp.full((D,), own_square)])
    norm_terms = norm_terms.reshape(-1, 128)
    if paired:
        norm_all = total_over_all(norm_terms, split, deep)
    else:
        norm_all = lax.psum(norm_terms, ("mp", "dp", "outer"))
    norm_all = norm_all.reshape(3, D)
    norm_full = norm_all[:2]
    grad_norm = jnp.sqrt(norm_all[2, 0] + jnp.sum(norm_full * norm_full))
    factor = clip_level / jnp.maximum(grad_norm, clip_level)
    norm_gradient = lax.dynamic_slice_in_dim(
        norm_full, lax.axis_index("dp") * (D // deep), D // deep, 1
    )
    gradients = [
        (plan.spread(v, cut) if paired else v).reshape(master.shape)
        for v, cut, master in zip(
            sums, cuts, (project_master, mixing_master, expand_master, shrink_master)
        )
    ]
    states = (
        (project_master, project_first, project_second, D ** (-0.5)),
        (mixing_master, mixing_first, mixing_second, (D // 32) ** (-0.5)),
        (expand_master, expand_first, expand_second, D ** (-0.5)),
        (shrink_master, shrink_first, shrink_second, FF ** (-0.5)),
    )
    results = [block_out, input_grad]
    for (master, first, second, rate), gradient in zip(states, gradients):
        results += adam_update(master, first, second, factor * gradient, rate, decay_rate)
    results += adam_update(norm_master, norm_first, norm_second, factor * norm_gradient, 0.3, 0.0)
    return (*results, grad_norm)


def solution(mesh):
    in_specs = (
        P(("dp", "outer"), "mp", None),
        P(("dp", "outer"), "mp", None),
        P(("dp", "outer"), None),
        P("dp", "mp", None),
        P("dp", "mp", None),
        P("dp", "mp", None),
        P("mp", None, "dp"),
        P("mp", None, "dp"),
        P("mp", None, "dp"),
        P("dp", "mp"),
        P("dp", "mp"),
        P("dp", "mp"),
        P("mp", "dp"),
        P("mp", "dp"),
        P("mp", "dp"),
        P(None, "dp"),
        P(None, "dp"),
        P(None, "dp"),
    )
    out_specs = (
        P(("dp", "outer"), "mp", None),
        P(("dp", "outer"), "mp", None),
        P("dp", "mp", None),
        P("dp", "mp", None),
        P("dp", "mp", None),
        P("dp", "mp", None),
        P("mp", None, "dp"),
        P("mp", None, "dp"),
        P("mp", None, "dp"),
        P("mp", None, "dp"),
        P("dp", "mp"),
        P("dp", "mp"),
        P("dp", "mp"),
        P("dp", "mp"),
        P("mp", "dp"),
        P("mp", "dp"),
        P("mp", "dp"),
        P("mp", "dp"),
        P(None, "dp"),
        P(None, "dp"),
        P(None, "dp"),
        P(None, "dp"),
        P(),
    )
    return jax.shard_map(local, mesh=mesh, in_specs=in_specs, out_specs=out_specs, check_vma=False)
```

```python
from functools import partial
import math

import jax
import jax.numpy as jnp
from jax import lax
from jax.experimental import pallas as pl
from jax.experimental.pallas import tpu as pltpu
from jax.sharding import PartitionSpec as P

D = 1024
HD = 64
ROT = 32
FF = 4096
STEP = 10


norm_epsilon = 1e-05
beta_one = 0.9
beta_two = 0.95
adam_epsilon = 1e-08
decay_rate = 0.1
clip_level = 1.0
masked_value = -1e30


def layout(sizes_row, count):
    number = jnp.arange(sizes_row.shape[0], dtype=jnp.int32)
    ends = jnp.sum(jnp.where(number[None, :] <= number[:, None], sizes_row[None, :], 0), axis=1)
    tokens = jnp.arange(count, dtype=jnp.int32)
    passed = (ends[:, None] <= tokens[None, :]).astype(jnp.int32)
    begins = jnp.sum(passed * sizes_row[:, None], axis=0)
    return (begins, tokens - begins)


def turns(places):
    half_rot = ROT // 2
    counter = jnp.arange(half_rot, dtype=jnp.float32)
    frequency = jnp.exp(counter * (-2.0 * math.log(10000.0) / ROT))
    angles = places.astype(jnp.float32)[None, :] * frequency[:, None]
    return jnp.cos(angles), jnp.sin(angles)


BQ = 256
BK = 256


def attend_kernel(together, parts, later, *refs):
    facts = refs[0]
    projected_refs = refs[1 : 1 + parts]
    back_refs = refs[1 + parts : 1 + 2 * parts]
    start_ref, cos_ref, sin_ref = refs[1 + 2 * parts : 4 + 2 * parts]
    refs = refs[: 4 + 2 * parts] + refs[4 + 2 * parts + later :]
    mixed_refs = refs[4 + 2 * parts : 4 + 3 * parts]
    grad_refs = refs[4 + 3 * parts : 4 + 4 * parts]
    (
        query_ref,
        key_columns_ref,
        value_columns_ref,
        key_ref,
        value_ref,
        back_ref,
        query_grad_ref,
        key_grad_ref,
        value_grad_ref,
        shifted_ref,
        share_grad_ref,
        top_ref,
    ) = refs[4 + 4 * parts :]
    width = projected_refs[0].shape[1]
    count = width * parts
    blocks = count // BQ
    turn = facts[blocks]
    half = ROT // 2
    scale = HD ** (-0.5)
    nt = (((1,), (1,)), ((), ()))

    def place_of(part):
        if parts == 1:
            return pl.ds(0, width)
        block = lax.rem(part * (blocks // parts) + blocks - turn, blocks)
        return pl.ds(pl.multiple_of(block * BQ, BQ), width)

    for part in range(parts):
        columns = slice(part * width, (part + 1) * width)
        cosine, sine = cos_ref[:, place_of(part)], sin_ref[:, place_of(part)]
        projected_ref = projected_refs[part]

        def turned(at):
            first = projected_ref[at : at + half]
            second = projected_ref[at + half : at + ROT]
            return jnp.concatenate(
                [
                    first * cosine - second * sine,
                    second * cosine + first * sine,
                    projected_ref[at + ROT : at + HD],
                ],
                axis=0,
            ).astype(jnp.bfloat16)

        for h in range(together):
            base = h * 3 * HD
            query_ref[h, :, columns] = (turned(base).astype(jnp.float32) * scale).astype(
                jnp.bfloat16
            )
            keys = turned(base + HD)
            values = projected_ref[base + 2 * HD : base + 3 * HD].astype(jnp.bfloat16)
            key_columns_ref[h, :, columns] = keys
            value_columns_ref[h, :, columns] = values
            key_ref[h, columns] = keys.T
            value_ref[h, columns] = values.T
            back_ref[h, :, columns] = back_refs[part][h * HD : (h + 1) * HD]
    key_grad_ref[...] = jnp.zeros_like(key_grad_ref)
    value_grad_ref[...] = jnp.zeros_like(value_grad_ref)
    key_at = lax.broadcasted_iota(jnp.int32, (BK, BQ), 0)
    query_at = lax.broadcasted_iota(jnp.int32, (1, BQ), 1)

    def stored(block):
        if parts == 1:
            return pl.ds(pl.multiple_of(block * BQ, BQ), BQ)
        return pl.ds(pl.multiple_of(lax.rem(block + turn, blocks) * BQ, BQ), BQ)

    def query_block(i, _):
        columns = stored(i)
        start = start_ref[:, pl.ds(pl.multiple_of(i * BQ, BQ), BQ)]
        own = query_at + i * BQ
        lowest = facts[i]
        queries = [query_ref[h, :, columns] for h in range(together)]
        backs = [back_ref[h, :, columns] for h in range(together)]

        def in_pairs(body, carry):
            twos = lax.div(i + 1 - lowest, 2)
            carry = lax.fori_loop(
                0, twos, lambda n, c: body((lowest + 2 * n, lowest + 2 * n + 1), c), carry
            )
            return lax.fori_loop(lowest + 2 * twos, i + 1, lambda n, c: body((n,), c), carry)

        def scores(group, carry):
            made = []
            for j in group:
                rows = stored(j)
                allowed = (key_at >= start - j * BK) & (key_at <= own - j * BK)
                for h in range(together):
                    raw = jnp.dot(
                        key_ref[h, rows, :], queries[h], preferred_element_type=jnp.float32
                    )
                    share_grad = jnp.dot(
                        value_ref[h, rows, :], backs[h], preferred_element_type=jnp.float32
                    )
                    masked = jnp.where(allowed, raw, masked_value)
                    here = jnp.max(masked, axis=0, keepdims=True)
                    shifted = jnp.exp(masked - here)
                    shifted_ref[h, j] = shifted
                    share_grad_ref[h, j] = share_grad
                    top_ref[h, j] = here
                    made.append(
                        (
                            here,
                            jnp.sum(shifted, axis=0, keepdims=True),
                            jnp.sum(shifted * share_grad, axis=0, keepdims=True),
                        )
                    )
            out = []
            for h in range(together):
                top, total, inner = carry[h]
                for here, here_total, here_inner in made[h::together]:
                    new = jnp.maximum(top, here)
                    old_by, here_by = jnp.exp(top - new), jnp.exp(here - new)
                    total = total * old_by + here_total * here_by
                    inner = inner * old_by + here_inner * here_by
                    top = new
                out.append((top, total, inner))
            return tuple(out)

        zero = jnp.zeros((1, BQ), jnp.float32)
        empty = (jnp.full((1, BQ), masked_value, jnp.float32), zero, zero)
        stats = in_pairs(scores, (empty,) * together)
        inverse = [1.0 / s[1] for s in stats]
        inners = [s[2] * r for s, r in zip(stats, inverse)]

        def sums(group, carry):
            out = list(carry)
            for j in group:
                rows = stored(j)
                for h in range(together):
                    mixed, query_grad = out[h]
                    by = jnp.exp(top_ref[h, j] - stats[h][0]) * inverse[h]
                    probs = shifted_ref[h, j] * by
                    shares = probs.astype(jnp.bfloat16)
                    score_grad = (probs * (share_grad_ref[h, j] - inners[h])).astype(jnp.bfloat16)
                    mixed = mixed + jnp.dot(
                        value_columns_ref[h, :, rows], shares, preferred_element_type=jnp.float32
                    )
                    query_grad = query_grad + jnp.dot(
                        key_columns_ref[h, :, rows], score_grad, preferred_element_type=jnp.float32
                    )
                    value_grad_ref[h, :, rows] += lax.dot_general(
                        backs[h], shares, nt, preferred_element_type=jnp.float32
                    )
                    key_grad_ref[h, :, rows] += lax.dot_general(
                        queries[h], score_grad, nt, preferred_element_type=jnp.float32
                    )
                    out[h] = (mixed, query_grad)
            return tuple(out)

        nothing = jnp.zeros((HD, BQ), jnp.float32)
        results = in_pairs(sums, ((nothing, nothing),) * together)
        for h in range(together):
            back_ref[h, :, columns] = results[h][0].astype(jnp.bfloat16)
            query_grad_ref[h, :, columns] = results[h][1] * scale
        return 0

    lax.fori_loop(0, blocks, query_block, 0)
    for part in range(parts):
        columns = slice(part * width, (part + 1) * width)
        cosine, sine = cos_ref[:, place_of(part)], sin_ref[:, place_of(part)]

        def turned_back(ref, h):
            first, second = ref[h, :half, columns], ref[h, half:ROT, columns]
            return jnp.concatenate(
                [
                    first * cosine + second * sine,
                    second * cosine - first * sine,
                    ref[h, ROT:, columns],
                ],
                axis=0,
            ).astype(jnp.bfloat16)

        for h in range(together):
            base = h * 3 * HD
            mixed_refs[part][h * HD : (h + 1) * HD] = back_ref[h, :, columns]
            grad_refs[part][base : base + HD] = turned_back(query_grad_ref, h)
            grad_refs[part][base + HD : base + 2 * HD] = turned_back(key_grad_ref, h)
            grad_refs[part][base + 2 * HD : base + 3 * HD] = value_grad_ref[h, :, columns].astype(
                jnp.bfloat16
            )


def attend(projected, back, begins, cosine, sine, offset, after=()):
    parts = len(projected)
    heads = back[0].shape[0] // HD
    width = back[0].shape[1]
    count = begins.shape[0]
    together = 2 if heads % 2 == 0 else 1
    blocks = count // BK
    half = ROT // 2
    turn = jnp.asarray(offset * ((blocks // parts) if parts > 1 else 0), jnp.int32)
    facts = jnp.concatenate([begins[::BQ] // BK, turn[None]])
    whole = lambda rows: pl.BlockSpec((rows, count), lambda g, *_: (0, 0))
    mine = lambda rows: pl.BlockSpec((rows, width), lambda g, *_: (g, 0))
    results = pl.pallas_call(
        partial(attend_kernel, together, parts, len(after)),
        grid_spec=pltpu.PrefetchScalarGridSpec(
            num_scalar_prefetch=1,
            grid=(heads // together,),
            in_specs=[mine(together * 3 * HD)] * parts
            + [mine(together * HD)] * parts
            + [whole(1), whole(half), whole(half)]
            + [pl.BlockSpec(memory_space=pl.ANY)] * len(after),
            out_specs=[mine(together * HD)] * parts + [mine(together * 3 * HD)] * parts,
            scratch_shapes=[
                pltpu.VMEM((together, HD, count), jnp.bfloat16),
                pltpu.VMEM((together, HD, count), jnp.bfloat16),
                pltpu.VMEM((together, HD, count), jnp.bfloat16),
                pltpu.VMEM((together, count, HD), jnp.bfloat16),
                pltpu.VMEM((together, count, HD), jnp.bfloat16),
                pltpu.VMEM((together, HD, count), jnp.bfloat16),
                pltpu.VMEM((together, HD, count), jnp.float32),
                pltpu.VMEM((together, HD, count), jnp.float32),
                pltpu.VMEM((together, HD, count), jnp.float32),
                pltpu.VMEM((together, blocks, BK, BQ), jnp.float32),
                pltpu.VMEM((together, blocks, BK, BQ), jnp.float32),
                pltpu.VMEM((together, blocks, 1, BQ), jnp.float32),
            ],
        ),
        out_shape=[jax.ShapeDtypeStruct((heads * HD, width), jnp.bfloat16)] * parts
        + [jax.ShapeDtypeStruct((heads * 3 * HD, width), jnp.bfloat16)] * parts,
        compiler_params=pltpu.CompilerParams(vmem_limit_bytes=48 * 2**20),
        cost_estimate=pl.CostEstimate(
            flops=2**20,
            bytes_accessed=2**20,
            transcendentals=0,
        ),
    )(facts, *projected, *back, begins[None, :], cosine, sine, *after)
    return results[:parts], results[parts:]


def layer_norm(rows_in, gain, bias):
    mean = jnp.mean(rows_in, axis=1, keepdims=True)
    centred = rows_in - mean
    spread = jnp.mean(centred * centred, axis=1, keepdims=True)
    normed = centred * lax.rsqrt(spread + norm_epsilon)
    return normed * gain + bias


def adam_update(master, first, second, gradient, rate, decay):
    first_new = beta_one * first + (1.0 - beta_one) * gradient
    second_new = beta_two * second + (1.0 - beta_two) * gradient * gradient
    first_hat = first_new / (1.0 - beta_one**STEP)
    second_hat = second_new / (1.0 - beta_two**STEP)
    master_new = master - rate * (
        first_hat / (jnp.sqrt(second_hat) + adam_epsilon) + decay * master
    )
    return (master_new, first_new, second_new, master_new.astype(jnp.bfloat16))


def product(pattern, left, right):
    return jnp.einsum(pattern, left, right, preferred_element_type=jnp.float32)


def gelu_both(lifted, active_grad):
    activated, pull = jax.vjp(partial(jax.nn.gelu, approximate=True), lifted)
    return pull(active_grad)[0].astype(jnp.bfloat16)


def gelu(lifted):
    return jax.nn.gelu(lifted, approximate=True).astype(jnp.bfloat16)


def swap(array, axis, bit):
    size = lax.axis_size(axis)
    return lax.ppermute(array, axis, [(i, i ^ bit) for i in range(size)])


def follow(array, *before):
    return lax.optimization_barrier((array, *before))[0]


def ordered(index, mine, other, axis):
    return jnp.where(
        index == 0,
        jnp.concatenate([mine, other], axis=axis),
        jnp.concatenate([other, mine], axis=axis),
    )


UNITS = 512
ROWS = 640


def feed_kernel(
    earlier,
    hidden_ref,
    back_ref,
    expand_ref,
    shrink_ref,
    *refs,
):
    if earlier:
        expand_before, shrink_before = refs[:2]
        refs = refs[2:]
    (
        expand_grad,
        shrink_grad,
        hidden_part,
        branch_part,
        activated_ref,
        lifted_grad_ref,
        turned_ref,
        hidden_sum,
        branch_sum,
    ) = refs
    step, steps = pl.program_id(0), pl.num_programs(0)
    tokens = hidden_ref.shape[0]
    f32 = jnp.float32
    nt = (((1,), (1,)), ((), ()))
    tn = (((0,), (0,)), ((), ()))
    slope = 0.7978845608028654

    @pl.when(step == 0)
    def _():
        turned_ref[...] = hidden_ref[...].T

    def block(at, first):
        hidden = hidden_ref[at, :]
        back = back_ref[at, :]
        lifted = jnp.dot(hidden, expand_ref[...], preferred_element_type=f32)
        active_grad = lax.dot_general(back, shrink_ref[...], nt, preferred_element_type=f32)
        square = lifted * lifted
        curve = jnp.tanh(slope * (lifted + 0.044715 * (square * lifted)))
        rise = 0.5 * (1.0 + curve)
        activated = (lifted * rise).astype(jnp.bfloat16)
        bend = 0.5 * lifted * (1.0 - curve * curve) * (slope + (3.0 * 0.044715 * slope) * square)
        lifted_grad = (active_grad * (rise + bend)).astype(jnp.bfloat16)
        activated_ref[at, :] = activated
        lifted_grad_ref[at, :] = lifted_grad
        branch = jnp.dot(activated, shrink_ref[...], preferred_element_type=f32)
        hidden_grad = lax.dot_general(lifted_grad, expand_ref[...], nt, preferred_element_type=f32)
        if first:
            branch_sum[at, :] = branch
            hidden_sum[at, :] = hidden_grad
        else:
            branch_sum[at, :] += branch
            hidden_sum[at, :] += hidden_grad

    def blocks(first):
        def one(i, _):
            block(pl.ds(pl.multiple_of(i * ROWS, ROWS), ROWS), first)
            return 0

        lax.fori_loop(0, tokens // ROWS, one, 0)

    @pl.when(step == 0)
    def _():
        blocks(True)

    @pl.when(step > 0)
    def _():
        blocks(False)

    made = lax.dot_general(activated_ref[...], back_ref[...], tn, preferred_element_type=f32)
    shrink_grad[...] = made + shrink_before[...] if earlier else made
    made = jnp.dot(turned_ref[...], lifted_grad_ref[...], preferred_element_type=f32)
    expand_grad[...] = made + expand_before[...] if earlier else made

    @pl.when(step == steps - 1)
    def _():
        hidden_part[...] = hidden_sum[...].astype(hidden_part.dtype)
        branch_part[...] = branch_sum[...].astype(branch_part.dtype)


def feed(hidden, back, expand, shrink, before, branch_type):
    tokens, width = hidden.shape
    units = 2 * expand.shape[2]
    tile = min(UNITS, expand.shape[2])
    steps = units // tile
    low, f32 = jnp.bfloat16, jnp.float32
    whole = pl.BlockSpec((tokens, width), lambda n: (0, 0), pipeline_mode=pl.Buffered(1))
    columns = pl.BlockSpec((width, tile), lambda n: (0, n))
    rows = pl.BlockSpec((tile, width), lambda n: (n, 0))
    return pl.pallas_call(
        partial(feed_kernel, bool(before)),
        grid=(steps,),
        in_specs=[
            whole,
            whole,
            pl.BlockSpec((None, width, tile), lambda n: (n * 2 // steps, 0, n % (steps // 2))),
            rows,
        ]
        + [columns, rows] * bool(before),
        out_specs=[columns, rows, whole, whole],
        out_shape=[
            jax.ShapeDtypeStruct((width, units), f32),
            jax.ShapeDtypeStruct((units, width), f32),
            jax.ShapeDtypeStruct((tokens, width), f32),
            jax.ShapeDtypeStruct((tokens, width), branch_type),
        ],
        scratch_shapes=[
            pltpu.VMEM((tokens, tile), low),
            pltpu.VMEM((tokens, tile), low),
            pltpu.VMEM((width, tokens), low),
            pltpu.VMEM((tokens, width), f32),
            pltpu.VMEM((tokens, width), f32),
        ],
        compiler_params=pltpu.CompilerParams(vmem_limit_bytes=56 * 2**20),
        cost_estimate=pl.CostEstimate(flops=2**20, bytes_accessed=2**20, transcendentals=0),
    )(hidden, back, expand, shrink, *before)


MESH = pl.DeviceIdType.MESH


def opening_kernel(
    expand_ref,
    shrink_ref,
    project_ref,
    mixing_ref,
    norm_ref,
    inputs_ref,
    back_ref,
    expand_out,
    shrink_out,
    project_out,
    mixing_out,
    norm_out,
    hidden_ref,
    other_back,
    expand_low,
    shrink_low,
    norm_low,
    norm_all,
    own_sem,
    norm_send,
    norm_recv,
    line_send,
    line_recv,
    far_send,
    far_recv,
    near_send,
    near_recv,
    row_sem,
):
    place, deep = lax.axis_index("dp"), 4
    outer = lax.axis_index("outer")
    far, near = outer // 2, outer % 2
    far_id = {"outer": (outer + 2) % 4}
    near_id = {"outer": outer + 1 - 2 * near}
    rows = expand_ref.shape[0]
    half = expand_ref.shape[1] // 2
    part = half // 2

    barrier = pltpu.get_barrier_semaphore()
    for step in range(1, deep):
        pl.semaphore_signal(
            barrier, inc=1, device_id={"dp": (place + step) % deep}, device_id_type=MESH
        )
    pl.semaphore_signal(barrier, inc=1, device_id=far_id, device_id_type=MESH)
    pl.semaphore_signal(barrier, inc=1, device_id=near_id, device_id_type=MESH)
    row_id = {"mp": 1 - lax.axis_index("mp")}
    pl.semaphore_signal(barrier, inc=1, device_id=row_id, device_id_type=MESH)

    expand_low[...] = expand_ref[...].astype(jnp.bfloat16)
    norm_low[...] = jnp.zeros_like(norm_low)
    norm_low[0:2] = norm_ref[...].astype(jnp.bfloat16).astype(jnp.float32)
    pl.semaphore_wait(barrier, deep + 2)

    def piece(w, which, at, side):
        across = pl.ds(pl.multiple_of(at * rows, rows), rows)
        along = pl.ds(pl.multiple_of(side * part, part), part)
        if w == 0:
            return expand_out.at[which, across, along]
        return shrink_out.at[which, along, across]

    def mine(w):
        along = pl.ds(pl.multiple_of(near * half + far * part, part), part)
        return expand_low.at[:, along] if w == 0 else shrink_low.at[along, :]

    def remote(source, target, send, recv, device):
        return pltpu.make_async_remote_copy(
            src_ref=source,
            dst_ref=target,
            send_sem=send,
            recv_sem=recv,
            device_id=device,
            device_id_type=MESH,
        )

    def line(w, way, step, source, at):
        to = place + 1 if way == 0 else place - 1
        return remote(
            source,
            piece(w, 0, at, far),
            line_send.at[w, way, step],
            line_recv.at[w, way, step],
            {"dp": to},
        )

    def can_send(way):
        return place < deep - 1 if way == 0 else place > 0

    def start_own(w):
        for way in range(2):

            @pl.when(can_send(way))
            def _(way=way):
                line(w, way, 0, mine(w), place).start()

    def own_copies(w):
        out = []
        for which in range(2):
            side = near + which - 2 * near * which
            along = pl.ds(pl.multiple_of(side * half, half), half)
            across = pl.ds(pl.multiple_of(place * rows, rows), rows)
            if w == 0:
                pair = (expand_low.at[:, along], expand_out.at[which, across, :])
            else:
                pair = (shrink_low.at[along, :], shrink_out.at[which, :, across])
            out.append(pltpu.make_async_copy(*pair, own_sem.at[w, which]))
        return out

    start_own(0)
    row_copy = remote(back_ref, other_back, row_sem.at[0], row_sem.at[1], row_id)
    row_copy.start()
    norm_copies = []
    for step in range(1, deep):
        copy = remote(
            norm_low,
            norm_all.at[step],
            norm_send.at[step],
            norm_recv.at[step],
            {"dp": (place + step) % deep},
        )
        copy.start()
        norm_copies.append(copy)
    shrink_low[...] = shrink_ref[...].astype(jnp.bfloat16)
    start_own(1)
    for w in range(2):
        for copy in own_copies(w):
            copy.start()
    for source, target in ((project_ref, project_out), (mixing_ref, mixing_out)):
        units = target.shape[0]
        target[...] = source[pl.ds(pl.multiple_of(near * units, units), units), :].astype(
            jnp.bfloat16
        )
    norm_all[0] = norm_low[...]
    for copy in norm_copies:
        copy.wait()
    for at in range(deep):
        norm_out[:, at * rows : (at + 1) * rows] = norm_all[(place - at + deep) % deep]
    gain, bias = norm_out[0:1], norm_out[1:2]
    tokens = inputs_ref.shape[0]
    height = 128

    def normalize(i, _):
        at = pl.ds(pl.multiple_of(i * height, height), height)
        x = inputs_ref[at, :].astype(jnp.float32)
        mean = jnp.mean(x, axis=1, keepdims=True)
        centred = x - mean
        spread = jnp.mean(centred * centred, axis=1, keepdims=True)
        normed = centred * lax.rsqrt(spread + norm_epsilon)
        hidden_ref[at, :] = (normed * gain + bias).astype(jnp.bfloat16)
        return 0

    lax.fori_loop(0, tokens // height, normalize, 0)

    def arrives(way, step):
        return place >= step if way == 0 else place + step < deep

    def at_of(way, step):
        return place - step if way == 0 else place + step

    def to_far(w, way, step):
        at = at_of(way, step)
        return remote(
            piece(w, 0, at, far),
            piece(w, 0, at, far),
            far_send.at[w, way, step - 1],
            far_recv.at[w, way, step - 1],
            far_id,
        )

    def from_far(w, way, step):
        at = at_of(way, step)
        return remote(
            piece(w, 0, at, 1 - far),
            piece(w, 0, at, 1 - far),
            far_send.at[w, way, step - 1],
            far_recv.at[w, way, step - 1],
            far_id,
        )

    def to_near(w, way, step, other):
        at = at_of(way, step)
        side = 1 - far if other else far
        return remote(
            piece(w, 0, at, side),
            piece(w, 1, at, side),
            near_send.at[w, way, step - 1, other],
            near_recv.at[w, way, step - 1, other],
            near_id,
        )

    order = [(w, step) for w in range(2) for step in range(1, deep)]

    def first_half(w, step):
        for way in range(2):

            @pl.when(arrives(way, step))
            def _(way=way):
                at = at_of(way, step)
                line(w, way, step - 1, mine(w), at).wait_recv()
                if step < deep - 1:

                    @pl.when(can_send(way))
                    def _():
                        line(w, way, step, piece(w, 0, at, far), at).start()

                to_far(w, way, step).start()
                to_near(w, way, step, 0).start()

    def second_half(w, step):
        for way in range(2):

            @pl.when(arrives(way, step))
            def _(way=way):
                from_far(w, way, step).wait_recv()
                to_near(w, way, step, 1).start()

    for n, (w, step) in enumerate(order):
        first_half(w, step)
        if n:
            second_half(*order[n - 1])
    second_half(*order[-1])
    row_copy.wait()
    for w in range(2):
        for copy in own_copies(w):
            copy.wait()
        for way in range(2):

            @pl.when(can_send(way))
            def _(way=way):
                line(w, way, 0, mine(w), place).wait_send()

            for step in range(1, deep):

                @pl.when(arrives(way, step))
                def _(way=way, step=step):
                    at = at_of(way, step)
                    if step < deep - 1:

                        @pl.when(can_send(way))
                        def _():
                            line(w, way, step, piece(w, 0, at, far), at).wait_send()

                    to_far(w, way, step).wait_send()
                    for other in range(2):
                        to_near(w, way, step, other).wait_send()
                        to_near(w, way, step, other).wait_recv()


def opening(expand, shrink, project, mixing, norm, inputs, back):
    deep = 4
    here = lambda: pl.BlockSpec(memory_space=pltpu.VMEM)
    rows, units = expand.shape
    low = jnp.bfloat16
    sem = pltpu.SemaphoreType.DMA
    return pl.pallas_call(
        opening_kernel,
        in_specs=[here() for _ in range(6)] + [pl.BlockSpec(memory_space=pl.ANY)],
        out_specs=[pl.BlockSpec(memory_space=pl.ANY)] * 2
        + [here() for _ in range(4)]
        + [pl.BlockSpec(memory_space=pl.ANY)],
        out_shape=[
            jax.ShapeDtypeStruct((2, rows * deep, units // 2), low),
            jax.ShapeDtypeStruct((2, units // 2, rows * deep), low),
            jax.ShapeDtypeStruct((project.shape[0] // 2, project.shape[1]), low),
            jax.ShapeDtypeStruct((mixing.shape[0] // 2, mixing.shape[1]), low),
            jax.ShapeDtypeStruct((8, rows * deep), jnp.float32),
            jax.ShapeDtypeStruct(inputs.shape, low),
            jax.ShapeDtypeStruct(back.shape, low),
        ],
        scratch_shapes=[
            pltpu.VMEM(expand.shape, low),
            pltpu.VMEM(shrink.shape, low),
            pltpu.VMEM((8, norm.shape[1]), jnp.float32),
            pltpu.VMEM((deep, 8, norm.shape[1]), jnp.float32),
            sem((2, 2)),
            sem((deep,)),
            sem((deep,)),
            sem((2, 2, deep)),
            sem((2, 2, deep)),
            sem((2, 2, deep)),
            sem((2, 2, deep)),
            sem((2, 2, deep, 2)),
            sem((2, 2, deep, 2)),
            sem((2,)),
        ],
        compiler_params=pltpu.CompilerParams(
            collective_id=1, has_side_effects=True, vmem_limit_bytes=40 * 2**20
        ),
        cost_estimate=pl.CostEstimate(flops=0, bytes_accessed=2**20, transcendentals=0),
    )(expand, shrink, project, mixing, norm, inputs, back)


def closing_kernel(
    later,
    project_hbm,
    *refs,
):
    sources = (project_hbm, *refs[:9])
    part_own, part_other, gain_ref = refs[9:12]
    input_grad, norm_grad, project_share, mixing_share = refs[12 + later : 16 + later]
    refs = refs[16 + later :]
    held = refs[:10]
    (
        part_in,
        total_ref,
        sent_ref,
        come_ref,
        out_ref,
        project_sib,
        project_land,
        project_own,
        mixing_sib,
        mixing_land,
        mixing_own,
        project_far,
        project_come,
        mixing_far,
        mixing_come,
        project_line,
        project_lands,
        mixing_line,
        mixing_lands,
        held_sem,
        part_sem,
        out_sem,
        row_send,
        row_recv,
        near_send,
        near_recv,
        far_send,
        far_recv,
        line_send,
        line_recv,
    ) = refs[10:]
    (
        project,
        grads_other,
        grads_own,
        hidden_other,
        hidden_own,
        mixed_other,
        mixed_own,
        back_other,
        back_own,
        inputs,
    ) = held
    low, f32 = jnp.bfloat16, jnp.float32
    tn = (((0,), (0,)), ((), ()))
    place, deep = lax.axis_index("dp"), 4
    outer = lax.axis_index("outer")
    far, near = outer // 2, outer % 2
    row_id = {"mp": 1 - lax.axis_index("mp")}
    far_id = {"outer": (outer + 2) % 4}
    near_id = {"outer": outer + 1 - 2 * near}

    copies = [
        pltpu.make_async_copy(source, target, held_sem.at[n])
        for n, (source, target) in enumerate(zip(sources, held))
    ]
    for copy in copies:
        copy.start()
    barrier = pltpu.get_barrier_semaphore()
    for device in (row_id, far_id, near_id):
        pl.semaphore_signal(barrier, inc=1, device_id=device, device_id_type=MESH)
    for step in range(1, deep):
        pl.semaphore_signal(
            barrier, inc=1, device_id={"dp": (place + step) % deep}, device_id_type=MESH
        )
    height = 256
    tokens, width = hidden_own.shape
    blocks = tokens // height
    at = [slice(n * height, (n + 1) * height) for n in range(blocks)]

    def remote(source, target, send, recv, device):
        return pltpu.make_async_remote_copy(
            src_ref=source,
            dst_ref=target,
            send_sem=send,
            recv_sem=recv,
            device_id=device,
            device_id_type=MESH,
        )

    loads = [
        pltpu.make_async_copy(source.at[at[n]], part_in.at[(k * blocks + n) % 2], part_sem.at[(k * blocks + n) % 2])
        for k, source in enumerate((part_other, part_own))
        for n in range(blocks)
    ]
    loads[0].start()
    loads[1].start()

    copies[0].wait()
    copies[1].wait()
    pl.semaphore_wait(barrier, deep + 2)
    row_copies = []
    for n in range(blocks):
        made = lax.dot_general(grads_other[:, at[n]], project[...], tn, preferred_element_type=f32)
        loads[n].wait()
        sent_ref[at[n], :] = (part_in[n % 2] + made).astype(low)
        loads[n + 2].start()
        copy = remote(
            sent_ref.at[at[n]], come_ref.at[at[n]], row_send.at[n], row_recv.at[n], row_id
        )
        copy.start()
        row_copies.append(copy)

    for n in range(2, 9):
        copies[n].wait()
    half = project_own.shape[0]
    few = mixing_own.shape[0]
    near_copies = []
    for n in range(half // height):
        rows = slice(half + n * height, half + (n + 1) * height)
        project_sib[at[n], :] = jnp.dot(
            grads_own[rows, :], hidden_own[...], preferred_element_type=f32
        ) + jnp.dot(grads_other[rows, :], hidden_other[...], preferred_element_type=f32)
        near_copies.append(
            remote(
                project_sib.at[at[n]],
                project_land.at[at[n]],
                near_send.at[n],
                near_recv.at[n],
                near_id,
            )
        )
        near_copies[-1].start()
    mixing_sib[...] = jnp.dot(
        mixed_own[few:, :], back_own[...], preferred_element_type=f32
    ) + jnp.dot(mixed_other[few:, :], back_other[...], preferred_element_type=f32)
    near_copies.append(
        remote(mixing_sib, mixing_land, near_send.at[3], near_recv.at[3], near_id)
    )
    near_copies[-1].start()
    for n in range(half // height):
        made = jnp.dot(
            grads_own[at[n], :], hidden_own[...], preferred_element_type=f32
        ) + jnp.dot(grads_other[at[n], :], hidden_other[...], preferred_element_type=f32)
        near_copies[n].wait()
        project_own[at[n], :] = made + project_land[at[n], :]

    def to_far(own, send, come, n):
        size = send.shape[0]
        send[...] = own[pl.ds(pl.multiple_of((1 - far) * size, size), size), :].astype(low)
        copy = remote(send, come, far_send.at[n], far_recv.at[n], far_id)
        copy.start()
        return copy

    far_copies = [to_far(project_own, project_far, project_come, 0)]
    made = jnp.dot(mixed_own[:few, :], back_own[...], preferred_element_type=f32) + jnp.dot(
        mixed_other[:few, :], back_other[...], preferred_element_type=f32
    )
    near_copies[3].wait()
    mixing_own[...] = made + mixing_land[...]
    far_copies.append(to_far(mixing_own, mixing_far, mixing_come, 1))

    for n in range(blocks):
        made = lax.dot_general(grads_own[:, at[n]], project[...], tn, preferred_element_type=f32)
        loads[blocks + n].wait()
        total_ref[at[n], :] = part_in[(blocks + n) % 2] + made
        if n + 2 < blocks:
            loads[blocks + n + 2].start()

    line_copies = []
    for k, (own, come, line, lands) in enumerate(
        (
            (project_own, project_come, project_line, project_lands),
            (mixing_own, mixing_come, mixing_line, mixing_lands),
        )
    ):
        size = come.shape[0]
        keep = pl.ds(pl.multiple_of(far * size, size), size)
        far_copies[k].wait()
        own[keep, :] = own[keep, :] + come[...].astype(f32)
        piece = width // deep
        for step in range(1, deep):
            target = (place + step) % deep
            line[step] = own[keep, pl.ds(pl.multiple_of(target * piece, piece), piece)].astype(low)
            copy = remote(
                line.at[step],
                lands.at[step],
                line_send.at[k, step],
                line_recv.at[k, step],
                {"dp": target},
            )
            copy.start()
            line_copies.append(copy)

    copies[9].wait()
    gain = gain_ref[0:1]
    gain_sum = jnp.zeros((1, width), f32)
    bias_sum = jnp.zeros((1, width), f32)
    out_copies = []
    for n in range(blocks):
        row_copies[n].wait()
        if n >= 2:
            out_copies[n - 2].wait()

        def some(i, carry):
            gain_sum, bias_sum = carry
            small = 64
            rows = pl.ds(pl.multiple_of(n * height + i * small, small), small)
            x = inputs[rows, :].astype(f32)
            mean = jnp.mean(x, axis=1, keepdims=True)
            centred = x - mean
            spread = jnp.mean(centred * centred, axis=1, keepdims=True)
            inverse = lax.rsqrt(spread + norm_epsilon)
            normed = centred * inverse
            grad = total_ref[rows, :] + come_ref[rows, :].astype(f32)
            scaled = grad * gain
            middle = jnp.mean(scaled, axis=1, keepdims=True)
            along = jnp.mean(scaled * normed, axis=1, keepdims=True)
            result = inverse * (scaled - middle - normed * along)
            out_ref[n % 2, pl.ds(pl.multiple_of(i * small, small), small), :] = (
                back_own[rows, :].astype(f32) + result
            )
            gain_sum = gain_sum + jnp.sum(grad * normed, axis=0, keepdims=True)
            bias_sum = bias_sum + jnp.sum(grad, axis=0, keepdims=True)
            return gain_sum, bias_sum

        gain_sum, bias_sum = lax.fori_loop(0, height // 64, some, (gain_sum, bias_sum))
        out_copies.append(
            pltpu.make_async_copy(out_ref.at[n % 2], input_grad.at[at[n]], out_sem.at[n % 2])
        )
        out_copies[-1].start()
    norm_grad[...] = jnp.zeros_like(norm_grad)
    norm_grad[0:1] = gain_sum
    norm_grad[1:2] = bias_sum
    for copy in line_copies:
        copy.wait()
    for own, lands, share in (
        (project_own, project_lands, project_share),
        (mixing_own, mixing_lands, mixing_share),
    ):
        size, piece = share.shape
        result = own[
            pl.ds(pl.multiple_of(far * size, size), size),
            pl.ds(pl.multiple_of(place * piece, piece), piece),
        ]
        for step in range(1, deep):
            result = result + lands[step].astype(f32)
        share[...] = result
    for copy in out_copies[-2:]:
        copy.wait()


def closing(project, grads, hiddens, mixed, backs, inputs, parts, gain, after):
    deep = 4
    low, f32 = jnp.bfloat16, jnp.float32
    tokens, width = inputs.shape
    half, few = grads[0].shape[0] // 2, mixed[0].shape[0] // 2
    piece = width // deep
    anywhere = pl.BlockSpec(memory_space=pl.ANY)
    here = lambda: pl.BlockSpec(memory_space=pltpu.VMEM)
    held = (
        project,
        grads[1],
        grads[0],
        hiddens[1],
        hiddens[0],
        mixed[1],
        mixed[0],
        backs[1],
        backs[0],
        inputs,
    )
    sem = pltpu.SemaphoreType.DMA
    space = pltpu.VMEM
    return pl.pallas_call(
        partial(closing_kernel, len(after)),
        in_specs=[anywhere] * 12 + [here()] + [anywhere] * len(after),
        out_specs=[anywhere, here(), here(), here()],
        out_shape=[
            jax.ShapeDtypeStruct((tokens, width), f32),
            jax.ShapeDtypeStruct((8, width), f32),
            jax.ShapeDtypeStruct((half // 2, piece), f32),
            jax.ShapeDtypeStruct((few // 2, piece), f32),
        ],
        scratch_shapes=[space(v.shape, v.dtype) for v in held]
        + [
            space((2, 256, width), f32),
            space((tokens, width), f32),
            space((tokens, width), low),
            space((tokens, width), low),
            space((2, 256, width), f32),
            space((half, width), f32),
            space((half, width), f32),
            space((half, width), f32),
            space((few, width), f32),
            space((few, width), f32),
            space((few, width), f32),
            space((half // 2, width), low),
            space((half // 2, width), low),
            space((few // 2, width), low),
            space((few // 2, width), low),
            space((deep, half // 2, piece), low),
            space((deep, half // 2, piece), low),
            space((deep, few // 2, piece), low),
            space((deep, few // 2, piece), low),
            sem((len(held),)),
            sem((2,)),
            sem((2,)),
            sem((tokens // 256,)),
            sem((tokens // 256,)),
            sem((4,)),
            sem((4,)),
            sem((2,)),
            sem((2,)),
            sem((2, deep)),
            sem((2, deep)),
        ],
        compiler_params=pltpu.CompilerParams(
            collective_id=3, has_side_effects=True, vmem_limit_bytes=62 * 2**20
        ),
        cost_estimate=pl.CostEstimate(flops=2**20, bytes_accessed=2**20, transcendentals=0),
    )(*held, *parts, gain, *after)


def total_kernel(term_ref, out_ref, first, second, first_send, first_recv, second_send, second_recv):
    split, outers, deep = first.shape[0] // 4, 4, second.shape[0]
    plane = split * outers
    place = lax.axis_index("dp")
    me = lax.axis_index("mp") * outers + lax.axis_index("outer")

    def plane_id(step):
        other = (me + step) % plane
        return {"mp": other // outers, "outer": other % outers}

    def line_id(step):
        return {"dp": (place + step) % deep}

    barrier = pltpu.get_barrier_semaphore()
    for step in range(1, plane):
        pl.semaphore_signal(barrier, inc=1, device_id=plane_id(step), device_id_type=MESH)
    for step in range(1, deep):
        pl.semaphore_signal(barrier, inc=1, device_id=line_id(step), device_id_type=MESH)
    pl.semaphore_wait(barrier, plane + deep - 2)

    def exchange(source, slots, send, recv, size, device):
        copies = []
        for step in range(1, size):
            copy = pltpu.make_async_remote_copy(
                src_ref=source,
                dst_ref=slots.at[step],
                send_sem=send.at[step],
                recv_sem=recv.at[step],
                device_id=device(step),
                device_id_type=MESH,
            )
            copy.start()
            copies.append(copy)
        slots[0] = source[...]
        for copy in copies:
            copy.wait()

    exchange(term_ref, first, first_send, first_recv, plane, plane_id)
    total = first[me]
    for at in range(1, plane):
        total = total + first[(me + plane - at) % plane]
    out_ref[...] = total
    exchange(out_ref, second, second_send, second_recv, deep, line_id)
    total = second[place]
    for at in range(1, deep):
        total = total + second[(place + deep - at) % deep]
    out_ref[...] = total


def total_over_all(term, split, deep):
    plane = split * 4
    sem = pltpu.SemaphoreType.DMA
    return pl.pallas_call(
        total_kernel,
        in_specs=[pl.BlockSpec(memory_space=pltpu.VMEM)],
        out_specs=pl.BlockSpec(memory_space=pltpu.VMEM),
        out_shape=jax.ShapeDtypeStruct(term.shape, term.dtype),
        scratch_shapes=[
            pltpu.VMEM((plane, *term.shape), term.dtype),
            pltpu.VMEM((deep, *term.shape), term.dtype),
            sem((plane,)),
            sem((plane,)),
            sem((deep,)),
            sem((deep,)),
        ],
        compiler_params=pltpu.CompilerParams(collective_id=2, has_side_effects=True),
    )(term)


class Paired:
    def __init__(self):
        outer = lax.axis_index("outer")
        self.far, self.near = outer // 2, outer % 2
        self.place = lax.axis_index("dp")
        self.deep = lax.axis_size("dp")

    def gather(self, own, cut, depth):
        own = lax.all_gather(own, "dp", axis=depth, tiled=True)
        return jnp.concatenate([own, swap(own, "outer", 1)], axis=cut)

    def gather_few(self, own, cut, depth):
        wide = list(own.shape)
        piece = wide[depth]
        wide[depth] *= self.deep
        out = jnp.zeros(wide, own.dtype)
        for step in range(self.deep):
            pairs = [(i, (i + step) % self.deep) for i in range(self.deep)]
            come = lax.ppermute(own, "dp", pairs) if step else own
            at = lax.rem(self.place - step + self.deep, self.deep)
            out = lax.dynamic_update_slice_in_dim(out, come, at * piece, depth)
        return jnp.concatenate([out, swap(out, "outer", 1)], axis=cut)

    def pair_sum(self, own, sibling, cut):
        own = own + swap(sibling, "outer", 1)
        half = own.shape[cut] // 2
        keep = lax.dynamic_slice_in_dim(own, self.far * half, half, cut)
        send = lax.dynamic_slice_in_dim(own, (1 - self.far) * half, half, cut)
        send = send.astype(jnp.bfloat16)
        return keep, swap(send, "outer", 2), send

    def line_sum(self, keep, come, depth):
        keep = keep + come.astype(jnp.float32)
        piece = keep.shape[depth] // self.deep

        def part(at):
            return lax.dynamic_slice_in_dim(keep, at * piece, piece, depth)

        result = part(self.place)
        for step in range(1, self.deep):
            target = lax.rem(self.place + step, self.deep)
            pairs = [(i, (i + step) % self.deep) for i in range(self.deep)]
            result = result + lax.ppermute(
                part(target).astype(jnp.bfloat16), "dp", pairs
            ).astype(jnp.float32)
        return result

    def spread(self, share, cut):
        pair = ordered(self.far, share, swap(share, "outer", 2), cut)
        return ordered(self.near, pair, swap(pair, "outer", 1), cut)


def local(
    inputs,
    cotangent,
    lengths,
    project_master,
    project_first,
    project_second,
    mixing_master,
    mixing_first,
    mixing_second,
    expand_master,
    expand_first,
    expand_second,
    shrink_master,
    shrink_first,
    shrink_second,
    norm_master,
    norm_first,
    norm_second,
):
    split, deep = lax.axis_size("mp"), lax.axis_size("dp")
    heads_here = project_master.shape[1]
    width = inputs.shape[1]
    paired = (
        split == 2
        and lax.axis_size("outer") == 4
        and heads_here % 4 == 0
        and width % BQ == 0
    )
    position = lax.axis_index("mp")
    count = width * split
    project_flat = project_master.transpose(1, 2, 0).reshape(heads_here * 3 * HD, -1)
    mixing_flat = mixing_master.reshape(heads_here * HD, mixing_master.shape[2])
    masters = (project_flat, mixing_flat, expand_master, shrink_master)
    cuts, depths = (0, 0, 1, 0), (1, 1, 0, 1)
    rows_local = inputs[0].astype(jnp.float32)
    begins, places = layout(lengths[0], count)
    cosine, sine = turns(places)
    if paired:
        plan = Paired()
        expand, shrink, project, mixing, norm_weight, hidden_local, other_back = opening(
            expand_master,
            shrink_master,
            project_flat,
            mixing_flat,
            norm_master,
            inputs[0],
            cotangent[0],
        )
        backs = [cotangent[0], other_back]
        shrink = shrink.reshape(-1, shrink.shape[2])
        project = plan.gather(project, 0, 1)
        mixing = plan.gather_few(mixing, 0, 1)
        hiddens = [hidden_local, swap(hidden_local, "mp", 1)]
    else:
        norm_weight = lax.all_gather(norm_master.astype(jnp.bfloat16), "dp", axis=1, tiled=True)
        gain = norm_weight[0].astype(jnp.float32)
        bias = norm_weight[1].astype(jnp.float32)
        shaped, norm_pull = jax.vjp(layer_norm, rows_local, gain, bias)
        hidden_local = shaped.astype(jnp.bfloat16)
        project, mixing, expand, shrink = (
            lax.all_gather(master.astype(jnp.bfloat16), "dp", axis=depth, tiled=True)
            for master, depth in zip(masters, depths)
        )
        backs = [lax.all_gather(cotangent[0], "mp", axis=0, tiled=True)]
        hiddens = [lax.all_gather(hidden_local, "mp", axis=0, tiled=True)]

    def over_tokens(pattern, lefts, rights):
        return sum(product(pattern, left, right) for left, right in zip(lefts, rights))

    back_local = cotangent[0].astype(jnp.float32)
    if paired:
        *grads, hidden_own, branch_own = feed(
            hiddens[0], backs[0], expand, shrink, (), jnp.float32
        )
        expand_grad, shrink_grad, hidden_other, branch_other = feed(
            hiddens[1], backs[1], expand, shrink, grads, jnp.bfloat16
        )
        hidden_parts = [hidden_own, hidden_other]
        half = expand_grad.shape[1] // 2
        shrink_keep, shrink_come, shrink_sent = plan.pair_sum(shrink_grad[:half], shrink_grad[half:], 0)
        expand_keep, expand_come, expand_sent = plan.pair_sum(
            expand_grad[:, :half], expand_grad[:, half:], 1
        )
        branch_come = swap(branch_other, "mp", 1)
        mixing_other = swap(mixing, "mp", 1)
        projected = [product("td,ed->et", hidden, project) for hidden in hiddens]
        mixed_backs = [product("td,fd->ft", back, mixing).astype(jnp.bfloat16) for back in backs]
        mixed, projected_grads = attend(
            projected,
            mixed_backs,
            begins,
            cosine,
            sine,
            position,
            (shrink_sent, expand_sent),
        )
        input_grad, norm_terms, project_sum, mixing_sum = closing(
            project,
            projected_grads,
            hiddens,
            mixed,
            backs,
            inputs[0],
            (hidden_own, hidden_other),
            norm_weight,
            (shrink_come, expand_come, branch_come),
        )
        norm_terms = norm_terms[:2]
        mixed_come = swap(follow(mixed[1], norm_terms), "mp", 1)
        shrink_sum = plan.line_sum(shrink_keep, shrink_come, 1)
        expand_sum = plan.line_sum(expand_keep, expand_come, 0)
        branch = (
            branch_own
            + branch_come.astype(jnp.float32)
            + product("ft,fd->td", mixed[0], mixing)
            + product("ft,fd->td", mixed_come, mixing_other)
        )
    else:
        lifteds = [product("td,df->tf", hidden, expand) for hidden in hiddens]
        activated = [gelu(lifted) for lifted in lifteds]
        active_grads = [product("td,fd->tf", back, shrink) for back in backs]
        lifted_grads = [gelu_both(a, b) for a, b in zip(lifteds, active_grads)]
        hidden_parts = [product("tf,df->td", v, expand) for v in lifted_grads]
        branch_parts = [product("tf,fd->td", v, shrink) for v in activated]
        projected = [product("td,ed->et", hidden, project) for hidden in hiddens]
        mixed_backs = [product("td,fd->ft", back, mixing).astype(jnp.bfloat16) for back in backs]
        mixed, projected_grads = attend(projected, mixed_backs, begins, cosine, sine, position)
        project_sum, mixing_sum, expand_sum, shrink_sum = (
            lax.psum(
                lax.psum_scatter(
                    over_tokens(pattern, lefts, rights),
                    "dp",
                    scatter_dimension=depth,
                    tiled=True,
                ),
                "outer",
            )
            for pattern, lefts, rights, depth in (
                ("et,td->ed", projected_grads, hiddens, 1),
                ("ft,td->fd", mixed, backs, 1),
                ("td,tf->df", hiddens, lifted_grads, 0),
                ("tf,td->fd", activated, backs, 1),
            )
        )
        hidden_grad, branch = (
            lax.psum_scatter(v, "mp", scatter_dimension=0, tiled=True)
            for v in (
                hidden_parts[0] + product("et,ed->td", projected_grads[0], project),
                branch_parts[0] + product("ft,fd->td", mixed[0], mixing),
            )
        )
        rows_grad, gain_grad, bias_grad = norm_pull(hidden_grad)
        input_grad = back_local + rows_grad
        norm_terms = jnp.stack([gain_grad, bias_grad])
    input_grad = input_grad[None]
    block_out = (rows_local + branch).astype(jnp.bfloat16)[None]
    sums = (project_sum, mixing_sum, expand_sum, shrink_sum)
    own_square = sum(jnp.sum(v * v) for v in sums)
    if not paired:
        own_square = own_square / lax.axis_size("outer")
    norm_terms = jnp.concatenate([norm_terms, jnp.full((1, D), own_square)]).reshape(-1, 128)
    if paired:
        norm_all = total_over_all(norm_terms, split, deep)
    else:
        norm_all = lax.psum(norm_terms, ("mp", "dp", "outer"))
    norm_all = norm_all.reshape(3, D)
    norm_full = norm_all[:2]
    grad_norm = jnp.sqrt(norm_all[2, 0] + jnp.sum(norm_full * norm_full))
    factor = clip_level / jnp.maximum(grad_norm, clip_level)
    norm_gradient = lax.dynamic_slice_in_dim(
        norm_full, lax.axis_index("dp") * (D // deep), D // deep, 1
    )
    gradients = [plan.spread(v, cut) if paired else v for v, cut in zip(sums, cuts)]
    gradients[0] = gradients[0].reshape(heads_here, 3 * HD, -1).transpose(2, 0, 1)
    gradients[1] = gradients[1].reshape(mixing_master.shape)
    states = (
        (project_master, project_first, project_second, D ** (-0.5)),
        (mixing_master, mixing_first, mixing_second, (D // 32) ** (-0.5)),
        (expand_master, expand_first, expand_second, D ** (-0.5)),
        (shrink_master, shrink_first, shrink_second, FF ** (-0.5)),
    )
    results = [block_out, input_grad]
    for (master, first, second, rate), gradient in zip(states, gradients):
        results += adam_update(master, first, second, factor * gradient, rate, decay_rate)
    results += adam_update(norm_master, norm_first, norm_second, factor * norm_gradient, 0.3, 0.0)
    return (*results, grad_norm)


def solution(mesh):
    in_specs = (
        P(("dp", "outer"), "mp", None),
        P(("dp", "outer"), "mp", None),
        P(("dp", "outer"), None),
        P("dp", "mp", None),
        P("dp", "mp", None),
        P("dp", "mp", None),
        P("mp", None, "dp"),
        P("mp", None, "dp"),
        P("mp", None, "dp"),
        P("dp", "mp"),
        P("dp", "mp"),
        P("dp", "mp"),
        P("mp", "dp"),
        P("mp", "dp"),
        P("mp", "dp"),
        P(None, "dp"),
        P(None, "dp"),
        P(None, "dp"),
    )
    out_specs = (
        P(("dp", "outer"), "mp", None),
        P(("dp", "outer"), "mp", None),
        P("dp", "mp", None),
        P("dp", "mp", None),
        P("dp", "mp", None),
        P("dp", "mp", None),
        P("mp", None, "dp"),
        P("mp", None, "dp"),
        P("mp", None, "dp"),
        P("mp", None, "dp"),
        P("dp", "mp"),
        P("dp", "mp"),
        P("dp", "mp"),
        P("dp", "mp"),
        P("mp", "dp"),
        P("mp", "dp"),
        P("mp", "dp"),
        P("mp", "dp"),
        P(None, "dp"),
        P(None, "dp"),
        P(None, "dp"),
        P(None, "dp"),
        P(),
    )
    return jax.shard_map(local, mesh=mesh, in_specs=in_specs, out_specs=out_specs, check_vma=False)
```

```python
from functools import partial
import math

import jax
import jax.numpy as jnp
from jax import lax
from jax.experimental import pallas as pl
from jax.experimental.pallas import tpu as pltpu
from jax.sharding import PartitionSpec as P

D = 1024
HD = 64
ROT = 32
FF = 4096
STEP = 10


norm_epsilon = 1e-05
beta_one = 0.9
beta_two = 0.95
adam_epsilon = 1e-08
decay_rate = 0.1
clip_level = 1.0
masked_value = -1e30


def layout(sizes_row, count):
    number = jnp.arange(sizes_row.shape[0], dtype=jnp.int32)
    ends = jnp.sum(jnp.where(number[None, :] <= number[:, None], sizes_row[None, :], 0), axis=1)
    tokens = jnp.arange(count, dtype=jnp.int32)
    passed = (ends[:, None] <= tokens[None, :]).astype(jnp.int32)
    begins = jnp.sum(passed * sizes_row[:, None], axis=0)
    return (begins, tokens - begins)


def turns(places):
    half_rot = ROT // 2
    counter = jnp.arange(half_rot, dtype=jnp.float32)
    frequency = jnp.exp(counter * (-2.0 * math.log(10000.0) / ROT))
    angles = places.astype(jnp.float32)[None, :] * frequency[:, None]
    return jnp.cos(angles), jnp.sin(angles)


BQ = 256
BK = 256


def attend_kernel(together, parts, later, *refs):
    facts = refs[0]
    projected_refs = refs[1 : 1 + parts]
    back_refs = refs[1 + parts : 1 + 2 * parts]
    start_ref, cos_ref, sin_ref = refs[1 + 2 * parts : 4 + 2 * parts]
    refs = refs[: 4 + 2 * parts] + refs[4 + 2 * parts + later :]
    mixed_refs = refs[4 + 2 * parts : 4 + 3 * parts]
    grad_refs = refs[4 + 3 * parts : 4 + 4 * parts]
    (
        query_ref,
        key_columns_ref,
        value_columns_ref,
        key_ref,
        value_ref,
        back_ref,
        query_grad_ref,
        key_grad_ref,
        value_grad_ref,
        shifted_ref,
        share_grad_ref,
        top_ref,
    ) = refs[4 + 4 * parts :]
    width = projected_refs[0].shape[1]
    count = width * parts
    blocks = count // BQ
    turn = facts[blocks]
    half = ROT // 2
    scale = HD ** (-0.5)
    nt = (((1,), (1,)), ((), ()))

    def place_of(part):
        if parts == 1:
            return pl.ds(0, width)
        block = lax.rem(part * (blocks // parts) + blocks - turn, blocks)
        return pl.ds(pl.multiple_of(block * BQ, BQ), width)

    for part in range(parts):
        columns = slice(part * width, (part + 1) * width)
        cosine, sine = cos_ref[:, place_of(part)], sin_ref[:, place_of(part)]
        projected_ref = projected_refs[part]

        def turned(at):
            first = projected_ref[at : at + half]
            second = projected_ref[at + half : at + ROT]
            return jnp.concatenate(
                [
                    first * cosine - second * sine,
                    second * cosine + first * sine,
                    projected_ref[at + ROT : at + HD],
                ],
                axis=0,
            ).astype(jnp.bfloat16)

        for h in range(together):
            base = h * 3 * HD
            query_ref[h, :, columns] = (turned(base).astype(jnp.float32) * scale).astype(
                jnp.bfloat16
            )
            keys = turned(base + HD)
            values = projected_ref[base + 2 * HD : base + 3 * HD].astype(jnp.bfloat16)
            key_columns_ref[h, :, columns] = keys
            value_columns_ref[h, :, columns] = values
            key_ref[h, columns] = keys.T
            value_ref[h, columns] = values.T
            back_ref[h, :, columns] = back_refs[part][h * HD : (h + 1) * HD]
    key_grad_ref[...] = jnp.zeros_like(key_grad_ref)
    value_grad_ref[...] = jnp.zeros_like(value_grad_ref)
    key_at = lax.broadcasted_iota(jnp.int32, (BK, BQ), 0)
    query_at = lax.broadcasted_iota(jnp.int32, (1, BQ), 1)

    def stored(block):
        if parts == 1:
            return pl.ds(pl.multiple_of(block * BQ, BQ), BQ)
        return pl.ds(pl.multiple_of(lax.rem(block + turn, blocks) * BQ, BQ), BQ)

    def query_block(i, _):
        columns = stored(i)
        start = start_ref[:, pl.ds(pl.multiple_of(i * BQ, BQ), BQ)]
        own = query_at + i * BQ
        lowest = facts[i]
        queries = [query_ref[h, :, columns] for h in range(together)]
        backs = [back_ref[h, :, columns] for h in range(together)]

        def in_pairs(body, carry):
            twos = lax.div(i + 1 - lowest, 2)
            carry = lax.fori_loop(
                0, twos, lambda n, c: body((lowest + 2 * n, lowest + 2 * n + 1), c), carry
            )
            return lax.fori_loop(lowest + 2 * twos, i + 1, lambda n, c: body((n,), c), carry)

        def scores(group, carry):
            made = []
            for j in group:
                rows = stored(j)
                allowed = (key_at >= start - j * BK) & (key_at <= own - j * BK)
                for h in range(together):
                    raw = jnp.dot(
                        key_ref[h, rows, :], queries[h], preferred_element_type=jnp.float32
                    )
                    share_grad = jnp.dot(
                        value_ref[h, rows, :], backs[h], preferred_element_type=jnp.float32
                    )
                    masked = jnp.where(allowed, raw, masked_value)
                    here = jnp.max(masked, axis=0, keepdims=True)
                    shifted = jnp.exp(masked - here)
                    shifted_ref[h, j] = shifted
                    share_grad_ref[h, j] = share_grad
                    top_ref[h, j] = here
                    made.append(
                        (
                            here,
                            jnp.sum(shifted, axis=0, keepdims=True),
                            jnp.sum(shifted * share_grad, axis=0, keepdims=True),
                        )
                    )
            out = []
            for h in range(together):
                top, total, inner = carry[h]
                for here, here_total, here_inner in made[h::together]:
                    new = jnp.maximum(top, here)
                    old_by, here_by = jnp.exp(top - new), jnp.exp(here - new)
                    total = total * old_by + here_total * here_by
                    inner = inner * old_by + here_inner * here_by
                    top = new
                out.append((top, total, inner))
            return tuple(out)

        zero = jnp.zeros((1, BQ), jnp.float32)
        empty = (jnp.full((1, BQ), masked_value, jnp.float32), zero, zero)
        stats = in_pairs(scores, (empty,) * together)
        inverse = [1.0 / s[1] for s in stats]
        inners = [s[2] * r for s, r in zip(stats, inverse)]

        def sums(group, carry):
            out = list(carry)
            for j in group:
                rows = stored(j)
                for h in range(together):
                    mixed, query_grad = out[h]
                    by = jnp.exp(top_ref[h, j] - stats[h][0]) * inverse[h]
                    probs = shifted_ref[h, j] * by
                    shares = probs.astype(jnp.bfloat16)
                    score_grad = (probs * (share_grad_ref[h, j] - inners[h])).astype(jnp.bfloat16)
                    mixed = mixed + jnp.dot(
                        value_columns_ref[h, :, rows], shares, preferred_element_type=jnp.float32
                    )
                    query_grad = query_grad + jnp.dot(
                        key_columns_ref[h, :, rows], score_grad, preferred_element_type=jnp.float32
                    )
                    value_grad_ref[h, :, rows] += lax.dot_general(
                        backs[h], shares, nt, preferred_element_type=jnp.float32
                    )
                    key_grad_ref[h, :, rows] += lax.dot_general(
                        queries[h], score_grad, nt, preferred_element_type=jnp.float32
                    )
                    out[h] = (mixed, query_grad)
            return tuple(out)

        nothing = jnp.zeros((HD, BQ), jnp.float32)
        results = in_pairs(sums, ((nothing, nothing),) * together)
        for h in range(together):
            back_ref[h, :, columns] = results[h][0].astype(jnp.bfloat16)
            query_grad_ref[h, :, columns] = results[h][1] * scale
        return 0

    lax.fori_loop(0, blocks, query_block, 0)
    for part in range(parts):
        columns = slice(part * width, (part + 1) * width)
        cosine, sine = cos_ref[:, place_of(part)], sin_ref[:, place_of(part)]

        def turned_back(ref, h):
            first, second = ref[h, :half, columns], ref[h, half:ROT, columns]
            return jnp.concatenate(
                [
                    first * cosine + second * sine,
                    second * cosine - first * sine,
                    ref[h, ROT:, columns],
                ],
                axis=0,
            ).astype(jnp.bfloat16)

        for h in range(together):
            base = h * 3 * HD
            mixed_refs[part][h * HD : (h + 1) * HD] = back_ref[h, :, columns]
            grad_refs[part][base : base + HD] = turned_back(query_grad_ref, h)
            grad_refs[part][base + HD : base + 2 * HD] = turned_back(key_grad_ref, h)
            grad_refs[part][base + 2 * HD : base + 3 * HD] = value_grad_ref[h, :, columns].astype(
                jnp.bfloat16
            )


def attend(projected, back, begins, cosine, sine, offset, after=()):
    parts = len(projected)
    heads = back[0].shape[0] // HD
    width = back[0].shape[1]
    count = begins.shape[0]
    together = 2 if heads % 2 == 0 else 1
    blocks = count // BK
    half = ROT // 2
    turn = jnp.asarray(offset * ((blocks // parts) if parts > 1 else 0), jnp.int32)
    facts = jnp.concatenate([begins[::BQ] // BK, turn[None]])
    whole = lambda rows: pl.BlockSpec((rows, count), lambda g, *_: (0, 0))
    mine = lambda rows: pl.BlockSpec((rows, width), lambda g, *_: (g, 0))
    results = pl.pallas_call(
        partial(attend_kernel, together, parts, len(after)),
        grid_spec=pltpu.PrefetchScalarGridSpec(
            num_scalar_prefetch=1,
            grid=(heads // together,),
            in_specs=[mine(together * 3 * HD)] * parts
            + [mine(together * HD)] * parts
            + [whole(1), whole(half), whole(half)]
            + [pl.BlockSpec(memory_space=pl.ANY)] * len(after),
            out_specs=[mine(together * HD)] * parts + [mine(together * 3 * HD)] * parts,
            scratch_shapes=[
                pltpu.VMEM((together, HD, count), jnp.bfloat16),
                pltpu.VMEM((together, HD, count), jnp.bfloat16),
                pltpu.VMEM((together, HD, count), jnp.bfloat16),
                pltpu.VMEM((together, count, HD), jnp.bfloat16),
                pltpu.VMEM((together, count, HD), jnp.bfloat16),
                pltpu.VMEM((together, HD, count), jnp.bfloat16),
                pltpu.VMEM((together, HD, count), jnp.float32),
                pltpu.VMEM((together, HD, count), jnp.float32),
                pltpu.VMEM((together, HD, count), jnp.float32),
                pltpu.VMEM((together, blocks, BK, BQ), jnp.float32),
                pltpu.VMEM((together, blocks, BK, BQ), jnp.float32),
                pltpu.VMEM((together, blocks, 1, BQ), jnp.float32),
            ],
        ),
        out_shape=[jax.ShapeDtypeStruct((heads * HD, width), jnp.bfloat16)] * parts
        + [jax.ShapeDtypeStruct((heads * 3 * HD, width), jnp.bfloat16)] * parts,
        compiler_params=pltpu.CompilerParams(vmem_limit_bytes=48 * 2**20),
        cost_estimate=pl.CostEstimate(
            flops=2**20,
            bytes_accessed=2**20,
            transcendentals=0,
        ),
    )(facts, *projected, *back, begins[None, :], cosine, sine, *after)
    return results[:parts], results[parts:]


def layer_norm(rows_in, gain, bias):
    mean = jnp.mean(rows_in, axis=1, keepdims=True)
    centred = rows_in - mean
    spread = jnp.mean(centred * centred, axis=1, keepdims=True)
    normed = centred * lax.rsqrt(spread + norm_epsilon)
    return normed * gain + bias


def adam_update(master, first, second, gradient, rate, decay):
    first_new = beta_one * first + (1.0 - beta_one) * gradient
    second_new = beta_two * second + (1.0 - beta_two) * gradient * gradient
    first_hat = first_new / (1.0 - beta_one**STEP)
    second_hat = second_new / (1.0 - beta_two**STEP)
    master_new = master - rate * (
        first_hat / (jnp.sqrt(second_hat) + adam_epsilon) + decay * master
    )
    return (master_new, first_new, second_new, master_new.astype(jnp.bfloat16))


def product(pattern, left, right):
    return jnp.einsum(pattern, left, right, preferred_element_type=jnp.float32)


def gelu_both(lifted, active_grad):
    activated, pull = jax.vjp(partial(jax.nn.gelu, approximate=True), lifted)
    return pull(active_grad)[0].astype(jnp.bfloat16)


def gelu(lifted):
    return jax.nn.gelu(lifted, approximate=True).astype(jnp.bfloat16)


def swap(array, axis, bit):
    size = lax.axis_size(axis)
    return lax.ppermute(array, axis, [(i, i ^ bit) for i in range(size)])


def follow(array, *before):
    return lax.optimization_barrier((array, *before))[0]


ROWS = 640


MESH = pl.DeviceIdType.MESH


def feed_kernel(exchange, hidden_ref, back_ref, expand_ref, shrink_ref, *refs):
    step, steps = pl.program_id(0), pl.num_programs(0)
    f32 = jnp.float32
    if exchange:
        (
            expand_before,
            shrink_before,
            keep_ref,
            away_ref,
            land_hbm,
            hidden_part,
            branch_part,
            activated_ref,
            lifted_grad_ref,
            hidden_sum,
            branch_sum,
            send_ref,
            land_ref,
            near_send,
            near_recv,
            load_sem,
        ) = refs
        outer = lax.axis_index("outer")
        far, near = outer // 2, outer % 2
        near_id = {"outer": outer + 1 - 2 * near}

        def near_copy(tile, k):
            return pltpu.make_async_remote_copy(
                src_ref=send_ref.at[k],
                dst_ref=land_hbm.at[tile, k],
                send_sem=near_send.at[tile, k],
                recv_sem=near_recv.at[tile, k],
                device_id=near_id,
                device_id_type=MESH,
            )

        def load(tile, k):
            return pltpu.make_async_copy(land_hbm.at[tile, k], land_ref.at[k], load_sem.at[k])

        @pl.when(step == 0)
        def _():
            barrier = pltpu.get_barrier_semaphore()
            pl.semaphore_signal(
                barrier, inc=1, device_id=near_id, device_id_type=MESH
            )
            pl.semaphore_wait(barrier, 1)

        for tile in range(2):

            @pl.when(step == 2 + tile)
            def _(tile=tile):
                for k in range(2):
                    near_copy(tile, k).wait_recv()
                    load(tile, k).start()

    else:
        (
            expand_grad,
            shrink_grad,
            hidden_part,
            branch_part,
            activated_ref,
            lifted_grad_ref,
            hidden_sum,
            branch_sum,
        ) = refs
    tokens = hidden_ref.shape[0]
    nt = (((1,), (1,)), ((), ()))
    tn = (((0,), (0,)), ((), ()))
    slope = 0.7978845608028654

    def block(at, first):
        hidden = hidden_ref[at, :]
        back = back_ref[at, :]
        lifted = jnp.dot(hidden, expand_ref[...], preferred_element_type=f32)
        active_grad = lax.dot_general(back, shrink_ref[...], nt, preferred_element_type=f32)
        square = lifted * lifted
        curve = jnp.tanh(slope * (lifted + 0.044715 * (square * lifted)))
        rise = 0.5 * (1.0 + curve)
        activated = (lifted * rise).astype(jnp.bfloat16)
        bend = 0.5 * lifted * (1.0 - curve * curve) * (slope + (3.0 * 0.044715 * slope) * square)
        lifted_grad = (active_grad * (rise + bend)).astype(jnp.bfloat16)
        activated_ref[at, :] = activated
        lifted_grad_ref[at, :] = lifted_grad
        branch = jnp.dot(activated, shrink_ref[...], preferred_element_type=f32)
        hidden_grad = lax.dot_general(lifted_grad, expand_ref[...], nt, preferred_element_type=f32)
        if first:
            branch_sum[at, :] = branch
            hidden_sum[at, :] = hidden_grad
        else:
            branch_sum[at, :] += branch
            hidden_sum[at, :] += hidden_grad

    def blocks(first):
        def one(i, _):
            block(pl.ds(pl.multiple_of(i * ROWS, ROWS), ROWS), first)
            return 0

        lax.fori_loop(0, tokens // ROWS, one, 0)

    @pl.when(step == 0)
    def _():
        blocks(True)

    @pl.when(step > 0)
    def _():
        blocks(False)

    def gradient(k):
        made_of = ((activated_ref, back_ref), (lifted_grad_ref, hidden_ref))[k]
        made = lax.dot_general(made_of[0][...], made_of[1][...], tn, preferred_element_type=f32)
        return made + (shrink_before, expand_before)[k][...] if exchange else made

    if not exchange:
        shrink_grad[...] = gradient(0)
        expand_grad[...] = gradient(1)
    else:
        for tile in range(2):

            @pl.when(step == tile)
            def _(tile=tile):
                for k in range(2):
                    if tile:
                        near_copy(tile - 1, k).wait_send()
                    send_ref[k] = gradient(k)
                    near_copy(tile, k).start()

            @pl.when(step == 2 + tile)
            def _(tile=tile):
                for k in range(2):
                    load(tile, k).wait()
                    total = gradient(k) + land_ref[k]

                    @pl.when(far == tile)
                    def _():
                        keep_ref[k] = total

                    @pl.when(far != tile)
                    def _():
                        away_ref[k] = total.astype(jnp.bfloat16)

                    if tile == 0:
                        near_copy(1, k).wait_send()

    @pl.when(step == steps - 1)
    def _():
        hidden_part[...] = hidden_sum[...].astype(hidden_part.dtype)
        branch_part[...] = branch_sum[...].astype(branch_part.dtype)


def feed(hidden, back, expand, shrink, before, branch_type):
    tokens, width = hidden.shape
    units = 2 * expand.shape[2]
    steps = 4
    tile = units // steps
    exchange = bool(before)
    low, f32 = jnp.bfloat16, jnp.float32
    turn = steps // 2 if exchange else 0
    whole = pl.BlockSpec((tokens, width), lambda n: (0, 0), pipeline_mode=pl.Buffered(1))
    rows = pl.BlockSpec((tile, width), lambda n: ((n + turn) % steps, 0))
    quarter = pl.BlockSpec((2, tile, width), lambda n: (0, 0, 0), pipeline_mode=pl.Buffered(1))
    columns = pl.BlockSpec(
        (None, width, tile),
        lambda n: ((n + turn) % steps // 2, 0, (n + turn) % 2),
    )
    grads = jax.ShapeDtypeStruct((units, width), f32)
    sem = pltpu.SemaphoreType.DMA
    return pl.pallas_call(
        partial(feed_kernel, exchange),
        grid=(steps,),
        in_specs=[whole, whole, columns, rows] + [rows, rows] * exchange,
        out_specs=(
            [quarter, quarter, pl.BlockSpec(memory_space=pl.ANY)] if exchange else [rows, rows]
        )
        + [whole, whole],
        out_shape=(
            [
                jax.ShapeDtypeStruct((2, tile, width), f32),
                jax.ShapeDtypeStruct((2, tile, width), low),
                jax.ShapeDtypeStruct((2, 2, tile, width), f32),
            ]
            if exchange
            else [grads, grads]
        )
        + [
            jax.ShapeDtypeStruct((tokens, width), f32),
            jax.ShapeDtypeStruct((tokens, width), branch_type),
        ],
        scratch_shapes=[
            pltpu.VMEM((tokens, tile), low),
            pltpu.VMEM((tokens, tile), low),
            pltpu.VMEM((tokens, width), f32),
            pltpu.VMEM((tokens, width), f32),
        ]
        + [
            pltpu.VMEM((2, tile, width), f32),
            pltpu.VMEM((2, tile, width), f32),
            sem((2, 2)),
            sem((2, 2)),
            sem((2,)),
        ]
        * exchange,
        compiler_params=pltpu.CompilerParams(
            vmem_limit_bytes=60 * 2**20,
            **(dict(collective_id=4, has_side_effects=True) if exchange else {}),
        ),
        cost_estimate=pl.CostEstimate(flops=2**20, bytes_accessed=2**20, transcendentals=0),
    )(hidden, back, expand, shrink, *before)


def most_of(tokens):
    return tokens * 4 // 5 // 16 * 16


def opening_kernel(
    expand_ref,
    shrink_ref,
    project_ref,
    mixing_ref,
    norm_ref,
    inputs_ref,
    back_ref,
    expand_out,
    shrink_out,
    project_out,
    mixing_out,
    norm_out,
    hidden_ref,
    other_back,
    expand_low,
    shrink_low,
    norm_low,
    norm_all,
    own_sem,
    norm_send,
    norm_recv,
    line_send,
    line_recv,
    far_send,
    far_recv,
    near_send,
    near_recv,
    row_sem,
):
    place, deep = lax.axis_index("dp"), 4
    outer = lax.axis_index("outer")
    far, near = outer // 2, outer % 2
    far_id = {"outer": (outer + 2) % 4}
    near_id = {"outer": outer + 1 - 2 * near}
    rows = expand_ref.shape[0]
    half = expand_ref.shape[1] // 2
    part = half // 2

    barrier = pltpu.get_barrier_semaphore()
    for step in range(1, deep):
        pl.semaphore_signal(
            barrier, inc=1, device_id={"dp": (place + step) % deep}, device_id_type=MESH
        )
    pl.semaphore_signal(barrier, inc=1, device_id=far_id, device_id_type=MESH)
    pl.semaphore_signal(barrier, inc=1, device_id=near_id, device_id_type=MESH)
    row_id = {"mp": 1 - lax.axis_index("mp")}
    pl.semaphore_signal(barrier, inc=1, device_id=row_id, device_id_type=MESH)

    expand_low[...] = expand_ref[...].astype(jnp.bfloat16)
    norm_low[...] = jnp.zeros_like(norm_low)
    norm_low[0:2] = norm_ref[...].astype(jnp.bfloat16).astype(jnp.float32)
    pl.semaphore_wait(barrier, deep + 2)

    def piece(w, which, at, side):
        across = pl.ds(pl.multiple_of(at * rows, rows), rows)
        along = pl.ds(pl.multiple_of(side * part, part), part)
        if w == 0:
            return expand_out.at[which, across, along]
        return shrink_out.at[which, along, across]

    def mine(w):
        along = pl.ds(pl.multiple_of(near * half + far * part, part), part)
        return expand_low.at[:, along] if w == 0 else shrink_low.at[along, :]

    def remote(source, target, send, recv, device):
        return pltpu.make_async_remote_copy(
            src_ref=source,
            dst_ref=target,
            send_sem=send,
            recv_sem=recv,
            device_id=device,
            device_id_type=MESH,
        )

    def line(w, way, step, source, at):
        to = place + 1 if way == 0 else place - 1
        return remote(
            source,
            piece(w, 0, at, far),
            line_send.at[w, way, step],
            line_recv.at[w, way, step],
            {"dp": to},
        )

    def can_send(way):
        return place < deep - 1 if way == 0 else place > 0

    def start_own(w):
        for way in range(2):

            @pl.when(can_send(way))
            def _(way=way):
                line(w, way, 0, mine(w), place).start()

    def own_copies(w):
        out = []
        for which in range(2):
            side = near + which - 2 * near * which
            along = pl.ds(pl.multiple_of(side * half, half), half)
            across = pl.ds(pl.multiple_of(place * rows, rows), rows)
            if w == 0:
                pair = (expand_low.at[:, along], expand_out.at[which, across, :])
            else:
                pair = (shrink_low.at[along, :], shrink_out.at[which, :, across])
            out.append(pltpu.make_async_copy(*pair, own_sem.at[w, which]))
        return out

    start_own(0)
    most = most_of(back_ref.shape[0])
    row_copy = remote(
        back_ref.at[slice(0, most)],
        other_back.at[slice(0, most)],
        row_sem.at[0],
        row_sem.at[1],
        row_id,
    )
    row_copy.start()
    norm_copies = []
    for step in range(1, deep):
        copy = remote(
            norm_low,
            norm_all.at[step],
            norm_send.at[step],
            norm_recv.at[step],
            {"dp": (place + step) % deep},
        )
        copy.start()
        norm_copies.append(copy)
    shrink_low[...] = shrink_ref[...].astype(jnp.bfloat16)
    start_own(1)
    for w in range(2):
        for copy in own_copies(w):
            copy.start()
    for source, target in ((project_ref, project_out), (mixing_ref, mixing_out)):
        units = target.shape[0]
        target[...] = source[pl.ds(pl.multiple_of(near * units, units), units), :].astype(
            jnp.bfloat16
        )
    norm_all[0] = norm_low[...]
    for copy in norm_copies:
        copy.wait()
    for at in range(deep):
        norm_out[:, at * rows : (at + 1) * rows] = norm_all[(place - at + deep) % deep]
    gain, bias = norm_out[0:1], norm_out[1:2]
    tokens = inputs_ref.shape[0]
    height = 128

    def normalize(i, _):
        at = pl.ds(pl.multiple_of(i * height, height), height)
        x = inputs_ref[at, :].astype(jnp.float32)
        mean = jnp.mean(x, axis=1, keepdims=True)
        centred = x - mean
        spread = jnp.mean(centred * centred, axis=1, keepdims=True)
        normed = centred * lax.rsqrt(spread + norm_epsilon)
        hidden_ref[at, :] = (normed * gain + bias).astype(jnp.bfloat16)
        return 0

    lax.fori_loop(0, tokens // height, normalize, 0)

    def arrives(way, step):
        return place >= step if way == 0 else place + step < deep

    def at_of(way, step):
        return place - step if way == 0 else place + step

    def to_far(w, way, step):
        at = at_of(way, step)
        return remote(
            piece(w, 0, at, far),
            piece(w, 0, at, far),
            far_send.at[w, way, step - 1],
            far_recv.at[w, way, step - 1],
            far_id,
        )

    def from_far(w, way, step):
        at = at_of(way, step)
        return remote(
            piece(w, 0, at, 1 - far),
            piece(w, 0, at, 1 - far),
            far_send.at[w, way, step - 1],
            far_recv.at[w, way, step - 1],
            far_id,
        )

    def to_near(w, way, step, other):
        at = at_of(way, step)
        side = 1 - far if other else far
        return remote(
            piece(w, 0, at, side),
            piece(w, 1, at, side),
            near_send.at[w, way, step - 1, other],
            near_recv.at[w, way, step - 1, other],
            near_id,
        )

    order = [(w, step) for w in range(2) for step in range(1, deep)]

    def first_half(w, step):
        for way in range(2):

            @pl.when(arrives(way, step))
            def _(way=way):
                at = at_of(way, step)
                line(w, way, step - 1, mine(w), at).wait_recv()
                if step < deep - 1:

                    @pl.when(can_send(way))
                    def _():
                        line(w, way, step, piece(w, 0, at, far), at).start()

                to_far(w, way, step).start()
                to_near(w, way, step, 0).start()

    def second_half(w, step):
        for way in range(2):

            @pl.when(arrives(way, step))
            def _(way=way):
                from_far(w, way, step).wait_recv()
                to_near(w, way, step, 1).start()

    for n, (w, step) in enumerate(order):
        first_half(w, step)
        if n:
            second_half(*order[n - 1])
    second_half(*order[-1])
    row_copy.wait()
    for w in range(2):
        for copy in own_copies(w):
            copy.wait()
        for way in range(2):

            @pl.when(can_send(way))
            def _(way=way):
                line(w, way, 0, mine(w), place).wait_send()

            for step in range(1, deep):

                @pl.when(arrives(way, step))
                def _(way=way, step=step):
                    at = at_of(way, step)
                    if step < deep - 1:

                        @pl.when(can_send(way))
                        def _():
                            line(w, way, step, piece(w, 0, at, far), at).wait_send()

                    to_far(w, way, step).wait_send()
                    for other in range(2):
                        to_near(w, way, step, other).wait_send()
                        to_near(w, way, step, other).wait_recv()


def opening(expand, shrink, project, mixing, norm, inputs, back):
    deep = 4
    here = lambda: pl.BlockSpec(memory_space=pltpu.VMEM)
    rows, units = expand.shape
    low = jnp.bfloat16
    sem = pltpu.SemaphoreType.DMA
    return pl.pallas_call(
        opening_kernel,
        in_specs=[here() for _ in range(6)] + [pl.BlockSpec(memory_space=pl.ANY)],
        out_specs=[pl.BlockSpec(memory_space=pl.ANY)] * 2
        + [here() for _ in range(4)]
        + [pl.BlockSpec(memory_space=pl.ANY)],
        out_shape=[
            jax.ShapeDtypeStruct((2, rows * deep, units // 2), low),
            jax.ShapeDtypeStruct((2, units // 2, rows * deep), low),
            jax.ShapeDtypeStruct((project.shape[0] // 2, project.shape[1]), low),
            jax.ShapeDtypeStruct((mixing.shape[0] // 2, mixing.shape[1]), low),
            jax.ShapeDtypeStruct((8, rows * deep), jnp.float32),
            jax.ShapeDtypeStruct(inputs.shape, low),
            jax.ShapeDtypeStruct(back.shape, low),
        ],
        scratch_shapes=[
            pltpu.VMEM(expand.shape, low),
            pltpu.VMEM(shrink.shape, low),
            pltpu.VMEM((8, norm.shape[1]), jnp.float32),
            pltpu.VMEM((deep, 8, norm.shape[1]), jnp.float32),
            sem((2, 2)),
            sem((deep,)),
            sem((deep,)),
            sem((2, 2, deep)),
            sem((2, 2, deep)),
            sem((2, 2, deep)),
            sem((2, 2, deep)),
            sem((2, 2, deep, 2)),
            sem((2, 2, deep, 2)),
            sem((2,)),
        ],
        compiler_params=pltpu.CompilerParams(
            collective_id=1, has_side_effects=True, vmem_limit_bytes=40 * 2**20
        ),
        cost_estimate=pl.CostEstimate(flops=0, bytes_accessed=2**20, transcendentals=0),
    )(expand, shrink, project, mixing, norm, inputs, back)


def closing_kernel(
    later,
    project_hbm,
    *refs,
):
    sources = (project_hbm, *refs[:9])
    part_own, part_other, feed_keep, feed_come, gain_ref = refs[9:14]
    input_grad, small_sum, mixed_come = refs[14 + later : 17 + later]
    full_refs = refs[17 + later : 21 + later]
    refs = refs[21 + later :]
    held = refs[:10]
    (
        part_in,
        total_ref,
        sent_ref,
        come_ref,
        project_land,
        project_own,
        mixing_land,
        mixing_own,
        project_far,
        project_come,
        mixing_far,
        mixing_come,
        project_line,
        project_lands,
        mixing_line,
        mixing_lands,
        feed_in,
        feed_line,
        feed_lands,
        feed_share,
        expand_share,
        project_share,
        mixing_share,
        small_ref,
        plane_lands,
        deep_lands,
        held_sem,
        part_sem,
        out_sem,
        feed_sem,
        feed_send,
        feed_recv,
        spread_sem,
        spread_far_send,
        spread_far_recv,
        spread_near_send,
        spread_near_recv,
        plane_send,
        plane_recv,
        deep_send,
        deep_recv,
        row_send,
        row_recv,
        mixed_sem,
        near_send,
        near_recv,
        far_send,
        far_recv,
        line_send,
        line_recv,
    ) = refs[10:]
    (
        project,
        grads_other,
        grads_own,
        hidden_other,
        hidden_own,
        mixed_other,
        mixed_own,
        back_other,
        back_own,
        inputs,
    ) = held
    low, f32 = jnp.bfloat16, jnp.float32
    tn = (((0,), (0,)), ((), ()))
    place, deep, outers = lax.axis_index("dp"), 4, 4
    outer = lax.axis_index("outer")
    far, near = outer // 2, outer % 2
    row_id = {"mp": 1 - lax.axis_index("mp")}
    far_id = {"outer": (outer + 2) % 4}
    near_id = {"outer": outer + 1 - 2 * near}

    copies = [
        pltpu.make_async_copy(source, target, held_sem.at[n])
        for n, (source, target) in enumerate(zip(sources, held))
    ]
    for copy in copies[:2]:
        copy.start()
    barrier = pltpu.get_barrier_semaphore()
    plane = 2 * outers
    me = lax.axis_index("mp") * outers + outer

    def plane_id(step):
        other = (me + step) % plane
        return {"mp": other // outers, "outer": other % outers}

    for step in range(1, plane):
        pl.semaphore_signal(barrier, inc=1, device_id=plane_id(step), device_id_type=MESH)
    for step in range(1, deep):
        pl.semaphore_signal(
            barrier, inc=1, device_id={"dp": (place + step) % deep}, device_id_type=MESH
        )
    height = 256
    tokens, width = hidden_own.shape
    blocks = tokens // height
    at = [slice(n * height, (n + 1) * height) for n in range(blocks)]

    def remote(source, target, send, recv, device):
        return pltpu.make_async_remote_copy(
            src_ref=source,
            dst_ref=target,
            send_sem=send,
            recv_sem=recv,
            device_id=device,
            device_id_type=MESH,
        )

    loads = [
        pltpu.make_async_copy(source.at[at[n]], part_in.at[(k * blocks + n) % 2], part_sem.at[(k * blocks + n) % 2])
        for k, source in enumerate((part_other, part_own))
        for n in range(blocks)
    ]
    loads[0].start()
    loads[1].start()
    for copy in copies[2:]:
        copy.start()
    quarter = feed_keep.shape[1]
    feed_copies = [
        (
            pltpu.make_async_copy(
                feed_keep.at[k],
                total_ref.at[slice(k * quarter, (k + 1) * quarter)],
                feed_sem.at[k],
            ),
            pltpu.make_async_copy(feed_come.at[k], feed_in.at[k], feed_sem.at[2 + k]),
        )
        for k in range(2)
    ]
    for pair in feed_copies:
        for copy in pair:
            copy.start()

    copies[0].wait()
    copies[1].wait()
    pl.semaphore_wait(barrier, plane + deep - 2)
    row_copies = []
    for n in range(blocks):
        made = lax.dot_general(grads_other[:, at[n]], project[...], tn, preferred_element_type=f32)
        loads[n].wait()
        sent_ref[at[n], :] = (part_in[n % 2] + made).astype(low)
        loads[n + 2].start()
        copy = remote(
            sent_ref.at[at[n]], come_ref.at[at[n]], row_send.at[n], row_recv.at[n], row_id
        )
        copy.start()
        row_copies.append(copy)

    copies[5].wait()
    mixed_copy = remote(mixed_other, mixed_come, mixed_sem.at[0], mixed_sem.at[1], row_id)
    mixed_copy.start()

    piece = width // deep

    def columns(place):
        return pl.ds(pl.multiple_of(place * piece, piece), piece)

    line_copies = []
    for k in range(2):
        for copy in feed_copies[k]:
            copy.wait()
        rows = slice(k * quarter, (k + 1) * quarter)
        for step in range(1, deep):
            target = (place + step) % deep
            feed_line[k, step - 1] = (
                total_ref[rows, columns(target)] + feed_in[k, :, columns(target)].astype(f32)
            ).astype(low)
            line_copies.append(
                remote(
                    feed_line.at[k, step - 1],
                    feed_lands.at[k, step - 1],
                    feed_send.at[k, step - 1],
                    feed_recv.at[k, step - 1],
                    {"dp": target},
                )
            )
            line_copies[-1].start()
        feed_share[k] = total_ref[rows, columns(place)] + feed_in[k, :, columns(place)].astype(f32)

    for n in (2, 3, 4, 6, 7, 8):
        copies[n].wait()
    half = project_own.shape[0]
    few = mixing_own.shape[0]
    near_copies = []
    for n in range(half // height):
        rows = slice(half + n * height, half + (n + 1) * height)
        total_ref[at[n], :] = jnp.dot(
            grads_own[rows, :], hidden_own[...], preferred_element_type=f32
        ) + jnp.dot(grads_other[rows, :], hidden_other[...], preferred_element_type=f32)
        near_copies.append(
            remote(
                total_ref.at[at[n]],
                project_land.at[at[n]],
                near_send.at[n],
                near_recv.at[n],
                near_id,
            )
        )
        near_copies[-1].start()
    total_ref[half : half + few, :] = jnp.dot(
        mixed_own[few:, :], back_own[...], preferred_element_type=f32
    ) + jnp.dot(mixed_other[few:, :], back_other[...], preferred_element_type=f32)
    near_copies.append(
        remote(
            total_ref.at[slice(half, half + few)],
            mixing_land,
            near_send.at[3],
            near_recv.at[3],
            near_id,
        )
    )
    near_copies[-1].start()
    for n in range(half // height):
        made = jnp.dot(
            grads_own[at[n], :], hidden_own[...], preferred_element_type=f32
        ) + jnp.dot(grads_other[at[n], :], hidden_other[...], preferred_element_type=f32)
        near_copies[n].wait()
        project_own[at[n], :] = made + project_land[at[n], :]

    def to_far(own, send, come, n):
        size = send.shape[0]
        send[...] = own[pl.ds(pl.multiple_of((1 - far) * size, size), size), :].astype(low)
        copy = remote(send, come, far_send.at[n], far_recv.at[n], far_id)
        copy.start()
        return copy

    far_copies = [to_far(project_own, project_far, project_come, 0)]
    made = jnp.dot(mixed_own[:few, :], back_own[...], preferred_element_type=f32) + jnp.dot(
        mixed_other[:few, :], back_other[...], preferred_element_type=f32
    )
    near_copies[3].wait()
    mixing_own[...] = made + mixing_land[...]
    far_copies.append(to_far(mixing_own, mixing_far, mixing_come, 1))

    for n in range(blocks):
        made = lax.dot_general(grads_own[:, at[n]], project[...], tn, preferred_element_type=f32)
        loads[blocks + n].wait()
        total_ref[at[n], :] = part_in[(blocks + n) % 2] + made
        if n + 2 < blocks:
            loads[blocks + n + 2].start()

    for k, (own, come, line, lands) in enumerate(
        (
            (project_own, project_come, project_line, project_lands),
            (mixing_own, mixing_come, mixing_line, mixing_lands),
        )
    ):
        size = come.shape[0]
        keep = pl.ds(pl.multiple_of(far * size, size), size)
        far_copies[k].wait()
        own[keep, :] = own[keep, :] + come[...].astype(f32)
        for step in range(1, deep):
            target = (place + step) % deep
            line[step - 1] = own[keep, columns(target)].astype(low)
            copy = remote(
                line.at[step - 1],
                lands.at[step - 1],
                line_send.at[k, step - 1],
                line_recv.at[k, step - 1],
                {"dp": target},
            )
            copy.start()
            line_copies.append(copy)

    shares = (feed_share.at[0], expand_share, project_share, mixing_share)

    def place_in(k, near, far):
        if k == 1:
            return full_refs[k].at[:, pl.ds(pl.multiple_of((2 * near + far) * quarter, quarter), quarter)]
        size = shares[k].shape[0]
        return full_refs[k].at[pl.ds(pl.multiple_of((2 * near + far) * size, size), size)]

    def spread(k):
        if k < 2:
            result, lands = feed_share[k], feed_lands.at[k]
        else:
            own, lands = ((project_own, project_lands), (mixing_own, mixing_lands))[k - 2]
            size = shares[k].shape[0]
            result = own[pl.ds(pl.multiple_of(far * size, size), size), columns(place)]
        for copy in line_copies[3 * k : 3 * k + 3]:
            copy.wait()
        for step in range(1, deep):
            result = result + lands[step - 1].astype(f32)
        shares[k][...] = result.T if k == 1 else result
        here = place_in(k, near, far)
        copies = [
            pltpu.make_async_copy(shares[k], here, spread_sem.at[k]),
            remote(shares[k], here, spread_far_send.at[k], spread_far_recv.at[k], far_id),
            remote(shares[k], here, spread_near_send.at[k, 0], spread_near_recv.at[k, 0], near_id),
        ]
        for copy in copies:
            copy.start()
        return copies, jnp.sum(result * result)

    def pass_on(k, copies):
        copies[1].wait()
        there = place_in(k, near, 1 - far)
        copy = remote(
            there, there, spread_near_send.at[k, 1], spread_near_recv.at[k, 1], near_id
        )
        copy.start()
        return copy

    copies[9].wait()
    gain = gain_ref[0:1]
    gain_sum = jnp.zeros((1, width), f32)
    bias_sum = jnp.zeros((1, width), f32)
    out_copies, spreads, passed = [], [], []
    square = jnp.float32(0.0)
    for n in range(blocks):
        if n == blocks - 2:
            for k in range(2):
                copies, more = spread(k)
                spreads.append(copies)
                square = square + more
        if n == blocks - 1:
            for k in range(2, 4):
                copies, more = spread(k)
                spreads.append(copies)
                square = square + more
        row_copies[n].wait()
        if n >= 2:
            out_copies[n - 2].wait()

        def some(i, carry):
            gain_sum, bias_sum = carry
            small = 64
            rows = pl.ds(pl.multiple_of(n * height + i * small, small), small)
            x = inputs[rows, :].astype(f32)
            mean = jnp.mean(x, axis=1, keepdims=True)
            centred = x - mean
            spread = jnp.mean(centred * centred, axis=1, keepdims=True)
            inverse = lax.rsqrt(spread + norm_epsilon)
            normed = centred * inverse
            grad = total_ref[rows, :] + come_ref[rows, :].astype(f32)
            scaled = grad * gain
            middle = jnp.mean(scaled, axis=1, keepdims=True)
            along = jnp.mean(scaled * normed, axis=1, keepdims=True)
            result = inverse * (scaled - middle - normed * along)
            part_in[n % 2, pl.ds(pl.multiple_of(i * small, small), small), :] = (
                back_own[rows, :].astype(f32) + result
            )
            gain_sum = gain_sum + jnp.sum(grad * normed, axis=0, keepdims=True)
            bias_sum = bias_sum + jnp.sum(grad, axis=0, keepdims=True)
            return gain_sum, bias_sum

        gain_sum, bias_sum = lax.fori_loop(0, height // 64, some, (gain_sum, bias_sum))
        out_copies.append(
            pltpu.make_async_copy(part_in.at[n % 2], input_grad.at[at[n]], out_sem.at[n % 2])
        )
        out_copies[-1].start()
    for k in range(4):
        passed.append(pass_on(k, spreads[k]))

    small_ref[...] = jnp.full(small_ref.shape, square)
    small_ref[0:1] = gain_sum
    small_ref[1:2] = bias_sum

    def everywhere(lands, send, recv, size, index, device):
        copies = []
        for step in range(1, size):
            copy = remote(small_ref, lands.at[step], send.at[step], recv.at[step], device(step))
            copy.start()
            copies.append(copy)
        lands[0] = small_ref[...]
        for copy in copies:
            copy.wait()
        total = lands[index]
        for at in range(1, size):
            total = total + lands[(index + size - at) % size]
        small_ref[...] = total

    everywhere(plane_lands, plane_send, plane_recv, plane, me, plane_id)
    everywhere(
        deep_lands, deep_send, deep_recv, deep, place, lambda step: {"dp": (place + step) % deep}
    )
    small_sum[...] = small_ref[...]
    for k in range(4):
        spreads[k][0].wait()
        spreads[k][2].wait()
        passed[k].wait()
    mixed_copy.wait()
    for copy in out_copies[-2:]:
        copy.wait()


def closing(project, grads, hiddens, mixed, backs, inputs, parts, feeds, gain, after):
    deep = 4
    low, f32 = jnp.bfloat16, jnp.float32
    tokens, width = inputs.shape
    half, few = grads[0].shape[0] // 2, mixed[0].shape[0] // 2
    piece = width // deep
    quarter = feeds[0].shape[1]
    anywhere = pl.BlockSpec(memory_space=pl.ANY)
    here = lambda: pl.BlockSpec(memory_space=pltpu.VMEM)
    held = (
        project,
        grads[1],
        grads[0],
        hiddens[1],
        hiddens[0],
        mixed[1],
        mixed[0],
        backs[1],
        backs[0],
        inputs,
    )
    sem = pltpu.SemaphoreType.DMA
    space = pltpu.VMEM
    return pl.pallas_call(
        partial(closing_kernel, len(after)),
        in_specs=[anywhere] * 14 + [here()] + [anywhere] * len(after),
        out_specs=[anywhere, here()] + [anywhere] * 5,
        out_shape=[
            jax.ShapeDtypeStruct((tokens, width), f32),
            jax.ShapeDtypeStruct((8, width), f32),
            jax.ShapeDtypeStruct(mixed[1].shape, low),
        ]
        + [
            jax.ShapeDtypeStruct(shape, f32)
            for shape in (
                (4 * quarter, piece),
                (piece, 4 * quarter),
                (2 * half, piece),
                (2 * few, piece),
            )
        ],
        scratch_shapes=[space(v.shape, v.dtype) for v in held]
        + [
            space((2, 256, width), f32),
            space((tokens, width), f32),
            space((tokens, width), low),
            space((tokens, width), low),
            space((half, width), f32),
            space((half, width), f32),
            space((few, width), f32),
            space((few, width), f32),
            space((half // 2, width), low),
            space((half // 2, width), low),
            space((few // 2, width), low),
            space((few // 2, width), low),
            space((deep - 1, half // 2, piece), low),
            space((deep - 1, half // 2, piece), low),
            space((deep - 1, few // 2, piece), low),
            space((deep - 1, few // 2, piece), low),
            space((2, quarter, width), low),
            space((2, deep - 1, quarter, piece), low),
            space((2, deep - 1, quarter, piece), low),
            space((2, quarter, piece), f32),
            space((piece, quarter), f32),
            space((half // 2, piece), f32),
            space((few // 2, piece), f32),
            space((8, width), f32),
            space((8, 8, width), f32),
            space((deep, 8, width), f32),
            sem((len(held),)),
            sem((2,)),
            sem((2,)),
            sem((4,)),
            sem((2, deep - 1)),
            sem((2, deep - 1)),
            sem((4,)),
            sem((4,)),
            sem((4,)),
            sem((4, 2)),
            sem((4, 2)),
            sem((8,)),
            sem((8,)),
            sem((deep,)),
            sem((deep,)),
            sem((tokens // 256,)),
            sem((tokens // 256,)),
            sem((2,)),
            sem((4,)),
            sem((4,)),
            sem((2,)),
            sem((2,)),
            sem((2, deep)),
            sem((2, deep)),
        ],
        compiler_params=pltpu.CompilerParams(
            collective_id=3, has_side_effects=True, vmem_limit_bytes=62 * 2**20
        ),
        cost_estimate=pl.CostEstimate(flops=2**20, bytes_accessed=2**20, transcendentals=0),
    )(*held, *parts, *feeds, gain, *after)


class Paired:
    def __init__(self):
        self.place = lax.axis_index("dp")
        self.deep = lax.axis_size("dp")

    def gather(self, own, cut, depth):
        return lax.all_gather(own, "dp", axis=depth, tiled=True)

    def gather_few(self, own):
        size = self.deep
        return [
            lax.ppermute(own, "dp", [(i, (i + step) % size) for i in range(size)])
            for step in range(1, size)
        ]

    def placed(self, own, come, depth):
        wide = list(own.shape)
        piece = wide[depth]
        wide[depth] *= self.deep
        out = jnp.zeros(wide, own.dtype)
        for step, one in enumerate([own, *come]):
            at = lax.rem(self.place - step + self.deep, self.deep)
            out = lax.dynamic_update_slice_in_dim(out, one, at * piece, depth)
        return out

    def paired(self, half, cut):
        return jnp.concatenate([half, swap(half, "outer", 1)], axis=cut)


def local(
    inputs,
    cotangent,
    lengths,
    project_master,
    project_first,
    project_second,
    mixing_master,
    mixing_first,
    mixing_second,
    expand_master,
    expand_first,
    expand_second,
    shrink_master,
    shrink_first,
    shrink_second,
    norm_master,
    norm_first,
    norm_second,
):
    split, deep = lax.axis_size("mp"), lax.axis_size("dp")
    heads_here = project_master.shape[1]
    width = inputs.shape[1]
    paired = (
        split == 2
        and lax.axis_size("outer") == 4
        and heads_here % 4 == 0
        and width % BQ == 0
    )
    position = lax.axis_index("mp")
    count = width * split
    project_flat = project_master.transpose(1, 2, 0).reshape(heads_here * 3 * HD, -1)
    mixing_flat = mixing_master.reshape(heads_here * HD, mixing_master.shape[2])
    masters = (project_flat, mixing_flat, expand_master, shrink_master)
    depths = (1, 1, 0, 1)
    rows_local = inputs[0].astype(jnp.float32)
    begins, places = layout(lengths[0], count)
    cosine, sine = turns(places)
    if paired:
        plan = Paired()
        expand, shrink, project, mixing, norm_weight, hidden_local, other_back = opening(
            expand_master,
            shrink_master,
            project_flat,
            mixing_flat,
            norm_master,
            inputs[0],
            cotangent[0],
        )
        most = most_of(width)
        other_back = lax.dynamic_update_slice(
            other_back, swap(cotangent[0, most:], "mp", 1), (most, 0)
        )
        backs = [cotangent[0], other_back]
        shrink = shrink.reshape(-1, shrink.shape[2])
        project_half = plan.gather(project, 0, 1)
        mixing_come = plan.gather_few(mixing)
        hiddens = [hidden_local, swap(hidden_local, "mp", 1)]
    else:
        norm_weight = lax.all_gather(norm_master.astype(jnp.bfloat16), "dp", axis=1, tiled=True)
        gain = norm_weight[0].astype(jnp.float32)
        bias = norm_weight[1].astype(jnp.float32)
        shaped, norm_pull = jax.vjp(layer_norm, rows_local, gain, bias)
        hidden_local = shaped.astype(jnp.bfloat16)
        project, mixing, expand, shrink = (
            lax.all_gather(master.astype(jnp.bfloat16), "dp", axis=depth, tiled=True)
            for master, depth in zip(masters, depths)
        )
        backs = [lax.all_gather(cotangent[0], "mp", axis=0, tiled=True)]
        hiddens = [lax.all_gather(hidden_local, "mp", axis=0, tiled=True)]

    def over_tokens(pattern, lefts, rights):
        return sum(product(pattern, left, right) for left, right in zip(lefts, rights))

    back_local = cotangent[0].astype(jnp.float32)
    if paired:
        *grads, hidden_own, branch_own = feed(
            hiddens[0], backs[0], expand, shrink, (), jnp.float32
        )
        project = plan.paired(follow(project_half, branch_own), 0)
        mixing_come = [follow(v, branch_own) for v in mixing_come]
        mixing = plan.paired(plan.placed(mixing, mixing_come, 1), 0)
        feed_keep, feed_away, _, hidden_other, branch_other = feed(
            hiddens[1], backs[1], expand, shrink, grads, jnp.bfloat16
        )
        feed_come = swap(feed_away, "outer", 2)
        branch_come = swap(branch_other, "mp", 1)
        mixing_other = swap(mixing, "mp", 1)
        projected = [product("td,ed->et", hidden, project) for hidden in hiddens]
        mixed_backs = [product("td,fd->ft", back, mixing).astype(jnp.bfloat16) for back in backs]
        mixed, projected_grads = attend(
            projected,
            mixed_backs,
            begins,
            cosine,
            sine,
            position,
            (feed_away, branch_other),
        )
        input_grad, small_sum, mixed_come, shrink_sum, expand_sum, project_sum, mixing_sum = closing(
            project,
            projected_grads,
            hiddens,
            mixed,
            backs,
            inputs[0],
            (hidden_own, hidden_other),
            (feed_keep, feed_come),
            norm_weight,
            (branch_come,),
        )
        mixed_own = follow(mixed[0], small_sum)
        branch = (
            branch_own
            + branch_come.astype(jnp.float32)
            + product("ft,fd->td", mixed_own, mixing)
            + product("ft,fd->td", mixed_come, mixing_other)
        )
    else:
        lifteds = [product("td,df->tf", hidden, expand) for hidden in hiddens]
        activated = [gelu(lifted) for lifted in lifteds]
        active_grads = [product("td,fd->tf", back, shrink) for back in backs]
        lifted_grads = [gelu_both(a, b) for a, b in zip(lifteds, active_grads)]
        hidden_parts = [product("tf,df->td", v, expand) for v in lifted_grads]
        branch_parts = [product("tf,fd->td", v, shrink) for v in activated]
        projected = [product("td,ed->et", hidden, project) for hidden in hiddens]
        mixed_backs = [product("td,fd->ft", back, mixing).astype(jnp.bfloat16) for back in backs]
        mixed, projected_grads = attend(projected, mixed_backs, begins, cosine, sine, position)
        project_sum, mixing_sum, expand_sum, shrink_sum = (
            lax.psum(
                lax.psum_scatter(
                    over_tokens(pattern, lefts, rights),
                    "dp",
                    scatter_dimension=depth,
                    tiled=True,
                ),
                "outer",
            )
            for pattern, lefts, rights, depth in (
                ("et,td->ed", projected_grads, hiddens, 1),
                ("ft,td->fd", mixed, backs, 1),
                ("td,tf->df", hiddens, lifted_grads, 0),
                ("tf,td->fd", activated, backs, 1),
            )
        )
        hidden_grad, branch = (
            lax.psum_scatter(v, "mp", scatter_dimension=0, tiled=True)
            for v in (
                hidden_parts[0] + product("et,ed->td", projected_grads[0], project),
                branch_parts[0] + product("ft,fd->td", mixed[0], mixing),
            )
        )
        rows_grad, gain_grad, bias_grad = norm_pull(hidden_grad)
        input_grad = back_local + rows_grad
        norm_terms = jnp.stack([gain_grad, bias_grad])
    input_grad = input_grad[None]
    block_out = (rows_local + branch).astype(jnp.bfloat16)[None]
    sums = (project_sum, mixing_sum, expand_sum, shrink_sum)
    if not paired:
        own_square = sum(jnp.sum(v * v) for v in sums) / lax.axis_size("outer")
        small_sum = lax.psum(
            jnp.concatenate([norm_terms, jnp.full((1, D), own_square)]), ("mp", "dp", "outer")
        )
    norm_full = small_sum[:2]
    grad_norm = jnp.sqrt(small_sum[2, 0] + jnp.sum(norm_full * norm_full))
    factor = clip_level / jnp.maximum(grad_norm, clip_level)
    norm_gradient = lax.dynamic_slice_in_dim(
        norm_full, lax.axis_index("dp") * (D // deep), D // deep, 1
    )
    gradients = list(sums)
    gradients[0] = gradients[0].reshape(heads_here, 3 * HD, -1).transpose(2, 0, 1)
    gradients[1] = gradients[1].reshape(mixing_master.shape)
    states = (
        (project_master, project_first, project_second, D ** (-0.5)),
        (mixing_master, mixing_first, mixing_second, (D // 32) ** (-0.5)),
        (expand_master, expand_first, expand_second, D ** (-0.5)),
        (shrink_master, shrink_first, shrink_second, FF ** (-0.5)),
    )
    results = [block_out, input_grad]
    for (master, first, second, rate), gradient in zip(states, gradients):
        results += adam_update(master, first, second, factor * gradient, rate, decay_rate)
    results += adam_update(norm_master, norm_first, norm_second, factor * norm_gradient, 0.3, 0.0)
    return (*results, grad_norm)


def solution(mesh):
    in_specs = (
        P(("dp", "outer"), "mp", None),
        P(("dp", "outer"), "mp", None),
        P(("dp", "outer"), None),
        P("dp", "mp", None),
        P("dp", "mp", None),
        P("dp", "mp", None),
        P("mp", None, "dp"),
        P("mp", None, "dp"),
        P("mp", None, "dp"),
        P("dp", "mp"),
        P("dp", "mp"),
        P("dp", "mp"),
        P("mp", "dp"),
        P("mp", "dp"),
        P("mp", "dp"),
        P(None, "dp"),
        P(None, "dp"),
        P(None, "dp"),
    )
    out_specs = (
        P(("dp", "outer"), "mp", None),
        P(("dp", "outer"), "mp", None),
        P("dp", "mp", None),
        P("dp", "mp", None),
        P("dp", "mp", None),
        P("dp", "mp", None),
        P("mp", None, "dp"),
        P("mp", None, "dp"),
        P("mp", None, "dp"),
        P("mp", None, "dp"),
        P("dp", "mp"),
        P("dp", "mp"),
        P("dp", "mp"),
        P("dp", "mp"),
        P("mp", "dp"),
        P("mp", "dp"),
        P("mp", "dp"),
        P("mp", "dp"),
        P(None, "dp"),
        P(None, "dp"),
        P(None, "dp"),
        P(None, "dp"),
        P(),
    )
    return jax.shard_map(local, mesh=mesh, in_specs=in_specs, out_specs=out_specs, check_vma=False)
```

```python
from functools import partial
import math

import jax
import jax.numpy as jnp
from jax import lax
from jax.experimental import pallas as pl
from jax.experimental.pallas import tpu as pltpu
from jax.sharding import PartitionSpec as P

D = 1024
HD = 64
ROT = 32
FF = 4096
STEP = 10


norm_epsilon = 1e-05
beta_one = 0.9
beta_two = 0.95
adam_epsilon = 1e-08
decay_rate = 0.1
clip_level = 1.0
masked_value = -1e30


def layout(sizes_row, count):
    number = jnp.arange(sizes_row.shape[0], dtype=jnp.int32)
    ends = jnp.sum(jnp.where(number[None, :] <= number[:, None], sizes_row[None, :], 0), axis=1)
    tokens = jnp.arange(count, dtype=jnp.int32)
    passed = (ends[:, None] <= tokens[None, :]).astype(jnp.int32)
    begins = jnp.sum(passed * sizes_row[:, None], axis=0)
    return (begins, tokens - begins)


def turns(places):
    half_rot = ROT // 2
    counter = jnp.arange(half_rot, dtype=jnp.float32)
    frequency = jnp.exp(counter * (-2.0 * math.log(10000.0) / ROT))
    angles = places.astype(jnp.float32)[None, :] * frequency[:, None]
    return jnp.cos(angles), jnp.sin(angles)


BQ = 256
BK = 256


def attend_kernel(together, parts, later, *refs):
    facts = refs[0]
    projected_refs = refs[1 : 1 + parts]
    back_refs = refs[1 + parts : 1 + 2 * parts]
    start_ref, cos_ref, sin_ref = refs[1 + 2 * parts : 4 + 2 * parts]
    refs = refs[: 4 + 2 * parts] + refs[4 + 2 * parts + later :]
    mixed_refs = refs[4 + 2 * parts : 4 + 3 * parts]
    grad_refs = refs[4 + 3 * parts : 4 + 4 * parts]
    (
        query_ref,
        key_columns_ref,
        value_columns_ref,
        key_ref,
        value_ref,
        back_ref,
        query_grad_ref,
        key_grad_ref,
        value_grad_ref,
        shifted_ref,
        share_grad_ref,
        top_ref,
    ) = refs[4 + 4 * parts :]
    width = projected_refs[0].shape[1]
    count = width * parts
    blocks = count // BQ
    turn = facts[blocks]
    half = ROT // 2
    scale = HD ** (-0.5)

    def place_of(part):
        if parts == 1:
            return pl.ds(0, width)
        block = lax.rem(part * (blocks // parts) + blocks - turn, blocks)
        return pl.ds(pl.multiple_of(block * BQ, BQ), width)

    for part in range(parts):
        columns = slice(part * width, (part + 1) * width)
        cosine, sine = cos_ref[:, place_of(part)], sin_ref[:, place_of(part)]
        projected_ref = projected_refs[part]

        def turned(at):
            first = projected_ref[at : at + half]
            second = projected_ref[at + half : at + ROT]
            return jnp.concatenate(
                [
                    first * cosine - second * sine,
                    second * cosine + first * sine,
                    projected_ref[at + ROT : at + HD],
                ],
                axis=0,
            ).astype(jnp.bfloat16)

        for h in range(together):
            base = h * 3 * HD
            query_ref[h, :, columns] = (turned(base).astype(jnp.float32) * scale).astype(
                jnp.bfloat16
            )
            keys = turned(base + HD)
            values = projected_ref[base + 2 * HD : base + 3 * HD].astype(jnp.bfloat16)
            key_columns_ref[h, :, columns] = keys
            value_columns_ref[h, :, columns] = values
            key_ref[h, columns] = keys.T
            value_ref[h, columns] = values.T
            back_ref[h, :, columns] = back_refs[part][h * HD : (h + 1) * HD]
    key_grad_ref[...] = jnp.zeros_like(key_grad_ref)
    value_grad_ref[...] = jnp.zeros_like(value_grad_ref)
    key_at = lax.broadcasted_iota(jnp.int32, (BK, BQ), 0)
    query_at = lax.broadcasted_iota(jnp.int32, (1, BQ), 1)

    def stored(block):
        if parts == 1:
            return pl.ds(pl.multiple_of(block * BQ, BQ), BQ)
        return pl.ds(pl.multiple_of(lax.rem(block + turn, blocks) * BQ, BQ), BQ)

    def query_block(i, _):
        columns = stored(i)
        start = start_ref[:, pl.ds(pl.multiple_of(i * BQ, BQ), BQ)]
        own = query_at + i * BQ
        lowest = facts[i]
        queries = [query_ref[h, :, columns] for h in range(together)]
        backs = [back_ref[h, :, columns] for h in range(together)]
        query_rows = [queries[h].T for h in range(together)]
        back_rows = [backs[h].T for h in range(together)]

        def in_pairs(body, carry):
            twos = lax.div(i + 1 - lowest, 2)
            carry = lax.fori_loop(
                0, twos, lambda n, c: body((lowest + 2 * n, lowest + 2 * n + 1), c), carry
            )
            return lax.fori_loop(lowest + 2 * twos, i + 1, lambda n, c: body((n,), c), carry)

        def scores(group, carry):
            made = []
            for j in group:
                rows = stored(j)
                allowed = (key_at >= start - j * BK) & (key_at <= own - j * BK)
                for h in range(together):
                    raw = jnp.dot(
                        key_ref[h, rows, :], queries[h], preferred_element_type=jnp.float32
                    )
                    share_grad = jnp.dot(
                        value_ref[h, rows, :], backs[h], preferred_element_type=jnp.float32
                    )
                    masked = jnp.where(allowed, raw, masked_value)
                    here = jnp.max(masked, axis=0, keepdims=True)
                    shifted = jnp.exp(masked - here)
                    shifted_ref[h, j] = shifted
                    share_grad_ref[h, j] = share_grad
                    top_ref[h, j] = here
                    made.append(
                        (
                            here,
                            jnp.sum(shifted, axis=0, keepdims=True),
                            jnp.sum(shifted * share_grad, axis=0, keepdims=True),
                        )
                    )
            out = []
            for h in range(together):
                top, total, inner = carry[h]
                for here, here_total, here_inner in made[h::together]:
                    new = jnp.maximum(top, here)
                    old_by, here_by = jnp.exp(top - new), jnp.exp(here - new)
                    total = total * old_by + here_total * here_by
                    inner = inner * old_by + here_inner * here_by
                    top = new
                out.append((top, total, inner))
            return tuple(out)

        zero = jnp.zeros((1, BQ), jnp.float32)
        empty = (jnp.full((1, BQ), masked_value, jnp.float32), zero, zero)
        stats = in_pairs(scores, (empty,) * together)
        inverse = [1.0 / s[1] for s in stats]
        inners = [s[2] * r for s, r in zip(stats, inverse)]

        def sums(group, carry):
            out = list(carry)
            for j in group:
                rows = stored(j)
                for h in range(together):
                    mixed, query_grad = out[h]
                    by = jnp.exp(top_ref[h, j] - stats[h][0]) * inverse[h]
                    probs = shifted_ref[h, j] * by
                    shares = probs.astype(jnp.bfloat16)
                    score_grad = (probs * (share_grad_ref[h, j] - inners[h])).astype(jnp.bfloat16)
                    mixed = mixed + jnp.dot(
                        value_columns_ref[h, :, rows], shares, preferred_element_type=jnp.float32
                    )
                    query_grad = query_grad + jnp.dot(
                        key_columns_ref[h, :, rows], score_grad, preferred_element_type=jnp.float32
                    )
                    value_grad_ref[h, rows, :] += jnp.dot(
                        shares, back_rows[h], preferred_element_type=jnp.float32
                    )
                    key_grad_ref[h, rows, :] += jnp.dot(
                        score_grad, query_rows[h], preferred_element_type=jnp.float32
                    )
                    out[h] = (mixed, query_grad)
            return tuple(out)

        nothing = jnp.zeros((HD, BQ), jnp.float32)
        results = in_pairs(sums, ((nothing, nothing),) * together)
        for h in range(together):
            back_ref[h, :, columns] = results[h][0].astype(jnp.bfloat16)
            query_grad_ref[h, :, columns] = results[h][1] * scale
        return 0

    lax.fori_loop(0, blocks, query_block, 0)
    for part in range(parts):
        columns = slice(part * width, (part + 1) * width)
        cosine, sine = cos_ref[:, place_of(part)], sin_ref[:, place_of(part)]

        def turned_back(grad):
            first, second = grad[:half], grad[half:ROT]
            return jnp.concatenate(
                [
                    first * cosine + second * sine,
                    second * cosine - first * sine,
                    grad[ROT:],
                ],
                axis=0,
            ).astype(jnp.bfloat16)

        for h in range(together):
            base = h * 3 * HD
            mixed_refs[part][h * HD : (h + 1) * HD] = back_ref[h, :, columns]
            grad_refs[part][base : base + HD] = turned_back(query_grad_ref[h, :, columns])
            grad_refs[part][base + HD : base + 2 * HD] = turned_back(key_grad_ref[h, columns, :].T)
            grad_refs[part][base + 2 * HD : base + 3 * HD] = value_grad_ref[
                h, columns, :
            ].T.astype(jnp.bfloat16)


def attend(projected, back, begins, cosine, sine, offset, after=()):
    parts = len(projected)
    heads = back[0].shape[0] // HD
    width = back[0].shape[1]
    count = begins.shape[0]
    together = 2 if heads % 2 == 0 else 1
    blocks = count // BK
    half = ROT // 2
    turn = jnp.asarray(offset * ((blocks // parts) if parts > 1 else 0), jnp.int32)
    facts = jnp.concatenate([begins[::BQ] // BK, turn[None]])
    whole = lambda rows: pl.BlockSpec((rows, count), lambda g, *_: (0, 0))
    mine = lambda rows: pl.BlockSpec((rows, width), lambda g, *_: (g, 0))
    results = pl.pallas_call(
        partial(attend_kernel, together, parts, len(after)),
        grid_spec=pltpu.PrefetchScalarGridSpec(
            num_scalar_prefetch=1,
            grid=(heads // together,),
            in_specs=[mine(together * 3 * HD)] * parts
            + [mine(together * HD)] * parts
            + [whole(1), whole(half), whole(half)]
            + [pl.BlockSpec(memory_space=pl.ANY)] * len(after),
            out_specs=[mine(together * HD)] * parts + [mine(together * 3 * HD)] * parts,
            scratch_shapes=[
                pltpu.VMEM((together, HD, count), jnp.bfloat16),
                pltpu.VMEM((together, HD, count), jnp.bfloat16),
                pltpu.VMEM((together, HD, count), jnp.bfloat16),
                pltpu.VMEM((together, count, HD), jnp.bfloat16),
                pltpu.VMEM((together, count, HD), jnp.bfloat16),
                pltpu.VMEM((together, HD, count), jnp.bfloat16),
                pltpu.VMEM((together, HD, count), jnp.float32),
                pltpu.VMEM((together, count, HD), jnp.float32),
                pltpu.VMEM((together, count, HD), jnp.float32),
                pltpu.VMEM((together, blocks, BK, BQ), jnp.float32),
                pltpu.VMEM((together, blocks, BK, BQ), jnp.float32),
                pltpu.VMEM((together, blocks, 1, BQ), jnp.float32),
            ],
        ),
        out_shape=[jax.ShapeDtypeStruct((heads * HD, width), jnp.bfloat16)] * parts
        + [jax.ShapeDtypeStruct((heads * 3 * HD, width), jnp.bfloat16)] * parts,
        compiler_params=pltpu.CompilerParams(vmem_limit_bytes=48 * 2**20),
        cost_estimate=pl.CostEstimate(
            flops=2**20,
            bytes_accessed=2**20,
            transcendentals=0,
        ),
    )(facts, *projected, *back, begins[None, :], cosine, sine, *after)
    return results[:parts], results[parts:]


def layer_norm(rows_in, gain, bias):
    mean = jnp.mean(rows_in, axis=1, keepdims=True)
    centred = rows_in - mean
    spread = jnp.mean(centred * centred, axis=1, keepdims=True)
    normed = centred * lax.rsqrt(spread + norm_epsilon)
    return normed * gain + bias


def adam_update(master, first, second, gradient, rate, decay):
    first_new = beta_one * first + (1.0 - beta_one) * gradient
    second_new = beta_two * second + (1.0 - beta_two) * gradient * gradient
    first_hat = first_new / (1.0 - beta_one**STEP)
    second_hat = second_new / (1.0 - beta_two**STEP)
    master_new = master - rate * (
        first_hat / (jnp.sqrt(second_hat) + adam_epsilon) + decay * master
    )
    return (master_new, first_new, second_new, master_new.astype(jnp.bfloat16))


def product(pattern, left, right):
    return jnp.einsum(pattern, left, right, preferred_element_type=jnp.float32)


def gelu_both(lifted, active_grad):
    activated, pull = jax.vjp(partial(jax.nn.gelu, approximate=True), lifted)
    return pull(active_grad)[0].astype(jnp.bfloat16)


def gelu(lifted):
    return jax.nn.gelu(lifted, approximate=True).astype(jnp.bfloat16)


def swap(array, axis, bit):
    size = lax.axis_size(axis)
    return lax.ppermute(array, axis, [(i, i ^ bit) for i in range(size)])


def follow(array, *before):
    return lax.optimization_barrier((array, *before))[0]


ROWS = 640


MESH = pl.DeviceIdType.MESH


def feed_kernel(exchange, later, hidden_ref, back_ref, expand_ref, shrink_ref, *refs):
    step, steps = pl.program_id(0), pl.num_programs(0)
    f32 = jnp.float32
    if exchange:
        expand_before, shrink_before = refs[:2]
        (
            keep_ref,
            away_ref,
            land_hbm,
            hidden_part,
            branch_part,
            activated_ref,
            lifted_grad_ref,
            hidden_sum,
            branch_sum,
            send_ref,
            land_ref,
            near_send,
            near_recv,
            load_sem,
        ) = refs[2 + later :]
        outer = lax.axis_index("outer")
        far, near = outer // 2, outer % 2
        near_id = {"outer": outer + 1 - 2 * near}

        def near_copy(tile, k):
            return pltpu.make_async_remote_copy(
                src_ref=send_ref.at[k],
                dst_ref=land_hbm.at[tile, k],
                send_sem=near_send.at[tile, k],
                recv_sem=near_recv.at[tile, k],
                device_id=near_id,
                device_id_type=MESH,
            )

        def load(tile, k):
            return pltpu.make_async_copy(land_hbm.at[tile, k], land_ref.at[k], load_sem.at[k])

        @pl.when(step == 0)
        def _():
            barrier = pltpu.get_barrier_semaphore()
            pl.semaphore_signal(
                barrier, inc=1, device_id=near_id, device_id_type=MESH
            )
            pl.semaphore_wait(barrier, 1)

        for tile in range(2):

            @pl.when(step == 2 + tile)
            def _(tile=tile):
                for k in range(2):
                    near_copy(tile, k).wait_recv()
                    load(tile, k).start()

    else:
        (
            expand_grad,
            shrink_grad,
            hidden_part,
            branch_part,
            activated_ref,
            lifted_grad_ref,
            hidden_sum,
            branch_sum,
        ) = refs
    tokens = hidden_ref.shape[0]
    nt = (((1,), (1,)), ((), ()))
    tn = (((0,), (0,)), ((), ()))
    slope = 0.7978845608028654

    def block(at, first):
        hidden = hidden_ref[at, :]
        back = back_ref[at, :]
        lifted = jnp.dot(hidden, expand_ref[...], preferred_element_type=f32)
        active_grad = lax.dot_general(back, shrink_ref[...], nt, preferred_element_type=f32)
        square = lifted * lifted
        curve = jnp.tanh(slope * (lifted + 0.044715 * (square * lifted)))
        rise = 0.5 * (1.0 + curve)
        activated = (lifted * rise).astype(jnp.bfloat16)
        bend = 0.5 * lifted * (1.0 - curve * curve) * (slope + (3.0 * 0.044715 * slope) * square)
        lifted_grad = (active_grad * (rise + bend)).astype(jnp.bfloat16)
        activated_ref[at, :] = activated
        lifted_grad_ref[at, :] = lifted_grad
        branch = jnp.dot(activated, shrink_ref[...], preferred_element_type=f32)
        hidden_grad = lax.dot_general(lifted_grad, expand_ref[...], nt, preferred_element_type=f32)
        if first:
            branch_sum[at, :] = branch
            hidden_sum[at, :] = hidden_grad
        else:
            branch_sum[at, :] += branch
            hidden_sum[at, :] += hidden_grad

    def blocks(first):
        def one(i, _):
            block(pl.ds(pl.multiple_of(i * ROWS, ROWS), ROWS), first)
            return 0

        lax.fori_loop(0, tokens // ROWS, one, 0)

    @pl.when(step == 0)
    def _():
        blocks(True)

    @pl.when(step > 0)
    def _():
        blocks(False)

    def gradient(k):
        made_of = ((activated_ref, back_ref), (lifted_grad_ref, hidden_ref))[k]
        made = lax.dot_general(made_of[0][...], made_of[1][...], tn, preferred_element_type=f32)
        return made + (shrink_before, expand_before)[k][...] if exchange else made

    if not exchange:
        shrink_grad[...] = gradient(0)
        expand_grad[...] = gradient(1)
    else:
        for tile in range(2):

            @pl.when(step == tile)
            def _(tile=tile):
                for k in range(2):
                    if tile:
                        near_copy(tile - 1, k).wait_send()
                    send_ref[k] = gradient(k)
                    near_copy(tile, k).start()

            @pl.when(step == 2 + tile)
            def _(tile=tile):
                for k in range(2):
                    load(tile, k).wait()
                    total = gradient(k) + land_ref[k]

                    @pl.when(far == tile)
                    def _():
                        keep_ref[k] = total

                    @pl.when(far != tile)
                    def _():
                        away_ref[k] = total.astype(jnp.bfloat16)

                    if tile == 0:
                        near_copy(1, k).wait_send()

    @pl.when(step == steps - 1)
    def _():
        hidden_part[...] = hidden_sum[...].astype(hidden_part.dtype)
        branch_part[...] = branch_sum[...].astype(branch_part.dtype)


def feed(hidden, back, expand, shrink, before, branch_type, after=()):
    tokens, width = hidden.shape
    units = 2 * expand.shape[2]
    steps = 4
    tile = units // steps
    exchange = bool(before)
    low, f32 = jnp.bfloat16, jnp.float32
    turn = steps // 2 if exchange else 0
    whole = pl.BlockSpec((tokens, width), lambda n: (0, 0), pipeline_mode=pl.Buffered(1))
    rows = pl.BlockSpec((tile, width), lambda n: ((n + turn) % steps, 0))
    quarter = pl.BlockSpec((2, tile, width), lambda n: (0, 0, 0), pipeline_mode=pl.Buffered(1))
    columns = pl.BlockSpec(
        (None, width, tile),
        lambda n: ((n + turn) % steps // 2, 0, (n + turn) % 2),
    )
    grads = jax.ShapeDtypeStruct((units, width), f32)
    sem = pltpu.SemaphoreType.DMA
    return pl.pallas_call(
        partial(feed_kernel, exchange, len(after)),
        grid=(steps,),
        in_specs=[whole, whole, columns, rows]
        + [rows, rows] * exchange
        + [pl.BlockSpec(memory_space=pl.ANY)] * len(after),
        out_specs=(
            [quarter, quarter, pl.BlockSpec(memory_space=pl.ANY)] if exchange else [rows, rows]
        )
        + [whole, whole],
        out_shape=(
            [
                jax.ShapeDtypeStruct((2, tile, width), f32),
                jax.ShapeDtypeStruct((2, tile, width), low),
                jax.ShapeDtypeStruct((2, 2, tile, width), f32),
            ]
            if exchange
            else [grads, grads]
        )
        + [
            jax.ShapeDtypeStruct((tokens, width), f32),
            jax.ShapeDtypeStruct((tokens, width), branch_type),
        ],
        scratch_shapes=[
            pltpu.VMEM((tokens, tile), low),
            pltpu.VMEM((tokens, tile), low),
            pltpu.VMEM((tokens, width), f32),
            pltpu.VMEM((tokens, width), f32),
        ]
        + [
            pltpu.VMEM((2, tile, width), f32),
            pltpu.VMEM((2, tile, width), f32),
            sem((2, 2)),
            sem((2, 2)),
            sem((2,)),
        ]
        * exchange,
        compiler_params=pltpu.CompilerParams(
            vmem_limit_bytes=60 * 2**20,
            **(dict(collective_id=4, has_side_effects=True) if exchange else {}),
        ),
        cost_estimate=pl.CostEstimate(flops=2**20, bytes_accessed=2**20, transcendentals=0),
    )(hidden, back, expand, shrink, *before, *after)


def opening_kernel(
    expand_hbm,
    shrink_hbm,
    project_hbm,
    mixing_hbm,
    inputs_hbm,
    norm_ref,
    back_ref,
    expand_out,
    shrink_out,
    later_out,
    norm_out,
    hidden_ref,
    other_back,
    expand_ref,
    shrink_ref,
    project_ref,
    mixing_ref,
    inputs_ref,
    expand_low,
    shrink_low,
    norm_low,
    norm_all,
    load_sem,
    own_sem,
    norm_send,
    norm_recv,
    line_send,
    line_recv,
    far_send,
    far_recv,
    near_send,
    near_recv,
    row_sem,
):
    place, deep = lax.axis_index("dp"), 4
    outer = lax.axis_index("outer")
    far, near = outer // 2, outer % 2
    far_id = {"outer": (outer + 2) % 4}
    near_id = {"outer": outer + 1 - 2 * near}
    rows = expand_ref.shape[0]
    half = expand_ref.shape[1] // 2
    part = half // 2

    loads = [
        pltpu.make_async_copy(source, target, load_sem.at[n])
        for n, (source, target) in enumerate(
            (
                (expand_hbm, expand_ref),
                (shrink_hbm, shrink_ref),
                (project_hbm, project_ref),
                (mixing_hbm, mixing_ref),
                (inputs_hbm, inputs_ref),
            )
        )
    ]
    loads[0].start()
    loads[1].start()
    barrier = pltpu.get_barrier_semaphore()
    for step in range(1, deep):
        pl.semaphore_signal(
            barrier, inc=1, device_id={"dp": (place + step) % deep}, device_id_type=MESH
        )
    pl.semaphore_signal(barrier, inc=1, device_id=far_id, device_id_type=MESH)
    pl.semaphore_signal(barrier, inc=1, device_id=near_id, device_id_type=MESH)
    row_id = {"mp": 1 - lax.axis_index("mp")}
    pl.semaphore_signal(barrier, inc=1, device_id=row_id, device_id_type=MESH)

    for load in loads[2:]:
        load.start()
    norm_low[...] = jnp.zeros_like(norm_low)
    norm_low[0:2] = norm_ref[...].astype(jnp.bfloat16).astype(jnp.float32)
    pl.semaphore_wait(barrier, deep + 2)

    def piece(w, which, at, side):
        across = pl.ds(pl.multiple_of(at * rows, rows), rows)
        along = pl.ds(pl.multiple_of(side * part, part), part)
        if w == 0:
            return expand_out.at[which, across, along]
        return shrink_out.at[which, along, across]

    def mine(w):
        along = pl.ds(pl.multiple_of(near * half + far * part, part), part)
        return expand_low.at[:, along] if w == 0 else shrink_low.at[along, :]

    def remote(source, target, send, recv, device):
        return pltpu.make_async_remote_copy(
            src_ref=source,
            dst_ref=target,
            send_sem=send,
            recv_sem=recv,
            device_id=device,
            device_id_type=MESH,
        )

    def line(w, way, step, source, at):
        to = place + 1 if way == 0 else place - 1
        return remote(
            source,
            piece(w, 0, at, far),
            line_send.at[w, way, step],
            line_recv.at[w, way, step],
            {"dp": to},
        )

    def can_send(way):
        return place < deep - 1 if way == 0 else place > 0

    def start_own(w):
        for way in range(2):

            @pl.when(can_send(way))
            def _(way=way):
                line(w, way, 0, mine(w), place).start()

    def own_copies(w):
        out = []
        for which in range(2):
            side = near + which - 2 * near * which
            along = pl.ds(pl.multiple_of(side * half, half), half)
            across = pl.ds(pl.multiple_of(place * rows, rows), rows)
            if w == 0:
                pair = (expand_low.at[:, along], expand_out.at[which, across, :])
            else:
                pair = (shrink_low.at[along, :], shrink_out.at[which, :, across])
            out.append(pltpu.make_async_copy(*pair, own_sem.at[w, which]))
        return out

    row_copy = remote(back_ref, other_back, row_sem.at[0], row_sem.at[1], row_id)
    row_copy.start()
    loads[0].wait()
    expand_low[...] = expand_ref[...].astype(jnp.bfloat16)
    start_own(0)
    norm_copies = []
    for step in range(1, deep):
        copy = remote(
            norm_low,
            norm_all.at[step],
            norm_send.at[step],
            norm_recv.at[step],
            {"dp": (place + step) % deep},
        )
        copy.start()
        norm_copies.append(copy)
    loads[1].wait()
    shrink_low[...] = shrink_ref[...].astype(jnp.bfloat16)
    start_own(1)
    for w in range(2):
        for copy in own_copies(w):
            copy.start()
    for load in loads[2:]:
        load.wait()
    first = 0
    for source in (project_ref, mixing_ref):
        units = source.shape[0] // 2
        later_out[first : first + units] = source[
            pl.ds(pl.multiple_of(near * units, units), units), :
        ].astype(jnp.bfloat16)
        first += units
    norm_all[0] = norm_low[...]
    for copy in norm_copies:
        copy.wait()
    for at in range(deep):
        norm_out[:, at * rows : (at + 1) * rows] = norm_all[(place - at + deep) % deep]
    gain, bias = norm_out[0:1], norm_out[1:2]
    tokens = inputs_ref.shape[0]
    height = 128

    def normalize(i, _):
        at = pl.ds(pl.multiple_of(i * height, height), height)
        x = inputs_ref[at, :].astype(jnp.float32)
        mean = jnp.mean(x, axis=1, keepdims=True)
        centred = x - mean
        spread = jnp.mean(centred * centred, axis=1, keepdims=True)
        normed = centred * lax.rsqrt(spread + norm_epsilon)
        hidden_ref[at, :] = (normed * gain + bias).astype(jnp.bfloat16)
        return 0

    lax.fori_loop(0, tokens // height, normalize, 0)

    def arrives(way, step):
        return place >= step if way == 0 else place + step < deep

    def at_of(way, step):
        return place - step if way == 0 else place + step

    def to_far(w, way, step):
        at = at_of(way, step)
        return remote(
            piece(w, 0, at, far),
            piece(w, 0, at, far),
            far_send.at[w, way, step - 1],
            far_recv.at[w, way, step - 1],
            far_id,
        )

    def from_far(w, way, step):
        at = at_of(way, step)
        return remote(
            piece(w, 0, at, 1 - far),
            piece(w, 0, at, 1 - far),
            far_send.at[w, way, step - 1],
            far_recv.at[w, way, step - 1],
            far_id,
        )

    def to_near(w, way, step, other):
        at = at_of(way, step)
        side = 1 - far if other else far
        return remote(
            piece(w, 0, at, side),
            piece(w, 1, at, side),
            near_send.at[w, way, step - 1, other],
            near_recv.at[w, way, step - 1, other],
            near_id,
        )

    order = [(w, step) for w in range(2) for step in range(1, deep)]

    def first_half(w, step):
        for way in range(2):

            @pl.when(arrives(way, step))
            def _(way=way):
                at = at_of(way, step)
                line(w, way, step - 1, mine(w), at).wait_recv()
                if step < deep - 1:

                    @pl.when(can_send(way))
                    def _():
                        line(w, way, step, piece(w, 0, at, far), at).start()

                to_far(w, way, step).start()
                to_near(w, way, step, 0).start()

    def second_half(w, step):
        for way in range(2):

            @pl.when(arrives(way, step))
            def _(way=way):
                from_far(w, way, step).wait_recv()
                to_near(w, way, step, 1).start()

    for n, (w, step) in enumerate(order):
        first_half(w, step)
        if n:
            second_half(*order[n - 1])
    second_half(*order[-1])
    row_copy.wait()
    for w in range(2):
        for copy in own_copies(w):
            copy.wait()
        for way in range(2):

            @pl.when(can_send(way))
            def _(way=way):
                line(w, way, 0, mine(w), place).wait_send()

            for step in range(1, deep):

                @pl.when(arrives(way, step))
                def _(way=way, step=step):
                    at = at_of(way, step)
                    if step < deep - 1:

                        @pl.when(can_send(way))
                        def _():
                            line(w, way, step, piece(w, 0, at, far), at).wait_send()

                    to_far(w, way, step).wait_send()
                    for other in range(2):
                        to_near(w, way, step, other).wait_send()
                        to_near(w, way, step, other).wait_recv()


def project_kernel(hidden_ref, back_ref, own_ref, sibling_ref, projected_ref, mixed_back_ref):
    nt = (((1,), (1,)), ((), ()))
    cut = own_ref.shape[0] * 3 // 4
    few = own_ref.shape[0] - cut
    for n, weights in enumerate((own_ref, sibling_ref)):
        projected_ref[n * cut : (n + 1) * cut] = lax.dot_general(
            weights[:cut], hidden_ref[...], nt, preferred_element_type=jnp.float32
        )
        mixed_back_ref[n * few : (n + 1) * few] = lax.dot_general(
            weights[cut:], back_ref[...], nt, preferred_element_type=jnp.float32
        ).astype(jnp.bfloat16)


def project_all(hidden, back, own, sibling):
    tokens, width = hidden.shape
    cut = own.shape[0] * 3 // 4
    rows = pl.BlockSpec((256, width), lambda n: (n, 0))
    whole = pl.BlockSpec(own.shape, lambda n: (0, 0), pipeline_mode=pl.Buffered(1))
    columns = lambda height: pl.BlockSpec((height, 256), lambda n: (0, n))
    return pl.pallas_call(
        project_kernel,
        grid=(tokens // 256,),
        in_specs=[rows, rows, whole, whole],
        out_specs=[columns(2 * cut), columns(2 * (own.shape[0] - cut))],
        out_shape=[
            jax.ShapeDtypeStruct((2 * cut, tokens), jnp.float32),
            jax.ShapeDtypeStruct((2 * (own.shape[0] - cut), tokens), jnp.bfloat16),
        ],
        compiler_params=pltpu.CompilerParams(vmem_limit_bytes=60 * 2**20),
        cost_estimate=pl.CostEstimate(flops=2**20, bytes_accessed=2**20, transcendentals=0),
    )(hidden, back, own, sibling)


def opening(expand, shrink, project, mixing, norm, inputs, back):
    deep = 4
    here = lambda: pl.BlockSpec(memory_space=pltpu.VMEM)
    rows, units = expand.shape
    later = project.shape[0] + mixing.shape[0]
    low = jnp.bfloat16
    sem = pltpu.SemaphoreType.DMA
    return pl.pallas_call(
        opening_kernel,
        in_specs=[pl.BlockSpec(memory_space=pl.ANY)] * 5
        + [here(), pl.BlockSpec(memory_space=pl.ANY)],
        out_specs=[pl.BlockSpec(memory_space=pl.ANY)] * 2
        + [here() for _ in range(3)]
        + [pl.BlockSpec(memory_space=pl.ANY)],
        out_shape=[
            jax.ShapeDtypeStruct((2, rows * deep, units // 2), low),
            jax.ShapeDtypeStruct((2, units // 2, rows * deep), low),
            jax.ShapeDtypeStruct((later // 2, project.shape[1]), low),
            jax.ShapeDtypeStruct((8, rows * deep), jnp.float32),
            jax.ShapeDtypeStruct(inputs.shape, low),
            jax.ShapeDtypeStruct(back.shape, low),
        ],
        scratch_shapes=[
            pltpu.VMEM(v.shape, v.dtype) for v in (expand, shrink, project, mixing, inputs)
        ]
        + [
            pltpu.VMEM(expand.shape, low),
            pltpu.VMEM(shrink.shape, low),
            pltpu.VMEM((8, norm.shape[1]), jnp.float32),
            pltpu.VMEM((deep, 8, norm.shape[1]), jnp.float32),
            sem((5,)),
            sem((2, 2)),
            sem((deep,)),
            sem((deep,)),
            sem((2, 2, deep)),
            sem((2, 2, deep)),
            sem((2, 2, deep)),
            sem((2, 2, deep)),
            sem((2, 2, deep, 2)),
            sem((2, 2, deep, 2)),
            sem((2,)),
        ],
        compiler_params=pltpu.CompilerParams(
            collective_id=1, has_side_effects=True, vmem_limit_bytes=60 * 2**20
        ),
        cost_estimate=pl.CostEstimate(flops=0, bytes_accessed=2**20, transcendentals=0),
    )(expand, shrink, project, mixing, inputs, norm, back)


def closing_kernel(
    later,
    own_weights,
    sibling_weights,
    *refs,
):
    sources = (own_weights, *refs[:9])
    part_own, part_other, feed_keep, feed_come, gain_ref = refs[9:14]
    input_grad, small_sum, mixed_come = refs[14 + later : 17 + later]
    full_refs = refs[17 + later : 21 + later]
    refs = refs[21 + later :]
    held = refs[:10]
    (
        part_in,
        total_ref,
        sent_ref,
        come_ref,
        project_land,
        project_own,
        mixing_land,
        mixing_own,
        project_far,
        project_come,
        mixing_far,
        mixing_come,
        project_line,
        project_lands,
        mixing_line,
        mixing_lands,
        feed_in,
        feed_line,
        feed_lands,
        feed_share,
        expand_share,
        project_share,
        mixing_share,
        small_ref,
        plane_lands,
        deep_lands,
        held_sem,
        half_sem,
        part_sem,
        out_sem,
        feed_sem,
        feed_send,
        feed_recv,
        spread_sem,
        spread_far_send,
        spread_far_recv,
        spread_near_send,
        spread_near_recv,
        plane_send,
        plane_recv,
        deep_send,
        deep_recv,
        row_send,
        row_recv,
        mixed_sem,
        near_send,
        near_recv,
        far_send,
        far_recv,
        line_send,
        line_recv,
    ) = refs[10:]
    (
        project,
        grads_other,
        grads_own,
        hidden_other,
        hidden_own,
        mixed_other,
        mixed_own,
        back_other,
        back_own,
        inputs,
    ) = held
    low, f32 = jnp.bfloat16, jnp.float32
    tn = (((0,), (0,)), ((), ()))
    place, deep, outers = lax.axis_index("dp"), 4, 4
    outer = lax.axis_index("outer")
    far, near = outer // 2, outer % 2
    row_id = {"mp": 1 - lax.axis_index("mp")}
    far_id = {"outer": (outer + 2) % 4}
    near_id = {"outer": outer + 1 - 2 * near}

    copies = [
        pltpu.make_async_copy(source, target, held_sem.at[n])
        for n, (source, target) in enumerate(zip(sources, held))
        if n
    ]
    copies.insert(0, None)
    cut = project.shape[0] // 2
    halves = [
        pltpu.make_async_copy(
            source.at[slice(0, cut)], project.at[slice(n * cut, (n + 1) * cut)], half_sem.at[n]
        )
        for n, source in enumerate((own_weights, sibling_weights))
    ]
    for copy in (*halves, copies[1]):
        copy.start()
    barrier = pltpu.get_barrier_semaphore()
    plane = 2 * outers
    me = lax.axis_index("mp") * outers + outer

    def plane_id(step):
        other = (me + step) % plane
        return {"mp": other // outers, "outer": other % outers}

    for step in range(1, plane):
        pl.semaphore_signal(barrier, inc=1, device_id=plane_id(step), device_id_type=MESH)
    for step in range(1, deep):
        pl.semaphore_signal(
            barrier, inc=1, device_id={"dp": (place + step) % deep}, device_id_type=MESH
        )
    height = 256
    tokens, width = hidden_own.shape
    blocks = tokens // height
    at = [slice(n * height, (n + 1) * height) for n in range(blocks)]

    def remote(source, target, send, recv, device):
        return pltpu.make_async_remote_copy(
            src_ref=source,
            dst_ref=target,
            send_sem=send,
            recv_sem=recv,
            device_id=device,
            device_id_type=MESH,
        )

    loads = [
        pltpu.make_async_copy(source.at[at[n]], part_in.at[(k * blocks + n) % 2], part_sem.at[(k * blocks + n) % 2])
        for k, source in enumerate((part_other, part_own))
        for n in range(blocks)
    ]
    loads[0].start()
    loads[1].start()
    for copy in copies[2:]:
        copy.start()
    quarter = feed_keep.shape[1]
    feed_copies = [
        (
            pltpu.make_async_copy(
                feed_keep.at[k],
                total_ref.at[slice(k * quarter, (k + 1) * quarter)],
                feed_sem.at[k],
            ),
            pltpu.make_async_copy(feed_come.at[k], feed_in.at[k], feed_sem.at[2 + k]),
        )
        for k in range(2)
    ]
    for pair in feed_copies:
        for copy in pair:
            copy.start()

    for copy in (*halves, copies[1]):
        copy.wait()
    pl.semaphore_wait(barrier, plane + deep - 2)
    row_copies = []
    for n in range(blocks):
        made = lax.dot_general(grads_other[:, at[n]], project[...], tn, preferred_element_type=f32)
        loads[n].wait()
        sent_ref[at[n], :] = (part_in[n % 2] + made).astype(low)
        loads[n + 2].start()
        copy = remote(
            sent_ref.at[at[n]], come_ref.at[at[n]], row_send.at[n], row_recv.at[n], row_id
        )
        copy.start()
        row_copies.append(copy)

    copies[5].wait()
    mixed_copy = remote(mixed_other, mixed_come, mixed_sem.at[0], mixed_sem.at[1], row_id)
    mixed_copy.start()

    piece = width // deep

    def columns(place):
        return pl.ds(pl.multiple_of(place * piece, piece), piece)

    line_copies = []
    for k in range(2):
        for copy in feed_copies[k]:
            copy.wait()
        rows = slice(k * quarter, (k + 1) * quarter)
        for step in range(1, deep):
            target = (place + step) % deep
            feed_line[k, step - 1] = (
                total_ref[rows, columns(target)] + feed_in[k, :, columns(target)].astype(f32)
            ).astype(low)
            line_copies.append(
                remote(
                    feed_line.at[k, step - 1],
                    feed_lands.at[k, step - 1],
                    feed_send.at[k, step - 1],
                    feed_recv.at[k, step - 1],
                    {"dp": target},
                )
            )
            line_copies[-1].start()
        feed_share[k] = total_ref[rows, columns(place)] + feed_in[k, :, columns(place)].astype(f32)

    for n in (2, 3, 4, 6, 7, 8):
        copies[n].wait()
    half = project_own.shape[0]
    few = mixing_own.shape[0]
    near_copies = []
    for n in range(half // height):
        rows = slice(half + n * height, half + (n + 1) * height)
        total_ref[at[n], :] = jnp.dot(
            grads_own[rows, :], hidden_own[...], preferred_element_type=f32
        ) + jnp.dot(grads_other[rows, :], hidden_other[...], preferred_element_type=f32)
        near_copies.append(
            remote(
                total_ref.at[at[n]],
                project_land.at[at[n]],
                near_send.at[n],
                near_recv.at[n],
                near_id,
            )
        )
        near_copies[-1].start()
    total_ref[half : half + few, :] = jnp.dot(
        mixed_own[few:, :], back_own[...], preferred_element_type=f32
    ) + jnp.dot(mixed_other[few:, :], back_other[...], preferred_element_type=f32)
    near_copies.append(
        remote(
            total_ref.at[slice(half, half + few)],
            mixing_land,
            near_send.at[3],
            near_recv.at[3],
            near_id,
        )
    )
    near_copies[-1].start()
    for n in range(half // height):
        made = jnp.dot(
            grads_own[at[n], :], hidden_own[...], preferred_element_type=f32
        ) + jnp.dot(grads_other[at[n], :], hidden_other[...], preferred_element_type=f32)
        near_copies[n].wait()
        project_own[at[n], :] = made + project_land[at[n], :]

    def to_far(own, send, come, n):
        size = send.shape[0]
        send[...] = own[pl.ds(pl.multiple_of((1 - far) * size, size), size), :].astype(low)
        copy = remote(send, come, far_send.at[n], far_recv.at[n], far_id)
        copy.start()
        return copy

    far_copies = [to_far(project_own, project_far, project_come, 0)]
    made = jnp.dot(mixed_own[:few, :], back_own[...], preferred_element_type=f32) + jnp.dot(
        mixed_other[:few, :], back_other[...], preferred_element_type=f32
    )
    near_copies[3].wait()
    mixing_own[...] = made + mixing_land[...]
    far_copies.append(to_far(mixing_own, mixing_far, mixing_come, 1))

    for n in range(blocks):
        made = lax.dot_general(grads_own[:, at[n]], project[...], tn, preferred_element_type=f32)
        loads[blocks + n].wait()
        total_ref[at[n], :] = part_in[(blocks + n) % 2] + made
        if n + 2 < blocks:
            loads[blocks + n + 2].start()

    for k, (own, come, line, lands) in enumerate(
        (
            (project_own, project_come, project_line, project_lands),
            (mixing_own, mixing_come, mixing_line, mixing_lands),
        )
    ):
        size = come.shape[0]
        keep = pl.ds(pl.multiple_of(far * size, size), size)
        far_copies[k].wait()
        own[keep, :] = own[keep, :] + come[...].astype(f32)
        for step in range(1, deep):
            target = (place + step) % deep
            line[step - 1] = own[keep, columns(target)].astype(low)
            copy = remote(
                line.at[step - 1],
                lands.at[step - 1],
                line_send.at[k, step - 1],
                line_recv.at[k, step - 1],
                {"dp": target},
            )
            copy.start()
            line_copies.append(copy)

    shares = (feed_share.at[0], expand_share, project_share, mixing_share)

    def place_in(k, near, far):
        if k == 1:
            return full_refs[k].at[:, pl.ds(pl.multiple_of((2 * near + far) * quarter, quarter), quarter)]
        size = shares[k].shape[0]
        return full_refs[k].at[pl.ds(pl.multiple_of((2 * near + far) * size, size), size)]

    def spread(k):
        if k < 2:
            result, lands = feed_share[k], feed_lands.at[k]
        else:
            own, lands = ((project_own, project_lands), (mixing_own, mixing_lands))[k - 2]
            size = shares[k].shape[0]
            result = own[pl.ds(pl.multiple_of(far * size, size), size), columns(place)]
        for copy in line_copies[3 * k : 3 * k + 3]:
            copy.wait()
        for step in range(1, deep):
            result = result + lands[step - 1].astype(f32)
        shares[k][...] = result.T if k == 1 else result
        here = place_in(k, near, far)
        copies = [
            pltpu.make_async_copy(shares[k], here, spread_sem.at[k]),
            remote(shares[k], here, spread_far_send.at[k], spread_far_recv.at[k], far_id),
            remote(shares[k], here, spread_near_send.at[k, 0], spread_near_recv.at[k, 0], near_id),
        ]
        for copy in copies:
            copy.start()
        return copies, jnp.sum(result * result)

    def pass_on(k, copies):
        copies[1].wait()
        there = place_in(k, near, 1 - far)
        copy = remote(
            there, there, spread_near_send.at[k, 1], spread_near_recv.at[k, 1], near_id
        )
        copy.start()
        return copy

    copies[9].wait()
    gain = gain_ref[0:1]
    gain_sum = jnp.zeros((1, width), f32)
    bias_sum = jnp.zeros((1, width), f32)
    out_copies, spreads, passed = [], [], []
    square = jnp.float32(0.0)
    for n in range(blocks):
        if n == blocks - 2:
            for k in range(2):
                copies, more = spread(k)
                spreads.append(copies)
                square = square + more
        if n == blocks - 1:
            for k in range(2, 4):
                copies, more = spread(k)
                spreads.append(copies)
                square = square + more
        row_copies[n].wait()
        if n >= 2:
            out_copies[n - 2].wait()

        def some(i, carry):
            gain_sum, bias_sum = carry
            small = 64
            rows = pl.ds(pl.multiple_of(n * height + i * small, small), small)
            x = inputs[rows, :].astype(f32)
            mean = jnp.mean(x, axis=1, keepdims=True)
            centred = x - mean
            spread = jnp.mean(centred * centred, axis=1, keepdims=True)
            inverse = lax.rsqrt(spread + norm_epsilon)
            normed = centred * inverse
            grad = total_ref[rows, :] + come_ref[rows, :].astype(f32)
            scaled = grad * gain
            middle = jnp.mean(scaled, axis=1, keepdims=True)
            along = jnp.mean(scaled * normed, axis=1, keepdims=True)
            result = inverse * (scaled - middle - normed * along)
            part_in[n % 2, pl.ds(pl.multiple_of(i * small, small), small), :] = (
                back_own[rows, :].astype(f32) + result
            )
            gain_sum = gain_sum + jnp.sum(grad * normed, axis=0, keepdims=True)
            bias_sum = bias_sum + jnp.sum(grad, axis=0, keepdims=True)
            return gain_sum, bias_sum

        gain_sum, bias_sum = lax.fori_loop(0, height // 64, some, (gain_sum, bias_sum))
        out_copies.append(
            pltpu.make_async_copy(part_in.at[n % 2], input_grad.at[at[n]], out_sem.at[n % 2])
        )
        out_copies[-1].start()
    for k in range(4):
        passed.append(pass_on(k, spreads[k]))

    small_ref[...] = jnp.full(small_ref.shape, square)
    small_ref[0:1] = gain_sum
    small_ref[1:2] = bias_sum

    def everywhere(lands, send, recv, size, index, device):
        copies = []
        for step in range(1, size):
            copy = remote(small_ref, lands.at[step], send.at[step], recv.at[step], device(step))
            copy.start()
            copies.append(copy)
        lands[0] = small_ref[...]
        for copy in copies:
            copy.wait()
        total = lands[index]
        for at in range(1, size):
            total = total + lands[(index + size - at) % size]
        small_ref[...] = total

    everywhere(plane_lands, plane_send, plane_recv, plane, me, plane_id)
    everywhere(
        deep_lands, deep_send, deep_recv, deep, place, lambda step: {"dp": (place + step) % deep}
    )
    small_sum[...] = small_ref[...]
    for k in range(4):
        spreads[k][0].wait()
        spreads[k][2].wait()
        passed[k].wait()
    mixed_copy.wait()
    for copy in out_copies[-2:]:
        copy.wait()


def closing(weights, grads, hiddens, mixed, backs, inputs, parts, feeds, gain, after):
    deep = 4
    low, f32 = jnp.bfloat16, jnp.float32
    tokens, width = inputs.shape
    half, few = grads[0].shape[0] // 2, mixed[0].shape[0] // 2
    piece = width // deep
    quarter = feeds[0].shape[1]
    anywhere = pl.BlockSpec(memory_space=pl.ANY)
    here = lambda: pl.BlockSpec(memory_space=pltpu.VMEM)
    held = (
        jax.ShapeDtypeStruct(grads[0].shape[:1] + (width,), low),
        grads[1],
        grads[0],
        hiddens[1],
        hiddens[0],
        mixed[1],
        mixed[0],
        backs[1],
        backs[0],
        inputs,
    )
    sem = pltpu.SemaphoreType.DMA
    space = pltpu.VMEM
    return pl.pallas_call(
        partial(closing_kernel, len(after)),
        in_specs=[anywhere] * 15 + [here()] + [anywhere] * len(after),
        out_specs=[anywhere, here()] + [anywhere] * 5,
        out_shape=[
            jax.ShapeDtypeStruct((tokens, width), f32),
            jax.ShapeDtypeStruct((8, width), f32),
            jax.ShapeDtypeStruct(mixed[1].shape, low),
        ]
        + [
            jax.ShapeDtypeStruct(shape, f32)
            for shape in (
                (4 * quarter, piece),
                (piece, 4 * quarter),
                (2 * half, piece),
                (2 * few, piece),
            )
        ],
        scratch_shapes=[space(v.shape, v.dtype) for v in held]
        + [
            space((2, 256, width), f32),
            space((tokens, width), f32),
            space((tokens, width), low),
            space((tokens, width), low),
            space((half, width), f32),
            space((half, width), f32),
            space((few, width), f32),
            space((few, width), f32),
            space((half // 2, width), low),
            space((half // 2, width), low),
            space((few // 2, width), low),
            space((few // 2, width), low),
            space((deep - 1, half // 2, piece), low),
            space((deep - 1, half // 2, piece), low),
            space((deep - 1, few // 2, piece), low),
            space((deep - 1, few // 2, piece), low),
            space((2, quarter, width), low),
            space((2, deep - 1, quarter, piece), low),
            space((2, deep - 1, quarter, piece), low),
            space((2, quarter, piece), f32),
            space((piece, quarter), f32),
            space((half // 2, piece), f32),
            space((few // 2, piece), f32),
            space((8, width), f32),
            space((8, 8, width), f32),
            space((deep, 8, width), f32),
            sem((len(held),)),
            sem((2,)),
            sem((2,)),
            sem((2,)),
            sem((4,)),
            sem((2, deep - 1)),
            sem((2, deep - 1)),
            sem((4,)),
            sem((4,)),
            sem((4,)),
            sem((4, 2)),
            sem((4, 2)),
            sem((8,)),
            sem((8,)),
            sem((deep,)),
            sem((deep,)),
            sem((tokens // 256,)),
            sem((tokens // 256,)),
            sem((2,)),
            sem((4,)),
            sem((4,)),
            sem((2,)),
            sem((2,)),
            sem((2, deep)),
            sem((2, deep)),
        ],
        compiler_params=pltpu.CompilerParams(
            collective_id=3, has_side_effects=True, vmem_limit_bytes=62 * 2**20
        ),
        cost_estimate=pl.CostEstimate(flops=2**20, bytes_accessed=2**20, transcendentals=0),
    )(*weights, *held[1:], *parts, *feeds, gain, *after)


def local(
    inputs,
    cotangent,
    lengths,
    project_master,
    project_first,
    project_second,
    mixing_master,
    mixing_first,
    mixing_second,
    expand_master,
    expand_first,
    expand_second,
    shrink_master,
    shrink_first,
    shrink_second,
    norm_master,
    norm_first,
    norm_second,
):
    split, deep = lax.axis_size("mp"), lax.axis_size("dp")
    heads_here = project_master.shape[1]
    width = inputs.shape[1]
    paired = (
        split == 2
        and lax.axis_size("outer") == 4
        and heads_here % 4 == 0
        and width % BQ == 0
    )
    position = lax.axis_index("mp")
    count = width * split
    project_flat = project_master.transpose(1, 2, 0).reshape(heads_here * 3 * HD, -1)
    mixing_flat = mixing_master.reshape(heads_here * HD, mixing_master.shape[2])
    masters = (project_flat, mixing_flat, expand_master, shrink_master)
    depths = (1, 1, 0, 1)
    rows_local = inputs[0].astype(jnp.float32)
    begins, places = layout(lengths[0], count)
    cosine, sine = turns(places)
    if paired:
        expand, shrink, later, norm_weight, hidden_local, other_back = opening(
            expand_master,
            shrink_master,
            project_flat,
            mixing_flat,
            norm_master,
            inputs[0],
            cotangent[0],
        )
        backs = [cotangent[0], other_back]
        shrink = shrink.reshape(-1, shrink.shape[2])
        later = lax.all_gather(later, "dp", axis=1, tiled=True)
        hiddens = [hidden_local, swap(hidden_local, "mp", 1)]
    else:
        norm_weight = lax.all_gather(norm_master.astype(jnp.bfloat16), "dp", axis=1, tiled=True)
        gain = norm_weight[0].astype(jnp.float32)
        bias = norm_weight[1].astype(jnp.float32)
        shaped, norm_pull = jax.vjp(layer_norm, rows_local, gain, bias)
        hidden_local = shaped.astype(jnp.bfloat16)
        project, mixing, expand, shrink = (
            lax.all_gather(master.astype(jnp.bfloat16), "dp", axis=depth, tiled=True)
            for master, depth in zip(masters, depths)
        )
        backs = [lax.all_gather(cotangent[0], "mp", axis=0, tiled=True)]
        hiddens = [lax.all_gather(hidden_local, "mp", axis=0, tiled=True)]

    def over_tokens(pattern, lefts, rights):
        return sum(product(pattern, left, right) for left, right in zip(lefts, rights))

    back_local = cotangent[0].astype(jnp.float32)
    if paired:
        *grads, hidden_own, branch_own = feed(
            hiddens[0], backs[0], expand, shrink, (), jnp.float32
        )
        later = follow(later, branch_own)
        later = [later, swap(later, "outer", 1)]
        cut = later[0].shape[0] * 3 // 4
        mixing = jnp.concatenate([v[cut:] for v in later])
        own_columns = project_all(hiddens[0], backs[0], *later)
        feed_keep, feed_away, _, hidden_other, branch_other = feed(
            hiddens[1], backs[1], expand, follow(shrink, *own_columns), grads, jnp.bfloat16
        )
        feed_come = swap(feed_away, "outer", 2)
        branch_come = swap(branch_other, "mp", 1)
        mixing_other = swap(mixing, "mp", 1)
        other_columns = project_all(hiddens[1], backs[1], *later)
        projected, mixed_backs = zip(own_columns, other_columns)
        mixed, projected_grads = attend(
            projected,
            mixed_backs,
            begins,
            cosine,
            sine,
            position,
            (feed_away, branch_other),
        )
        input_grad, small_sum, mixed_come, shrink_sum, expand_sum, project_sum, mixing_sum = closing(
            later,
            projected_grads,
            hiddens,
            mixed,
            backs,
            inputs[0],
            (hidden_own, hidden_other),
            (feed_keep, feed_come),
            norm_weight,
            (branch_come,),
        )
        mixed_own = follow(mixed[0], small_sum)
        branch = (
            branch_own
            + branch_come.astype(jnp.float32)
            + product("ft,fd->td", mixed_own, mixing)
            + product("ft,fd->td", mixed_come, mixing_other)
        )
    else:
        lifteds = [product("td,df->tf", hidden, expand) for hidden in hiddens]
        activated = [gelu(lifted) for lifted in lifteds]
        active_grads = [product("td,fd->tf", back, shrink) for back in backs]
        lifted_grads = [gelu_both(a, b) for a, b in zip(lifteds, active_grads)]
        hidden_parts = [product("tf,df->td", v, expand) for v in lifted_grads]
        branch_parts = [product("tf,fd->td", v, shrink) for v in activated]
        projected = [product("td,ed->et", hidden, project) for hidden in hiddens]
        mixed_backs = [product("td,fd->ft", back, mixing).astype(jnp.bfloat16) for back in backs]
        mixed, projected_grads = attend(projected, mixed_backs, begins, cosine, sine, position)
        project_sum, mixing_sum, expand_sum, shrink_sum = (
            lax.psum(
                lax.psum_scatter(
                    over_tokens(pattern, lefts, rights),
                    "dp",
                    scatter_dimension=depth,
                    tiled=True,
                ),
                "outer",
            )
            for pattern, lefts, rights, depth in (
                ("et,td->ed", projected_grads, hiddens, 1),
                ("ft,td->fd", mixed, backs, 1),
                ("td,tf->df", hiddens, lifted_grads, 0),
                ("tf,td->fd", activated, backs, 1),
            )
        )
        hidden_grad, branch = (
            lax.psum_scatter(v, "mp", scatter_dimension=0, tiled=True)
            for v in (
                hidden_parts[0] + product("et,ed->td", projected_grads[0], project),
                branch_parts[0] + product("ft,fd->td", mixed[0], mixing),
            )
        )
        rows_grad, gain_grad, bias_grad = norm_pull(hidden_grad)
        input_grad = back_local + rows_grad
        norm_terms = jnp.stack([gain_grad, bias_grad])
    input_grad = input_grad[None]
    block_out = (rows_local + branch).astype(jnp.bfloat16)[None]
    sums = (project_sum, mixing_sum, expand_sum, shrink_sum)
    if not paired:
        own_square = sum(jnp.sum(v * v) for v in sums) / lax.axis_size("outer")
        small_sum = lax.psum(
            jnp.concatenate([norm_terms, jnp.full((1, D), own_square)]), ("mp", "dp", "outer")
        )
    norm_full = small_sum[:2]
    grad_norm = jnp.sqrt(small_sum[2, 0] + jnp.sum(norm_full * norm_full))
    factor = clip_level / jnp.maximum(grad_norm, clip_level)
    norm_gradient = lax.dynamic_slice_in_dim(
        norm_full, lax.axis_index("dp") * (D // deep), D // deep, 1
    )
    gradients = list(sums)
    gradients[0] = gradients[0].reshape(heads_here, 3 * HD, -1).transpose(2, 0, 1)
    gradients[1] = gradients[1].reshape(mixing_master.shape)
    states = (
        (project_master, project_first, project_second, D ** (-0.5)),
        (mixing_master, mixing_first, mixing_second, (D // 32) ** (-0.5)),
        (expand_master, expand_first, expand_second, D ** (-0.5)),
        (shrink_master, shrink_first, shrink_second, FF ** (-0.5)),
    )
    results = [block_out, input_grad]
    for (master, first, second, rate), gradient in zip(states, gradients):
        results += adam_update(master, first, second, factor * gradient, rate, decay_rate)
    results += adam_update(norm_master, norm_first, norm_second, factor * norm_gradient, 0.3, 0.0)
    return (*results, grad_norm)


def solution(mesh):
    in_specs = (
        P(("dp", "outer"), "mp", None),
        P(("dp", "outer"), "mp", None),
        P(("dp", "outer"), None),
        P("dp", "mp", None),
        P("dp", "mp", None),
        P("dp", "mp", None),
        P("mp", None, "dp"),
        P("mp", None, "dp"),
        P("mp", None, "dp"),
        P("dp", "mp"),
        P("dp", "mp"),
        P("dp", "mp"),
        P("mp", "dp"),
        P("mp", "dp"),
        P("mp", "dp"),
        P(None, "dp"),
        P(None, "dp"),
        P(None, "dp"),
    )
    out_specs = (
        P(("dp", "outer"), "mp", None),
        P(("dp", "outer"), "mp", None),
        P("dp", "mp", None),
        P("dp", "mp", None),
        P("dp", "mp", None),
        P("dp", "mp", None),
        P("mp", None, "dp"),
        P("mp", None, "dp"),
        P("mp", None, "dp"),
        P("mp", None, "dp"),
        P("dp", "mp"),
        P("dp", "mp"),
        P("dp", "mp"),
        P("dp", "mp"),
        P("mp", "dp"),
        P("mp", "dp"),
        P("mp", "dp"),
        P("mp", "dp"),
        P(None, "dp"),
        P(None, "dp"),
        P(None, "dp"),
        P(None, "dp"),
        P(),
    )
    return jax.shard_map(local, mesh=mesh, in_specs=in_specs, out_specs=out_specs, check_vma=False)
```

```python
from functools import partial
import math

import jax
import jax.numpy as jnp
from jax import lax
from jax.experimental import pallas as pl
from jax.experimental.pallas import tpu as pltpu
from jax.sharding import PartitionSpec as P

D = 1024
HD = 64
ROT = 32
FF = 4096
STEP = 10


norm_epsilon = 1e-05
beta_one = 0.9
beta_two = 0.95
adam_epsilon = 1e-08
decay_rate = 0.1
clip_level = 1.0
masked_value = -1e30


def layout(sizes_row, count):
    number = jnp.arange(sizes_row.shape[0], dtype=jnp.int32)
    ends = jnp.sum(jnp.where(number[None, :] <= number[:, None], sizes_row[None, :], 0), axis=1)
    tokens = jnp.arange(count, dtype=jnp.int32)
    passed = (ends[:, None] <= tokens[None, :]).astype(jnp.int32)
    begins = jnp.sum(passed * sizes_row[:, None], axis=0)
    return (begins, tokens - begins)


def turns(places):
    half_rot = ROT // 2
    counter = jnp.arange(half_rot, dtype=jnp.float32)
    frequency = jnp.exp(counter * (-2.0 * math.log(10000.0) / ROT))
    angles = places.astype(jnp.float32)[None, :] * frequency[:, None]
    return jnp.cos(angles), jnp.sin(angles)


BQ = 256
BK = 256


def attend_kernel(together, parts, later, *refs):
    facts = refs[0]
    projected_refs = refs[1 : 1 + parts]
    back_refs = refs[1 + parts : 1 + 2 * parts]
    start_ref, cos_ref, sin_ref = refs[1 + 2 * parts : 4 + 2 * parts]
    refs = refs[: 4 + 2 * parts] + refs[4 + 2 * parts + later :]
    mixed_refs = refs[4 + 2 * parts : 4 + 3 * parts]
    grad_refs = refs[4 + 3 * parts : 4 + 4 * parts]
    (
        query_ref,
        key_columns_ref,
        value_columns_ref,
        key_ref,
        value_ref,
        back_ref,
        query_grad_ref,
        key_grad_ref,
        value_grad_ref,
        shifted_ref,
        share_grad_ref,
        top_ref,
    ) = refs[4 + 4 * parts :]
    width = projected_refs[0].shape[1]
    count = width * parts
    blocks = count // BQ
    turn = facts[blocks]
    half = ROT // 2
    scale = HD ** (-0.5)

    def place_of(part):
        if parts == 1:
            return pl.ds(0, width)
        block = lax.rem(part * (blocks // parts) + blocks - turn, blocks)
        return pl.ds(pl.multiple_of(block * BQ, BQ), width)

    for part in range(parts):
        columns = slice(part * width, (part + 1) * width)
        cosine, sine = cos_ref[:, place_of(part)], sin_ref[:, place_of(part)]
        projected_ref = projected_refs[part]

        def turned(at):
            first = projected_ref[at : at + half]
            second = projected_ref[at + half : at + ROT]
            return jnp.concatenate(
                [
                    first * cosine - second * sine,
                    second * cosine + first * sine,
                    projected_ref[at + ROT : at + HD],
                ],
                axis=0,
            ).astype(jnp.bfloat16)

        for h in range(together):
            base = h * 3 * HD
            query_ref[h, :, columns] = (turned(base).astype(jnp.float32) * scale).astype(
                jnp.bfloat16
            )
            keys = turned(base + HD)
            values = projected_ref[base + 2 * HD : base + 3 * HD].astype(jnp.bfloat16)
            key_columns_ref[h, :, columns] = keys
            value_columns_ref[h, :, columns] = values
            key_ref[h, columns] = keys.T
            value_ref[h, columns] = values.T
            back_ref[h, :, columns] = back_refs[part][h * HD : (h + 1) * HD]
    key_grad_ref[...] = jnp.zeros_like(key_grad_ref)
    value_grad_ref[...] = jnp.zeros_like(value_grad_ref)
    key_at = lax.broadcasted_iota(jnp.int32, (BK, BQ), 0)
    query_at = lax.broadcasted_iota(jnp.int32, (1, BQ), 1)

    def stored(block):
        if parts == 1:
            return pl.ds(pl.multiple_of(block * BQ, BQ), BQ)
        return pl.ds(pl.multiple_of(lax.rem(block + turn, blocks) * BQ, BQ), BQ)

    def query_block(i, _):
        columns = stored(i)
        start = start_ref[:, pl.ds(pl.multiple_of(i * BQ, BQ), BQ)]
        own = query_at + i * BQ
        lowest = facts[i]
        queries = [query_ref[h, :, columns] for h in range(together)]
        backs = [back_ref[h, :, columns] for h in range(together)]
        query_rows = [queries[h].T for h in range(together)]
        back_rows = [backs[h].T for h in range(together)]

        def in_pairs(body, carry):
            twos = lax.div(i + 1 - lowest, 2)
            carry = lax.fori_loop(
                0, twos, lambda n, c: body((lowest + 2 * n, lowest + 2 * n + 1), c), carry
            )
            return lax.fori_loop(lowest + 2 * twos, i + 1, lambda n, c: body((n,), c), carry)

        def scores(group, carry):
            made = []
            for j in group:
                rows = stored(j)
                allowed = (key_at >= start - j * BK) & (key_at <= own - j * BK)
                for h in range(together):
                    raw = jnp.dot(
                        key_ref[h, rows, :], queries[h], preferred_element_type=jnp.float32
                    )
                    share_grad = jnp.dot(
                        value_ref[h, rows, :], backs[h], preferred_element_type=jnp.float32
                    )
                    masked = jnp.where(allowed, raw, masked_value)
                    here = jnp.max(masked, axis=0, keepdims=True)
                    shifted = jnp.exp(masked - here)
                    shifted_ref[h, j] = shifted
                    share_grad_ref[h, j] = share_grad
                    top_ref[h, j] = here
                    made.append(
                        (
                            here,
                            jnp.sum(shifted, axis=0, keepdims=True),
                            jnp.sum(shifted * share_grad, axis=0, keepdims=True),
                        )
                    )
            out = []
            for h in range(together):
                top, total, inner = carry[h]
                for here, here_total, here_inner in made[h::together]:
                    new = jnp.maximum(top, here)
                    old_by, here_by = jnp.exp(top - new), jnp.exp(here - new)
                    total = total * old_by + here_total * here_by
                    inner = inner * old_by + here_inner * here_by
                    top = new
                out.append((top, total, inner))
            return tuple(out)

        zero = jnp.zeros((1, BQ), jnp.float32)
        empty = (jnp.full((1, BQ), masked_value, jnp.float32), zero, zero)
        stats = in_pairs(scores, (empty,) * together)
        inverse = [1.0 / s[1] for s in stats]
        inners = [s[2] * r for s, r in zip(stats, inverse)]

        def sums(group, carry):
            out = list(carry)
            for j in group:
                rows = stored(j)
                for h in range(together):
                    mixed, query_grad = out[h]
                    by = jnp.exp(top_ref[h, j] - stats[h][0]) * inverse[h]
                    probs = shifted_ref[h, j] * by
                    shares = probs.astype(jnp.bfloat16)
                    score_grad = (probs * (share_grad_ref[h, j] - inners[h])).astype(jnp.bfloat16)
                    mixed = mixed + jnp.dot(
                        value_columns_ref[h, :, rows], shares, preferred_element_type=jnp.float32
                    )
                    query_grad = query_grad + jnp.dot(
                        key_columns_ref[h, :, rows], score_grad, preferred_element_type=jnp.float32
                    )
                    value_grad_ref[h, rows, :] += jnp.dot(
                        shares, back_rows[h], preferred_element_type=jnp.float32
                    )
                    key_grad_ref[h, rows, :] += jnp.dot(
                        score_grad, query_rows[h], preferred_element_type=jnp.float32
                    )
                    out[h] = (mixed, query_grad)
            return tuple(out)

        nothing = jnp.zeros((HD, BQ), jnp.float32)
        results = in_pairs(sums, ((nothing, nothing),) * together)
        for h in range(together):
            back_ref[h, :, columns] = results[h][0].astype(jnp.bfloat16)
            query_grad_ref[h, :, columns] = results[h][1] * scale
        return 0

    lax.fori_loop(0, blocks, query_block, 0)
    for part in range(parts):
        columns = slice(part * width, (part + 1) * width)
        cosine, sine = cos_ref[:, place_of(part)], sin_ref[:, place_of(part)]

        def turned_back(grad):
            first, second = grad[:half], grad[half:ROT]
            return jnp.concatenate(
                [
                    first * cosine + second * sine,
                    second * cosine - first * sine,
                    grad[ROT:],
                ],
                axis=0,
            ).astype(jnp.bfloat16)

        for h in range(together):
            base = h * 3 * HD
            mixed_refs[part][h * HD : (h + 1) * HD] = back_ref[h, :, columns]
            grad_refs[part][base : base + HD] = turned_back(query_grad_ref[h, :, columns])
            grad_refs[part][base + HD : base + 2 * HD] = turned_back(key_grad_ref[h, columns, :].T)
            grad_refs[part][base + 2 * HD : base + 3 * HD] = value_grad_ref[
                h, columns, :
            ].T.astype(jnp.bfloat16)


def attend(projected, back, begins, cosine, sine, offset, after=()):
    parts = len(projected)
    heads = back[0].shape[0] // HD
    width = back[0].shape[1]
    count = begins.shape[0]
    together = 2 if heads % 2 == 0 else 1
    blocks = count // BK
    half = ROT // 2
    turn = jnp.asarray(offset * ((blocks // parts) if parts > 1 else 0), jnp.int32)
    facts = jnp.concatenate([begins[::BQ] // BK, turn[None]])
    whole = lambda rows: pl.BlockSpec((rows, count), lambda g, *_: (0, 0))
    mine = lambda rows: pl.BlockSpec((rows, width), lambda g, *_: (g, 0))
    results = pl.pallas_call(
        partial(attend_kernel, together, parts, len(after)),
        grid_spec=pltpu.PrefetchScalarGridSpec(
            num_scalar_prefetch=1,
            grid=(heads // together,),
            in_specs=[mine(together * 3 * HD)] * parts
            + [mine(together * HD)] * parts
            + [whole(1), whole(half), whole(half)]
            + [pl.BlockSpec(memory_space=pl.ANY)] * len(after),
            out_specs=[mine(together * HD)] * parts + [mine(together * 3 * HD)] * parts,
            scratch_shapes=[
                pltpu.VMEM((together, HD, count), jnp.bfloat16),
                pltpu.VMEM((together, HD, count), jnp.bfloat16),
                pltpu.VMEM((together, HD, count), jnp.bfloat16),
                pltpu.VMEM((together, count, HD), jnp.bfloat16),
                pltpu.VMEM((together, count, HD), jnp.bfloat16),
                pltpu.VMEM((together, HD, count), jnp.bfloat16),
                pltpu.VMEM((together, HD, count), jnp.float32),
                pltpu.VMEM((together, count, HD), jnp.float32),
                pltpu.VMEM((together, count, HD), jnp.float32),
                pltpu.VMEM((together, blocks, BK, BQ), jnp.float32),
                pltpu.VMEM((together, blocks, BK, BQ), jnp.float32),
                pltpu.VMEM((together, blocks, 1, BQ), jnp.float32),
            ],
        ),
        out_shape=[jax.ShapeDtypeStruct((heads * HD, width), jnp.bfloat16)] * parts
        + [jax.ShapeDtypeStruct((heads * 3 * HD, width), jnp.bfloat16)] * parts,
        compiler_params=pltpu.CompilerParams(vmem_limit_bytes=48 * 2**20),
        cost_estimate=pl.CostEstimate(
            flops=2**20,
            bytes_accessed=2**20,
            transcendentals=0,
        ),
    )(facts, *projected, *back, begins[None, :], cosine, sine, *after)
    return results[:parts], results[parts:]


def layer_norm(rows_in, gain, bias):
    mean = jnp.mean(rows_in, axis=1, keepdims=True)
    centred = rows_in - mean
    spread = jnp.mean(centred * centred, axis=1, keepdims=True)
    normed = centred * lax.rsqrt(spread + norm_epsilon)
    return normed * gain + bias


def adam_update(master, first, second, gradient, rate, decay):
    first_new = beta_one * first + (1.0 - beta_one) * gradient
    second_new = beta_two * second + (1.0 - beta_two) * gradient * gradient
    first_hat = first_new / (1.0 - beta_one**STEP)
    second_hat = second_new / (1.0 - beta_two**STEP)
    master_new = master - rate * (
        first_hat / (jnp.sqrt(second_hat) + adam_epsilon) + decay * master
    )
    return (master_new, first_new, second_new, master_new.astype(jnp.bfloat16))


def product(pattern, left, right):
    return jnp.einsum(pattern, left, right, preferred_element_type=jnp.float32)


def gelu_both(lifted, active_grad):
    activated, pull = jax.vjp(partial(jax.nn.gelu, approximate=True), lifted)
    return pull(active_grad)[0].astype(jnp.bfloat16)


def gelu(lifted):
    return jax.nn.gelu(lifted, approximate=True).astype(jnp.bfloat16)


def swap(array, axis, bit):
    size = lax.axis_size(axis)
    return lax.ppermute(array, axis, [(i, i ^ bit) for i in range(size)])


def follow(array, *before):
    return lax.optimization_barrier((array, *before))[0]


ROWS = 640


MESH = pl.DeviceIdType.MESH


def feed_kernel(exchange, later, hidden_ref, back_ref, expand_ref, shrink_ref, *refs):
    step, steps = pl.program_id(0), pl.num_programs(0)
    f32 = jnp.float32
    if exchange:
        expand_before, shrink_before = refs[:2]
        (
            keep_ref,
            away_ref,
            land_hbm,
            hidden_part,
            branch_part,
            activated_ref,
            lifted_grad_ref,
            hidden_sum,
            branch_sum,
            send_ref,
            land_ref,
            near_send,
            near_recv,
            load_sem,
        ) = refs[2 + later :]
        outer = lax.axis_index("outer")
        far, near = outer // 2, outer % 2
        near_id = {"outer": outer + 1 - 2 * near}

        def near_copy(tile, k):
            return pltpu.make_async_remote_copy(
                src_ref=send_ref.at[k],
                dst_ref=land_hbm.at[tile, k],
                send_sem=near_send.at[tile, k],
                recv_sem=near_recv.at[tile, k],
                device_id=near_id,
                device_id_type=MESH,
            )

        def load(tile, k):
            return pltpu.make_async_copy(land_hbm.at[tile, k], land_ref.at[k], load_sem.at[k])

        @pl.when(step == 0)
        def _():
            barrier = pltpu.get_barrier_semaphore()
            pl.semaphore_signal(
                barrier, inc=1, device_id=near_id, device_id_type=MESH
            )
            pl.semaphore_wait(barrier, 1)

        for tile in range(2):

            @pl.when(step == 2 + tile)
            def _(tile=tile):
                for k in range(2):
                    near_copy(tile, k).wait_recv()
                    load(tile, k).start()

    else:
        (
            expand_grad,
            shrink_grad,
            hidden_part,
            branch_part,
            activated_ref,
            lifted_grad_ref,
            hidden_sum,
            branch_sum,
        ) = refs
    tokens = hidden_ref.shape[0]
    nt = (((1,), (1,)), ((), ()))
    tn = (((0,), (0,)), ((), ()))
    slope = 0.7978845608028654

    def block(at, first):
        hidden = hidden_ref[at, :]
        back = back_ref[at, :]
        lifted = jnp.dot(hidden, expand_ref[...], preferred_element_type=f32)
        active_grad = lax.dot_general(back, shrink_ref[...], nt, preferred_element_type=f32)
        square = lifted * lifted
        curve = jnp.tanh(slope * (lifted + 0.044715 * (square * lifted)))
        rise = 0.5 * (1.0 + curve)
        activated = (lifted * rise).astype(jnp.bfloat16)
        bend = 0.5 * lifted * (1.0 - curve * curve) * (slope + (3.0 * 0.044715 * slope) * square)
        lifted_grad = (active_grad * (rise + bend)).astype(jnp.bfloat16)
        activated_ref[at, :] = activated
        lifted_grad_ref[at, :] = lifted_grad
        branch = jnp.dot(activated, shrink_ref[...], preferred_element_type=f32)
        hidden_grad = lax.dot_general(lifted_grad, expand_ref[...], nt, preferred_element_type=f32)
        if first:
            branch_sum[at, :] = branch
            hidden_sum[at, :] = hidden_grad
        else:
            branch_sum[at, :] += branch
            hidden_sum[at, :] += hidden_grad

    def blocks(first):
        def one(i, _):
            block(pl.ds(pl.multiple_of(i * ROWS, ROWS), ROWS), first)
            return 0

        lax.fori_loop(0, tokens // ROWS, one, 0)

    @pl.when(step == 0)
    def _():
        blocks(True)

    @pl.when(step > 0)
    def _():
        blocks(False)

    def gradient(k):
        made_of = ((activated_ref, back_ref), (lifted_grad_ref, hidden_ref))[k]
        made = lax.dot_general(made_of[0][...], made_of[1][...], tn, preferred_element_type=f32)
        return made + (shrink_before, expand_before)[k][...] if exchange else made

    if not exchange:
        shrink_grad[...] = gradient(0)
        expand_grad[...] = gradient(1)
    else:
        for tile in range(2):

            @pl.when(step == tile)
            def _(tile=tile):
                for k in range(2):
                    if tile:
                        near_copy(tile - 1, k).wait_send()
                    send_ref[k] = gradient(k)
                    near_copy(tile, k).start()

            @pl.when(step == 2 + tile)
            def _(tile=tile):
                for k in range(2):
                    load(tile, k).wait()
                    total = gradient(k) + land_ref[k]

                    @pl.when(far == tile)
                    def _():
                        keep_ref[k] = total

                    @pl.when(far != tile)
                    def _():
                        away_ref[k] = total.astype(jnp.bfloat16)

                    if tile == 0:
                        near_copy(1, k).wait_send()

    @pl.when(step == steps - 1)
    def _():
        hidden_part[...] = hidden_sum[...].astype(hidden_part.dtype)
        branch_part[...] = branch_sum[...].astype(branch_part.dtype)


def feed(hidden, back, expand, shrink, before, branch_type, after=()):
    tokens, width = hidden.shape
    units = 2 * expand.shape[2]
    steps = 4
    tile = units // steps
    exchange = bool(before)
    low, f32 = jnp.bfloat16, jnp.float32
    turn = steps // 2 if exchange else 0
    whole = pl.BlockSpec((tokens, width), lambda n: (0, 0), pipeline_mode=pl.Buffered(1))
    rows = pl.BlockSpec((tile, width), lambda n: ((n + turn) % steps, 0))
    quarter = pl.BlockSpec((2, tile, width), lambda n: (0, 0, 0), pipeline_mode=pl.Buffered(1))
    columns = pl.BlockSpec(
        (None, width, tile),
        lambda n: ((n + turn) % steps // 2, 0, (n + turn) % 2),
    )
    grads = jax.ShapeDtypeStruct((units, width), f32)
    sem = pltpu.SemaphoreType.DMA
    return pl.pallas_call(
        partial(feed_kernel, exchange, len(after)),
        grid=(steps,),
        in_specs=[whole, whole, columns, rows]
        + [rows, rows] * exchange
        + [pl.BlockSpec(memory_space=pl.ANY)] * len(after),
        out_specs=(
            [quarter, quarter, pl.BlockSpec(memory_space=pl.ANY)] if exchange else [rows, rows]
        )
        + [whole, whole],
        out_shape=(
            [
                jax.ShapeDtypeStruct((2, tile, width), f32),
                jax.ShapeDtypeStruct((2, tile, width), low),
                jax.ShapeDtypeStruct((2, 2, tile, width), f32),
            ]
            if exchange
            else [grads, grads]
        )
        + [
            jax.ShapeDtypeStruct((tokens, width), f32),
            jax.ShapeDtypeStruct((tokens, width), branch_type),
        ],
        scratch_shapes=[
            pltpu.VMEM((tokens, tile), low),
            pltpu.VMEM((tokens, tile), low),
            pltpu.VMEM((tokens, width), f32),
            pltpu.VMEM((tokens, width), f32),
        ]
        + [
            pltpu.VMEM((2, tile, width), f32),
            pltpu.VMEM((2, tile, width), f32),
            sem((2, 2)),
            sem((2, 2)),
            sem((2,)),
        ]
        * exchange,
        compiler_params=pltpu.CompilerParams(
            vmem_limit_bytes=60 * 2**20,
            **(dict(collective_id=4, has_side_effects=True) if exchange else {}),
        ),
        cost_estimate=pl.CostEstimate(flops=2**20, bytes_accessed=2**20, transcendentals=0),
    )(hidden, back, expand, shrink, *before, *after)


def opening_kernel(
    expand_hbm,
    shrink_hbm,
    project_hbm,
    mixing_hbm,
    inputs_hbm,
    norm_ref,
    back_ref,
    expand_out,
    shrink_out,
    later_out,
    norm_out,
    hidden_ref,
    other_back,
    expand_ref,
    shrink_ref,
    project_ref,
    mixing_ref,
    inputs_ref,
    expand_low,
    shrink_low,
    norm_low,
    norm_all,
    load_sem,
    own_sem,
    norm_send,
    norm_recv,
    line_send,
    line_recv,
    far_send,
    far_recv,
    near_send,
    near_recv,
    row_sem,
):
    place, deep = lax.axis_index("dp"), 4
    outer = lax.axis_index("outer")
    far, near = outer // 2, outer % 2
    far_id = {"outer": (outer + 2) % 4}
    near_id = {"outer": outer + 1 - 2 * near}
    rows = expand_ref.shape[0]
    half = expand_ref.shape[1] // 2
    part = half // 2

    loads = [
        pltpu.make_async_copy(source, target, load_sem.at[n])
        for n, (source, target) in enumerate(
            (
                (expand_hbm, expand_ref),
                (shrink_hbm, shrink_ref),
                (project_hbm, project_ref),
                (mixing_hbm, mixing_ref),
                (inputs_hbm, inputs_ref),
            )
        )
    ]
    loads[0].start()
    loads[1].start()
    barrier = pltpu.get_barrier_semaphore()
    for step in range(1, deep):
        pl.semaphore_signal(
            barrier, inc=1, device_id={"dp": (place + step) % deep}, device_id_type=MESH
        )
    pl.semaphore_signal(barrier, inc=1, device_id=far_id, device_id_type=MESH)
    pl.semaphore_signal(barrier, inc=1, device_id=near_id, device_id_type=MESH)
    row_id = {"mp": 1 - lax.axis_index("mp")}
    pl.semaphore_signal(barrier, inc=1, device_id=row_id, device_id_type=MESH)

    for load in loads[2:]:
        load.start()
    norm_low[...] = jnp.zeros_like(norm_low)
    norm_low[0:2] = norm_ref[...].astype(jnp.bfloat16).astype(jnp.float32)
    pl.semaphore_wait(barrier, deep + 2)

    def piece(w, which, at, side):
        across = pl.ds(pl.multiple_of(at * rows, rows), rows)
        along = pl.ds(pl.multiple_of(side * part, part), part)
        if w == 0:
            return expand_out.at[which, across, along]
        return shrink_out.at[which, along, across]

    def mine(w):
        along = pl.ds(pl.multiple_of(near * half + far * part, part), part)
        return expand_low.at[:, along] if w == 0 else shrink_low.at[along, :]

    def remote(source, target, send, recv, device):
        return pltpu.make_async_remote_copy(
            src_ref=source,
            dst_ref=target,
            send_sem=send,
            recv_sem=recv,
            device_id=device,
            device_id_type=MESH,
        )

    def line(w, way, step, source, at):
        to = place + 1 if way == 0 else place - 1
        return remote(
            source,
            piece(w, 0, at, far),
            line_send.at[w, way, step],
            line_recv.at[w, way, step],
            {"dp": to},
        )

    def can_send(way):
        return place < deep - 1 if way == 0 else place > 0

    def start_own(w):
        for way in range(2):

            @pl.when(can_send(way))
            def _(way=way):
                line(w, way, 0, mine(w), place).start()

    def own_copies(w):
        out = []
        for which in range(2):
            side = near + which - 2 * near * which
            along = pl.ds(pl.multiple_of(side * half, half), half)
            across = pl.ds(pl.multiple_of(place * rows, rows), rows)
            if w == 0:
                pair = (expand_low.at[:, along], expand_out.at[which, across, :])
            else:
                pair = (shrink_low.at[along, :], shrink_out.at[which, :, across])
            out.append(pltpu.make_async_copy(*pair, own_sem.at[w, which]))
        return out

    row_copy = remote(back_ref, other_back, row_sem.at[0], row_sem.at[1], row_id)
    row_copy.start()
    loads[0].wait()
    expand_low[...] = expand_ref[...].astype(jnp.bfloat16)
    start_own(0)
    norm_copies = []
    for step in range(1, deep):
        copy = remote(
            norm_low,
            norm_all.at[step],
            norm_send.at[step],
            norm_recv.at[step],
            {"dp": (place + step) % deep},
        )
        copy.start()
        norm_copies.append(copy)
    loads[1].wait()
    shrink_low[...] = shrink_ref[...].astype(jnp.bfloat16)
    start_own(1)
    for w in range(2):
        for copy in own_copies(w):
            copy.start()
    for load in loads[2:]:
        load.wait()
    first = 0
    for source in (project_ref, mixing_ref):
        units = source.shape[0] // 2
        later_out[first : first + units] = source[
            pl.ds(pl.multiple_of(near * units, units), units), :
        ].astype(jnp.bfloat16)
        first += units
    norm_all[0] = norm_low[...]
    for copy in norm_copies:
        copy.wait()
    for at in range(deep):
        norm_out[:, at * rows : (at + 1) * rows] = norm_all[(place - at + deep) % deep]
    gain, bias = norm_out[0:1], norm_out[1:2]
    tokens = inputs_ref.shape[0]
    height = 128

    def normalize(i, _):
        at = pl.ds(pl.multiple_of(i * height, height), height)
        x = inputs_ref[at, :].astype(jnp.float32)
        mean = jnp.mean(x, axis=1, keepdims=True)
        centred = x - mean
        spread = jnp.mean(centred * centred, axis=1, keepdims=True)
        normed = centred * lax.rsqrt(spread + norm_epsilon)
        hidden_ref[at, :] = (normed * gain + bias).astype(jnp.bfloat16)
        return 0

    lax.fori_loop(0, tokens // height, normalize, 0)

    def arrives(way, step):
        return place >= step if way == 0 else place + step < deep

    def at_of(way, step):
        return place - step if way == 0 else place + step

    def to_far(w, way, step):
        at = at_of(way, step)
        return remote(
            piece(w, 0, at, far),
            piece(w, 0, at, far),
            far_send.at[w, way, step - 1],
            far_recv.at[w, way, step - 1],
            far_id,
        )

    def from_far(w, way, step):
        at = at_of(way, step)
        return remote(
            piece(w, 0, at, 1 - far),
            piece(w, 0, at, 1 - far),
            far_send.at[w, way, step - 1],
            far_recv.at[w, way, step - 1],
            far_id,
        )

    def to_near(w, way, step, other):
        at = at_of(way, step)
        side = 1 - far if other else far
        return remote(
            piece(w, 0, at, side),
            piece(w, 1, at, side),
            near_send.at[w, way, step - 1, other],
            near_recv.at[w, way, step - 1, other],
            near_id,
        )

    order = [(w, step) for w in range(2) for step in range(1, deep)]

    def first_half(w, step):
        for way in range(2):

            @pl.when(arrives(way, step))
            def _(way=way):
                at = at_of(way, step)
                line(w, way, step - 1, mine(w), at).wait_recv()
                if step < deep - 1:

                    @pl.when(can_send(way))
                    def _():
                        line(w, way, step, piece(w, 0, at, far), at).start()

                to_far(w, way, step).start()
                to_near(w, way, step, 0).start()

    def second_half(w, step):
        for way in range(2):

            @pl.when(arrives(way, step))
            def _(way=way):
                from_far(w, way, step).wait_recv()
                to_near(w, way, step, 1).start()

    for n, (w, step) in enumerate(order):
        first_half(w, step)
        if n:
            second_half(*order[n - 1])
    second_half(*order[-1])
    row_copy.wait()
    for w in range(2):
        for copy in own_copies(w):
            copy.wait()
        for way in range(2):

            @pl.when(can_send(way))
            def _(way=way):
                line(w, way, 0, mine(w), place).wait_send()

            for step in range(1, deep):

                @pl.when(arrives(way, step))
                def _(way=way, step=step):
                    at = at_of(way, step)
                    if step < deep - 1:

                        @pl.when(can_send(way))
                        def _():
                            line(w, way, step, piece(w, 0, at, far), at).wait_send()

                    to_far(w, way, step).wait_send()
                    for other in range(2):
                        to_near(w, way, step, other).wait_send()
                        to_near(w, way, step, other).wait_recv()


def project_kernel(hidden_ref, back_ref, own_ref, sibling_ref, projected_ref, mixed_back_ref):
    nt = (((1,), (1,)), ((), ()))
    cut = own_ref.shape[0] * 3 // 4
    few = own_ref.shape[0] - cut
    for n, weights in enumerate((own_ref, sibling_ref)):
        projected_ref[n * cut : (n + 1) * cut] = lax.dot_general(
            weights[:cut], hidden_ref[...], nt, preferred_element_type=jnp.float32
        )
        mixed_back_ref[n * few : (n + 1) * few] = lax.dot_general(
            weights[cut:], back_ref[...], nt, preferred_element_type=jnp.float32
        ).astype(jnp.bfloat16)


def project_all(hidden, back, own, sibling):
    tokens, width = hidden.shape
    cut = own.shape[0] * 3 // 4
    rows = pl.BlockSpec((256, width), lambda n: (n, 0))
    whole = pl.BlockSpec(own.shape, lambda n: (0, 0), pipeline_mode=pl.Buffered(1))
    columns = lambda height: pl.BlockSpec((height, 256), lambda n: (0, n))
    return pl.pallas_call(
        project_kernel,
        grid=(tokens // 256,),
        in_specs=[rows, rows, whole, whole],
        out_specs=[columns(2 * cut), columns(2 * (own.shape[0] - cut))],
        out_shape=[
            jax.ShapeDtypeStruct((2 * cut, tokens), jnp.float32),
            jax.ShapeDtypeStruct((2 * (own.shape[0] - cut), tokens), jnp.bfloat16),
        ],
        compiler_params=pltpu.CompilerParams(vmem_limit_bytes=60 * 2**20),
        cost_estimate=pl.CostEstimate(flops=2**20, bytes_accessed=2**20, transcendentals=0),
    )(hidden, back, own, sibling)


def opening(expand, shrink, project, mixing, norm, inputs, back):
    deep = 4
    here = lambda: pl.BlockSpec(memory_space=pltpu.VMEM)
    rows, units = expand.shape
    later = project.shape[0] + mixing.shape[0]
    low = jnp.bfloat16
    sem = pltpu.SemaphoreType.DMA
    return pl.pallas_call(
        opening_kernel,
        in_specs=[pl.BlockSpec(memory_space=pl.ANY)] * 5
        + [here(), pl.BlockSpec(memory_space=pl.ANY)],
        out_specs=[pl.BlockSpec(memory_space=pl.ANY)] * 2
        + [here() for _ in range(3)]
        + [pl.BlockSpec(memory_space=pl.ANY)],
        out_shape=[
            jax.ShapeDtypeStruct((2, rows * deep, units // 2), low),
            jax.ShapeDtypeStruct((2, units // 2, rows * deep), low),
            jax.ShapeDtypeStruct((later // 2, project.shape[1]), low),
            jax.ShapeDtypeStruct((8, rows * deep), jnp.float32),
            jax.ShapeDtypeStruct(inputs.shape, low),
            jax.ShapeDtypeStruct(back.shape, low),
        ],
        scratch_shapes=[
            pltpu.VMEM(v.shape, v.dtype) for v in (expand, shrink, project, mixing, inputs)
        ]
        + [
            pltpu.VMEM(expand.shape, low),
            pltpu.VMEM(shrink.shape, low),
            pltpu.VMEM((8, norm.shape[1]), jnp.float32),
            pltpu.VMEM((deep, 8, norm.shape[1]), jnp.float32),
            sem((5,)),
            sem((2, 2)),
            sem((deep,)),
            sem((deep,)),
            sem((2, 2, deep)),
            sem((2, 2, deep)),
            sem((2, 2, deep)),
            sem((2, 2, deep)),
            sem((2, 2, deep, 2)),
            sem((2, 2, deep, 2)),
            sem((2,)),
        ],
        compiler_params=pltpu.CompilerParams(
            collective_id=1, has_side_effects=True, vmem_limit_bytes=60 * 2**20
        ),
        cost_estimate=pl.CostEstimate(flops=0, bytes_accessed=2**20, transcendentals=0),
    )(expand, shrink, project, mixing, inputs, norm, back)


def closing_kernel(
    later,
    own_weights,
    sibling_weights,
    *refs,
):
    sources = (own_weights, *refs[:9])
    part_own, part_other, feed_keep, feed_come, gain_ref = refs[9:14]
    input_grad, small_sum, mixed_come = refs[14 + later : 17 + later]
    full_refs = refs[17 + later : 21 + later]
    refs = refs[21 + later :]
    held = refs[:10]
    (
        part_in,
        total_ref,
        sent_ref,
        come_ref,
        project_land,
        project_own,
        mixing_land,
        mixing_own,
        project_far,
        project_come,
        mixing_far,
        mixing_come,
        project_line,
        project_lands,
        mixing_line,
        mixing_lands,
        feed_in,
        feed_line,
        feed_lands,
        feed_share,
        expand_share,
        project_share,
        mixing_share,
        small_ref,
        plane_lands,
        deep_lands,
        held_sem,
        half_sem,
        part_sem,
        out_sem,
        feed_sem,
        feed_send,
        feed_recv,
        spread_sem,
        spread_far_send,
        spread_far_recv,
        spread_near_send,
        spread_near_recv,
        plane_send,
        plane_recv,
        deep_send,
        deep_recv,
        row_send,
        row_recv,
        mixed_sem,
        near_send,
        near_recv,
        far_send,
        far_recv,
        line_send,
        line_recv,
    ) = refs[10:]
    (
        project,
        grads_other,
        grads_own,
        hidden_other,
        hidden_own,
        mixed_other,
        mixed_own,
        back_other,
        back_own,
        inputs,
    ) = held
    low, f32 = jnp.bfloat16, jnp.float32
    tn = (((0,), (0,)), ((), ()))
    place, deep, outers = lax.axis_index("dp"), 4, 4
    outer = lax.axis_index("outer")
    far, near = outer // 2, outer % 2
    row_id = {"mp": 1 - lax.axis_index("mp")}
    far_id = {"outer": (outer + 2) % 4}
    near_id = {"outer": outer + 1 - 2 * near}

    copies = [
        pltpu.make_async_copy(source, target, held_sem.at[n])
        for n, (source, target) in enumerate(zip(sources, held))
        if n
    ]
    copies.insert(0, None)
    quarter = feed_keep.shape[1]
    feed_copies = [
        (
            pltpu.make_async_copy(
                feed_keep.at[k],
                total_ref.at[slice(k * quarter, (k + 1) * quarter)],
                feed_sem.at[k],
            ),
            pltpu.make_async_copy(feed_come.at[k], feed_in.at[k], feed_sem.at[2 + k]),
        )
        for k in range(2)
    ]
    for pair in feed_copies:
        for copy in pair:
            copy.start()
    cut = project.shape[0] // 2
    halves = [
        pltpu.make_async_copy(
            source.at[slice(0, cut)], project.at[slice(n * cut, (n + 1) * cut)], half_sem.at[n]
        )
        for n, source in enumerate((own_weights, sibling_weights))
    ]
    for copy in (*halves, copies[1]):
        copy.start()
    barrier = pltpu.get_barrier_semaphore()
    plane = 2 * outers
    me = lax.axis_index("mp") * outers + outer

    def plane_id(step):
        other = (me + step) % plane
        return {"mp": other // outers, "outer": other % outers}

    for step in range(1, plane):
        pl.semaphore_signal(barrier, inc=1, device_id=plane_id(step), device_id_type=MESH)
    for step in range(1, deep):
        pl.semaphore_signal(
            barrier, inc=1, device_id={"dp": (place + step) % deep}, device_id_type=MESH
        )
    height = 256
    tokens, width = hidden_own.shape
    blocks = tokens // height
    at = [slice(n * height, (n + 1) * height) for n in range(blocks)]

    def remote(source, target, send, recv, device):
        return pltpu.make_async_remote_copy(
            src_ref=source,
            dst_ref=target,
            send_sem=send,
            recv_sem=recv,
            device_id=device,
            device_id_type=MESH,
        )

    loads = [
        pltpu.make_async_copy(source.at[at[n]], part_in.at[(k * blocks + n) % 2], part_sem.at[(k * blocks + n) % 2])
        for k, source in enumerate((part_other, part_own))
        for n in range(blocks)
    ]
    loads[0].start()
    loads[1].start()
    for copy in copies[2:]:
        copy.start()
    pl.semaphore_wait(barrier, plane + deep - 2)

    piece = width // deep

    def columns(place):
        return pl.ds(pl.multiple_of(place * piece, piece), piece)

    line_copies = []
    for k in range(2):
        for copy in feed_copies[k]:
            copy.wait()
        rows = slice(k * quarter, (k + 1) * quarter)
        for step in range(1, deep):
            target = (place + step) % deep
            feed_line[k, step - 1] = (
                total_ref[rows, columns(target)] + feed_in[k, :, columns(target)].astype(f32)
            ).astype(low)
            line_copies.append(
                remote(
                    feed_line.at[k, step - 1],
                    feed_lands.at[k, step - 1],
                    feed_send.at[k, step - 1],
                    feed_recv.at[k, step - 1],
                    {"dp": target},
                )
            )
            line_copies[-1].start()
        feed_share[k] = total_ref[rows, columns(place)] + feed_in[k, :, columns(place)].astype(f32)

    for copy in (*halves, copies[1]):
        copy.wait()
    row_copies = []
    for n in range(blocks):
        made = lax.dot_general(grads_other[:, at[n]], project[...], tn, preferred_element_type=f32)
        loads[n].wait()
        sent_ref[at[n], :] = (part_in[n % 2] + made).astype(low)
        loads[n + 2].start()
        copy = remote(
            sent_ref.at[at[n]], come_ref.at[at[n]], row_send.at[n], row_recv.at[n], row_id
        )
        copy.start()
        row_copies.append(copy)

    copies[5].wait()
    mixed_copy = remote(
        mixed_other.at[slice(0, mixed_come.shape[0])],
        mixed_come,
        mixed_sem.at[0],
        mixed_sem.at[1],
        row_id,
    )
    mixed_copy.start()

    for n in (2, 3, 4, 6, 7, 8):
        copies[n].wait()
    half = project_own.shape[0]
    few = mixing_own.shape[0]
    near_copies = []
    for n in range(half // height):
        rows = slice(half + n * height, half + (n + 1) * height)
        total_ref[at[n], :] = jnp.dot(
            grads_own[rows, :], hidden_own[...], preferred_element_type=f32
        ) + jnp.dot(grads_other[rows, :], hidden_other[...], preferred_element_type=f32)
        near_copies.append(
            remote(
                total_ref.at[at[n]],
                project_land.at[at[n]],
                near_send.at[n],
                near_recv.at[n],
                near_id,
            )
        )
        near_copies[-1].start()
    total_ref[half : half + few, :] = jnp.dot(
        mixed_own[few:, :], back_own[...], preferred_element_type=f32
    ) + jnp.dot(mixed_other[few:, :], back_other[...], preferred_element_type=f32)
    near_copies.append(
        remote(
            total_ref.at[slice(half, half + few)],
            mixing_land,
            near_send.at[3],
            near_recv.at[3],
            near_id,
        )
    )
    near_copies[-1].start()
    for n in range(half // height):
        made = jnp.dot(
            grads_own[at[n], :], hidden_own[...], preferred_element_type=f32
        ) + jnp.dot(grads_other[at[n], :], hidden_other[...], preferred_element_type=f32)
        near_copies[n].wait()
        project_own[at[n], :] = made + project_land[at[n], :]

    def to_far(own, send, come, n):
        size = send.shape[0]
        send[...] = own[pl.ds(pl.multiple_of((1 - far) * size, size), size), :].astype(low)
        copy = remote(send, come, far_send.at[n], far_recv.at[n], far_id)
        copy.start()
        return copy

    far_copies = [to_far(project_own, project_far, project_come, 0)]
    made = jnp.dot(mixed_own[:few, :], back_own[...], preferred_element_type=f32) + jnp.dot(
        mixed_other[:few, :], back_other[...], preferred_element_type=f32
    )
    near_copies[3].wait()
    mixing_own[...] = made + mixing_land[...]
    far_copies.append(to_far(mixing_own, mixing_far, mixing_come, 1))

    for n in range(blocks):
        made = lax.dot_general(grads_own[:, at[n]], project[...], tn, preferred_element_type=f32)
        loads[blocks + n].wait()
        total_ref[at[n], :] = part_in[(blocks + n) % 2] + made
        if n + 2 < blocks:
            loads[blocks + n + 2].start()

    for k, (own, come, line, lands) in enumerate(
        (
            (project_own, project_come, project_line, project_lands),
            (mixing_own, mixing_come, mixing_line, mixing_lands),
        )
    ):
        size = come.shape[0]
        keep = pl.ds(pl.multiple_of(far * size, size), size)
        far_copies[k].wait()
        own[keep, :] = own[keep, :] + come[...].astype(f32)
        for step in range(1, deep):
            target = (place + step) % deep
            line[step - 1] = own[keep, columns(target)].astype(low)
            copy = remote(
                line.at[step - 1],
                lands.at[step - 1],
                line_send.at[k, step - 1],
                line_recv.at[k, step - 1],
                {"dp": target},
            )
            copy.start()
            line_copies.append(copy)

    shares = (feed_share.at[0], expand_share, project_share, mixing_share)

    def place_in(k, near, far):
        if k == 1:
            return full_refs[k].at[:, pl.ds(pl.multiple_of((2 * near + far) * quarter, quarter), quarter)]
        size = shares[k].shape[0]
        return full_refs[k].at[pl.ds(pl.multiple_of((2 * near + far) * size, size), size)]

    def spread(k):
        if k < 2:
            result, lands = feed_share[k], feed_lands.at[k]
        else:
            own, lands = ((project_own, project_lands), (mixing_own, mixing_lands))[k - 2]
            size = shares[k].shape[0]
            result = own[pl.ds(pl.multiple_of(far * size, size), size), columns(place)]
        for copy in line_copies[3 * k : 3 * k + 3]:
            copy.wait()
        for step in range(1, deep):
            result = result + lands[step - 1].astype(f32)
        shares[k][...] = result.T if k == 1 else result
        here = place_in(k, near, far)
        copies = [
            pltpu.make_async_copy(shares[k], here, spread_sem.at[k]),
            remote(shares[k], here, spread_far_send.at[k], spread_far_recv.at[k], far_id),
            remote(shares[k], here, spread_near_send.at[k, 0], spread_near_recv.at[k, 0], near_id),
        ]
        for copy in copies:
            copy.start()
        return copies, jnp.sum(result * result)

    def pass_on(k, copies):
        copies[1].wait()
        there = place_in(k, near, 1 - far)
        copy = remote(
            there, there, spread_near_send.at[k, 1], spread_near_recv.at[k, 1], near_id
        )
        copy.start()
        return copy

    copies[9].wait()
    gain = gain_ref[0:1]
    gain_sum = jnp.zeros((1, width), f32)
    bias_sum = jnp.zeros((1, width), f32)
    out_copies, spreads, passed = [], [], []
    square = jnp.float32(0.0)
    for n in range(blocks):
        if n == blocks - 2:
            for k in range(2):
                copies, more = spread(k)
                spreads.append(copies)
                square = square + more
        if n == blocks - 1:
            for k in range(2, 4):
                copies, more = spread(k)
                spreads.append(copies)
                square = square + more
        row_copies[n].wait()
        if n >= 2:
            out_copies[n - 2].wait()

        def some(i, carry):
            gain_sum, bias_sum = carry
            small = 64
            rows = pl.ds(pl.multiple_of(n * height + i * small, small), small)
            x = inputs[rows, :].astype(f32)
            mean = jnp.mean(x, axis=1, keepdims=True)
            centred = x - mean
            spread = jnp.mean(centred * centred, axis=1, keepdims=True)
            inverse = lax.rsqrt(spread + norm_epsilon)
            normed = centred * inverse
            grad = total_ref[rows, :] + come_ref[rows, :].astype(f32)
            scaled = grad * gain
            middle = jnp.mean(scaled, axis=1, keepdims=True)
            along = jnp.mean(scaled * normed, axis=1, keepdims=True)
            result = inverse * (scaled - middle - normed * along)
            part_in[n % 2, pl.ds(pl.multiple_of(i * small, small), small), :] = (
                back_own[rows, :].astype(f32) + result
            )
            gain_sum = gain_sum + jnp.sum(grad * normed, axis=0, keepdims=True)
            bias_sum = bias_sum + jnp.sum(grad, axis=0, keepdims=True)
            return gain_sum, bias_sum

        gain_sum, bias_sum = lax.fori_loop(0, height // 64, some, (gain_sum, bias_sum))
        out_copies.append(
            pltpu.make_async_copy(part_in.at[n % 2], input_grad.at[at[n]], out_sem.at[n % 2])
        )
        out_copies[-1].start()
    for k in range(2):
        passed.append(pass_on(k, spreads[k]))

    small_ref[...] = jnp.full(small_ref.shape, square)
    small_ref[0:1] = gain_sum
    small_ref[1:2] = bias_sum

    def everywhere(lands, send, recv, size, index, device):
        copies = []
        for step in range(1, size):
            copy = remote(small_ref, lands.at[step], send.at[step], recv.at[step], device(step))
            copy.start()
            copies.append(copy)
        lands[0] = small_ref[...]
        for copy in copies:
            copy.wait()
        total = lands[index]
        for at in range(1, size):
            total = total + lands[(index + size - at) % size]
        small_ref[...] = total

    everywhere(plane_lands, plane_send, plane_recv, plane, me, plane_id)
    everywhere(
        deep_lands, deep_send, deep_recv, deep, place, lambda step: {"dp": (place + step) % deep}
    )
    for k in range(2, 4):
        passed.append(pass_on(k, spreads[k]))
    small = small_ref[0:2]
    norm = jnp.sqrt(small_ref[2:3] + jnp.sum(small * small))
    small_sum[...] = small_ref[...]
    small_sum[2:3] = norm
    small_sum[3:4] = clip_level / jnp.maximum(norm, clip_level)
    for k in range(4):
        spreads[k][0].wait()
        spreads[k][2].wait()
        passed[k].wait()
    mixed_copy.wait()
    for copy in out_copies[-2:]:
        copy.wait()


def closing(weights, grads, hiddens, mixed, backs, inputs, parts, feeds, gain, after):
    deep = 4
    low, f32 = jnp.bfloat16, jnp.float32
    tokens, width = inputs.shape
    half, few = grads[0].shape[0] // 2, mixed[0].shape[0] // 2
    piece = width // deep
    quarter = feeds[0].shape[1]
    anywhere = pl.BlockSpec(memory_space=pl.ANY)
    here = lambda: pl.BlockSpec(memory_space=pltpu.VMEM)
    held = (
        jax.ShapeDtypeStruct(grads[0].shape[:1] + (width,), low),
        grads[1],
        grads[0],
        hiddens[1],
        hiddens[0],
        mixed[1],
        mixed[0],
        backs[1],
        backs[0],
        inputs,
    )
    sem = pltpu.SemaphoreType.DMA
    space = pltpu.VMEM
    return pl.pallas_call(
        partial(closing_kernel, len(after)),
        in_specs=[anywhere] * 15 + [here()] + [anywhere] * len(after),
        out_specs=[anywhere, here()] + [anywhere] * 5,
        out_shape=[
            jax.ShapeDtypeStruct((tokens, width), f32),
            jax.ShapeDtypeStruct((8, width), f32),
            jax.ShapeDtypeStruct((few, tokens), low),
        ]
        + [
            jax.ShapeDtypeStruct(shape, f32)
            for shape in (
                (4 * quarter, piece),
                (piece, 4 * quarter),
                (2 * half, piece),
                (2 * few, piece),
            )
        ],
        scratch_shapes=[space(v.shape, v.dtype) for v in held]
        + [
            space((2, 256, width), f32),
            space((tokens, width), f32),
            space((tokens, width), low),
            space((tokens, width), low),
            space((half, width), f32),
            space((half, width), f32),
            space((few, width), f32),
            space((few, width), f32),
            space((half // 2, width), low),
            space((half // 2, width), low),
            space((few // 2, width), low),
            space((few // 2, width), low),
            space((deep - 1, half // 2, piece), low),
            space((deep - 1, half // 2, piece), low),
            space((deep - 1, few // 2, piece), low),
            space((deep - 1, few // 2, piece), low),
            space((2, quarter, width), low),
            space((2, deep - 1, quarter, piece), low),
            space((2, deep - 1, quarter, piece), low),
            space((2, quarter, piece), f32),
            space((piece, quarter), f32),
            space((half // 2, piece), f32),
            space((few // 2, piece), f32),
            space((8, width), f32),
            space((8, 8, width), f32),
            space((deep, 8, width), f32),
            sem((len(held),)),
            sem((2,)),
            sem((2,)),
            sem((2,)),
            sem((4,)),
            sem((2, deep - 1)),
            sem((2, deep - 1)),
            sem((4,)),
            sem((4,)),
            sem((4,)),
            sem((4, 2)),
            sem((4, 2)),
            sem((8,)),
            sem((8,)),
            sem((deep,)),
            sem((deep,)),
            sem((tokens // 256,)),
            sem((tokens // 256,)),
            sem((2,)),
            sem((4,)),
            sem((4,)),
            sem((2,)),
            sem((2,)),
            sem((2, deep)),
            sem((2, deep)),
        ],
        compiler_params=pltpu.CompilerParams(
            collective_id=3, has_side_effects=True, vmem_limit_bytes=62 * 2**20
        ),
        cost_estimate=pl.CostEstimate(flops=2**20, bytes_accessed=2**20, transcendentals=0),
    )(*weights, *held[1:], *parts, *feeds, gain, *after)


def local(
    inputs,
    cotangent,
    lengths,
    project_master,
    project_first,
    project_second,
    mixing_master,
    mixing_first,
    mixing_second,
    expand_master,
    expand_first,
    expand_second,
    shrink_master,
    shrink_first,
    shrink_second,
    norm_master,
    norm_first,
    norm_second,
):
    split, deep = lax.axis_size("mp"), lax.axis_size("dp")
    heads_here = project_master.shape[1]
    width = inputs.shape[1]
    paired = (
        split == 2
        and lax.axis_size("outer") == 4
        and heads_here % 4 == 0
        and width % BQ == 0
    )
    position = lax.axis_index("mp")
    count = width * split
    project_flat = project_master.transpose(1, 2, 0).reshape(heads_here * 3 * HD, -1)
    mixing_flat = mixing_master.reshape(heads_here * HD, mixing_master.shape[2])
    masters = (project_flat, mixing_flat, expand_master, shrink_master)
    depths = (1, 1, 0, 1)
    rows_local = inputs[0].astype(jnp.float32)
    begins, places = layout(lengths[0], count)
    cosine, sine = turns(places)
    if paired:
        expand, shrink, later, norm_weight, hidden_local, other_back = opening(
            expand_master,
            shrink_master,
            project_flat,
            mixing_flat,
            norm_master,
            inputs[0],
            cotangent[0],
        )
        backs = [cotangent[0], other_back]
        shrink = shrink.reshape(-1, shrink.shape[2])
        later = lax.all_gather(later, "dp", axis=1, tiled=True)
        hiddens = [hidden_local, swap(hidden_local, "mp", 1)]
    else:
        norm_weight = lax.all_gather(norm_master.astype(jnp.bfloat16), "dp", axis=1, tiled=True)
        gain = norm_weight[0].astype(jnp.float32)
        bias = norm_weight[1].astype(jnp.float32)
        shaped, norm_pull = jax.vjp(layer_norm, rows_local, gain, bias)
        hidden_local = shaped.astype(jnp.bfloat16)
        project, mixing, expand, shrink = (
            lax.all_gather(master.astype(jnp.bfloat16), "dp", axis=depth, tiled=True)
            for master, depth in zip(masters, depths)
        )
        backs = [lax.all_gather(cotangent[0], "mp", axis=0, tiled=True)]
        hiddens = [lax.all_gather(hidden_local, "mp", axis=0, tiled=True)]

    def over_tokens(pattern, lefts, rights):
        return sum(product(pattern, left, right) for left, right in zip(lefts, rights))

    back_local = cotangent[0].astype(jnp.float32)
    if paired:
        *grads, hidden_own, branch_own = feed(
            hiddens[0], backs[0], expand, shrink, (), jnp.float32
        )
        later = follow(later, branch_own)
        later = [later, swap(later, "outer", 1)]
        cut = later[0].shape[0] * 3 // 4
        mixing = jnp.concatenate([v[cut:] for v in later])
        own_columns = project_all(hiddens[0], backs[0], *later)
        feed_keep, feed_away, _, hidden_other, branch_other = feed(
            hiddens[1], backs[1], expand, follow(shrink, *own_columns), grads, jnp.bfloat16
        )
        feed_come = swap(feed_away, "outer", 2)
        branch_come = swap(branch_other, "mp", 1)
        mixing_other = swap(mixing, "mp", 1)
        other_columns = project_all(hiddens[1], backs[1], *later)
        projected, mixed_backs = zip(own_columns, other_columns)
        mixed, projected_grads = attend(
            projected,
            mixed_backs,
            begins,
            cosine,
            sine,
            position,
            (feed_away, branch_other),
        )
        input_grad, small_sum, mixed_come, shrink_sum, expand_sum, project_sum, mixing_sum = closing(
            later,
            projected_grads,
            hiddens,
            mixed,
            backs,
            inputs[0],
            (hidden_own, hidden_other),
            (feed_keep, feed_come),
            norm_weight,
            (branch_come,),
        )
        mixed_own = follow(mixed[0], small_sum)
        few = mixed_come.shape[0]
        mixed_last = swap(follow(mixed[1], small_sum)[few:], "mp", 1)
        branch = (
            branch_own
            + branch_come.astype(jnp.float32)
            + product("ft,fd->td", mixed_own, mixing)
            + product("ft,fd->td", mixed_come, mixing_other[:few])
            + product("ft,fd->td", mixed_last, mixing_other[few:])
        )
    else:
        lifteds = [product("td,df->tf", hidden, expand) for hidden in hiddens]
        activated = [gelu(lifted) for lifted in lifteds]
        active_grads = [product("td,fd->tf", back, shrink) for back in backs]
        lifted_grads = [gelu_both(a, b) for a, b in zip(lifteds, active_grads)]
        hidden_parts = [product("tf,df->td", v, expand) for v in lifted_grads]
        branch_parts = [product("tf,fd->td", v, shrink) for v in activated]
        projected = [product("td,ed->et", hidden, project) for hidden in hiddens]
        mixed_backs = [product("td,fd->ft", back, mixing).astype(jnp.bfloat16) for back in backs]
        mixed, projected_grads = attend(projected, mixed_backs, begins, cosine, sine, position)
        project_sum, mixing_sum, expand_sum, shrink_sum = (
            lax.psum(
                lax.psum_scatter(
                    over_tokens(pattern, lefts, rights),
                    "dp",
                    scatter_dimension=depth,
                    tiled=True,
                ),
                "outer",
            )
            for pattern, lefts, rights, depth in (
                ("et,td->ed", projected_grads, hiddens, 1),
                ("ft,td->fd", mixed, backs, 1),
                ("td,tf->df", hiddens, lifted_grads, 0),
                ("tf,td->fd", activated, backs, 1),
            )
        )
        hidden_grad, branch = (
            lax.psum_scatter(v, "mp", scatter_dimension=0, tiled=True)
            for v in (
                hidden_parts[0] + product("et,ed->td", projected_grads[0], project),
                branch_parts[0] + product("ft,fd->td", mixed[0], mixing),
            )
        )
        rows_grad, gain_grad, bias_grad = norm_pull(hidden_grad)
        input_grad = back_local + rows_grad
        norm_terms = jnp.stack([gain_grad, bias_grad])
    input_grad = input_grad[None]
    block_out = (rows_local + branch).astype(jnp.bfloat16)[None]
    sums = (project_sum, mixing_sum, expand_sum, shrink_sum)
    if not paired:
        own_square = sum(jnp.sum(v * v) for v in sums) / lax.axis_size("outer")
        small_sum = lax.psum(
            jnp.concatenate([norm_terms, jnp.full((1, D), own_square)]), ("mp", "dp", "outer")
        )
        square = small_sum[2, 0] + jnp.sum(small_sum[:2] * small_sum[:2])
        grad_norm = jnp.sqrt(square)
        factor = clip_level / jnp.maximum(grad_norm, clip_level)
    else:
        grad_norm, factor = small_sum[2, 0], small_sum[3, 0]
    norm_full = small_sum[:2]
    norm_gradient = lax.dynamic_slice_in_dim(
        norm_full, lax.axis_index("dp") * (D // deep), D // deep, 1
    )
    gradients = list(sums)
    gradients[0] = gradients[0].reshape(heads_here, 3 * HD, -1).transpose(2, 0, 1)
    gradients[1] = gradients[1].reshape(mixing_master.shape)
    states = (
        (project_master, project_first, project_second, D ** (-0.5)),
        (mixing_master, mixing_first, mixing_second, (D // 32) ** (-0.5)),
        (expand_master, expand_first, expand_second, D ** (-0.5)),
        (shrink_master, shrink_first, shrink_second, FF ** (-0.5)),
    )
    results = [block_out, input_grad]
    for (master, first, second, rate), gradient in zip(states, gradients):
        results += adam_update(master, first, second, factor * gradient, rate, decay_rate)
    results += adam_update(norm_master, norm_first, norm_second, factor * norm_gradient, 0.3, 0.0)
    return (*results, grad_norm)


def solution(mesh):
    in_specs = (
        P(("dp", "outer"), "mp", None),
        P(("dp", "outer"), "mp", None),
        P(("dp", "outer"), None),
        P("dp", "mp", None),
        P("dp", "mp", None),
        P("dp", "mp", None),
        P("mp", None, "dp"),
        P("mp", None, "dp"),
        P("mp", None, "dp"),
        P("dp", "mp"),
        P("dp", "mp"),
        P("dp", "mp"),
        P("mp", "dp"),
        P("mp", "dp"),
        P("mp", "dp"),
        P(None, "dp"),
        P(None, "dp"),
        P(None, "dp"),
    )
    out_specs = (
        P(("dp", "outer"), "mp", None),
        P(("dp", "outer"), "mp", None),
        P("dp", "mp", None),
        P("dp", "mp", None),
        P("dp", "mp", None),
        P("dp", "mp", None),
        P("mp", None, "dp"),
        P("mp", None, "dp"),
        P("mp", None, "dp"),
        P("mp", None, "dp"),
        P("dp", "mp"),
        P("dp", "mp"),
        P("dp", "mp"),
        P("dp", "mp"),
        P("mp", "dp"),
        P("mp", "dp"),
        P("mp", "dp"),
        P("mp", "dp"),
        P(None, "dp"),
        P(None, "dp"),
        P(None, "dp"),
        P(None, "dp"),
        P(),
    )
    return jax.shard_map(local, mesh=mesh, in_specs=in_specs, out_specs=out_specs, check_vma=False)
```

```python
from functools import partial
import math

import jax
import jax.numpy as jnp
from jax import lax
from jax.experimental import pallas as pl
from jax.experimental.pallas import tpu as pltpu
from jax.sharding import PartitionSpec as P

D = 1024
HD = 64
ROT = 32
FF = 4096
STEP = 10


norm_epsilon = 1e-05
beta_one = 0.9
beta_two = 0.95
adam_epsilon = 1e-08
decay_rate = 0.1
clip_level = 1.0
masked_value = -1e30


def layout(sizes_row, count):
    number = jnp.arange(sizes_row.shape[0], dtype=jnp.int32)
    ends = jnp.sum(jnp.where(number[None, :] <= number[:, None], sizes_row[None, :], 0), axis=1)
    tokens = jnp.arange(count, dtype=jnp.int32)
    passed = (ends[:, None] <= tokens[None, :]).astype(jnp.int32)
    begins = jnp.sum(passed * sizes_row[:, None], axis=0)
    return (begins, tokens - begins)


def turns(places):
    half_rot = ROT // 2
    counter = jnp.arange(half_rot, dtype=jnp.float32)
    frequency = jnp.exp(counter * (-2.0 * math.log(10000.0) / ROT))
    angles = places.astype(jnp.float32)[None, :] * frequency[:, None]
    return jnp.cos(angles), jnp.sin(angles)


BQ = 256
BK = 256


def attend_kernel(together, parts, later, *refs):
    facts = refs[0]
    projected_refs = refs[1 : 1 + parts]
    back_refs = refs[1 + parts : 1 + 2 * parts]
    start_ref, cos_ref, sin_ref = refs[1 + 2 * parts : 4 + 2 * parts]
    refs = refs[: 4 + 2 * parts] + refs[4 + 2 * parts + later :]
    mixed_refs = refs[4 + 2 * parts : 4 + 3 * parts]
    grad_refs = refs[4 + 3 * parts : 4 + 4 * parts]
    (
        query_ref,
        key_columns_ref,
        value_columns_ref,
        key_ref,
        value_ref,
        back_ref,
        query_grad_ref,
        key_grad_ref,
        value_grad_ref,
        shifted_ref,
        share_grad_ref,
        top_ref,
    ) = refs[4 + 4 * parts :]
    width = projected_refs[0].shape[1]
    count = width * parts
    blocks = count // BQ
    turn = facts[blocks]
    half = ROT // 2
    scale = HD ** (-0.5)

    def place_of(part):
        if parts == 1:
            return pl.ds(0, width)
        block = lax.rem(part * (blocks // parts) + blocks - turn, blocks)
        return pl.ds(pl.multiple_of(block * BQ, BQ), width)

    for part in range(parts):
        columns = slice(part * width, (part + 1) * width)
        cosine, sine = cos_ref[:, place_of(part)], sin_ref[:, place_of(part)]
        projected_ref = projected_refs[part]

        def turned(at):
            first = projected_ref[at : at + half]
            second = projected_ref[at + half : at + ROT]
            return jnp.concatenate(
                [
                    first * cosine - second * sine,
                    second * cosine + first * sine,
                    projected_ref[at + ROT : at + HD],
                ],
                axis=0,
            ).astype(jnp.bfloat16)

        for h in range(together):
            base = h * 3 * HD
            query_ref[h, :, columns] = (turned(base).astype(jnp.float32) * scale).astype(
                jnp.bfloat16
            )
            keys = turned(base + HD)
            values = projected_ref[base + 2 * HD : base + 3 * HD].astype(jnp.bfloat16)
            key_columns_ref[h, :, columns] = keys
            value_columns_ref[h, :, columns] = values
            key_ref[h, columns] = keys.T
            value_ref[h, columns] = values.T
            back_ref[h, :, columns] = back_refs[part][h * HD : (h + 1) * HD]
    key_grad_ref[...] = jnp.zeros_like(key_grad_ref)
    value_grad_ref[...] = jnp.zeros_like(value_grad_ref)
    key_at = lax.broadcasted_iota(jnp.int32, (BK, BQ), 0)
    query_at = lax.broadcasted_iota(jnp.int32, (1, BQ), 1)

    def stored(block):
        if parts == 1:
            return pl.ds(pl.multiple_of(block * BQ, BQ), BQ)
        return pl.ds(pl.multiple_of(lax.rem(block + turn, blocks) * BQ, BQ), BQ)

    def query_block(i, _):
        columns = stored(i)
        start = start_ref[:, pl.ds(pl.multiple_of(i * BQ, BQ), BQ)]
        own = query_at + i * BQ
        lowest = facts[i]
        queries = [query_ref[h, :, columns] for h in range(together)]
        backs = [back_ref[h, :, columns] for h in range(together)]
        query_rows = [queries[h].T for h in range(together)]
        back_rows = [backs[h].T for h in range(together)]

        def in_pairs(body, carry):
            twos = lax.div(i + 1 - lowest, 2)
            carry = lax.fori_loop(
                0, twos, lambda n, c: body((lowest + 2 * n, lowest + 2 * n + 1), c), carry
            )
            return lax.fori_loop(lowest + 2 * twos, i + 1, lambda n, c: body((n,), c), carry)

        def scores(group, carry):
            made = []
            for j in group:
                rows = stored(j)
                allowed = (key_at >= start - j * BK) & (key_at <= own - j * BK)
                for h in range(together):
                    raw = jnp.dot(
                        key_ref[h, rows, :], queries[h], preferred_element_type=jnp.float32
                    )
                    share_grad = jnp.dot(
                        value_ref[h, rows, :], backs[h], preferred_element_type=jnp.float32
                    )
                    masked = jnp.where(allowed, raw, masked_value)
                    here = jnp.max(masked, axis=0, keepdims=True)
                    shifted = jnp.exp(masked - here)
                    shifted_ref[h, j] = shifted
                    share_grad_ref[h, j] = share_grad
                    top_ref[h, j] = here
                    made.append(
                        (
                            here,
                            jnp.sum(shifted, axis=0, keepdims=True),
                            jnp.sum(shifted * share_grad, axis=0, keepdims=True),
                        )
                    )
            out = []
            for h in range(together):
                top, total, inner = carry[h]
                for here, here_total, here_inner in made[h::together]:
                    new = jnp.maximum(top, here)
                    old_by, here_by = jnp.exp(top - new), jnp.exp(here - new)
                    total = total * old_by + here_total * here_by
                    inner = inner * old_by + here_inner * here_by
                    top = new
                out.append((top, total, inner))
            return tuple(out)

        zero = jnp.zeros((1, BQ), jnp.float32)
        empty = (jnp.full((1, BQ), masked_value, jnp.float32), zero, zero)
        stats = in_pairs(scores, (empty,) * together)
        inverse = [1.0 / s[1] for s in stats]
        inners = [s[2] * r for s, r in zip(stats, inverse)]

        def sums(group, carry):
            out = list(carry)
            for j in group:
                rows = stored(j)
                for h in range(together):
                    mixed, query_grad = out[h]
                    by = jnp.exp(top_ref[h, j] - stats[h][0]) * inverse[h]
                    probs = shifted_ref[h, j] * by
                    shares = probs.astype(jnp.bfloat16)
                    score_grad = (probs * (share_grad_ref[h, j] - inners[h])).astype(jnp.bfloat16)
                    mixed = mixed + jnp.dot(
                        value_columns_ref[h, :, rows], shares, preferred_element_type=jnp.float32
                    )
                    query_grad = query_grad + jnp.dot(
                        key_columns_ref[h, :, rows], score_grad, preferred_element_type=jnp.float32
                    )
                    value_grad_ref[h, rows, :] += jnp.dot(
                        shares, back_rows[h], preferred_element_type=jnp.float32
                    )
                    key_grad_ref[h, rows, :] += jnp.dot(
                        score_grad, query_rows[h], preferred_element_type=jnp.float32
                    )
                    out[h] = (mixed, query_grad)
            return tuple(out)

        nothing = jnp.zeros((HD, BQ), jnp.float32)
        results = in_pairs(sums, ((nothing, nothing),) * together)
        for h in range(together):
            back_ref[h, :, columns] = results[h][0].astype(jnp.bfloat16)
            query_grad_ref[h, :, columns] = results[h][1] * scale
        return 0

    lax.fori_loop(0, blocks, query_block, 0)
    for part in range(parts):
        columns = slice(part * width, (part + 1) * width)
        cosine, sine = cos_ref[:, place_of(part)], sin_ref[:, place_of(part)]

        def turned_back(grad):
            first, second = grad[:half], grad[half:ROT]
            return jnp.concatenate(
                [
                    first * cosine + second * sine,
                    second * cosine - first * sine,
                    grad[ROT:],
                ],
                axis=0,
            ).astype(jnp.bfloat16)

        for h in range(together):
            base = h * 3 * HD
            mixed_refs[part][h * HD : (h + 1) * HD] = back_ref[h, :, columns]
            grad_refs[part][base : base + HD] = turned_back(query_grad_ref[h, :, columns])
            grad_refs[part][base + HD : base + 2 * HD] = turned_back(key_grad_ref[h, columns, :].T)
            grad_refs[part][base + 2 * HD : base + 3 * HD] = value_grad_ref[
                h, columns, :
            ].T.astype(jnp.bfloat16)


def attend(projected, back, begins, cosine, sine, offset, after=()):
    parts = len(projected)
    heads = back[0].shape[0] // HD
    width = back[0].shape[1]
    count = begins.shape[0]
    together = 2 if heads % 2 == 0 else 1
    blocks = count // BK
    half = ROT // 2
    turn = jnp.asarray(offset * ((blocks // parts) if parts > 1 else 0), jnp.int32)
    facts = jnp.concatenate([begins[::BQ] // BK, turn[None]])
    whole = lambda rows: pl.BlockSpec((rows, count), lambda g, *_: (0, 0))
    mine = lambda rows: pl.BlockSpec((rows, width), lambda g, *_: (g, 0))
    results = pl.pallas_call(
        partial(attend_kernel, together, parts, len(after)),
        grid_spec=pltpu.PrefetchScalarGridSpec(
            num_scalar_prefetch=1,
            grid=(heads // together,),
            in_specs=[mine(together * 3 * HD)] * parts
            + [mine(together * HD)] * parts
            + [whole(1), whole(half), whole(half)]
            + [pl.BlockSpec(memory_space=pl.ANY)] * len(after),
            out_specs=[mine(together * HD)] * parts + [mine(together * 3 * HD)] * parts,
            scratch_shapes=[
                pltpu.VMEM((together, HD, count), jnp.bfloat16),
                pltpu.VMEM((together, HD, count), jnp.bfloat16),
                pltpu.VMEM((together, HD, count), jnp.bfloat16),
                pltpu.VMEM((together, count, HD), jnp.bfloat16),
                pltpu.VMEM((together, count, HD), jnp.bfloat16),
                pltpu.VMEM((together, HD, count), jnp.bfloat16),
                pltpu.VMEM((together, HD, count), jnp.float32),
                pltpu.VMEM((together, count, HD), jnp.float32),
                pltpu.VMEM((together, count, HD), jnp.float32),
                pltpu.VMEM((together, blocks, BK, BQ), jnp.float32),
                pltpu.VMEM((together, blocks, BK, BQ), jnp.float32),
                pltpu.VMEM((together, blocks, 1, BQ), jnp.float32),
            ],
        ),
        out_shape=[jax.ShapeDtypeStruct((heads * HD, width), jnp.bfloat16)] * parts
        + [jax.ShapeDtypeStruct((heads * 3 * HD, width), jnp.bfloat16)] * parts,
        compiler_params=pltpu.CompilerParams(vmem_limit_bytes=48 * 2**20),
        cost_estimate=pl.CostEstimate(
            flops=2**20,
            bytes_accessed=2**20,
            transcendentals=0,
        ),
    )(facts, *projected, *back, begins[None, :], cosine, sine, *after)
    return results[:parts], results[parts:]


def layer_norm(rows_in, gain, bias):
    mean = jnp.mean(rows_in, axis=1, keepdims=True)
    centred = rows_in - mean
    spread = jnp.mean(centred * centred, axis=1, keepdims=True)
    normed = centred * lax.rsqrt(spread + norm_epsilon)
    return normed * gain + bias


def adam_update(master, first, second, gradient, rate, decay):
    first_new = beta_one * first + (1.0 - beta_one) * gradient
    second_new = beta_two * second + (1.0 - beta_two) * gradient * gradient
    first_hat = first_new / (1.0 - beta_one**STEP)
    second_hat = second_new / (1.0 - beta_two**STEP)
    master_new = master - rate * (
        first_hat / (jnp.sqrt(second_hat) + adam_epsilon) + decay * master
    )
    return (master_new, first_new, second_new, master_new.astype(jnp.bfloat16))


def product(pattern, left, right):
    return jnp.einsum(pattern, left, right, preferred_element_type=jnp.float32)


def gelu_both(lifted, active_grad):
    activated, pull = jax.vjp(partial(jax.nn.gelu, approximate=True), lifted)
    return pull(active_grad)[0].astype(jnp.bfloat16)


def gelu(lifted):
    return jax.nn.gelu(lifted, approximate=True).astype(jnp.bfloat16)


def swap(array, axis, bit):
    size = lax.axis_size(axis)
    return lax.ppermute(array, axis, [(i, i ^ bit) for i in range(size)])


def follow(array, *before):
    return lax.optimization_barrier((array, *before))[0]


ROWS = 640


MESH = pl.DeviceIdType.MESH


def feed_kernel(exchange, later, hidden_ref, back_ref, expand_ref, shrink_ref, *refs):
    step, steps = pl.program_id(0), pl.num_programs(0)
    f32 = jnp.float32
    if exchange:
        expand_before, shrink_before = refs[:2]
        (
            keep_ref,
            away_ref,
            land_hbm,
            hidden_part,
            branch_part,
            activated_ref,
            lifted_grad_ref,
            hidden_sum,
            branch_sum,
            send_ref,
            land_ref,
            near_send,
            near_recv,
            load_sem,
        ) = refs[2 + later :]
        outer = lax.axis_index("outer")
        far, near = outer // 2, outer % 2
        near_id = {"outer": outer + 1 - 2 * near}

        def near_copy(tile, k):
            return pltpu.make_async_remote_copy(
                src_ref=send_ref.at[k],
                dst_ref=land_hbm.at[tile, k],
                send_sem=near_send.at[tile, k],
                recv_sem=near_recv.at[tile, k],
                device_id=near_id,
                device_id_type=MESH,
            )

        def load(tile, k):
            return pltpu.make_async_copy(land_hbm.at[tile, k], land_ref.at[k], load_sem.at[k])

        @pl.when(step == 0)
        def _():
            barrier = pltpu.get_barrier_semaphore()
            pl.semaphore_signal(
                barrier, inc=1, device_id=near_id, device_id_type=MESH
            )
            pl.semaphore_wait(barrier, 1)

        for tile in range(2):

            @pl.when(step == 2 + tile)
            def _(tile=tile):
                for k in range(2):
                    near_copy(tile, k).wait_recv()
                    load(tile, k).start()

    else:
        (
            expand_grad,
            shrink_grad,
            hidden_part,
            branch_part,
            activated_ref,
            lifted_grad_ref,
            hidden_sum,
            branch_sum,
        ) = refs
    tokens = hidden_ref.shape[0]
    nt = (((1,), (1,)), ((), ()))
    tn = (((0,), (0,)), ((), ()))
    slope = 0.7978845608028654

    def block(at, first):
        hidden = hidden_ref[at, :]
        back = back_ref[at, :]
        lifted = jnp.dot(hidden, expand_ref[...], preferred_element_type=f32)
        active_grad = lax.dot_general(back, shrink_ref[...], nt, preferred_element_type=f32)
        square = lifted * lifted
        curve = jnp.tanh(slope * (lifted + 0.044715 * (square * lifted)))
        rise = 0.5 * (1.0 + curve)
        activated = (lifted * rise).astype(jnp.bfloat16)
        bend = 0.5 * lifted * (1.0 - curve * curve) * (slope + (3.0 * 0.044715 * slope) * square)
        lifted_grad = (active_grad * (rise + bend)).astype(jnp.bfloat16)
        activated_ref[at, :] = activated
        lifted_grad_ref[at, :] = lifted_grad
        branch = jnp.dot(activated, shrink_ref[...], preferred_element_type=f32)
        hidden_grad = lax.dot_general(lifted_grad, expand_ref[...], nt, preferred_element_type=f32)
        if first:
            branch_sum[at, :] = branch
            hidden_sum[at, :] = hidden_grad
        else:
            branch_sum[at, :] += branch
            hidden_sum[at, :] += hidden_grad

    def blocks(first):
        def one(i, _):
            block(pl.ds(pl.multiple_of(i * ROWS, ROWS), ROWS), first)
            return 0

        lax.fori_loop(0, tokens // ROWS, one, 0)

    @pl.when(step == 0)
    def _():
        blocks(True)

    @pl.when(step > 0)
    def _():
        blocks(False)

    def gradient(k):
        made_of = ((activated_ref, back_ref), (lifted_grad_ref, hidden_ref))[k]
        made = lax.dot_general(made_of[0][...], made_of[1][...], tn, preferred_element_type=f32)
        return made + (shrink_before, expand_before)[k][...] if exchange else made

    if not exchange:
        shrink_grad[...] = gradient(0)
        expand_grad[...] = gradient(1)
    else:
        for tile in range(2):

            @pl.when(step == tile)
            def _(tile=tile):
                for k in range(2):
                    if tile:
                        near_copy(tile - 1, k).wait_send()
                    send_ref[k] = gradient(k)
                    near_copy(tile, k).start()

            @pl.when(step == 2 + tile)
            def _(tile=tile):
                for k in range(2):
                    load(tile, k).wait()
                    total = gradient(k) + land_ref[k]

                    @pl.when(far == tile)
                    def _():
                        keep_ref[k] = total

                    @pl.when(far != tile)
                    def _():
                        away_ref[k] = total.astype(jnp.bfloat16)

                    if tile == 0:
                        near_copy(1, k).wait_send()

    @pl.when(step == steps - 1)
    def _():
        hidden_part[...] = hidden_sum[...].astype(hidden_part.dtype)
        branch_part[...] = branch_sum[...].astype(branch_part.dtype)


def feed(hidden, back, expand, shrink, before, branch_type, after=()):
    tokens, width = hidden.shape
    units = 2 * expand.shape[2]
    steps = 4
    tile = units // steps
    exchange = bool(before)
    low, f32 = jnp.bfloat16, jnp.float32
    turn = steps // 2 if exchange else 0
    whole = pl.BlockSpec((tokens, width), lambda n: (0, 0), pipeline_mode=pl.Buffered(1))
    rows = pl.BlockSpec((tile, width), lambda n: ((n + turn) % steps, 0))
    quarter = pl.BlockSpec((2, tile, width), lambda n: (0, 0, 0), pipeline_mode=pl.Buffered(1))
    columns = pl.BlockSpec(
        (None, width, tile),
        lambda n: ((n + turn) % steps // 2, 0, (n + turn) % 2),
    )
    grads = jax.ShapeDtypeStruct((units, width), f32)
    sem = pltpu.SemaphoreType.DMA
    return pl.pallas_call(
        partial(feed_kernel, exchange, len(after)),
        grid=(steps,),
        in_specs=[whole, whole, columns, rows]
        + [rows, rows] * exchange
        + [pl.BlockSpec(memory_space=pl.ANY)] * len(after),
        out_specs=(
            [quarter, quarter, pl.BlockSpec(memory_space=pl.ANY)] if exchange else [rows, rows]
        )
        + [whole, whole],
        out_shape=(
            [
                jax.ShapeDtypeStruct((2, tile, width), f32),
                jax.ShapeDtypeStruct((2, tile, width), low),
                jax.ShapeDtypeStruct((2, 2, tile, width), f32),
            ]
            if exchange
            else [grads, grads]
        )
        + [
            jax.ShapeDtypeStruct((tokens, width), f32),
            jax.ShapeDtypeStruct((tokens, width), branch_type),
        ],
        scratch_shapes=[
            pltpu.VMEM((tokens, tile), low),
            pltpu.VMEM((tokens, tile), low),
            pltpu.VMEM((tokens, width), f32),
            pltpu.VMEM((tokens, width), f32),
        ]
        + [
            pltpu.VMEM((2, tile, width), f32),
            pltpu.VMEM((2, tile, width), f32),
            sem((2, 2)),
            sem((2, 2)),
            sem((2,)),
        ]
        * exchange,
        compiler_params=pltpu.CompilerParams(
            vmem_limit_bytes=60 * 2**20,
            **(dict(collective_id=4, has_side_effects=True) if exchange else {}),
        ),
        cost_estimate=pl.CostEstimate(flops=2**20, bytes_accessed=2**20, transcendentals=0),
    )(hidden, back, expand, shrink, *before, *after)


def opening_kernel(
    expand_hbm,
    shrink_hbm,
    project_hbm,
    mixing_hbm,
    inputs_hbm,
    norm_ref,
    back_ref,
    expand_out,
    shrink_out,
    later_out,
    norm_out,
    hidden_ref,
    other_back,
    expand_ref,
    shrink_ref,
    project_ref,
    mixing_ref,
    inputs_ref,
    expand_low,
    shrink_low,
    norm_low,
    norm_all,
    load_sem,
    own_sem,
    norm_send,
    norm_recv,
    line_send,
    line_recv,
    far_send,
    far_recv,
    near_send,
    near_recv,
    row_sem,
):
    place, deep = lax.axis_index("dp"), 4
    outer = lax.axis_index("outer")
    far, near = outer // 2, outer % 2
    far_id = {"outer": (outer + 2) % 4}
    near_id = {"outer": outer + 1 - 2 * near}
    rows = expand_ref.shape[0]
    half = expand_ref.shape[1] // 2
    part = half // 2

    loads = [
        pltpu.make_async_copy(source, target, load_sem.at[n])
        for n, (source, target) in enumerate(
            (
                (expand_hbm, expand_ref),
                (shrink_hbm, shrink_ref),
                (project_hbm, project_ref),
                (mixing_hbm, mixing_ref),
                (inputs_hbm, inputs_ref),
            )
        )
    ]
    loads[0].start()
    loads[1].start()
    barrier = pltpu.get_barrier_semaphore()
    for step in range(1, deep):
        pl.semaphore_signal(
            barrier, inc=1, device_id={"dp": (place + step) % deep}, device_id_type=MESH
        )
    pl.semaphore_signal(barrier, inc=1, device_id=far_id, device_id_type=MESH)
    pl.semaphore_signal(barrier, inc=1, device_id=near_id, device_id_type=MESH)
    row_id = {"mp": 1 - lax.axis_index("mp")}
    pl.semaphore_signal(barrier, inc=1, device_id=row_id, device_id_type=MESH)

    for load in loads[2:]:
        load.start()
    norm_low[...] = jnp.zeros_like(norm_low)
    norm_low[0:2] = norm_ref[...].astype(jnp.bfloat16).astype(jnp.float32)
    pl.semaphore_wait(barrier, deep + 2)

    def piece(w, which, at, side):
        across = pl.ds(pl.multiple_of(at * rows, rows), rows)
        along = pl.ds(pl.multiple_of(side * part, part), part)
        if w == 0:
            return expand_out.at[which, across, along]
        return shrink_out.at[which, along, across]

    def mine(w):
        along = pl.ds(pl.multiple_of(near * half + far * part, part), part)
        return expand_low.at[:, along] if w == 0 else shrink_low.at[along, :]

    def remote(source, target, send, recv, device):
        return pltpu.make_async_remote_copy(
            src_ref=source,
            dst_ref=target,
            send_sem=send,
            recv_sem=recv,
            device_id=device,
            device_id_type=MESH,
        )

    def line(w, way, step, source, at):
        to = place + 1 if way == 0 else place - 1
        return remote(
            source,
            piece(w, 0, at, far),
            line_send.at[w, way, step],
            line_recv.at[w, way, step],
            {"dp": to},
        )

    def can_send(way):
        return place < deep - 1 if way == 0 else place > 0

    def start_own(w):
        for way in range(2):

            @pl.when(can_send(way))
            def _(way=way):
                line(w, way, 0, mine(w), place).start()

    def own_copies(w):
        out = []
        for which in range(2):
            side = near + which - 2 * near * which
            along = pl.ds(pl.multiple_of(side * half, half), half)
            across = pl.ds(pl.multiple_of(place * rows, rows), rows)
            if w == 0:
                pair = (expand_low.at[:, along], expand_out.at[which, across, :])
            else:
                pair = (shrink_low.at[along, :], shrink_out.at[which, :, across])
            out.append(pltpu.make_async_copy(*pair, own_sem.at[w, which]))
        return out

    row_copy = remote(back_ref, other_back, row_sem.at[0], row_sem.at[1], row_id)
    row_copy.start()
    loads[0].wait()
    expand_low[...] = expand_ref[...].astype(jnp.bfloat16)
    start_own(0)
    norm_copies = []
    for step in range(1, deep):
        copy = remote(
            norm_low,
            norm_all.at[step],
            norm_send.at[step],
            norm_recv.at[step],
            {"dp": (place + step) % deep},
        )
        copy.start()
        norm_copies.append(copy)
    loads[1].wait()
    shrink_low[...] = shrink_ref[...].astype(jnp.bfloat16)
    start_own(1)
    for w in range(2):
        for copy in own_copies(w):
            copy.start()
    for load in loads[2:]:
        load.wait()
    first = 0
    for source in (project_ref, mixing_ref):
        units = source.shape[0] // 2
        later_out[first : first + units] = source[
            pl.ds(pl.multiple_of(near * units, units), units), :
        ].astype(jnp.bfloat16)
        first += units
    norm_all[0] = norm_low[...]
    for copy in norm_copies:
        copy.wait()
    for at in range(deep):
        norm_out[:, at * rows : (at + 1) * rows] = norm_all[(place - at + deep) % deep]
    gain, bias = norm_out[0:1], norm_out[1:2]
    tokens = inputs_ref.shape[0]
    height = 128

    def normalize(i, _):
        at = pl.ds(pl.multiple_of(i * height, height), height)
        x = inputs_ref[at, :].astype(jnp.float32)
        mean = jnp.mean(x, axis=1, keepdims=True)
        centred = x - mean
        spread = jnp.mean(centred * centred, axis=1, keepdims=True)
        normed = centred * lax.rsqrt(spread + norm_epsilon)
        hidden_ref[at, :] = (normed * gain + bias).astype(jnp.bfloat16)
        return 0

    lax.fori_loop(0, tokens // height, normalize, 0)

    def arrives(way, step):
        return place >= step if way == 0 else place + step < deep

    def at_of(way, step):
        return place - step if way == 0 else place + step

    def to_far(w, way, step):
        at = at_of(way, step)
        return remote(
            piece(w, 0, at, far),
            piece(w, 0, at, far),
            far_send.at[w, way, step - 1],
            far_recv.at[w, way, step - 1],
            far_id,
        )

    def from_far(w, way, step):
        at = at_of(way, step)
        return remote(
            piece(w, 0, at, 1 - far),
            piece(w, 0, at, 1 - far),
            far_send.at[w, way, step - 1],
            far_recv.at[w, way, step - 1],
            far_id,
        )

    def to_near(w, way, step, other):
        at = at_of(way, step)
        side = 1 - far if other else far
        return remote(
            piece(w, 0, at, side),
            piece(w, 1, at, side),
            near_send.at[w, way, step - 1, other],
            near_recv.at[w, way, step - 1, other],
            near_id,
        )

    order = [(w, step) for w in range(2) for step in range(1, deep)]

    def first_half(w, step):
        for way in range(2):

            @pl.when(arrives(way, step))
            def _(way=way):
                at = at_of(way, step)
                line(w, way, step - 1, mine(w), at).wait_recv()
                if step < deep - 1:

                    @pl.when(can_send(way))
                    def _():
                        line(w, way, step, piece(w, 0, at, far), at).start()

                to_far(w, way, step).start()
                to_near(w, way, step, 0).start()

    def second_half(w, step):
        for way in range(2):

            @pl.when(arrives(way, step))
            def _(way=way):
                from_far(w, way, step).wait_recv()
                to_near(w, way, step, 1).start()

    for n, (w, step) in enumerate(order):
        first_half(w, step)
        if n:
            second_half(*order[n - 1])
    second_half(*order[-1])
    row_copy.wait()
    for w in range(2):
        for copy in own_copies(w):
            copy.wait()
        for way in range(2):

            @pl.when(can_send(way))
            def _(way=way):
                line(w, way, 0, mine(w), place).wait_send()

            for step in range(1, deep):

                @pl.when(arrives(way, step))
                def _(way=way, step=step):
                    at = at_of(way, step)
                    if step < deep - 1:

                        @pl.when(can_send(way))
                        def _():
                            line(w, way, step, piece(w, 0, at, far), at).wait_send()

                    to_far(w, way, step).wait_send()
                    for other in range(2):
                        to_near(w, way, step, other).wait_send()
                        to_near(w, way, step, other).wait_recv()


def project_kernel(hidden_ref, back_ref, own_ref, sibling_ref, projected_ref, mixed_back_ref):
    nt = (((1,), (1,)), ((), ()))
    cut = own_ref.shape[0] * 3 // 4
    few = own_ref.shape[0] - cut
    for n, weights in enumerate((own_ref, sibling_ref)):
        projected_ref[n * cut : (n + 1) * cut] = lax.dot_general(
            weights[:cut], hidden_ref[...], nt, preferred_element_type=jnp.float32
        )
        mixed_back_ref[n * few : (n + 1) * few] = lax.dot_general(
            weights[cut:], back_ref[...], nt, preferred_element_type=jnp.float32
        ).astype(jnp.bfloat16)


def project_all(hidden, back, own, sibling):
    tokens, width = hidden.shape
    cut = own.shape[0] * 3 // 4
    rows = pl.BlockSpec((256, width), lambda n: (n, 0))
    whole = pl.BlockSpec(own.shape, lambda n: (0, 0), pipeline_mode=pl.Buffered(1))
    columns = lambda height: pl.BlockSpec((height, 256), lambda n: (0, n))
    return pl.pallas_call(
        project_kernel,
        grid=(tokens // 256,),
        in_specs=[rows, rows, whole, whole],
        out_specs=[columns(2 * cut), columns(2 * (own.shape[0] - cut))],
        out_shape=[
            jax.ShapeDtypeStruct((2 * cut, tokens), jnp.float32),
            jax.ShapeDtypeStruct((2 * (own.shape[0] - cut), tokens), jnp.bfloat16),
        ],
        compiler_params=pltpu.CompilerParams(vmem_limit_bytes=60 * 2**20),
        cost_estimate=pl.CostEstimate(flops=2**20, bytes_accessed=2**20, transcendentals=0),
    )(hidden, back, own, sibling)


def opening(expand, shrink, project, mixing, norm, inputs, back):
    deep = 4
    here = lambda: pl.BlockSpec(memory_space=pltpu.VMEM)
    rows, units = expand.shape
    later = project.shape[0] + mixing.shape[0]
    low = jnp.bfloat16
    sem = pltpu.SemaphoreType.DMA
    return pl.pallas_call(
        opening_kernel,
        in_specs=[pl.BlockSpec(memory_space=pl.ANY)] * 5
        + [here(), pl.BlockSpec(memory_space=pl.ANY)],
        out_specs=[pl.BlockSpec(memory_space=pl.ANY)] * 2
        + [here() for _ in range(3)]
        + [pl.BlockSpec(memory_space=pl.ANY)],
        out_shape=[
            jax.ShapeDtypeStruct((2, rows * deep, units // 2), low),
            jax.ShapeDtypeStruct((2, units // 2, rows * deep), low),
            jax.ShapeDtypeStruct((later // 2, project.shape[1]), low),
            jax.ShapeDtypeStruct((8, rows * deep), jnp.float32),
            jax.ShapeDtypeStruct(inputs.shape, low),
            jax.ShapeDtypeStruct(back.shape, low),
        ],
        scratch_shapes=[
            pltpu.VMEM(v.shape, v.dtype) for v in (expand, shrink, project, mixing, inputs)
        ]
        + [
            pltpu.VMEM(expand.shape, low),
            pltpu.VMEM(shrink.shape, low),
            pltpu.VMEM((8, norm.shape[1]), jnp.float32),
            pltpu.VMEM((deep, 8, norm.shape[1]), jnp.float32),
            sem((5,)),
            sem((2, 2)),
            sem((deep,)),
            sem((deep,)),
            sem((2, 2, deep)),
            sem((2, 2, deep)),
            sem((2, 2, deep)),
            sem((2, 2, deep)),
            sem((2, 2, deep, 2)),
            sem((2, 2, deep, 2)),
            sem((2,)),
        ],
        compiler_params=pltpu.CompilerParams(
            collective_id=1, has_side_effects=True, vmem_limit_bytes=60 * 2**20
        ),
        cost_estimate=pl.CostEstimate(flops=0, bytes_accessed=2**20, transcendentals=0),
    )(expand, shrink, project, mixing, inputs, norm, back)


def closing_kernel(
    later,
    own_weights,
    sibling_weights,
    *refs,
):
    sources = (own_weights, *refs[:9])
    part_own, part_other, feed_keep, feed_come, gain_ref = refs[9:14]
    input_grad, small_sum, mixed_come = refs[14 + later : 17 + later]
    full_refs = refs[17 + later : 21 + later]
    refs = refs[21 + later :]
    held = refs[:10]
    (
        part_in,
        total_ref,
        sent_ref,
        come_ref,
        project_land,
        project_own,
        mixing_land,
        mixing_own,
        project_far,
        project_come,
        mixing_far,
        mixing_come,
        project_line,
        project_lands,
        mixing_line,
        mixing_lands,
        feed_in,
        feed_line,
        feed_lands,
        feed_share,
        expand_share,
        project_share,
        mixing_share,
        small_ref,
        plane_lands,
        deep_lands,
        held_sem,
        half_sem,
        part_sem,
        out_sem,
        feed_sem,
        feed_send,
        feed_recv,
        spread_sem,
        spread_far_send,
        spread_far_recv,
        spread_near_send,
        spread_near_recv,
        plane_send,
        plane_recv,
        deep_send,
        deep_recv,
        row_send,
        row_recv,
        mixed_sem,
        near_send,
        near_recv,
        far_send,
        far_recv,
        line_send,
        line_recv,
    ) = refs[10:]
    (
        project,
        grads_other,
        grads_own,
        hidden_other,
        hidden_own,
        mixed_other,
        mixed_own,
        back_other,
        back_own,
        inputs,
    ) = held
    low, f32 = jnp.bfloat16, jnp.float32
    tn = (((0,), (0,)), ((), ()))
    place, deep, outers = lax.axis_index("dp"), 4, 4
    outer = lax.axis_index("outer")
    far, near = outer // 2, outer % 2
    row_id = {"mp": 1 - lax.axis_index("mp")}
    far_id = {"outer": (outer + 2) % 4}
    near_id = {"outer": outer + 1 - 2 * near}

    copies = [
        pltpu.make_async_copy(source, target, held_sem.at[n])
        for n, (source, target) in enumerate(zip(sources, held))
        if n
    ]
    copies.insert(0, None)
    quarter = feed_keep.shape[1]
    feed_copies = [
        (
            pltpu.make_async_copy(
                feed_keep.at[k],
                total_ref.at[slice(k * quarter, (k + 1) * quarter)],
                feed_sem.at[k],
            ),
            pltpu.make_async_copy(feed_come.at[k], feed_in.at[k], feed_sem.at[2 + k]),
        )
        for k in range(2)
    ]
    for pair in feed_copies:
        for copy in pair:
            copy.start()
    cut = project.shape[0] // 2
    halves = [
        pltpu.make_async_copy(
            source.at[slice(0, cut)], project.at[slice(n * cut, (n + 1) * cut)], half_sem.at[n]
        )
        for n, source in enumerate((own_weights, sibling_weights))
    ]
    for copy in (*halves, copies[1]):
        copy.start()
    barrier = pltpu.get_barrier_semaphore()
    plane = 2 * outers
    me = lax.axis_index("mp") * outers + outer

    def plane_id(step):
        other = (me + step) % plane
        return {"mp": other // outers, "outer": other % outers}

    for step in range(1, plane):
        pl.semaphore_signal(barrier, inc=1, device_id=plane_id(step), device_id_type=MESH)
    for step in range(1, deep):
        pl.semaphore_signal(
            barrier, inc=1, device_id={"dp": (place + step) % deep}, device_id_type=MESH
        )
    height = 256
    tokens, width = hidden_own.shape
    blocks = tokens // height
    at = [slice(n * height, (n + 1) * height) for n in range(blocks)]

    def remote(source, target, send, recv, device):
        return pltpu.make_async_remote_copy(
            src_ref=source,
            dst_ref=target,
            send_sem=send,
            recv_sem=recv,
            device_id=device,
            device_id_type=MESH,
        )

    loads = [
        pltpu.make_async_copy(source.at[at[n]], part_in.at[(k * blocks + n) % 2], part_sem.at[(k * blocks + n) % 2])
        for k, source in enumerate((part_other, part_own))
        for n in range(blocks)
    ]
    loads[0].start()
    loads[1].start()
    pl.semaphore_wait(barrier, plane + deep - 2)

    piece = width // deep

    def columns(place):
        return pl.ds(pl.multiple_of(place * piece, piece), piece)

    line_copies = []
    for k in range(2):
        for copy in feed_copies[k]:
            copy.wait()
        rows = slice(k * quarter, (k + 1) * quarter)
        for step in range(1, deep):
            target = (place + step) % deep
            feed_line[k, step - 1] = (
                total_ref[rows, columns(target)] + feed_in[k, :, columns(target)].astype(f32)
            ).astype(low)
            line_copies.append(
                remote(
                    feed_line.at[k, step - 1],
                    feed_lands.at[k, step - 1],
                    feed_send.at[k, step - 1],
                    feed_recv.at[k, step - 1],
                    {"dp": target},
                )
            )
            line_copies[-1].start()
        feed_share[k] = total_ref[rows, columns(place)] + feed_in[k, :, columns(place)].astype(f32)

    for copy in (*halves, copies[1]):
        copy.wait()
    for copy in copies[2:]:
        copy.start()
    row_copies = []
    for n in range(blocks):
        made = lax.dot_general(grads_other[:, at[n]], project[...], tn, preferred_element_type=f32)
        loads[n].wait()
        sent_ref[at[n], :] = (part_in[n % 2] + made).astype(low)
        loads[n + 2].start()
        copy = remote(
            sent_ref.at[at[n]], come_ref.at[at[n]], row_send.at[n], row_recv.at[n], row_id
        )
        copy.start()
        row_copies.append(copy)

    copies[5].wait()
    mixed_copy = remote(
        mixed_other.at[slice(0, mixed_come.shape[0])],
        mixed_come,
        mixed_sem.at[0],
        mixed_sem.at[1],
        row_id,
    )
    mixed_copy.start()

    for n in (2, 3, 4, 6, 7, 8):
        copies[n].wait()
    half = project_own.shape[0]
    few = mixing_own.shape[0]
    near_copies = []
    for n in range(half // height):
        rows = slice(half + n * height, half + (n + 1) * height)
        total_ref[at[n], :] = jnp.dot(
            grads_own[rows, :], hidden_own[...], preferred_element_type=f32
        ) + jnp.dot(grads_other[rows, :], hidden_other[...], preferred_element_type=f32)
        near_copies.append(
            remote(
                total_ref.at[at[n]],
                project_land.at[at[n]],
                near_send.at[n],
                near_recv.at[n],
                near_id,
            )
        )
        near_copies[-1].start()
    total_ref[half : half + few, :] = jnp.dot(
        mixed_own[few:, :], back_own[...], preferred_element_type=f32
    ) + jnp.dot(mixed_other[few:, :], back_other[...], preferred_element_type=f32)
    near_copies.append(
        remote(
            total_ref.at[slice(half, half + few)],
            mixing_land,
            near_send.at[3],
            near_recv.at[3],
            near_id,
        )
    )
    near_copies[-1].start()
    for n in range(half // height):
        made = jnp.dot(
            grads_own[at[n], :], hidden_own[...], preferred_element_type=f32
        ) + jnp.dot(grads_other[at[n], :], hidden_other[...], preferred_element_type=f32)
        near_copies[n].wait()
        project_own[at[n], :] = made + project_land[at[n], :]

    def to_far(own, send, come, n):
        size = send.shape[0]
        send[...] = own[pl.ds(pl.multiple_of((1 - far) * size, size), size), :].astype(low)
        copy = remote(send, come, far_send.at[n], far_recv.at[n], far_id)
        copy.start()
        return copy

    far_copies = [to_far(project_own, project_far, project_come, 0)]
    made = jnp.dot(mixed_own[:few, :], back_own[...], preferred_element_type=f32) + jnp.dot(
        mixed_other[:few, :], back_other[...], preferred_element_type=f32
    )
    near_copies[3].wait()
    mixing_own[...] = made + mixing_land[...]
    far_copies.append(to_far(mixing_own, mixing_far, mixing_come, 1))

    for n in range(blocks):
        made = lax.dot_general(grads_own[:, at[n]], project[...], tn, preferred_element_type=f32)
        loads[blocks + n].wait()
        total_ref[at[n], :] = part_in[(blocks + n) % 2] + made
        if n + 2 < blocks:
            loads[blocks + n + 2].start()

    for k, (own, come, line, lands) in enumerate(
        (
            (project_own, project_come, project_line, project_lands),
            (mixing_own, mixing_come, mixing_line, mixing_lands),
        )
    ):
        size = come.shape[0]
        keep = pl.ds(pl.multiple_of(far * size, size), size)
        far_copies[k].wait()
        own[keep, :] = own[keep, :] + come[...].astype(f32)
        for step in range(1, deep):
            target = (place + step) % deep
            line[step - 1] = own[keep, columns(target)].astype(low)
            copy = remote(
                line.at[step - 1],
                lands.at[step - 1],
                line_send.at[k, step - 1],
                line_recv.at[k, step - 1],
                {"dp": target},
            )
            copy.start()
            line_copies.append(copy)

    shares = (feed_share.at[0], expand_share, project_share, mixing_share)

    def place_in(k, near, far):
        if k == 1:
            return full_refs[k].at[:, pl.ds(pl.multiple_of((2 * near + far) * quarter, quarter), quarter)]
        size = shares[k].shape[0]
        return full_refs[k].at[pl.ds(pl.multiple_of((2 * near + far) * size, size), size)]

    def spread(k):
        if k < 2:
            result, lands = feed_share[k], feed_lands.at[k]
        else:
            own, lands = ((project_own, project_lands), (mixing_own, mixing_lands))[k - 2]
            size = shares[k].shape[0]
            result = own[pl.ds(pl.multiple_of(far * size, size), size), columns(place)]
        for copy in line_copies[3 * k : 3 * k + 3]:
            copy.wait()
        for step in range(1, deep):
            result = result + lands[step - 1].astype(f32)
        shares[k][...] = result.T if k == 1 else result
        here = place_in(k, near, far)
        copies = [
            pltpu.make_async_copy(shares[k], here, spread_sem.at[k]),
            remote(shares[k], here, spread_far_send.at[k], spread_far_recv.at[k], far_id),
            remote(shares[k], here, spread_near_send.at[k, 0], spread_near_recv.at[k, 0], near_id),
        ]
        for copy in copies:
            copy.start()
        return copies, jnp.sum(result * result)

    def pass_on(k, copies):
        copies[1].wait()
        there = place_in(k, near, 1 - far)
        copy = remote(
            there, there, spread_near_send.at[k, 1], spread_near_recv.at[k, 1], near_id
        )
        copy.start()
        return copy

    copies[9].wait()
    gain = gain_ref[0:1]
    gain_sum = jnp.zeros((1, width), f32)
    bias_sum = jnp.zeros((1, width), f32)
    out_copies, spreads, passed = [], [], []
    square = jnp.float32(0.0)
    for n in range(blocks):
        if n == blocks - 2:
            for k in range(2):
                copies, more = spread(k)
                spreads.append(copies)
                square = square + more
        if n == blocks - 1:
            for k in range(2, 4):
                copies, more = spread(k)
                spreads.append(copies)
                square = square + more
        row_copies[n].wait()
        if n >= 2:
            out_copies[n - 2].wait()

        def some(i, carry):
            gain_sum, bias_sum = carry
            small = 64
            rows = pl.ds(pl.multiple_of(n * height + i * small, small), small)
            x = inputs[rows, :].astype(f32)
            mean = jnp.mean(x, axis=1, keepdims=True)
            centred = x - mean
            spread = jnp.mean(centred * centred, axis=1, keepdims=True)
            inverse = lax.rsqrt(spread + norm_epsilon)
            normed = centred * inverse
            grad = total_ref[rows, :] + come_ref[rows, :].astype(f32)
            scaled = grad * gain
            middle = jnp.mean(scaled, axis=1, keepdims=True)
            along = jnp.mean(scaled * normed, axis=1, keepdims=True)
            result = inverse * (scaled - middle - normed * along)
            part_in[n % 2, pl.ds(pl.multiple_of(i * small, small), small), :] = (
                back_own[rows, :].astype(f32) + result
            )
            gain_sum = gain_sum + jnp.sum(grad * normed, axis=0, keepdims=True)
            bias_sum = bias_sum + jnp.sum(grad, axis=0, keepdims=True)
            return gain_sum, bias_sum

        gain_sum, bias_sum = lax.fori_loop(0, height // 64, some, (gain_sum, bias_sum))
        out_copies.append(
            pltpu.make_async_copy(part_in.at[n % 2], input_grad.at[at[n]], out_sem.at[n % 2])
        )
        out_copies[-1].start()
    for k in range(2):
        passed.append(pass_on(k, spreads[k]))

    small_ref[...] = jnp.full(small_ref.shape, square)
    small_ref[0:1] = gain_sum
    small_ref[1:2] = bias_sum

    def everywhere(lands, send, recv, size, index, device):
        copies = []
        for step in range(1, size):
            copy = remote(small_ref, lands.at[step], send.at[step], recv.at[step], device(step))
            copy.start()
            copies.append(copy)
        lands[0] = small_ref[...]
        for copy in copies:
            copy.wait()
        total = lands[index]
        for at in range(1, size):
            total = total + lands[(index + size - at) % size]
        small_ref[...] = total

    everywhere(plane_lands, plane_send, plane_recv, plane, me, plane_id)
    everywhere(
        deep_lands, deep_send, deep_recv, deep, place, lambda step: {"dp": (place + step) % deep}
    )
    for k in range(2, 4):
        passed.append(pass_on(k, spreads[k]))
    small = small_ref[0:2]
    norm = jnp.sqrt(small_ref[2:3] + jnp.sum(small * small))
    small_sum[...] = small_ref[...]
    small_sum[2:3] = norm
    small_sum[3:4] = clip_level / jnp.maximum(norm, clip_level)
    for k in range(4):
        spreads[k][0].wait()
        spreads[k][2].wait()
        passed[k].wait()
    mixed_copy.wait()
    for copy in out_copies[-2:]:
        copy.wait()


def closing(weights, grads, hiddens, mixed, backs, inputs, parts, feeds, gain, after):
    deep = 4
    low, f32 = jnp.bfloat16, jnp.float32
    tokens, width = inputs.shape
    half, few = grads[0].shape[0] // 2, mixed[0].shape[0] // 2
    piece = width // deep
    quarter = feeds[0].shape[1]
    anywhere = pl.BlockSpec(memory_space=pl.ANY)
    here = lambda: pl.BlockSpec(memory_space=pltpu.VMEM)
    held = (
        jax.ShapeDtypeStruct(grads[0].shape[:1] + (width,), low),
        grads[1],
        grads[0],
        hiddens[1],
        hiddens[0],
        mixed[1],
        mixed[0],
        backs[1],
        backs[0],
        inputs,
    )
    sem = pltpu.SemaphoreType.DMA
    space = pltpu.VMEM
    return pl.pallas_call(
        partial(closing_kernel, len(after)),
        in_specs=[anywhere] * 15 + [here()] + [anywhere] * len(after),
        out_specs=[anywhere, here()] + [anywhere] * 5,
        out_shape=[
            jax.ShapeDtypeStruct((tokens, width), f32),
            jax.ShapeDtypeStruct((8, width), f32),
            jax.ShapeDtypeStruct((few, tokens), low),
        ]
        + [
            jax.ShapeDtypeStruct(shape, f32)
            for shape in (
                (4 * quarter, piece),
                (piece, 4 * quarter),
                (2 * half, piece),
                (2 * few, piece),
            )
        ],
        scratch_shapes=[space(v.shape, v.dtype) for v in held]
        + [
            space((2, 256, width), f32),
            space((tokens, width), f32),
            space((tokens, width), low),
            space((tokens, width), low),
            space((half, width), f32),
            space((half, width), f32),
            space((few, width), f32),
            space((few, width), f32),
            space((half // 2, width), low),
            space((half // 2, width), low),
            space((few // 2, width), low),
            space((few // 2, width), low),
            space((deep - 1, half // 2, piece), low),
            space((deep - 1, half // 2, piece), low),
            space((deep - 1, few // 2, piece), low),
            space((deep - 1, few // 2, piece), low),
            space((2, quarter, width), low),
            space((2, deep - 1, quarter, piece), low),
            space((2, deep - 1, quarter, piece), low),
            space((2, quarter, piece), f32),
            space((piece, quarter), f32),
            space((half // 2, piece), f32),
            space((few // 2, piece), f32),
            space((8, width), f32),
            space((8, 8, width), f32),
            space((deep, 8, width), f32),
            sem((len(held),)),
            sem((2,)),
            sem((2,)),
            sem((2,)),
            sem((4,)),
            sem((2, deep - 1)),
            sem((2, deep - 1)),
            sem((4,)),
            sem((4,)),
            sem((4,)),
            sem((4, 2)),
            sem((4, 2)),
            sem((8,)),
            sem((8,)),
            sem((deep,)),
            sem((deep,)),
            sem((tokens // 256,)),
            sem((tokens // 256,)),
            sem((2,)),
            sem((4,)),
            sem((4,)),
            sem((2,)),
            sem((2,)),
            sem((2, deep)),
            sem((2, deep)),
        ],
        compiler_params=pltpu.CompilerParams(
            collective_id=3, has_side_effects=True, vmem_limit_bytes=62 * 2**20
        ),
        cost_estimate=pl.CostEstimate(flops=2**20, bytes_accessed=2**20, transcendentals=0),
    )(*weights, *held[1:], *parts, *feeds, gain, *after)


def local(
    inputs,
    cotangent,
    lengths,
    project_master,
    project_first,
    project_second,
    mixing_master,
    mixing_first,
    mixing_second,
    expand_master,
    expand_first,
    expand_second,
    shrink_master,
    shrink_first,
    shrink_second,
    norm_master,
    norm_first,
    norm_second,
):
    split, deep = lax.axis_size("mp"), lax.axis_size("dp")
    heads_here = project_master.shape[1]
    width = inputs.shape[1]
    paired = (
        split == 2
        and lax.axis_size("outer") == 4
        and heads_here % 4 == 0
        and width % BQ == 0
    )
    position = lax.axis_index("mp")
    count = width * split
    project_flat = project_master.transpose(1, 2, 0).reshape(heads_here * 3 * HD, -1)
    mixing_flat = mixing_master.reshape(heads_here * HD, mixing_master.shape[2])
    masters = (project_flat, mixing_flat, expand_master, shrink_master)
    depths = (1, 1, 0, 1)
    rows_local = inputs[0].astype(jnp.float32)
    begins, places = layout(lengths[0], count)
    cosine, sine = turns(places)
    if paired:
        expand, shrink, later, norm_weight, hidden_local, other_back = opening(
            expand_master,
            shrink_master,
            project_flat,
            mixing_flat,
            norm_master,
            inputs[0],
            cotangent[0],
        )
        backs = [cotangent[0], other_back]
        shrink = shrink.reshape(-1, shrink.shape[2])
        later = lax.all_gather(later, "dp", axis=1, tiled=True)
        hiddens = [hidden_local, swap(hidden_local, "mp", 1)]
    else:
        norm_weight = lax.all_gather(norm_master.astype(jnp.bfloat16), "dp", axis=1, tiled=True)
        gain = norm_weight[0].astype(jnp.float32)
        bias = norm_weight[1].astype(jnp.float32)
        shaped, norm_pull = jax.vjp(layer_norm, rows_local, gain, bias)
        hidden_local = shaped.astype(jnp.bfloat16)
        project, mixing, expand, shrink = (
            lax.all_gather(master.astype(jnp.bfloat16), "dp", axis=depth, tiled=True)
            for master, depth in zip(masters, depths)
        )
        backs = [lax.all_gather(cotangent[0], "mp", axis=0, tiled=True)]
        hiddens = [lax.all_gather(hidden_local, "mp", axis=0, tiled=True)]

    def over_tokens(pattern, lefts, rights):
        return sum(product(pattern, left, right) for left, right in zip(lefts, rights))

    back_local = cotangent[0].astype(jnp.float32)
    if paired:
        *grads, hidden_own, branch_own = feed(
            hiddens[0], backs[0], expand, shrink, (), jnp.float32
        )
        later = follow(later, branch_own)
        later = [later, swap(later, "outer", 1)]
        cut = later[0].shape[0] * 3 // 4
        mixing = jnp.concatenate([v[cut:] for v in later])
        own_columns = project_all(hiddens[0], backs[0], *later)
        feed_keep, feed_away, _, hidden_other, branch_other = feed(
            hiddens[1], backs[1], expand, follow(shrink, *own_columns), grads, jnp.bfloat16
        )
        feed_come = swap(feed_away, "outer", 2)
        branch_come = swap(branch_other, "mp", 1)
        mixing_other = swap(mixing, "mp", 1)
        other_columns = project_all(hiddens[1], backs[1], *later)
        projected, mixed_backs = zip(own_columns, other_columns)
        mixed, projected_grads = attend(
            projected,
            mixed_backs,
            begins,
            cosine,
            sine,
            position,
            (feed_away, branch_other),
        )
        input_grad, small_sum, mixed_come, shrink_sum, expand_sum, project_sum, mixing_sum = closing(
            later,
            projected_grads,
            hiddens,
            mixed,
            backs,
            inputs[0],
            (hidden_own, hidden_other),
            (feed_keep, feed_come),
            norm_weight,
            (branch_come,),
        )
        mixed_own = follow(mixed[0], small_sum)
        few = mixed_come.shape[0]
        mixed_last = swap(follow(mixed[1], small_sum)[few:], "mp", 1)
        branch = (
            branch_own
            + branch_come.astype(jnp.float32)
            + product("ft,fd->td", mixed_own, mixing)
            + product("ft,fd->td", mixed_come, mixing_other[:few])
            + product("ft,fd->td", mixed_last, mixing_other[few:])
        )
    else:
        lifteds = [product("td,df->tf", hidden, expand) for hidden in hiddens]
        activated = [gelu(lifted) for lifted in lifteds]
        active_grads = [product("td,fd->tf", back, shrink) for back in backs]
        lifted_grads = [gelu_both(a, b) for a, b in zip(lifteds, active_grads)]
        hidden_parts = [product("tf,df->td", v, expand) for v in lifted_grads]
        branch_parts = [product("tf,fd->td", v, shrink) for v in activated]
        projected = [product("td,ed->et", hidden, project) for hidden in hiddens]
        mixed_backs = [product("td,fd->ft", back, mixing).astype(jnp.bfloat16) for back in backs]
        mixed, projected_grads = attend(projected, mixed_backs, begins, cosine, sine, position)
        project_sum, mixing_sum, expand_sum, shrink_sum = (
            lax.psum(
                lax.psum_scatter(
                    over_tokens(pattern, lefts, rights),
                    "dp",
                    scatter_dimension=depth,
                    tiled=True,
                ),
                "outer",
            )
            for pattern, lefts, rights, depth in (
                ("et,td->ed", projected_grads, hiddens, 1),
                ("ft,td->fd", mixed, backs, 1),
                ("td,tf->df", hiddens, lifted_grads, 0),
                ("tf,td->fd", activated, backs, 1),
            )
        )
        hidden_grad, branch = (
            lax.psum_scatter(v, "mp", scatter_dimension=0, tiled=True)
            for v in (
                hidden_parts[0] + product("et,ed->td", projected_grads[0], project),
                branch_parts[0] + product("ft,fd->td", mixed[0], mixing),
            )
        )
        rows_grad, gain_grad, bias_grad = norm_pull(hidden_grad)
        input_grad = back_local + rows_grad
        norm_terms = jnp.stack([gain_grad, bias_grad])
    input_grad = input_grad[None]
    block_out = (rows_local + branch).astype(jnp.bfloat16)[None]
    sums = (project_sum, mixing_sum, expand_sum, shrink_sum)
    if not paired:
        own_square = sum(jnp.sum(v * v) for v in sums) / lax.axis_size("outer")
        small_sum = lax.psum(
            jnp.concatenate([norm_terms, jnp.full((1, D), own_square)]), ("mp", "dp", "outer")
        )
        square = small_sum[2, 0] + jnp.sum(small_sum[:2] * small_sum[:2])
        grad_norm = jnp.sqrt(square)
        factor = clip_level / jnp.maximum(grad_norm, clip_level)
    else:
        grad_norm, factor = small_sum[2, 0], small_sum[3, 0]
    norm_full = small_sum[:2]
    norm_gradient = lax.dynamic_slice_in_dim(
        norm_full, lax.axis_index("dp") * (D // deep), D // deep, 1
    )
    gradients = list(sums)
    gradients[0] = gradients[0].reshape(heads_here, 3 * HD, -1).transpose(2, 0, 1)
    gradients[1] = gradients[1].reshape(mixing_master.shape)
    gradients[:2] = lax.optimization_barrier(gradients[:2])
    states = (
        (project_master, project_first, project_second, D ** (-0.5)),
        (mixing_master, mixing_first, mixing_second, (D // 32) ** (-0.5)),
        (expand_master, expand_first, expand_second, D ** (-0.5)),
        (shrink_master, shrink_first, shrink_second, FF ** (-0.5)),
    )
    results = [block_out, input_grad]
    for (master, first, second, rate), gradient in zip(states, gradients):
        results += adam_update(master, first, second, factor * gradient, rate, decay_rate)
    results += adam_update(norm_master, norm_first, norm_second, factor * norm_gradient, 0.3, 0.0)
    return (*results, grad_norm)


def solution(mesh):
    in_specs = (
        P(("dp", "outer"), "mp", None),
        P(("dp", "outer"), "mp", None),
        P(("dp", "outer"), None),
        P("dp", "mp", None),
        P("dp", "mp", None),
        P("dp", "mp", None),
        P("mp", None, "dp"),
        P("mp", None, "dp"),
        P("mp", None, "dp"),
        P("dp", "mp"),
        P("dp", "mp"),
        P("dp", "mp"),
        P("mp", "dp"),
        P("mp", "dp"),
        P("mp", "dp"),
        P(None, "dp"),
        P(None, "dp"),
        P(None, "dp"),
    )
    out_specs = (
        P(("dp", "outer"), "mp", None),
        P(("dp", "outer"), "mp", None),
        P("dp", "mp", None),
        P("dp", "mp", None),
        P("dp", "mp", None),
        P("dp", "mp", None),
        P("mp", None, "dp"),
        P("mp", None, "dp"),
        P("mp", None, "dp"),
        P("mp", None, "dp"),
        P("dp", "mp"),
        P("dp", "mp"),
        P("dp", "mp"),
        P("dp", "mp"),
        P("mp", "dp"),
        P("mp", "dp"),
        P("mp", "dp"),
        P("mp", "dp"),
        P(None, "dp"),
        P(None, "dp"),
        P(None, "dp"),
        P(None, "dp"),
        P(),
    )
    return jax.shard_map(local, mesh=mesh, in_specs=in_specs, out_specs=out_specs, check_vma=False)
```

```python
from functools import partial
import math

import jax
import jax.numpy as jnp
from jax import lax
from jax.experimental import pallas as pl
from jax.experimental.pallas import tpu as pltpu
from jax.sharding import PartitionSpec as P

D = 1024
HD = 64
ROT = 32
FF = 4096
STEP = 10


norm_epsilon = 1e-05
beta_one = 0.9
beta_two = 0.95
adam_epsilon = 1e-08
decay_rate = 0.1
clip_level = 1.0
masked_value = -1e30


def layout(sizes_row, count):
    number = jnp.arange(sizes_row.shape[0], dtype=jnp.int32)
    ends = jnp.sum(jnp.where(number[None, :] <= number[:, None], sizes_row[None, :], 0), axis=1)
    tokens = jnp.arange(count, dtype=jnp.int32)
    passed = (ends[:, None] <= tokens[None, :]).astype(jnp.int32)
    begins = jnp.sum(passed * sizes_row[:, None], axis=0)
    return (begins, tokens - begins)


def turns(places):
    half_rot = ROT // 2
    counter = jnp.arange(half_rot, dtype=jnp.float32)
    frequency = jnp.exp(counter * (-2.0 * math.log(10000.0) / ROT))
    angles = places.astype(jnp.float32)[None, :] * frequency[:, None]
    return jnp.cos(angles), jnp.sin(angles)


BQ = 256
BK = 256


def attend_kernel(together, parts, later, *refs):
    facts = refs[0]
    projected_refs = refs[1 : 1 + parts]
    back_refs = refs[1 + parts : 1 + 2 * parts]
    start_ref, cos_ref, sin_ref = refs[1 + 2 * parts : 4 + 2 * parts]
    refs = refs[: 4 + 2 * parts] + refs[4 + 2 * parts + later :]
    mixed_refs = refs[4 + 2 * parts : 4 + 3 * parts]
    grad_refs = refs[4 + 3 * parts : 4 + 4 * parts]
    (
        query_ref,
        key_columns_ref,
        value_columns_ref,
        key_ref,
        value_ref,
        back_ref,
        query_grad_ref,
        key_grad_ref,
        value_grad_ref,
        shifted_ref,
        share_grad_ref,
        top_ref,
    ) = refs[4 + 4 * parts :]
    width = projected_refs[0].shape[1]
    count = width * parts
    blocks = count // BQ
    turn = facts[blocks]
    half = ROT // 2
    scale = HD ** (-0.5)

    def place_of(part):
        if parts == 1:
            return pl.ds(0, width)
        block = lax.rem(part * (blocks // parts) + blocks - turn, blocks)
        return pl.ds(pl.multiple_of(block * BQ, BQ), width)

    for part in range(parts):
        columns = slice(part * width, (part + 1) * width)
        cosine, sine = cos_ref[:, place_of(part)], sin_ref[:, place_of(part)]
        projected_ref = projected_refs[part]

        def turned(at):
            first = projected_ref[at : at + half]
            second = projected_ref[at + half : at + ROT]
            return jnp.concatenate(
                [
                    first * cosine - second * sine,
                    second * cosine + first * sine,
                    projected_ref[at + ROT : at + HD],
                ],
                axis=0,
            ).astype(jnp.bfloat16)

        for h in range(together):
            base = h * 3 * HD
            query_ref[h, :, columns] = (turned(base).astype(jnp.float32) * scale).astype(
                jnp.bfloat16
            )
            keys = turned(base + HD)
            values = projected_ref[base + 2 * HD : base + 3 * HD].astype(jnp.bfloat16)
            key_columns_ref[h, :, columns] = keys
            value_columns_ref[h, :, columns] = values
            key_ref[h, columns] = keys.T
            value_ref[h, columns] = values.T
            back_ref[h, :, columns] = back_refs[part][h * HD : (h + 1) * HD]
    key_grad_ref[...] = jnp.zeros_like(key_grad_ref)
    value_grad_ref[...] = jnp.zeros_like(value_grad_ref)
    key_at = lax.broadcasted_iota(jnp.int32, (BK, BQ), 0)
    query_at = lax.broadcasted_iota(jnp.int32, (1, BQ), 1)

    def stored(block):
        if parts == 1:
            return pl.ds(pl.multiple_of(block * BQ, BQ), BQ)
        return pl.ds(pl.multiple_of(lax.rem(block + turn, blocks) * BQ, BQ), BQ)

    def query_block(i, _):
        columns = stored(i)
        start = start_ref[:, pl.ds(pl.multiple_of(i * BQ, BQ), BQ)]
        own = query_at + i * BQ
        lowest = facts[i]
        queries = [query_ref[h, :, columns] for h in range(together)]
        backs = [back_ref[h, :, columns] for h in range(together)]
        query_rows = [queries[h].T for h in range(together)]
        back_rows = [backs[h].T for h in range(together)]

        def in_pairs(body, carry):
            twos = lax.div(i + 1 - lowest, 2)
            carry = lax.fori_loop(
                0, twos, lambda n, c: body((lowest + 2 * n, lowest + 2 * n + 1), c), carry
            )
            return lax.fori_loop(lowest + 2 * twos, i + 1, lambda n, c: body((n,), c), carry)

        def scores(group, carry):
            made = []
            for j in group:
                rows = stored(j)
                allowed = (key_at >= start - j * BK) & (key_at <= own - j * BK)
                for h in range(together):
                    raw = jnp.dot(
                        key_ref[h, rows, :], queries[h], preferred_element_type=jnp.float32
                    )
                    share_grad = jnp.dot(
                        value_ref[h, rows, :], backs[h], preferred_element_type=jnp.float32
                    )
                    masked = jnp.where(allowed, raw, masked_value)
                    here = jnp.max(masked, axis=0, keepdims=True)
                    shifted = jnp.exp(masked - here)
                    shifted_ref[h, j] = shifted
                    share_grad_ref[h, j] = share_grad
                    top_ref[h, j] = here
                    made.append(
                        (
                            here,
                            jnp.sum(shifted, axis=0, keepdims=True),
                            jnp.sum(shifted * share_grad, axis=0, keepdims=True),
                        )
                    )
            out = []
            for h in range(together):
                top, total, inner = carry[h]
                for here, here_total, here_inner in made[h::together]:
                    new = jnp.maximum(top, here)
                    old_by, here_by = jnp.exp(top - new), jnp.exp(here - new)
                    total = total * old_by + here_total * here_by
                    inner = inner * old_by + here_inner * here_by
                    top = new
                out.append((top, total, inner))
            return tuple(out)

        zero = jnp.zeros((1, BQ), jnp.float32)
        empty = (jnp.full((1, BQ), masked_value, jnp.float32), zero, zero)
        stats = in_pairs(scores, (empty,) * together)
        inverse = [1.0 / s[1] for s in stats]
        inners = [s[2] * r for s, r in zip(stats, inverse)]

        def sums(group, carry):
            out = list(carry)
            for j in group:
                rows = stored(j)
                for h in range(together):
                    mixed, query_grad = out[h]
                    by = jnp.exp(top_ref[h, j] - stats[h][0]) * inverse[h]
                    probs = shifted_ref[h, j] * by
                    shares = probs.astype(jnp.bfloat16)
                    score_grad = (probs * (share_grad_ref[h, j] - inners[h])).astype(jnp.bfloat16)
                    mixed = mixed + jnp.dot(
                        value_columns_ref[h, :, rows], shares, preferred_element_type=jnp.float32
                    )
                    query_grad = query_grad + jnp.dot(
                        key_columns_ref[h, :, rows], score_grad, preferred_element_type=jnp.float32
                    )
                    value_grad_ref[h, rows, :] += jnp.dot(
                        shares, back_rows[h], preferred_element_type=jnp.float32
                    )
                    key_grad_ref[h, rows, :] += jnp.dot(
                        score_grad, query_rows[h], preferred_element_type=jnp.float32
                    )
                    out[h] = (mixed, query_grad)
            return tuple(out)

        nothing = jnp.zeros((HD, BQ), jnp.float32)
        results = in_pairs(sums, ((nothing, nothing),) * together)
        for h in range(together):
            back_ref[h, :, columns] = results[h][0].astype(jnp.bfloat16)
            query_grad_ref[h, :, columns] = results[h][1] * scale
        return 0

    lax.fori_loop(0, blocks, query_block, 0)
    for part in range(parts):
        columns = slice(part * width, (part + 1) * width)
        cosine, sine = cos_ref[:, place_of(part)], sin_ref[:, place_of(part)]

        def turned_back(grad):
            first, second = grad[:half], grad[half:ROT]
            return jnp.concatenate(
                [
                    first * cosine + second * sine,
                    second * cosine - first * sine,
                    grad[ROT:],
                ],
                axis=0,
            ).astype(jnp.bfloat16)

        for h in range(together):
            base = h * 3 * HD
            mixed_refs[part][h * HD : (h + 1) * HD] = back_ref[h, :, columns]
            grad_refs[part][base : base + HD] = turned_back(query_grad_ref[h, :, columns])
            grad_refs[part][base + HD : base + 2 * HD] = turned_back(key_grad_ref[h, columns, :].T)
            grad_refs[part][base + 2 * HD : base + 3 * HD] = value_grad_ref[
                h, columns, :
            ].T.astype(jnp.bfloat16)


def attend(projected, back, begins, cosine, sine, offset, after=()):
    parts = len(projected)
    heads = back[0].shape[0] // HD
    width = back[0].shape[1]
    count = begins.shape[0]
    together = 2 if heads % 2 == 0 else 1
    blocks = count // BK
    half = ROT // 2
    turn = jnp.asarray(offset * ((blocks // parts) if parts > 1 else 0), jnp.int32)
    facts = jnp.concatenate([begins[::BQ] // BK, turn[None]])
    whole = lambda rows: pl.BlockSpec((rows, count), lambda g, *_: (0, 0))
    mine = lambda rows: pl.BlockSpec((rows, width), lambda g, *_: (g, 0))
    results = pl.pallas_call(
        partial(attend_kernel, together, parts, len(after)),
        grid_spec=pltpu.PrefetchScalarGridSpec(
            num_scalar_prefetch=1,
            grid=(heads // together,),
            in_specs=[mine(together * 3 * HD)] * parts
            + [mine(together * HD)] * parts
            + [whole(1), whole(half), whole(half)]
            + [pl.BlockSpec(memory_space=pl.ANY)] * len(after),
            out_specs=[mine(together * HD)] * parts + [mine(together * 3 * HD)] * parts,
            scratch_shapes=[
                pltpu.VMEM((together, HD, count), jnp.bfloat16),
                pltpu.VMEM((together, HD, count), jnp.bfloat16),
                pltpu.VMEM((together, HD, count), jnp.bfloat16),
                pltpu.VMEM((together, count, HD), jnp.bfloat16),
                pltpu.VMEM((together, count, HD), jnp.bfloat16),
                pltpu.VMEM((together, HD, count), jnp.bfloat16),
                pltpu.VMEM((together, HD, count), jnp.float32),
                pltpu.VMEM((together, count, HD), jnp.float32),
                pltpu.VMEM((together, count, HD), jnp.float32),
                pltpu.VMEM((together, blocks, BK, BQ), jnp.float32),
                pltpu.VMEM((together, blocks, BK, BQ), jnp.float32),
                pltpu.VMEM((together, blocks, 1, BQ), jnp.float32),
            ],
        ),
        out_shape=[jax.ShapeDtypeStruct((heads * HD, width), jnp.bfloat16)] * parts
        + [jax.ShapeDtypeStruct((heads * 3 * HD, width), jnp.bfloat16)] * parts,
        compiler_params=pltpu.CompilerParams(vmem_limit_bytes=48 * 2**20),
        cost_estimate=pl.CostEstimate(
            flops=2**20,
            bytes_accessed=2**20,
            transcendentals=0,
        ),
    )(facts, *projected, *back, begins[None, :], cosine, sine, *after)
    return results[:parts], results[parts:]


def layer_norm(rows_in, gain, bias):
    mean = jnp.mean(rows_in, axis=1, keepdims=True)
    centred = rows_in - mean
    spread = jnp.mean(centred * centred, axis=1, keepdims=True)
    normed = centred * lax.rsqrt(spread + norm_epsilon)
    return normed * gain + bias


def adam_update(master, first, second, gradient, rate, decay):
    first_new = beta_one * first + (1.0 - beta_one) * gradient
    second_new = beta_two * second + (1.0 - beta_two) * gradient * gradient
    first_hat = first_new / (1.0 - beta_one**STEP)
    second_hat = second_new / (1.0 - beta_two**STEP)
    master_new = master - rate * (
        first_hat / (jnp.sqrt(second_hat) + adam_epsilon) + decay * master
    )
    return (master_new, first_new, second_new, master_new.astype(jnp.bfloat16))


def product(pattern, left, right):
    return jnp.einsum(pattern, left, right, preferred_element_type=jnp.float32)


def gelu_both(lifted, active_grad):
    activated, pull = jax.vjp(partial(jax.nn.gelu, approximate=True), lifted)
    return pull(active_grad)[0].astype(jnp.bfloat16)


def gelu(lifted):
    return jax.nn.gelu(lifted, approximate=True).astype(jnp.bfloat16)


def swap(array, axis, bit):
    size = lax.axis_size(axis)
    return lax.ppermute(array, axis, [(i, i ^ bit) for i in range(size)])


def follow(array, *before):
    return lax.optimization_barrier((array, *before))[0]


ROWS = 640


MESH = pl.DeviceIdType.MESH


def feed_kernel(exchange, later, hidden_ref, back_ref, expand_ref, shrink_ref, *refs):
    step, steps = pl.program_id(0), pl.num_programs(0)
    f32 = jnp.float32
    if exchange:
        expand_before, shrink_before = refs[:2]
        (
            keep_ref,
            away_ref,
            land_hbm,
            hidden_part,
            branch_part,
            activated_ref,
            lifted_grad_ref,
            hidden_sum,
            branch_sum,
            send_ref,
            land_ref,
            near_send,
            near_recv,
            load_sem,
        ) = refs[2 + later :]
        outer = lax.axis_index("outer")
        far, near = outer // 2, outer % 2
        near_id = {"outer": outer + 1 - 2 * near}

        def near_copy(tile, k):
            return pltpu.make_async_remote_copy(
                src_ref=send_ref.at[k],
                dst_ref=land_hbm.at[tile, k],
                send_sem=near_send.at[tile, k],
                recv_sem=near_recv.at[tile, k],
                device_id=near_id,
                device_id_type=MESH,
            )

        def load(tile, k):
            return pltpu.make_async_copy(land_hbm.at[tile, k], land_ref.at[k], load_sem.at[k])

        @pl.when(step == 0)
        def _():
            barrier = pltpu.get_barrier_semaphore()
            pl.semaphore_signal(
                barrier, inc=1, device_id=near_id, device_id_type=MESH
            )
            pl.semaphore_wait(barrier, 1)

        for tile in range(2):

            @pl.when(step == 2 + tile)
            def _(tile=tile):
                for k in range(2):
                    near_copy(tile, k).wait_recv()
                    load(tile, k).start()

    else:
        (
            expand_grad,
            shrink_grad,
            hidden_part,
            branch_part,
            activated_ref,
            lifted_grad_ref,
            hidden_sum,
            branch_sum,
        ) = refs
    tokens = hidden_ref.shape[0]
    nt = (((1,), (1,)), ((), ()))
    tn = (((0,), (0,)), ((), ()))
    slope = 0.7978845608028654

    def block(at, first):
        hidden = hidden_ref[at, :]
        back = back_ref[at, :]
        lifted = jnp.dot(hidden, expand_ref[...], preferred_element_type=f32)
        active_grad = lax.dot_general(back, shrink_ref[...], nt, preferred_element_type=f32)
        square = lifted * lifted
        curve = jnp.tanh(slope * (lifted + 0.044715 * (square * lifted)))
        rise = 0.5 * (1.0 + curve)
        activated = (lifted * rise).astype(jnp.bfloat16)
        bend = 0.5 * lifted * (1.0 - curve * curve) * (slope + (3.0 * 0.044715 * slope) * square)
        lifted_grad = (active_grad * (rise + bend)).astype(jnp.bfloat16)
        activated_ref[at, :] = activated
        lifted_grad_ref[at, :] = lifted_grad
        branch = jnp.dot(activated, shrink_ref[...], preferred_element_type=f32)
        hidden_grad = lax.dot_general(lifted_grad, expand_ref[...], nt, preferred_element_type=f32)
        if first:
            branch_sum[at, :] = branch
            hidden_sum[at, :] = hidden_grad
        else:
            branch_sum[at, :] += branch
            hidden_sum[at, :] += hidden_grad

    def blocks(first):
        def one(i, _):
            block(pl.ds(pl.multiple_of(i * ROWS, ROWS), ROWS), first)
            return 0

        lax.fori_loop(0, tokens // ROWS, one, 0)

    @pl.when(step == 0)
    def _():
        blocks(True)

    @pl.when(step > 0)
    def _():
        blocks(False)

    def gradient(k):
        made_of = ((activated_ref, back_ref), (lifted_grad_ref, hidden_ref))[k]
        made = lax.dot_general(made_of[0][...], made_of[1][...], tn, preferred_element_type=f32)
        return made + (shrink_before, expand_before)[k][...] if exchange else made

    if not exchange:
        shrink_grad[...] = gradient(0)
        expand_grad[...] = gradient(1)
    else:
        for tile in range(2):

            @pl.when(step == tile)
            def _(tile=tile):
                for k in range(2):
                    if tile:
                        near_copy(tile - 1, k).wait_send()
                    send_ref[k] = gradient(k)
                    near_copy(tile, k).start()

            @pl.when(step == 2 + tile)
            def _(tile=tile):
                for k in range(2):
                    load(tile, k).wait()
                    total = gradient(k) + land_ref[k]

                    @pl.when(far == tile)
                    def _():
                        keep_ref[k] = total

                    @pl.when(far != tile)
                    def _():
                        away_ref[k] = total.astype(jnp.bfloat16)

                    if tile == 0:
                        near_copy(1, k).wait_send()

    @pl.when(step == steps - 1)
    def _():
        hidden_part[...] = hidden_sum[...].astype(hidden_part.dtype)
        branch_part[...] = branch_sum[...].astype(branch_part.dtype)


def feed(hidden, back, expand, shrink, before, branch_type, after=()):
    tokens, width = hidden.shape
    units = 2 * expand.shape[2]
    steps = 4
    tile = units // steps
    exchange = bool(before)
    low, f32 = jnp.bfloat16, jnp.float32
    turn = steps // 2 if exchange else 0
    whole = pl.BlockSpec((tokens, width), lambda n: (0, 0), pipeline_mode=pl.Buffered(1))
    rows = pl.BlockSpec((tile, width), lambda n: ((n + turn) % steps, 0))
    quarter = pl.BlockSpec((2, tile, width), lambda n: (0, 0, 0), pipeline_mode=pl.Buffered(1))
    columns = pl.BlockSpec(
        (None, width, tile),
        lambda n: ((n + turn) % steps // 2, 0, (n + turn) % 2),
    )
    grads = jax.ShapeDtypeStruct((units, width), f32)
    sem = pltpu.SemaphoreType.DMA
    return pl.pallas_call(
        partial(feed_kernel, exchange, len(after)),
        grid=(steps,),
        in_specs=[whole, whole, columns, rows]
        + [rows, rows] * exchange
        + [pl.BlockSpec(memory_space=pl.ANY)] * len(after),
        out_specs=(
            [quarter, quarter, pl.BlockSpec(memory_space=pl.ANY)] if exchange else [rows, rows]
        )
        + [whole, whole],
        out_shape=(
            [
                jax.ShapeDtypeStruct((2, tile, width), f32),
                jax.ShapeDtypeStruct((2, tile, width), low),
                jax.ShapeDtypeStruct((2, 2, tile, width), f32),
            ]
            if exchange
            else [grads, grads]
        )
        + [
            jax.ShapeDtypeStruct((tokens, width), f32),
            jax.ShapeDtypeStruct((tokens, width), branch_type),
        ],
        scratch_shapes=[
            pltpu.VMEM((tokens, tile), low),
            pltpu.VMEM((tokens, tile), low),
            pltpu.VMEM((tokens, width), f32),
            pltpu.VMEM((tokens, width), f32),
        ]
        + [
            pltpu.VMEM((2, tile, width), f32),
            pltpu.VMEM((2, tile, width), f32),
            sem((2, 2)),
            sem((2, 2)),
            sem((2,)),
        ]
        * exchange,
        compiler_params=pltpu.CompilerParams(
            vmem_limit_bytes=60 * 2**20,
            **(dict(collective_id=4, has_side_effects=True) if exchange else {}),
        ),
        cost_estimate=pl.CostEstimate(flops=2**20, bytes_accessed=2**20, transcendentals=0),
    )(hidden, back, expand, shrink, *before, *after)


def opening_kernel(
    expand_hbm,
    shrink_hbm,
    project_hbm,
    mixing_hbm,
    inputs_hbm,
    norm_ref,
    back_ref,
    expand_out,
    shrink_out,
    later_out,
    norm_out,
    hidden_ref,
    other_back,
    expand_ref,
    shrink_ref,
    project_ref,
    mixing_ref,
    inputs_ref,
    expand_low,
    shrink_low,
    norm_low,
    norm_all,
    load_sem,
    own_sem,
    norm_send,
    norm_recv,
    line_send,
    line_recv,
    far_send,
    far_recv,
    near_send,
    near_recv,
    row_sem,
):
    place, deep = lax.axis_index("dp"), 4
    outer = lax.axis_index("outer")
    far, near = outer // 2, outer % 2
    far_id = {"outer": (outer + 2) % 4}
    near_id = {"outer": outer + 1 - 2 * near}
    rows = expand_ref.shape[0]
    half = expand_ref.shape[1] // 2
    part = half // 2

    loads = [
        pltpu.make_async_copy(source, target, load_sem.at[n])
        for n, (source, target) in enumerate(
            (
                (expand_hbm, expand_ref),
                (shrink_hbm, shrink_ref),
                (project_hbm, project_ref),
                (mixing_hbm, mixing_ref),
                (inputs_hbm, inputs_ref),
            )
        )
    ]
    loads[0].start()
    loads[1].start()
    barrier = pltpu.get_barrier_semaphore()
    for step in range(1, deep):
        pl.semaphore_signal(
            barrier, inc=1, device_id={"dp": (place + step) % deep}, device_id_type=MESH
        )
    pl.semaphore_signal(barrier, inc=1, device_id=far_id, device_id_type=MESH)
    pl.semaphore_signal(barrier, inc=1, device_id=near_id, device_id_type=MESH)
    row_id = {"mp": 1 - lax.axis_index("mp")}
    pl.semaphore_signal(barrier, inc=1, device_id=row_id, device_id_type=MESH)

    for load in loads[2:]:
        load.start()
    norm_low[...] = jnp.zeros_like(norm_low)
    norm_low[0:2] = norm_ref[...].astype(jnp.bfloat16).astype(jnp.float32)
    pl.semaphore_wait(barrier, deep + 2)

    def piece(w, which, at, side):
        across = pl.ds(pl.multiple_of(at * rows, rows), rows)
        along = pl.ds(pl.multiple_of(side * part, part), part)
        if w == 0:
            return expand_out.at[which, across, along]
        return shrink_out.at[which, along, across]

    def mine(w):
        along = pl.ds(pl.multiple_of(near * half + far * part, part), part)
        return expand_low.at[:, along] if w == 0 else shrink_low.at[along, :]

    def remote(source, target, send, recv, device):
        return pltpu.make_async_remote_copy(
            src_ref=source,
            dst_ref=target,
            send_sem=send,
            recv_sem=recv,
            device_id=device,
            device_id_type=MESH,
        )

    def line(w, way, step, source, at):
        to = place + 1 if way == 0 else place - 1
        return remote(
            source,
            piece(w, 0, at, far),
            line_send.at[w, way, step],
            line_recv.at[w, way, step],
            {"dp": to},
        )

    def can_send(way):
        return place < deep - 1 if way == 0 else place > 0

    def start_own(w):
        for way in range(2):

            @pl.when(can_send(way))
            def _(way=way):
                line(w, way, 0, mine(w), place).start()

    def own_copies(w):
        out = []
        for which in range(2):
            side = near + which - 2 * near * which
            along = pl.ds(pl.multiple_of(side * half, half), half)
            across = pl.ds(pl.multiple_of(place * rows, rows), rows)
            if w == 0:
                pair = (expand_low.at[:, along], expand_out.at[which, across, :])
            else:
                pair = (shrink_low.at[along, :], shrink_out.at[which, :, across])
            out.append(pltpu.make_async_copy(*pair, own_sem.at[w, which]))
        return out

    row_copy = remote(back_ref, other_back, row_sem.at[0], row_sem.at[1], row_id)
    row_copy.start()
    loads[0].wait()
    expand_low[...] = expand_ref[...].astype(jnp.bfloat16)
    start_own(0)
    norm_copies = []
    for step in range(1, deep):
        copy = remote(
            norm_low,
            norm_all.at[step],
            norm_send.at[step],
            norm_recv.at[step],
            {"dp": (place + step) % deep},
        )
        copy.start()
        norm_copies.append(copy)
    loads[1].wait()
    shrink_low[...] = shrink_ref[...].astype(jnp.bfloat16)
    start_own(1)
    for w in range(2):
        for copy in own_copies(w):
            copy.start()
    for load in loads[2:]:
        load.wait()
    first = 0
    for source in (project_ref, mixing_ref):
        units = source.shape[0] // 2
        later_out[first : first + units] = source[
            pl.ds(pl.multiple_of(near * units, units), units), :
        ].astype(jnp.bfloat16)
        first += units
    norm_all[0] = norm_low[...]
    for copy in norm_copies:
        copy.wait()
    for at in range(deep):
        norm_out[:, at * rows : (at + 1) * rows] = norm_all[(place - at + deep) % deep]
    gain, bias = norm_out[0:1], norm_out[1:2]
    tokens = inputs_ref.shape[0]
    height = 128

    def normalize(i, _):
        at = pl.ds(pl.multiple_of(i * height, height), height)
        x = inputs_ref[at, :].astype(jnp.float32)
        mean = jnp.mean(x, axis=1, keepdims=True)
        centred = x - mean
        spread = jnp.mean(centred * centred, axis=1, keepdims=True)
        normed = centred * lax.rsqrt(spread + norm_epsilon)
        hidden_ref[at, :] = (normed * gain + bias).astype(jnp.bfloat16)
        return 0

    lax.fori_loop(0, tokens // height, normalize, 0)

    def arrives(way, step):
        return place >= step if way == 0 else place + step < deep

    def at_of(way, step):
        return place - step if way == 0 else place + step

    def to_far(w, way, step):
        at = at_of(way, step)
        return remote(
            piece(w, 0, at, far),
            piece(w, 0, at, far),
            far_send.at[w, way, step - 1],
            far_recv.at[w, way, step - 1],
            far_id,
        )

    def from_far(w, way, step):
        at = at_of(way, step)
        return remote(
            piece(w, 0, at, 1 - far),
            piece(w, 0, at, 1 - far),
            far_send.at[w, way, step - 1],
            far_recv.at[w, way, step - 1],
            far_id,
        )

    def to_near(w, way, step, other):
        at = at_of(way, step)
        side = 1 - far if other else far
        return remote(
            piece(w, 0, at, side),
            piece(w, 1, at, side),
            near_send.at[w, way, step - 1, other],
            near_recv.at[w, way, step - 1, other],
            near_id,
        )

    order = [(w, step) for w in range(2) for step in range(1, deep)]

    def first_half(w, step):
        for way in range(2):

            @pl.when(arrives(way, step))
            def _(way=way):
                at = at_of(way, step)
                line(w, way, step - 1, mine(w), at).wait_recv()
                if step < deep - 1:

                    @pl.when(can_send(way))
                    def _():
                        line(w, way, step, piece(w, 0, at, far), at).start()

                to_far(w, way, step).start()
                to_near(w, way, step, 0).start()

    def second_half(w, step):
        for way in range(2):

            @pl.when(arrives(way, step))
            def _(way=way):
                from_far(w, way, step).wait_recv()
                to_near(w, way, step, 1).start()

    for n, (w, step) in enumerate(order):
        first_half(w, step)
        if n:
            second_half(*order[n - 1])
    second_half(*order[-1])
    row_copy.wait()
    for w in range(2):
        for copy in own_copies(w):
            copy.wait()
        for way in range(2):

            @pl.when(can_send(way))
            def _(way=way):
                line(w, way, 0, mine(w), place).wait_send()

            for step in range(1, deep):

                @pl.when(arrives(way, step))
                def _(way=way, step=step):
                    at = at_of(way, step)
                    if step < deep - 1:

                        @pl.when(can_send(way))
                        def _():
                            line(w, way, step, piece(w, 0, at, far), at).wait_send()

                    to_far(w, way, step).wait_send()
                    for other in range(2):
                        to_near(w, way, step, other).wait_send()
                        to_near(w, way, step, other).wait_recv()


def project_kernel(hidden_ref, back_ref, own_ref, sibling_ref, projected_ref, mixed_back_ref):
    nt = (((1,), (1,)), ((), ()))
    cut = own_ref.shape[0] * 3 // 4
    few = own_ref.shape[0] - cut
    for n, weights in enumerate((own_ref, sibling_ref)):
        projected_ref[n * cut : (n + 1) * cut] = lax.dot_general(
            weights[:cut], hidden_ref[...], nt, preferred_element_type=jnp.float32
        )
        mixed_back_ref[n * few : (n + 1) * few] = lax.dot_general(
            weights[cut:], back_ref[...], nt, preferred_element_type=jnp.float32
        ).astype(jnp.bfloat16)


def project_all(hidden, back, own, sibling):
    tokens, width = hidden.shape
    cut = own.shape[0] * 3 // 4
    rows = pl.BlockSpec((256, width), lambda n: (n, 0))
    whole = pl.BlockSpec(own.shape, lambda n: (0, 0), pipeline_mode=pl.Buffered(1))
    columns = lambda height: pl.BlockSpec((height, 256), lambda n: (0, n))
    return pl.pallas_call(
        project_kernel,
        grid=(tokens // 256,),
        in_specs=[rows, rows, whole, whole],
        out_specs=[columns(2 * cut), columns(2 * (own.shape[0] - cut))],
        out_shape=[
            jax.ShapeDtypeStruct((2 * cut, tokens), jnp.float32),
            jax.ShapeDtypeStruct((2 * (own.shape[0] - cut), tokens), jnp.bfloat16),
        ],
        compiler_params=pltpu.CompilerParams(vmem_limit_bytes=60 * 2**20),
        cost_estimate=pl.CostEstimate(flops=2**20, bytes_accessed=2**20, transcendentals=0),
    )(hidden, back, own, sibling)


def opening(expand, shrink, project, mixing, norm, inputs, back):
    deep = 4
    here = lambda: pl.BlockSpec(memory_space=pltpu.VMEM)
    rows, units = expand.shape
    later = project.shape[0] + mixing.shape[0]
    low = jnp.bfloat16
    sem = pltpu.SemaphoreType.DMA
    return pl.pallas_call(
        opening_kernel,
        in_specs=[pl.BlockSpec(memory_space=pl.ANY)] * 5
        + [here(), pl.BlockSpec(memory_space=pl.ANY)],
        out_specs=[pl.BlockSpec(memory_space=pl.ANY)] * 2
        + [here() for _ in range(3)]
        + [pl.BlockSpec(memory_space=pl.ANY)],
        out_shape=[
            jax.ShapeDtypeStruct((2, rows * deep, units // 2), low),
            jax.ShapeDtypeStruct((2, units // 2, rows * deep), low),
            jax.ShapeDtypeStruct((later // 2, project.shape[1]), low),
            jax.ShapeDtypeStruct((8, rows * deep), jnp.float32),
            jax.ShapeDtypeStruct(inputs.shape, low),
            jax.ShapeDtypeStruct(back.shape, low),
        ],
        scratch_shapes=[
            pltpu.VMEM(v.shape, v.dtype) for v in (expand, shrink, project, mixing, inputs)
        ]
        + [
            pltpu.VMEM(expand.shape, low),
            pltpu.VMEM(shrink.shape, low),
            pltpu.VMEM((8, norm.shape[1]), jnp.float32),
            pltpu.VMEM((deep, 8, norm.shape[1]), jnp.float32),
            sem((5,)),
            sem((2, 2)),
            sem((deep,)),
            sem((deep,)),
            sem((2, 2, deep)),
            sem((2, 2, deep)),
            sem((2, 2, deep)),
            sem((2, 2, deep)),
            sem((2, 2, deep, 2)),
            sem((2, 2, deep, 2)),
            sem((2,)),
        ],
        compiler_params=pltpu.CompilerParams(
            collective_id=1, has_side_effects=True, vmem_limit_bytes=60 * 2**20
        ),
        cost_estimate=pl.CostEstimate(flops=0, bytes_accessed=2**20, transcendentals=0),
    )(expand, shrink, project, mixing, inputs, norm, back)


def closing_kernel(
    later,
    own_weights,
    sibling_weights,
    *refs,
):
    sources = (own_weights, *refs[:9])
    part_own, part_other, feed_keep, feed_come, gain_ref = refs[9:14]
    input_grad, small_sum, mixed_come = refs[14 + later : 17 + later]
    full_refs = refs[17 + later : 21 + later]
    refs = refs[21 + later :]
    held = refs[:10]
    (
        part_in,
        total_ref,
        sent_ref,
        come_ref,
        project_land,
        project_own,
        mixing_land,
        mixing_own,
        project_far,
        project_come,
        mixing_far,
        mixing_come,
        project_line,
        project_lands,
        mixing_line,
        mixing_lands,
        feed_in,
        feed_line,
        feed_lands,
        feed_share,
        expand_share,
        project_share,
        mixing_share,
        small_ref,
        plane_lands,
        deep_lands,
        held_sem,
        half_sem,
        part_sem,
        out_sem,
        feed_sem,
        feed_send,
        feed_recv,
        spread_sem,
        spread_far_send,
        spread_far_recv,
        spread_near_send,
        spread_near_recv,
        plane_send,
        plane_recv,
        deep_send,
        deep_recv,
        row_send,
        row_recv,
        mixed_sem,
        near_send,
        near_recv,
        far_send,
        far_recv,
        line_send,
        line_recv,
    ) = refs[10:]
    (
        project,
        grads_other,
        grads_own,
        hidden_other,
        hidden_own,
        mixed_other,
        mixed_own,
        back_other,
        back_own,
        inputs,
    ) = held
    low, f32 = jnp.bfloat16, jnp.float32
    tn = (((0,), (0,)), ((), ()))
    place, deep, outers = lax.axis_index("dp"), 4, 4
    outer = lax.axis_index("outer")
    far, near = outer // 2, outer % 2
    row_id = {"mp": 1 - lax.axis_index("mp")}
    far_id = {"outer": (outer + 2) % 4}
    near_id = {"outer": outer + 1 - 2 * near}

    copies = [
        pltpu.make_async_copy(source, target, held_sem.at[n])
        for n, (source, target) in enumerate(zip(sources, held))
        if n
    ]
    copies.insert(0, None)
    quarter = feed_keep.shape[1]
    feed_copies = [
        (
            pltpu.make_async_copy(
                feed_keep.at[k],
                total_ref.at[slice(k * quarter, (k + 1) * quarter)],
                feed_sem.at[k],
            ),
            pltpu.make_async_copy(feed_come.at[k], feed_in.at[k], feed_sem.at[2 + k]),
        )
        for k in range(2)
    ]
    for pair in feed_copies:
        for copy in pair:
            copy.start()
    cut = project.shape[0] // 2
    halves = [
        pltpu.make_async_copy(
            source.at[slice(0, cut)], project.at[slice(n * cut, (n + 1) * cut)], half_sem.at[n]
        )
        for n, source in enumerate((own_weights, sibling_weights))
    ]
    for copy in (*halves, copies[1]):
        copy.start()
    barrier = pltpu.get_barrier_semaphore()
    plane = 2 * outers
    me = lax.axis_index("mp") * outers + outer

    def plane_id(step):
        other = (me + step) % plane
        return {"mp": other // outers, "outer": other % outers}

    for step in range(1, plane):
        pl.semaphore_signal(barrier, inc=1, device_id=plane_id(step), device_id_type=MESH)
    for step in range(1, deep):
        pl.semaphore_signal(
            barrier, inc=1, device_id={"dp": (place + step) % deep}, device_id_type=MESH
        )
    height = 256
    tokens, width = hidden_own.shape
    blocks = tokens // height
    at = [slice(n * height, (n + 1) * height) for n in range(blocks)]

    def remote(source, target, send, recv, device):
        return pltpu.make_async_remote_copy(
            src_ref=source,
            dst_ref=target,
            send_sem=send,
            recv_sem=recv,
            device_id=device,
            device_id_type=MESH,
        )

    loads = [
        pltpu.make_async_copy(source.at[at[n]], part_in.at[(k * blocks + n) % 2], part_sem.at[(k * blocks + n) % 2])
        for k, source in enumerate((part_other, part_own))
        for n in range(blocks)
    ]
    loads[0].start()
    loads[1].start()
    pl.semaphore_wait(barrier, plane + deep - 2)

    piece = width // deep

    def columns(place):
        return pl.ds(pl.multiple_of(place * piece, piece), piece)

    line_copies = []
    for k in range(2):
        for copy in feed_copies[k]:
            copy.wait()
        rows = slice(k * quarter, (k + 1) * quarter)
        for step in range(1, deep):
            target = (place + step) % deep
            feed_line[k, step - 1] = (
                total_ref[rows, columns(target)] + feed_in[k, :, columns(target)].astype(f32)
            ).astype(low)
            line_copies.append(
                remote(
                    feed_line.at[k, step - 1],
                    feed_lands.at[k, step - 1],
                    feed_send.at[k, step - 1],
                    feed_recv.at[k, step - 1],
                    {"dp": target},
                )
            )
            line_copies[-1].start()
        feed_share[k] = total_ref[rows, columns(place)] + feed_in[k, :, columns(place)].astype(f32)

    for copy in (*halves, copies[1]):
        copy.wait()
    for copy in copies[2:]:
        copy.start()
    row_copies = []
    for n in range(blocks):
        made = lax.dot_general(grads_other[:, at[n]], project[...], tn, preferred_element_type=f32)
        loads[n].wait()
        sent_ref[at[n], :] = (part_in[n % 2] + made).astype(low)
        loads[n + 2].start()
        copy = remote(
            sent_ref.at[at[n]], come_ref.at[at[n]], row_send.at[n], row_recv.at[n], row_id
        )
        copy.start()
        row_copies.append(copy)

    copies[5].wait()
    mixed_copy = remote(
        mixed_other.at[slice(0, mixed_come.shape[0])],
        mixed_come,
        mixed_sem.at[0],
        mixed_sem.at[1],
        row_id,
    )
    mixed_copy.start()

    for n in (2, 3, 4, 6, 7, 8):
        copies[n].wait()
    half = project_own.shape[0]
    few = mixing_own.shape[0]
    near_copies = []
    for n in range(half // height):
        rows = slice(half + n * height, half + (n + 1) * height)
        total_ref[at[n], :] = jnp.dot(
            grads_own[rows, :], hidden_own[...], preferred_element_type=f32
        ) + jnp.dot(grads_other[rows, :], hidden_other[...], preferred_element_type=f32)
        near_copies.append(
            remote(
                total_ref.at[at[n]],
                project_land.at[at[n]],
                near_send.at[n],
                near_recv.at[n],
                near_id,
            )
        )
        near_copies[-1].start()
    total_ref[half : half + few, :] = jnp.dot(
        mixed_own[few:, :], back_own[...], preferred_element_type=f32
    ) + jnp.dot(mixed_other[few:, :], back_other[...], preferred_element_type=f32)
    near_copies.append(
        remote(
            total_ref.at[slice(half, half + few)],
            mixing_land,
            near_send.at[3],
            near_recv.at[3],
            near_id,
        )
    )
    near_copies[-1].start()
    for n in range(half // height):
        made = jnp.dot(
            grads_own[at[n], :], hidden_own[...], preferred_element_type=f32
        ) + jnp.dot(grads_other[at[n], :], hidden_other[...], preferred_element_type=f32)
        near_copies[n].wait()
        project_own[at[n], :] = made + project_land[at[n], :]

    def to_far(own, send, come, n):
        size = send.shape[0]
        send[...] = own[pl.ds(pl.multiple_of((1 - far) * size, size), size), :].astype(low)
        copy = remote(send, come, far_send.at[n], far_recv.at[n], far_id)
        copy.start()
        return copy

    far_copies = [to_far(project_own, project_far, project_come, 0)]
    made = jnp.dot(mixed_own[:few, :], back_own[...], preferred_element_type=f32) + jnp.dot(
        mixed_other[:few, :], back_other[...], preferred_element_type=f32
    )
    near_copies[3].wait()
    mixing_own[...] = made + mixing_land[...]
    far_copies.append(to_far(mixing_own, mixing_far, mixing_come, 1))

    for n in range(blocks):
        made = lax.dot_general(grads_own[:, at[n]], project[...], tn, preferred_element_type=f32)
        loads[blocks + n].wait()
        total_ref[at[n], :] = part_in[(blocks + n) % 2] + made
        if n + 2 < blocks:
            loads[blocks + n + 2].start()

    for k, (own, come, line, lands) in enumerate(
        (
            (project_own, project_come, project_line, project_lands),
            (mixing_own, mixing_come, mixing_line, mixing_lands),
        )
    ):
        size = come.shape[0]
        keep = pl.ds(pl.multiple_of(far * size, size), size)
        far_copies[k].wait()
        own[keep, :] = own[keep, :] + come[...].astype(f32)
        for step in range(1, deep):
            target = (place + step) % deep
            line[step - 1] = own[keep, columns(target)].astype(low)
            copy = remote(
                line.at[step - 1],
                lands.at[step - 1],
                line_send.at[k, step - 1],
                line_recv.at[k, step - 1],
                {"dp": target},
            )
            copy.start()
            line_copies.append(copy)

    shares = (feed_share.at[0], expand_share, project_share, mixing_share)

    def place_in(k, near, far):
        if k == 1:
            return full_refs[k].at[:, pl.ds(pl.multiple_of((2 * near + far) * quarter, quarter), quarter)]
        size = shares[k].shape[0]
        return full_refs[k].at[pl.ds(pl.multiple_of((2 * near + far) * size, size), size)]

    def spread(k):
        if k < 2:
            result, lands = feed_share[k], feed_lands.at[k]
        else:
            own, lands = ((project_own, project_lands), (mixing_own, mixing_lands))[k - 2]
            size = shares[k].shape[0]
            result = own[pl.ds(pl.multiple_of(far * size, size), size), columns(place)]
        for copy in line_copies[3 * k : 3 * k + 3]:
            copy.wait()
        for step in range(1, deep):
            result = result + lands[step - 1].astype(f32)
        shares[k][...] = result.T if k == 1 else result
        here = place_in(k, near, far)
        copies = [
            pltpu.make_async_copy(shares[k], here, spread_sem.at[k]),
            remote(shares[k], here, spread_far_send.at[k], spread_far_recv.at[k], far_id),
            remote(shares[k], here, spread_near_send.at[k, 0], spread_near_recv.at[k, 0], near_id),
        ]
        for copy in copies:
            copy.start()
        return copies, jnp.sum(result * result)

    def pass_on(k, copies):
        copies[1].wait()
        there = place_in(k, near, 1 - far)
        copy = remote(
            there, there, spread_near_send.at[k, 1], spread_near_recv.at[k, 1], near_id
        )
        copy.start()
        return copy

    copies[9].wait()
    gain = gain_ref[0:1]
    gain_sum = jnp.zeros((1, width), f32)
    bias_sum = jnp.zeros((1, width), f32)
    out_copies, spreads, passed = [], [], []
    square = jnp.float32(0.0)
    for n in range(blocks):
        if n == blocks - 2:
            for k in range(2):
                copies, more = spread(k)
                spreads.append(copies)
                square = square + more
        if n == blocks - 1:
            for k in range(2, 4):
                copies, more = spread(k)
                spreads.append(copies)
                square = square + more
        row_copies[n].wait()
        if n >= 2:
            out_copies[n - 2].wait()

        def some(i, carry):
            gain_sum, bias_sum = carry
            small = 64
            rows = pl.ds(pl.multiple_of(n * height + i * small, small), small)
            x = inputs[rows, :].astype(f32)
            mean = jnp.mean(x, axis=1, keepdims=True)
            centred = x - mean
            spread = jnp.mean(centred * centred, axis=1, keepdims=True)
            inverse = lax.rsqrt(spread + norm_epsilon)
            normed = centred * inverse
            grad = total_ref[rows, :] + come_ref[rows, :].astype(f32)
            scaled = grad * gain
            middle = jnp.mean(scaled, axis=1, keepdims=True)
            along = jnp.mean(scaled * normed, axis=1, keepdims=True)
            result = inverse * (scaled - middle - normed * along)
            part_in[n % 2, pl.ds(pl.multiple_of(i * small, small), small), :] = (
                back_own[rows, :].astype(f32) + result
            )
            gain_sum = gain_sum + jnp.sum(grad * normed, axis=0, keepdims=True)
            bias_sum = bias_sum + jnp.sum(grad, axis=0, keepdims=True)
            return gain_sum, bias_sum

        gain_sum, bias_sum = lax.fori_loop(0, height // 64, some, (gain_sum, bias_sum))
        out_copies.append(
            pltpu.make_async_copy(part_in.at[n % 2], input_grad.at[at[n]], out_sem.at[n % 2])
        )
        out_copies[-1].start()
    for k in range(2):
        passed.append(pass_on(k, spreads[k]))

    small_ref[...] = jnp.full(small_ref.shape, square)
    small_ref[0:1] = gain_sum
    small_ref[1:2] = bias_sum

    def everywhere(lands, send, recv, size, index, device):
        copies = []
        for step in range(1, size):
            copy = remote(small_ref, lands.at[step], send.at[step], recv.at[step], device(step))
            copy.start()
            copies.append(copy)
        lands[0] = small_ref[...]
        for copy in copies:
            copy.wait()
        total = lands[index]
        for at in range(1, size):
            total = total + lands[(index + size - at) % size]
        small_ref[...] = total

    everywhere(plane_lands, plane_send, plane_recv, plane, me, plane_id)
    everywhere(
        deep_lands, deep_send, deep_recv, deep, place, lambda step: {"dp": (place + step) % deep}
    )
    for k in range(2, 4):
        passed.append(pass_on(k, spreads[k]))
    small = small_ref[0:2]
    norm = jnp.sqrt(small_ref[2:3] + jnp.sum(small * small))
    small_sum[...] = small_ref[...]
    small_sum[2:3] = norm
    small_sum[3:4] = clip_level / jnp.maximum(norm, clip_level)
    for k in range(4):
        spreads[k][0].wait()
        spreads[k][2].wait()
        passed[k].wait()
    mixed_copy.wait()
    for copy in out_copies[-2:]:
        copy.wait()


def closing(weights, grads, hiddens, mixed, backs, inputs, parts, feeds, gain, after):
    deep = 4
    low, f32 = jnp.bfloat16, jnp.float32
    tokens, width = inputs.shape
    half, few = grads[0].shape[0] // 2, mixed[0].shape[0] // 2
    piece = width // deep
    quarter = feeds[0].shape[1]
    anywhere = pl.BlockSpec(memory_space=pl.ANY)
    here = lambda: pl.BlockSpec(memory_space=pltpu.VMEM)
    held = (
        jax.ShapeDtypeStruct(grads[0].shape[:1] + (width,), low),
        grads[1],
        grads[0],
        hiddens[1],
        hiddens[0],
        mixed[1],
        mixed[0],
        backs[1],
        backs[0],
        inputs,
    )
    sem = pltpu.SemaphoreType.DMA
    space = pltpu.VMEM
    return pl.pallas_call(
        partial(closing_kernel, len(after)),
        in_specs=[anywhere] * 15 + [here()] + [anywhere] * len(after),
        out_specs=[anywhere, here()] + [anywhere] * 5,
        out_shape=[
            jax.ShapeDtypeStruct((tokens, width), f32),
            jax.ShapeDtypeStruct((8, width), f32),
            jax.ShapeDtypeStruct((few // 2, tokens), low),
        ]
        + [
            jax.ShapeDtypeStruct(shape, f32)
            for shape in (
                (4 * quarter, piece),
                (piece, 4 * quarter),
                (2 * half, piece),
                (2 * few, piece),
            )
        ],
        scratch_shapes=[space(v.shape, v.dtype) for v in held]
        + [
            space((2, 256, width), f32),
            space((tokens, width), f32),
            space((tokens, width), low),
            space((tokens, width), low),
            space((half, width), f32),
            space((half, width), f32),
            space((few, width), f32),
            space((few, width), f32),
            space((half // 2, width), low),
            space((half // 2, width), low),
            space((few // 2, width), low),
            space((few // 2, width), low),
            space((deep - 1, half // 2, piece), low),
            space((deep - 1, half // 2, piece), low),
            space((deep - 1, few // 2, piece), low),
            space((deep - 1, few // 2, piece), low),
            space((2, quarter, width), low),
            space((2, deep - 1, quarter, piece), low),
            space((2, deep - 1, quarter, piece), low),
            space((2, quarter, piece), f32),
            space((piece, quarter), f32),
            space((half // 2, piece), f32),
            space((few // 2, piece), f32),
            space((8, width), f32),
            space((8, 8, width), f32),
            space((deep, 8, width), f32),
            sem((len(held),)),
            sem((2,)),
            sem((2,)),
            sem((2,)),
            sem((4,)),
            sem((2, deep - 1)),
            sem((2, deep - 1)),
            sem((4,)),
            sem((4,)),
            sem((4,)),
            sem((4, 2)),
            sem((4, 2)),
            sem((8,)),
            sem((8,)),
            sem((deep,)),
            sem((deep,)),
            sem((tokens // 256,)),
            sem((tokens // 256,)),
            sem((2,)),
            sem((4,)),
            sem((4,)),
            sem((2,)),
            sem((2,)),
            sem((2, deep)),
            sem((2, deep)),
        ],
        compiler_params=pltpu.CompilerParams(
            collective_id=3, has_side_effects=True, vmem_limit_bytes=62 * 2**20
        ),
        cost_estimate=pl.CostEstimate(flops=2**20, bytes_accessed=2**20, transcendentals=0),
    )(*weights, *held[1:], *parts, *feeds, gain, *after)


def local(
    inputs,
    cotangent,
    lengths,
    project_master,
    project_first,
    project_second,
    mixing_master,
    mixing_first,
    mixing_second,
    expand_master,
    expand_first,
    expand_second,
    shrink_master,
    shrink_first,
    shrink_second,
    norm_master,
    norm_first,
    norm_second,
):
    split, deep = lax.axis_size("mp"), lax.axis_size("dp")
    heads_here = project_master.shape[1]
    width = inputs.shape[1]
    paired = (
        split == 2
        and lax.axis_size("outer") == 4
        and heads_here % 4 == 0
        and width % BQ == 0
    )
    position = lax.axis_index("mp")
    count = width * split
    project_flat = project_master.transpose(1, 2, 0).reshape(heads_here * 3 * HD, -1)
    mixing_flat = mixing_master.reshape(heads_here * HD, mixing_master.shape[2])
    masters = (project_flat, mixing_flat, expand_master, shrink_master)
    depths = (1, 1, 0, 1)
    rows_local = inputs[0].astype(jnp.float32)
    begins, places = layout(lengths[0], count)
    cosine, sine = turns(places)
    if paired:
        expand, shrink, later, norm_weight, hidden_local, other_back = opening(
            expand_master,
            shrink_master,
            project_flat,
            mixing_flat,
            norm_master,
            inputs[0],
            cotangent[0],
        )
        backs = [cotangent[0], other_back]
        shrink = shrink.reshape(-1, shrink.shape[2])
        later = lax.all_gather(later, "dp", axis=1, tiled=True)
        hiddens = [hidden_local, swap(hidden_local, "mp", 1)]
    else:
        norm_weight = lax.all_gather(norm_master.astype(jnp.bfloat16), "dp", axis=1, tiled=True)
        gain = norm_weight[0].astype(jnp.float32)
        bias = norm_weight[1].astype(jnp.float32)
        shaped, norm_pull = jax.vjp(layer_norm, rows_local, gain, bias)
        hidden_local = shaped.astype(jnp.bfloat16)
        project, mixing, expand, shrink = (
            lax.all_gather(master.astype(jnp.bfloat16), "dp", axis=depth, tiled=True)
            for master, depth in zip(masters, depths)
        )
        backs = [lax.all_gather(cotangent[0], "mp", axis=0, tiled=True)]
        hiddens = [lax.all_gather(hidden_local, "mp", axis=0, tiled=True)]

    def over_tokens(pattern, lefts, rights):
        return sum(product(pattern, left, right) for left, right in zip(lefts, rights))

    back_local = cotangent[0].astype(jnp.float32)
    if paired:
        *grads, hidden_own, branch_own = feed(
            hiddens[0], backs[0], expand, shrink, (), jnp.float32
        )
        later = follow(later, branch_own)
        later = [later, swap(later, "outer", 1)]
        cut = later[0].shape[0] * 3 // 4
        mixing = jnp.concatenate([v[cut:] for v in later])
        own_columns = project_all(hiddens[0], backs[0], *later)
        feed_keep, feed_away, _, hidden_other, branch_other = feed(
            hiddens[1], backs[1], expand, follow(shrink, *own_columns), grads, jnp.bfloat16
        )
        feed_come = swap(feed_away, "outer", 2)
        branch_come = swap(branch_other, "mp", 1)
        mixing_other = swap(mixing, "mp", 1)
        other_columns = project_all(hiddens[1], backs[1], *later)
        projected, mixed_backs = zip(own_columns, other_columns)
        mixed, projected_grads = attend(
            projected,
            mixed_backs,
            begins,
            cosine,
            sine,
            position,
            (feed_away, branch_other),
        )
        input_grad, small_sum, mixed_come, shrink_sum, expand_sum, project_sum, mixing_sum = closing(
            later,
            projected_grads,
            hiddens,
            mixed,
            backs,
            inputs[0],
            (hidden_own, hidden_other),
            (feed_keep, feed_come),
            norm_weight,
            (branch_come,),
        )
        mixed_own = follow(mixed[0], small_sum)
        few = mixed_come.shape[0]
        mixed_last = swap(follow(mixed[1], small_sum)[few:], "mp", 1)
        branch = (
            branch_own
            + branch_come.astype(jnp.float32)
            + product("ft,fd->td", mixed_own, mixing)
            + product("ft,fd->td", mixed_come, mixing_other[:few])
            + product("ft,fd->td", mixed_last, mixing_other[few:])
        )
    else:
        lifteds = [product("td,df->tf", hidden, expand) for hidden in hiddens]
        activated = [gelu(lifted) for lifted in lifteds]
        active_grads = [product("td,fd->tf", back, shrink) for back in backs]
        lifted_grads = [gelu_both(a, b) for a, b in zip(lifteds, active_grads)]
        hidden_parts = [product("tf,df->td", v, expand) for v in lifted_grads]
        branch_parts = [product("tf,fd->td", v, shrink) for v in activated]
        projected = [product("td,ed->et", hidden, project) for hidden in hiddens]
        mixed_backs = [product("td,fd->ft", back, mixing).astype(jnp.bfloat16) for back in backs]
        mixed, projected_grads = attend(projected, mixed_backs, begins, cosine, sine, position)
        project_sum, mixing_sum, expand_sum, shrink_sum = (
            lax.psum(
                lax.psum_scatter(
                    over_tokens(pattern, lefts, rights),
                    "dp",
                    scatter_dimension=depth,
                    tiled=True,
                ),
                "outer",
            )
            for pattern, lefts, rights, depth in (
                ("et,td->ed", projected_grads, hiddens, 1),
                ("ft,td->fd", mixed, backs, 1),
                ("td,tf->df", hiddens, lifted_grads, 0),
                ("tf,td->fd", activated, backs, 1),
            )
        )
        hidden_grad, branch = (
            lax.psum_scatter(v, "mp", scatter_dimension=0, tiled=True)
            for v in (
                hidden_parts[0] + product("et,ed->td", projected_grads[0], project),
                branch_parts[0] + product("ft,fd->td", mixed[0], mixing),
            )
        )
        rows_grad, gain_grad, bias_grad = norm_pull(hidden_grad)
        input_grad = back_local + rows_grad
        norm_terms = jnp.stack([gain_grad, bias_grad])
    input_grad = input_grad[None]
    block_out = (rows_local + branch).astype(jnp.bfloat16)[None]
    sums = (project_sum, mixing_sum, expand_sum, shrink_sum)
    if not paired:
        own_square = sum(jnp.sum(v * v) for v in sums) / lax.axis_size("outer")
        small_sum = lax.psum(
            jnp.concatenate([norm_terms, jnp.full((1, D), own_square)]), ("mp", "dp", "outer")
        )
        square = small_sum[2, 0] + jnp.sum(small_sum[:2] * small_sum[:2])
        grad_norm = jnp.sqrt(square)
        factor = clip_level / jnp.maximum(grad_norm, clip_level)
    else:
        grad_norm, factor = small_sum[2, 0], small_sum[3, 0]
    norm_full = small_sum[:2]
    norm_gradient = lax.dynamic_slice_in_dim(
        norm_full, lax.axis_index("dp") * (D // deep), D // deep, 1
    )
    gradients = list(sums)
    gradients[0] = gradients[0].reshape(heads_here, 3 * HD, -1).transpose(2, 0, 1)
    gradients[1] = gradients[1].reshape(mixing_master.shape)
    gradients[:2] = lax.optimization_barrier(gradients[:2])
    states = (
        (project_master, project_first, project_second, D ** (-0.5)),
        (mixing_master, mixing_first, mixing_second, (D // 32) ** (-0.5)),
        (expand_master, expand_first, expand_second, D ** (-0.5)),
        (shrink_master, shrink_first, shrink_second, FF ** (-0.5)),
    )
    results = [block_out, input_grad]
    for (master, first, second, rate), gradient in zip(states, gradients):
        results += adam_update(master, first, second, factor * gradient, rate, decay_rate)
    results += adam_update(norm_master, norm_first, norm_second, factor * norm_gradient, 0.3, 0.0)
    return (*results, grad_norm)


def solution(mesh):
    in_specs = (
        P(("dp", "outer"), "mp", None),
        P(("dp", "outer"), "mp", None),
        P(("dp", "outer"), None),
        P("dp", "mp", None),
        P("dp", "mp", None),
        P("dp", "mp", None),
        P("mp", None, "dp"),
        P("mp", None, "dp"),
        P("mp", None, "dp"),
        P("dp", "mp"),
        P("dp", "mp"),
        P("dp", "mp"),
        P("mp", "dp"),
        P("mp", "dp"),
        P("mp", "dp"),
        P(None, "dp"),
        P(None, "dp"),
        P(None, "dp"),
    )
    out_specs = (
        P(("dp", "outer"), "mp", None),
        P(("dp", "outer"), "mp", None),
        P("dp", "mp", None),
        P("dp", "mp", None),
        P("dp", "mp", None),
        P("dp", "mp", None),
        P("mp", None, "dp"),
        P("mp", None, "dp"),
        P("mp", None, "dp"),
        P("mp", None, "dp"),
        P("dp", "mp"),
        P("dp", "mp"),
        P("dp", "mp"),
        P("dp", "mp"),
        P("mp", "dp"),
        P("mp", "dp"),
        P("mp", "dp"),
        P("mp", "dp"),
        P(None, "dp"),
        P(None, "dp"),
        P(None, "dp"),
        P(None, "dp"),
        P(),
    )
    return jax.shard_map(local, mesh=mesh, in_specs=in_specs, out_specs=out_specs, check_vma=False)
```
